32 devices in a mesh: dp: 8 (over z, x), mp: 4 (over y, core).
Axes of the slice: x: 2, y: 2, z: 4, core: 2. Of those that a mesh axis runs over, the one named last changes fastest.
Arguments:
- history: bfloat16 [13, 16384, 2048], P(None, 'dp', 'mp'), may hold values from -6 to 6
- depth_weights: float32 [13], replicated, may hold values from -1.5 to 1.5
- segment_ids: int32 [16, 1024], P('dp'), may hold values from 0 to 3, never falling along the last dimension, each value on 1 to 512 neighbouring positions
- first_gain: float32 [2048], P('mp'), may hold values from 0.5 to 1.5
- first_bias: float32 [2048], P('mp'), may hold values from -1.5 to 1.5
- qkv_weight: bfloat16 [2048, 6144], P(None, 'mp'), may hold values from -0.125 to 0.125
- out_weight: bfloat16 [2048, 2048], P('mp'), may hold values from -0.5 to 0.5
- second_gain: float32 [2048], P('mp'), may hold values from 0.5 to 1.5
- second_bias: float32 [2048], P('mp'), may hold values from -1.5 to 1.5
- up_weight: bfloat16 [2048, 8192], P(None, 'mp'), may hold values from -0.125 to 0.125
- up_bias: float32 [8192], P('mp'), may hold values from -1.5 to 1.5
- down_weight: bfloat16 [8192, 2048], P('mp'), may hold values from -0.0625 to 0.0625
- down_bias: float32 [2048], P('mp'), may hold values from -1.5 to 1.5
- cotangent: bfloat16 [16384, 2048], P('dp', 'mp'), may hold values from -7.2 to 7.2
Outputs:
- block_out: bfloat16 [16384, 2048], P('dp', 'mp')
- history_grad: bfloat16 [13, 16384, 2048], P(None, 'dp', 'mp')
- depth_grad: float32 [13], replicated
- first_gain_grad: float32 [2048], P('mp')
- first_bias_grad: float32 [2048], P('mp')
- qkv_weight_grad: float32 [2048, 6144], P('dp', 'mp')
- out_weight_grad: float32 [2048, 2048], P('mp', 'dp')
- second_gain_grad: float32 [2048], P('mp')
- second_bias_grad: float32 [2048], P('mp')
- up_weight_grad: float32 [2048, 8192], P('dp', 'mp')
- up_bias_grad: float32 [8192], P('mp')
- down_weight_grad: float32 [8192, 2048], P('mp', 'dp')
- down_bias_grad: float32 [2048], P('mp')
The draws below stay inside these ranges and needn't reach their ends.
Inputs may be any that keep to these rules, and one draw needn't show every extreme that they name: `segment_ids`: segment numbers never fall along a packed row; in each row every document holds at most 512 tokens and one holds exactly that many.
All inputs are finite; a program needn't handle non-finite values.
Results may differ from the reference program's by a relative error of at most 0.015.
Values may be sent and summed in bfloat16 or wider, within the bound.
A program may use at most 384 MiB of HBM per device.

```python
import math
import jax
import jax.numpy as jnp
import numpy as np
from jax import lax

D = 2048
HEADS = 16
HEAD = 128
FF = 8192
HIST = 13
SEQ = 1024
ROWS = 16
TOKENS = 16384


def draw_cotangent(key, part):
    key = jax.random.fold_in(key, 11)
    row_pos = jnp.arange(TOKENS, dtype=jnp.float32) / max(TOKENS - 1, 1)
    base_draw = jnp.clip(jax.random.normal(key, (TOKENS, D), jnp.float32), -4.0, 4.0)
    row_scale = 0.6 * jnp.exp(row_pos * 1.0986122886681098)
    return (base_draw * row_scale[:, None]).astype(jnp.bfloat16)


def shard_levels(own_key, extent, cuts, least, high):
    factor_of, own = 1.0, jax.random.fold_in(own_key, 6)
    for dim, parts in cuts:
        heights = jnp.exp(jax.random.uniform(jax.random.fold_in(own, dim), (parts,), jnp.float32, least / len(cuts), high / len(cuts)))
        factor_of = factor_of * jnp.repeat(heights, extent[dim] // parts).reshape([-1 if axis == dim else 1 for axis in range(len(extent))])
    return factor_of


def profile(count, total, limit, skew):
    weights = [(1 << 20) // math.isqrt(standing ** skew) + 1 for standing in range(2, count + 1)]
    rest, holding = total - limit - (count - 1), [1] * (count - 1)
    while rest > 0:
        free = [i for i in range(count - 1) if holding[i] < limit]
        pool, budget = sum([weights[i] for i in free]), rest
        for i in free:
            addition = min(limit - holding[i], max(1, budget * weights[i] // pool), rest)
            holding[i] = holding[i] + addition
            rest = rest - addition
    return np.array([limit] + holding)


def ragged_sizes(rng, amount, total, bound, skew):
    if amount == 2:
        one = jax.random.randint(rng, (), max(1, total - bound), min(bound, total - 1) + 1)
        return jnp.stack([one, total - one])
    sizes = jnp.asarray(profile(amount, total, bound, skew), jnp.int32)
    couples = (amount - 1) // 2
    source_of, taker = sizes[1:1 + 2 * couples:2], sizes[2:2 + 2 * couples:2]
    room = jnp.minimum(source_of - 1, bound - taker)
    shifted = jax.random.randint(jax.random.fold_in(rng, 1), (couples,), 0, 1 << 20) % (room + 1)
    sizes = sizes.at[1:1 + 2 * couples:2].set(source_of - shifted).at[2:2 + 2 * couples:2].set(taker + shifted)
    return sizes[jax.random.permutation(jax.random.fold_in(rng, 2), amount)]


def centred(stream_key, shape, spread, limit, cuts=(), kind=jnp.bfloat16):
    values = spread * jax.random.normal(stream_key, shape, jnp.float32)
    if cuts:
        values = values * shard_levels(stream_key, shape, cuts, -0.22, 0.18)
    return jnp.clip(values, -limit, limit).astype(kind)


def setup_inputs(seed: int = 0) -> dict:
    keys = jax.random.split(jax.random.key(seed), 15)
    return {
        "history": centred(keys[0], (HIST, TOKENS, D), 1.0, 6.0, ((1, 8), (2, 4))),
        "depth_weights": centred(keys[1], (HIST,), 0.3, 1.5, (), jnp.float32),
        "segment_ids": jax.vmap(lambda own: jnp.searchsorted(jnp.cumsum(ragged_sizes(own, 4, SEQ, SEQ // 2, 2)), jnp.arange(SEQ), side="right"))(jax.random.split(keys[2], ROWS)).reshape((ROWS, SEQ)).astype(jnp.int32),
        "first_gain": jnp.clip(1.0 + 0.1 * jax.random.normal(keys[3], (D,), jnp.float32), 0.5, 1.5),
        "first_bias": centred(keys[4], (D,), 0.3, 1.5, ((0, 4),), jnp.float32),
        "qkv_weight": centred(keys[5], (D, 3 * D), D ** -0.5, 0.125, ((1, 4),)),
        "out_weight": centred(keys[6], (D, D), (D // 16) ** -0.5, 0.5, ((0, 4),)),
        "second_gain": jnp.clip(1.0 + 0.1 * jax.random.normal(keys[7], (D,), jnp.float32), 0.5, 1.5),
        "second_bias": centred(keys[8], (D,), 0.3, 1.5, ((0, 4),), jnp.float32),
        "up_weight": centred(keys[9], (D, FF), D ** -0.5, 0.125, ((1, 4),)),
        "up_bias": centred(keys[10], (FF,), 0.3, 1.5, ((0, 4),), jnp.float32),
        "down_weight": centred(keys[11], (FF, D), FF ** -0.5, 0.0625, ((0, 4),)),
        "down_bias": centred(keys[12], (D,), 0.3, 1.5, ((0, 4),), jnp.float32),
        "cotangent": draw_cotangent(jax.random.fold_in(keys[14], 71), 0),
    }


EPSILON = 1e-05
EXACT = lax.Precision.HIGHEST
SQRT_HALF = 0.7071067811865476

@jax.custom_vjp
def low(v):
    return lax.optimization_barrier(v.astype(jnp.bfloat16)).astype(jnp.float32)

@jax.custom_vjp
def low_back(v):
    return v

def low_keep(v):
    return (low(v), None)

def low_pass(kept, grad):
    return (grad,)

def back_keep(v):
    return (v, None)

def back_low(kept, grad):
    return (low(grad),)
low.defvjp(low_keep, low_pass)
low_back.defvjp(back_keep, back_low)

def gelu_value(up_proj):
    return 0.5 * up_proj * (1.0 + lax.erf(up_proj * SQRT_HALF))

def rope_tables(length, half_size):
    position = jnp.arange(length, dtype=jnp.float32)[:, None]
    rate = jnp.exp(jnp.arange(half_size, dtype=jnp.float32) * (-math.log(10000.0) / half_size))
    angle = position * rate[None, :]
    return (jnp.cos(angle)[:, None, :], jnp.sin(angle)[:, None, :])

def rotate(vector, cosine, sine):
    half_size = vector.shape[-1] // 2
    front_half = vector[..., :half_size]
    back_half = vector[..., half_size:]
    return jnp.concatenate([front_half * cosine - back_half * sine, back_half * cosine + front_half * sine], -1)

def layer_norm(values, gain_row, bias_row):
    row_mean = lax.optimization_barrier(jnp.mean(values, axis=-1, keepdims=True))
    variance = lax.optimization_barrier(jnp.mean(values * values, axis=-1, keepdims=True)) - row_mean * row_mean
    return (values - row_mean) * lax.rsqrt(variance + EPSILON) * gain_row + bias_row

def attend(query_vecs, key_vecs, value_vecs, seg_row):
    length = query_vecs.shape[0]
    block_rows = min(512, length)
    block_count = length // block_rows
    positions = jnp.arange(length, dtype=jnp.int32)
    score_scale = HEAD ** (-0.5)

    @jax.checkpoint
    def score_block(pieces):
        q_block, seg_block, row_ids = pieces
        scores = low_back(jnp.einsum('qhe,khe->hqk', q_block, key_vecs, precision=EXACT) * score_scale)
        allowed = (seg_block[:, None] == seg_row[None, :]) & (positions[None, :] <= row_ids[:, None])
        scores = jnp.where(allowed[None], scores, -1e+30)
        row_max = lax.optimization_barrier(jnp.max(scores, -1, keepdims=True))
        exp_scores = jnp.exp(scores - row_max)
        probabilities = low(exp_scores / lax.optimization_barrier(jnp.sum(exp_scores, -1, keepdims=True)))
        return jnp.einsum('hqk,khe->qhe', probabilities, value_vecs, precision=EXACT)
    block_outputs = lax.map(score_block, (query_vecs.reshape(block_count, block_rows, HEADS, HEAD), seg_row.reshape(block_count, block_rows), positions.reshape(block_count, block_rows)))
    return block_outputs.reshape(length, HEADS, HEAD)

def forward(hist_row, seg_row, params):
    depth, gain_one, bias_one, qkv_w, out_w, gain_two, bias_two, up_w, up_b, down_w, down_b = params
    length = hist_row.shape[1]
    cosine, sine = rope_tables(length, HEAD // 2)
    residual = jnp.einsum('j,jtd->td', depth, hist_row, precision=EXACT)
    normed1 = low(layer_norm(residual, gain_one, bias_one))
    projected = low_back(jnp.dot(normed1, qkv_w, precision=EXACT)).reshape(length, HEADS, 3, HEAD)
    query_vecs = low(rotate(projected[:, :, 0], cosine, sine))
    key_vecs = low(rotate(projected[:, :, 1], cosine, sine))
    value_vecs = low(projected[:, :, 2])
    attended = low_back(low(attend(query_vecs, key_vecs, value_vecs, seg_row))).reshape(length, D)
    hidden = residual + low_back(jnp.dot(attended, out_w, precision=EXACT))
    normed2 = low(layer_norm(hidden, gain_two, bias_two))
    up_proj = low_back(jnp.dot(normed2, up_w, precision=EXACT) + up_b)
    activated = low(gelu_value(up_proj))
    return hidden + low_back(jnp.dot(activated, down_w, precision=EXACT) + down_b)

def reference(history, depth_weights, segment_ids, first_gain, first_bias, qkv_weight, out_weight, second_gain, second_bias, up_weight, up_bias, down_weight, down_bias, cotangent):
    params = tuple((array.astype(jnp.float32) for array in (depth_weights, first_gain, first_bias, qkv_weight, out_weight, second_gain, second_bias, up_weight, up_bias, down_weight, down_bias)))

    def row_step(carry, row_index):
        totals, outputs, grad_hist = carry
        row_start = (row_index * SEQ).astype(jnp.int32)
        hist_row = lax.dynamic_slice_in_dim(history, row_start, SEQ, 1).astype(jnp.float32)
        seg_row = lax.dynamic_index_in_dim(segment_ids, row_index, 0, keepdims=False)
        grad_row = lax.dynamic_slice_in_dim(cotangent, row_start, SEQ, 0).astype(jnp.float32)

        def row_forward(hist_values, param_values):
            return forward(hist_values, seg_row, param_values)
        result, pullback = jax.vjp(row_forward, hist_row, params)
        hist_grad_row, param_grads = pullback(grad_row)
        totals = jax.tree.map(jnp.add, totals, param_grads)
        outputs = lax.dynamic_update_slice_in_dim(outputs, result.astype(jnp.bfloat16), row_start, 0)
        grad_hist = lax.dynamic_update_slice_in_dim(grad_hist, hist_grad_row.astype(jnp.bfloat16), row_start, 1)
        return ((totals, outputs, grad_hist), None)
    zero_grads = tuple((jnp.zeros_like(param) for param in params))
    initial = (zero_grads, jnp.zeros((TOKENS, D), jnp.bfloat16), jnp.zeros((HIST, TOKENS, D), jnp.bfloat16))
    (totals, outputs, grad_hist), unused = lax.scan(row_step, initial, jnp.arange(ROWS, dtype=jnp.int32))
    return (outputs, grad_hist, totals[0], totals[1], totals[2], totals[3], totals[4], totals[5], totals[6], totals[7], totals[8], totals[9], totals[10])
```

```python
import math

import jax
import jax.numpy as jnp
import numpy as np
from jax import lax
from jax.experimental import pallas as pl
from jax.experimental.pallas import tpu as pltpu
from jax.sharding import PartitionSpec as P

HEAD = 128
MAX_DOC = 512
EPSILON = 1e-05
SQRT_HALF = 0.7071067811865476
INV_ROOT_TWO_PI = 0.3989422804014327
LOG2E = 1.4426950408889634
SCALE = HEAD ** (-0.5)
MIB = 2**20
BF16 = jnp.bfloat16
F32 = jnp.float32


def dot_nn(a, b):
    return jnp.dot(a, b, preferred_element_type=F32)


def dot_nt(a, b):
    return lax.dot_general(a, b, (((1,), (1,)), ((), ())), preferred_element_type=F32)


def dot_tn(a, b):
    return lax.dot_general(a, b, (((0,), (0,)), ((), ())), preferred_element_type=F32)


def call(name, body, grid, args, in_specs, outs, out_specs, scratch=(), flops=0, trans=0, **kw):
    moved = sum(a.size * a.dtype.itemsize for a in args)
    moved += sum(math.prod(o.shape) * o.dtype.itemsize for o in outs)
    return pl.pallas_call(
        body,
        grid=grid,
        in_specs=in_specs,
        out_specs=out_specs,
        out_shape=outs,
        scratch_shapes=list(scratch),
        compiler_params=pltpu.CompilerParams(vmem_limit_bytes=60 * MIB),
        cost_estimate=pl.CostEstimate(flops=flops, bytes_accessed=moved, transcendentals=trans),
        name=name,
        **kw,
    )(*args)


def shape(dims, dtype):
    return jax.ShapeDtypeStruct(dims, dtype)


SMEM = pl.BlockSpec(memory_space=pltpu.SMEM)
ANY = pl.BlockSpec(memory_space=pl.ANY)


def rows_of(block):
    return pl.BlockSpec(block, lambda i: (i, 0))


def cols_of(block):
    return pl.BlockSpec(block, lambda i: (0, i))


def fixed(block):
    return pl.BlockSpec(block, lambda i: (0,) * len(block))


def start_all(copies):
    @pl.when(pl.program_id(0) == 0)
    def _():
        for one in copies:
            one.start()


def wait_all(copies):
    @pl.when(pl.program_id(0) == 0)
    def _():
        for one in copies:
            one.wait()


def row_blocks(me, n, width, source, target, sems, base):
    return [
        pltpu.make_async_copy(
            source.at[pl.ds(pl.multiple_of((me ^ j) * width, width), width), :],
            target.at[pl.ds(j * width, width), :],
            sems.at[base + j],
        )
        for j in range(n)
    ]


def col_blocks(me, n, width, source, target, sems, base):
    return [
        pltpu.make_async_copy(
            source.at[:, pl.ds(pl.multiple_of((me ^ j) * width, width), width)],
            target.at[:, pl.ds(j * width, width)],
            sems.at[base + j],
        )
        for j in range(n)
    ]


def stat_columns(first, second):
    lane = lax.broadcasted_iota(jnp.int32, (first.shape[0], 128), 1)
    return jnp.where(lane == 0, first, jnp.where(lane == 1, second, 0.0))


def fold_rows(values):
    return jnp.sum(values.reshape(values.shape[0] // 8, 8, values.shape[1]), 0)


def accumulate(ref, value):
    @pl.when(pl.program_id(0) == 0)
    def _():
        ref[...] = value

    @pl.when(pl.program_id(0) != 0)
    def _():
        ref[...] += value


def average_body(weights, history, wide, low):
    total = weights[0] * history[0].astype(F32)
    for j in range(1, history.shape[0]):
        total += weights[j] * history[j].astype(F32)
    wide[...] = total
    low[...] = total.astype(BF16)


def average(weights, history, row, length):
    count, _, width = history.shape
    tile = min(256, length)
    steps = length // tile
    return call(
        "average",
        average_body,
        (steps,),
        (weights, history),
        [SMEM, pl.BlockSpec((count, tile, width), lambda i: (0, row * steps + i, 0))],
        [shape((length, width), F32), shape((length, width), BF16)],
        [rows_of((tile, width))] * 2,
        flops=2 * count * length * width,
    )


def project_body(n, me, *refs):
    xs = refs[:n]
    gain, bias, cosine, sine, weight, qkv, normed, stat, held, sems = refs[n:]
    width = xs[0].shape[1]
    full = n * width
    copies = row_blocks(me[0], n, width, weight, held, sems, 0)
    start_all(copies)
    total = square = 0.0
    for x in xs:
        value = x[...].astype(F32)
        total += jnp.sum(value, 1, keepdims=True)
        square += jnp.sum(value * value, 1, keepdims=True)
    mean = total / full
    inv = lax.rsqrt(square / full - mean * mean + EPSILON)
    stat[...] = stat_columns(mean, inv)
    for j, x in enumerate(xs):
        part = slice(j * width, (j + 1) * width)
        normed[:, part] = (
            (x[...].astype(F32) - mean) * inv * gain[0:1, part] + bias[0:1, part]
        ).astype(BF16)
    wait_all(copies)
    for h in range(held.shape[1] // (3 * HEAD)):
        base = 3 * h * HEAD
        out = dot_nn(normed[...], held[:, base : base + 3 * HEAD])
        for s in range(2):
            v = out[:, s * HEAD : (s + 1) * HEAD]
            turned = v * cosine[...] + pltpu.roll(v, HEAD // 2, 1) * sine[...]
            qkv[:, base + s * HEAD : base + (s + 1) * HEAD] = turned.astype(BF16)
        qkv[:, base + 2 * HEAD : base + 3 * HEAD] = out[:, 2 * HEAD :].astype(BF16)


def project(me, xs, gain, bias, tables, weight):
    n, (length, width) = len(xs), xs[0].shape
    full, out = weight.shape
    tile = min(256, length)
    return call(
        "project",
        lambda *refs: project_body(n, *refs),
        (length // tile,),
        (me, *xs, gain, bias, *tables, weight),
        [SMEM]
        + [rows_of((tile, width))] * n
        + [fixed((8, full))] * 2
        + [rows_of((tile, HEAD))] * 2
        + [ANY],
        [shape((length, out), BF16), shape((length, full), BF16), shape((length, 128), F32)],
        [rows_of((tile, out)), rows_of((tile, full)), rows_of((tile, 128))],
        scratch=[pltpu.VMEM((full, out), BF16), pltpu.SemaphoreType.DMA((n,))],
        flops=2 * length * full * out,
    )


def windows(length):
    block = min(256, length)
    for i in range(length // block):
        low = max(0, i * block - (MAX_DOC - 1)) // block * block
        yield slice(i * block, (i + 1) * block), slice(low, (i + 1) * block)


def score_mask(start, q_part, k_part):
    dims = (k_part.stop - k_part.start, q_part.stop - q_part.start)
    k_pos = lax.broadcasted_iota(jnp.int32, dims, 0) + k_part.start
    q_pos = lax.broadcasted_iota(jnp.int32, dims, 1) + q_part.start
    return (k_pos >= start[0:1, q_part]) & (k_pos <= q_pos)


def attend_body(start, qkv, out, logs):
    length = qkv.shape[0]
    value_t = qkv[:, 2 * HEAD :].T
    for q_part, k_part in windows(length):
        query, key = qkv[q_part, :HEAD], qkv[k_part, HEAD : 2 * HEAD]
        scores = dot_nt(key, query) * (SCALE * LOG2E)
        scores = jnp.where(score_mask(start, q_part, k_part), scores, -1e30)
        top = jnp.max(scores, 0, keepdims=True)
        probs = jnp.exp2(scores - top)
        total = jnp.sum(probs, 0, keepdims=True)
        logs[0, :, q_part] = jnp.broadcast_to(top + jnp.log2(total), (8, q_part.stop - q_part.start))
        got = dot_nn(value_t[:, k_part], probs.astype(BF16)) / total
        out[q_part, :] = got.T.astype(BF16)


def attend(start, qkv):
    length, width = qkv.shape
    heads = width // (3 * HEAD)
    return call(
        "attend",
        attend_body,
        (heads,),
        (start, qkv),
        [fixed((8, length)), cols_of((length, 3 * HEAD))],
        [shape((length, heads * HEAD), BF16), shape((heads, 8, length), F32)],
        [cols_of((length, HEAD)), pl.BlockSpec((1, 8, length), lambda i: (i, 0, 0))],
        flops=4 * length * 768 * HEAD * heads,
    )


def attend_back_body(start, cosine, sine, qkv, grad, logs, out, key_sum, value_sum):
    length = qkv.shape[0]
    key_t = qkv[:, HEAD : 2 * HEAD].T
    key_sum[...] = jnp.zeros_like(key_sum)
    value_sum[...] = jnp.zeros_like(value_sum)

    def turn_back(v, part):
        return (
            v * cosine[part, :] - pltpu.roll(v, HEAD // 2, 1) * sine[part, :]
        ).astype(BF16)

    for q_part, k_part in windows(length):
        query, key = qkv[q_part, :HEAD], qkv[k_part, HEAD : 2 * HEAD]
        value, g = qkv[k_part, 2 * HEAD :], grad[q_part, :]
        scores = dot_nt(key, query) * (SCALE * LOG2E) - logs[0, 0:1, q_part]
        probs = jnp.exp2(jnp.where(score_mask(start, q_part, k_part), scores, -1e30))
        prob_grad = dot_nt(value, g)
        mean = jnp.sum(prob_grad * probs, 0, keepdims=True)
        score_grad = (probs * (prob_grad - mean)).astype(BF16)
        value_sum[k_part, :] += dot_nn(probs.astype(BF16), g)
        key_sum[k_part, :] += dot_nn(score_grad, query)
        query_grad = dot_nn(key_t[:, k_part], score_grad) * SCALE
        out[q_part, :HEAD] = turn_back(query_grad.T, q_part)
    for q_part, _ in windows(length):
        out[q_part, HEAD : 2 * HEAD] = turn_back(key_sum[q_part, :] * SCALE, q_part)
        out[q_part, 2 * HEAD :] = value_sum[q_part, :].astype(BF16)


def attend_back(start, tables, qkv, grad, logs):
    length, width = qkv.shape
    heads = width // (3 * HEAD)
    return call(
        "attend_back",
        attend_back_body,
        (heads,),
        (start, *tables, qkv, grad, logs),
        [fixed((8, length))]
        + [fixed((length, HEAD))] * 2
        + [
            cols_of((length, 3 * HEAD)),
            cols_of((length, HEAD)),
            pl.BlockSpec((1, 8, length), lambda i: (i, 0, 0)),
        ],
        [shape((length, width), BF16)],
        [cols_of((length, 3 * HEAD))],
        scratch=[pltpu.VMEM((length, HEAD), F32)] * 2,
        flops=10 * length * 768 * HEAD * heads,
    )[0]


def feed_body(n, me, *refs):
    attended, xs, outs_w = refs[:n], refs[n : 2 * n], refs[2 * n : 3 * n]
    own, gain, bias, up_bias, up_weight, down_weight = refs[3 * n : 3 * n + 6]
    hidden, normed, stat, activated, slope = refs[3 * n + 6 : 3 * n + 11]
    parts = refs[3 * n + 11 : 4 * n + 11]
    out_held, up_held, down_held, joined, whole, sems = refs[4 * n + 11 :]
    width = xs[0].shape[1]
    full = n * width
    inner = up_held.shape[1]
    out_copies = []
    for k in range(n):
        for j in range(n):
            out_copies.append(
                pltpu.make_async_copy(
                    outs_w[k].at[:, pl.ds(pl.multiple_of((me[0] ^ j) * width, width), width)],
                    out_held.at[pl.ds(k * width, width), pl.ds(j * width, width)],
                    sems.at[k * n + j],
                )
            )
    up_copies = row_blocks(me[0], n, width, up_weight, up_held, sems, n * n)
    down_copies = col_blocks(me[0], n, width, down_weight, down_held, sems, n * n + n)
    start_all(out_copies + up_copies + down_copies)
    for j in range(n):
        joined[:, j * width : (j + 1) * width] = attended[j][...]
    wait_all(out_copies)
    total = square = 0.0
    for j in range(n):
        part = slice(j * width, (j + 1) * width)
        base = own[...] if j == 0 else xs[j][...].astype(F32)
        value = base + dot_nn(joined[...], out_held[:, part])
        whole[:, part] = value
        if j == 0:
            hidden[...] = value
        total += jnp.sum(value, 1, keepdims=True)
        square += jnp.sum(value * value, 1, keepdims=True)
    mean = total / full
    inv = lax.rsqrt(square / full - mean * mean + EPSILON)
    stat[...] = stat_columns(mean, inv)
    for j in range(n):
        part = slice(j * width, (j + 1) * width)
        normed[:, part] = (
            (whole[:, part] - mean) * inv * gain[0:1, part] + bias[0:1, part]
        ).astype(BF16)
    wait_all(up_copies)
    step = min(512, inner)
    for c in range(inner // step):
        part = slice(c * step, (c + 1) * step)
        up = dot_nn(normed[...], up_held[:, part]) + up_bias[0:1, part]
        half = 0.5 * (1.0 + lax.erf(up * SQRT_HALF))
        activated[:, part] = (up * half).astype(BF16)
        slope[:, part] = (half + up * INV_ROOT_TWO_PI * jnp.exp(-0.5 * up * up)).astype(BF16)
    wait_all(down_copies)
    for j in range(n):
        parts[j][...] = dot_nn(
            activated[...], down_held[:, j * width : (j + 1) * width]
        ).astype(BF16)


def feed(me, attended, xs, outs_w, own, gain, bias, up_bias, up_weight, down_weight):
    n, (length, width) = len(xs), own.shape
    full, inner = up_weight.shape
    tile = min(256, length)
    got = call(
        "feed",
        lambda *refs: feed_body(n, *refs),
        (length // tile,),
        (me, *attended, *xs, *outs_w, own, gain, bias, up_bias, up_weight, down_weight),
        [SMEM]
        + [rows_of((tile, width))] * (2 * n)
        + [ANY] * n
        + [rows_of((tile, width))]
        + [fixed((8, full))] * 2
        + [fixed((8, inner))]
        + [ANY] * 2,
        [
            shape((length, width), F32),
            shape((length, full), BF16),
            shape((length, 128), F32),
            shape((length, inner), BF16),
            shape((length, inner), BF16),
        ]
        + [shape((length, width), BF16)] * n,
        [
            rows_of((tile, width)),
            rows_of((tile, full)),
            rows_of((tile, 128)),
            rows_of((tile, inner)),
            rows_of((tile, inner)),
        ]
        + [rows_of((tile, width))] * n,
        scratch=[
            pltpu.VMEM((full, full), BF16),
            pltpu.VMEM((full, inner), BF16),
            pltpu.VMEM((inner, full), BF16),
            pltpu.VMEM((tile, full), BF16),
            pltpu.VMEM((tile, full), F32),
            pltpu.SemaphoreType.DMA((n * n + 2 * n,)),
        ],
        flops=2 * length * full * (full + 2 * inner),
    )
    return (*got[:5], got[5:])


def row_stats(total, weighted):
    return stat_columns(total, weighted).T[0:8, :]


def feed_back_body(n, me, *refs):
    cots = refs[:n]
    slope, normed, gain, bias, up_weight, down_weight = refs[n : n + 6]
    cot_full, up_grad, sums, up_bias_sum, down_bias_sum = refs[n + 6 : n + 11]
    parts = refs[n + 11 : 2 * n + 11]
    up_held, down_held, sems = refs[2 * n + 11 :]
    width = cots[0].shape[1]
    inner = up_held.shape[1]
    down_copies = col_blocks(me[0], n, width, down_weight, down_held, sems, 0)
    up_copies = row_blocks(me[0], n, width, up_weight, up_held, sems, n)
    start_all(down_copies + up_copies)
    for j in range(n):
        cot_full[:, j * width : (j + 1) * width] = cots[j][...]
    accumulate(down_bias_sum, fold_rows(cots[0][...].astype(F32)))
    wait_all(down_copies)
    step = min(512, inner)
    for c in range(inner // step):
        part = slice(c * step, (c + 1) * step)
        value = dot_nt(cot_full[...], down_held[part, :]) * slope[:, part].astype(F32)
        up_grad[:, part] = value.astype(BF16)
    accumulate(up_bias_sum, fold_rows(up_grad[...].astype(F32)))
    wait_all(up_copies)
    total = weighted = 0.0
    for j in range(n):
        part = slice(j * width, (j + 1) * width)
        value = dot_nt(up_grad[...], up_held[part, :])
        parts[j][...] = value.astype(BF16)
        total += jnp.sum(value * gain[0:1, part], 1, keepdims=True)
        weighted += jnp.sum(
            value * (normed[:, part].astype(F32) - bias[0:1, part]), 1, keepdims=True
        )
    sums[...] = row_stats(total, weighted)


def feed_back(me, cots, slope, normed, gain, bias, up_weight, down_weight):
    n, (length, width) = len(cots), cots[0].shape
    full, inner = up_weight.shape
    tile = min(256, length)
    got = call(
        "feed_back",
        lambda *refs: feed_back_body(n, *refs),
        (length // tile,),
        (me, *cots, slope, normed, gain, bias, up_weight, down_weight),
        [SMEM]
        + [rows_of((tile, width))] * n
        + [rows_of((tile, inner)), rows_of((tile, full))]
        + [fixed((8, full))] * 2
        + [ANY] * 2,
        [
            shape((length, full), BF16),
            shape((length, inner), BF16),
            shape((8, length), F32),
            shape((8, inner), F32),
            shape((8, width), F32),
        ]
        + [shape((length, width), BF16)] * n,
        [
            rows_of((tile, full)),
            rows_of((tile, inner)),
            cols_of((8, tile)),
            fixed((8, inner)),
            fixed((8, width)),
        ]
        + [rows_of((tile, width))] * n,
        scratch=[
            pltpu.VMEM((full, inner), BF16),
            pltpu.VMEM((inner, full), BF16),
            pltpu.SemaphoreType.DMA((2 * n,)),
        ],
        flops=4 * length * full * inner,
    )
    return (*got[:5], got[5:])


def norm_back(refs, n_parts, source, stat, sums, gain, full):
    grad = refs[0][...].astype(F32)
    for ref in refs[1:n_parts]:
        grad += ref[...].astype(F32)
    columns = sums[...].T
    mean, inv = stat[:, 0:1], stat[:, 1:2]
    scaled = (source[...] - mean) * inv
    back = inv * (
        grad * gain[0:1, :] - columns[:, 0:1] * (1.0 / full) - scaled * (columns[:, 1:2] * (1.0 / full))
    )
    return back, fold_rows(grad * scaled), fold_rows(grad)


def hidden_back_body(k, full, *refs):
    parts = refs[:k]
    cot, hidden, stat, sums, gain, wide, low, gain_sum, bias_sum = refs[k:]
    back, gain_part, bias_part = norm_back(parts, k, hidden, stat, sums, gain, full)
    value = cot[...].astype(F32) + back
    wide[...] = value
    low[...] = value.astype(BF16)
    accumulate(gain_sum, gain_part)
    accumulate(bias_sum, bias_part)


def hidden_back(parts, cotangent, row, hidden, stat, sums, gain, full):
    k, (length, width) = len(parts), hidden.shape
    tile = min(256, length)
    steps = length // tile
    return call(
        "hidden_back",
        lambda *refs: hidden_back_body(k, full, *refs),
        (steps,),
        (*parts, cotangent, hidden, stat, sums, gain),
        [rows_of((tile, width))] * k
        + [
            pl.BlockSpec((tile, width), lambda i: (row * steps + i, 0)),
            rows_of((tile, width)),
            rows_of((tile, 128)),
            cols_of((8, tile)),
            fixed((8, width)),
        ],
        [shape((length, width), F32), shape((length, width), BF16)] + [shape((8, width), F32)] * 2,
        [rows_of((tile, width))] * 2 + [fixed((8, width))] * 2,
        flops=20 * length * width,
    )


def attended_back_body(n, me, *refs):
    grads = refs[:n]
    weight, joined, out, held, sems = refs[n:]
    width = grads[0].shape[1]
    copies = col_blocks(me[0], n, width, weight, held, sems, 0)
    start_all(copies)
    for j in range(n):
        joined[:, j * width : (j + 1) * width] = grads[j][...]
    wait_all(copies)
    out[...] = dot_nt(joined[...], held[...]).astype(BF16)


def attended_back(me, grads, weight):
    n, (length, width) = len(grads), grads[0].shape
    rows, full = weight.shape
    tile = min(256, length)
    return call(
        "attended_back",
        lambda *refs: attended_back_body(n, *refs),
        (length // tile,),
        (me, *grads, weight),
        [SMEM] + [rows_of((tile, width))] * n + [ANY],
        [shape((length, full), BF16), shape((length, rows), BF16)],
        [rows_of((tile, full)), rows_of((tile, rows))],
        scratch=[pltpu.VMEM((rows, full), BF16), pltpu.SemaphoreType.DMA((n,))],
        flops=2 * length * full * rows,
    )


def project_back_body(n, me, grad, normed, gain, bias, weight, sums, *refs):
    parts = refs[:n]
    held, sems = refs[n:]
    width = parts[0].shape[1]
    copies = row_blocks(me[0], n, width, weight, held, sems, 0)
    start_all(copies)
    wait_all(copies)
    total = weighted = 0.0
    for j in range(n):
        part = slice(j * width, (j + 1) * width)
        value = dot_nt(grad[...], held[part, :])
        parts[j][...] = value.astype(BF16)
        total += jnp.sum(value * gain[0:1, part], 1, keepdims=True)
        weighted += jnp.sum(
            value * (normed[:, part].astype(F32) - bias[0:1, part]), 1, keepdims=True
        )
    sums[...] = row_stats(total, weighted)


def project_back(me, n, grad, normed, gain, bias, weight):
    length, out = grad.shape
    full = weight.shape[0]
    width = full // n
    tile = min(256, length)
    got = call(
        "project_back",
        lambda *refs: project_back_body(n, *refs),
        (length // tile,),
        (me, grad, normed, gain, bias, weight),
        [SMEM, rows_of((tile, out)), rows_of((tile, full))] + [fixed((8, full))] * 2 + [ANY],
        [shape((8, length), F32)] + [shape((length, width), BF16)] * n,
        [cols_of((8, tile))] + [rows_of((tile, width))] * n,
        scratch=[pltpu.VMEM((full, out), BF16), pltpu.SemaphoreType.DMA((n,))],
        flops=2 * length * full * out,
    )
    return got[0], got[1:]


def average_back_body(k, full, count, *refs):
    weights, parts = refs[0], refs[1 : k + 1]
    source, stat, sums, gain, hidden_grad, history = refs[k + 1 : k + 7]
    grad_history, depth_sum, gain_sum, bias_sum = refs[-4:]
    back, gain_part, bias_part = norm_back(parts, k, source, stat, sums, gain, full)
    value = hidden_grad[...] + back
    accumulate(gain_sum, gain_part)
    accumulate(bias_sum, bias_part)
    lanes = value.shape[1] // 128
    for j in range(count):
        grad_history[j] = (weights[j] * value).astype(BF16)
        product = fold_rows(value * history[j].astype(F32))
        folded = product[:, 0:128]
        for c in range(1, lanes):
            folded += product[:, c * 128 : (c + 1) * 128]
        accumulate(depth_sum.at[j], folded)


def average_back(weights, parts, source, stat, sums, gain, hidden_grad, history, row, made):
    k, (length, width) = len(parts), source.shape
    count = history.shape[0]
    tile = min(256, length)
    steps = length // tile
    full = gain[1]
    block = pl.BlockSpec((count, tile, width), lambda i: (0, row * steps + i, 0))
    args = (weights, *parts, source, stat, sums, gain[0], hidden_grad, history)
    specs = (
        [SMEM]
        + [rows_of((tile, width))] * (k + 1)
        + [rows_of((tile, 128)), cols_of((8, tile)), fixed((8, width)), rows_of((tile, width)), block]
    )
    more = {}
    if made is not None:
        more = {"input_output_aliases": {len(args): 0}}
        args, specs = (*args, made), specs + [ANY]
    return call(
        "average_back",
        lambda *refs: average_back_body(k, full, count, *refs),
        (steps,),
        args,
        specs,
        [shape(history.shape, BF16), shape((count, 8, 128), F32)] + [shape((8, width), F32)] * 2,
        [block, fixed((count, 8, 128))] + [fixed((8, width))] * 2,
        flops=6 * count * length * width,
        **more,
    )


def weight_body(rows, me, *refs):
    out = refs[-1]
    total = dot_tn(refs[0][...], refs[rows][...])
    for r in range(1, rows):
        total += dot_tn(refs[r][...], refs[rows + r][...])
    out[...] = total.astype(BF16)


def divisor(size, most):
    return max(d for d in range(128, most + 1, 128) if size % d == 0)


def weight_grad(me, lefts, rights, width, turned):
    rows, (length, high), wide = len(lefts), lefts[0].shape, rights[0].shape[1]
    tall, across = divisor(high, 512), divisor(wide, 1024)
    if turned == 0:
        tall = min(tall, width)
    if turned == 1:
        across = min(across, width)
    per = width // (tall if turned == 0 else across)

    def place(i, j, me):
        if turned == 0:
            i = (me[0] ^ (i // per)) * per + i % per
        if turned == 1:
            j = (me[0] ^ (j // per)) * per + j % per
        return i, j

    return pl.pallas_call(
        lambda *refs: weight_body(rows, *refs),
        grid_spec=pltpu.PrefetchScalarGridSpec(
            num_scalar_prefetch=1,
            grid=(high // tall, wide // across),
            in_specs=[pl.BlockSpec((length, tall), lambda i, j, me: (0, i))] * rows
            + [pl.BlockSpec((length, across), lambda i, j, me: (0, j))] * rows,
            out_specs=pl.BlockSpec((tall, across), place),
        ),
        out_shape=shape((high, wide), BF16),
        compiler_params=pltpu.CompilerParams(vmem_limit_bytes=60 * MIB),
        cost_estimate=pl.CostEstimate(
            flops=2 * rows * length * high * wide,
            bytes_accessed=2 * (rows * length * (high + wide) + high * wide),
            transcendentals=0,
        ),
        name="weight_grad",
    )(me, *lefts, *rights)


class Ring:
    def __init__(self):
        self.n = lax.axis_size("mp")
        self.me = lax.axis_index("mp").astype(jnp.int32)
        self.pairs = self.n == 4
        self.core = [(i, i ^ 1) for i in range(self.n)]
        self.chip = [(i, i ^ 2) for i in range(self.n)]

    def over_core(self, value):
        return lax.ppermute(value, "mp", self.core)

    def over_chip(self, value):
        return lax.ppermute(value, "mp", self.chip)

    def gather(self, block):
        if self.pairs:
            sibling = self.over_core(block)
            across = self.over_chip(block)
            return [block, sibling, across, self.over_core(across)]
        every = lax.all_gather(block, "mp")
        return [
            lax.dynamic_index_in_dim(every, self.me ^ j, 0, keepdims=False) for j in range(self.n)
        ]

    def scatter(self, parts):
        if self.pairs:
            mine, other = self.over_core(parts[1]), self.over_core(parts[3])
            chip_sum = (parts[2].astype(F32) + other.astype(F32)).astype(BF16)
            return [parts[0], mine, self.over_chip(chip_sum)]
        stacked = jnp.stack([part.astype(F32) for part in parts])
        ordered = jnp.take(stacked, self.me ^ jnp.arange(self.n), axis=0)
        return [lax.psum_scatter(ordered, "mp", scatter_dimension=0, tiled=False)]

    def total(self, value):
        if self.pairs:
            value = value + self.over_core(value)
            return value + self.over_chip(value)
        return lax.psum(value, "mp")

    def out_blocks(self, weight):
        rows = weight.shape[0]
        groups = lax.axis_size("dp")
        if self.pairs and rows % (16 * groups) == 0:
            size = rows // groups
            piece = lax.dynamic_slice_in_dim(weight, lax.axis_index("dp") * size, size, 0)
            across = lax.all_gather(self.over_chip(piece), "dp", axis=0, tiled=True)
            return [weight, self.over_core(weight), across, self.over_core(across)]
        return self.gather(weight)


def tables_of(length):
    half = HEAD // 2
    rate = np.exp(np.arange(half, dtype=np.float64) * (-math.log(10000.0) / half))
    angle = np.arange(length, dtype=np.float64)[:, None] * rate[None, :]
    cosine, sine = np.cos(angle), np.sin(angle)
    return (
        jnp.asarray(np.concatenate([cosine, cosine], 1), F32),
        jnp.asarray(np.concatenate([-sine, sine], 1), F32),
    )


def local(
    history,
    depth_weights,
    segment_ids,
    first_gain,
    first_bias,
    qkv_weight,
    out_weight,
    second_gain,
    second_bias,
    up_weight,
    up_bias,
    down_weight,
    down_bias,
    cotangent,
):
    ring = Ring()
    n = ring.n
    me = ring.me[None]
    width = history.shape[2]
    full = n * width
    row_count, length = segment_ids.shape
    rows = range(row_count)
    tables = tables_of(length)
    earlier = (segment_ids[:, None, :] < segment_ids[:, :, None]).astype(jnp.int32)
    starts = jnp.broadcast_to(jnp.sum(earlier, -1)[:, None, :], (row_count, 8, length))

    vectors = jnp.stack([first_gain, first_bias, second_gain, second_bias])
    vectors = jnp.concatenate(ring.gather(jnp.repeat(vectors, 8, 0)), 1)
    gain1, bias1, gain2, bias2 = (vectors[8 * i : 8 * i + 8] for i in range(4))
    own1, own2 = gain1[:, :width], gain2[:, :width]
    up_bias8 = jnp.broadcast_to(up_bias[None], (8, up_bias.shape[0]))

    wide, low = zip(*[average(depth_weights, history, r, length) for r in rows])
    xs = [ring.gather(low[r]) for r in rows]
    cots = [
        ring.gather(lax.slice_in_dim(cotangent, r * length, (r + 1) * length)) for r in rows
    ]
    out_w = ring.out_blocks(out_weight)

    qkv, normed1, stat1, attended, logs = [], [], [], [], []
    for r in rows:
        got = project(me, xs[r], gain1, bias1, tables, qkv_weight)
        qkv.append(got[0])
        normed1.append(got[1])
        stat1.append(got[2])
        got = attend(starts[r], qkv[r])
        attended.append(got[0])
        logs.append(got[1])
    heads = [ring.gather(attended[r]) for r in rows]

    hidden, normed2, stat2, activated, slope, outputs = [], [], [], [], [], []
    for r in rows:
        got = feed(
            me, heads[r], xs[r], out_w, wide[r], gain2, bias2, up_bias8, up_weight, down_weight
        )
        hidden.append(got[0])
        normed2.append(got[1])
        stat2.append(got[2])
        activated.append(got[3])
        slope.append(got[4])
        branch = ring.scatter(got[5])
        mlp = sum(part.astype(F32) for part in branch)
        outputs.append((got[0] + (mlp + down_bias)).astype(BF16))

    cot_full, up_grad, parts2, sums2, up_bias_sum, down_bias_sum = [], [], [], [], 0.0, 0.0
    for r in rows:
        got = feed_back(
            me, cots[r], slope[r], normed2[r], gain2, bias2, up_weight, down_weight
        )
        cot_full.append(got[0])
        up_grad.append(got[1])
        sums2.append(ring.total(got[2]))
        up_bias_sum += got[3]
        down_bias_sum += got[4]
        parts2.append(ring.scatter(got[5]))

    down_part = weight_grad(me, activated, cot_full, width, 1)
    up_part = weight_grad(me, normed2, up_grad, width, 0)

    hidden_grad, gain2_sum, bias2_sum, grads = [], 0.0, 0.0, []
    for r in rows:
        got = hidden_back(parts2[r], cotangent, r, hidden[r], stat2[r], sums2[r], own2, full)
        hidden_grad.append(got[0])
        gain2_sum += got[2]
        bias2_sum += got[3]
        grads.append(ring.gather(got[1]))

    grad_full, qkv_grad, parts1, sums1 = [], [], [], []
    for r in rows:
        got = attended_back(me, grads[r], out_weight)
        grad_full.append(got[0])
        qkv_grad.append(attend_back(starts[r], tables, qkv[r], got[1], logs[r]))
        sums, parts = project_back(me, n, qkv_grad[r], normed1[r], gain1, bias1, qkv_weight)
        sums1.append(ring.total(sums))
        parts1.append(ring.scatter(parts))

    out_part = weight_grad(me, attended, grad_full, width, 1)
    qkv_part = weight_grad(me, normed1, qkv_grad, width, 0)

    grad_history, depth_sum, gain1_sum, bias1_sum = None, 0.0, 0.0, 0.0
    for r in rows:
        got = average_back(
            depth_weights,
            parts1[r],
            wide[r],
            stat1[r],
            sums1[r],
            (own1, full),
            hidden_grad[r],
            history,
            r,
            grad_history,
        )
        grad_history = got[0]
        depth_sum += got[1]
        gain1_sum += got[2]
        bias1_sum += got[3]

    down_total = lax.psum_scatter(down_part, "dp", scatter_dimension=1, tiled=True).astype(F32)
    up_total = lax.psum_scatter(up_part, "dp", scatter_dimension=0, tiled=True).astype(F32)
    out_total = lax.psum_scatter(out_part, "dp", scatter_dimension=1, tiled=True).astype(F32)
    qkv_total = lax.psum_scatter(qkv_part, "dp", scatter_dimension=0, tiled=True).astype(F32)

    early = lax.psum(
        tuple(jnp.sum(v, 0) for v in (up_bias_sum, down_bias_sum, gain2_sum, bias2_sum)), "dp"
    )
    late = lax.psum(
        (jnp.sum(gain1_sum, 0), jnp.sum(bias1_sum, 0), jnp.sum(depth_sum, (1, 2))), "dp"
    )
    depth_grad = lax.psum(late[2], "mp")
    return (
        jnp.concatenate(outputs),
        grad_history,
        depth_grad,
        late[0],
        late[1],
        qkv_total,
        out_total,
        early[2],
        early[3],
        up_total,
        early[0],
        down_total,
        early[1],
    )


def solution(mesh):
    placed = (
        P(None, "dp", "mp"),
        P(),
        P("dp", None),
        P("mp"),
        P("mp"),
        P(None, "mp"),
        P("mp", None),
        P("mp"),
        P("mp"),
        P(None, "mp"),
        P("mp"),
        P("mp", None),
        P("mp"),
        P("dp", "mp"),
    )
    return jax.shard_map(
        local,
        mesh=mesh,
        in_specs=placed,
        out_specs=(
            P("dp", "mp"),
            P(None, "dp", "mp"),
            P(),
            P("mp"),
            P("mp"),
            P("dp", "mp"),
            P("mp", "dp"),
            P("mp"),
            P("mp"),
            P("dp", "mp"),
            P("mp"),
            P("mp", "dp"),
            P("mp"),
        ),
        check_vma=False,
    )
```

```python
import math

import jax
import jax.numpy as jnp
import numpy as np
from jax import lax
from jax.experimental import pallas as pl
from jax.experimental.pallas import tpu as pltpu
from jax.sharding import PartitionSpec as P

HEAD = 128
MAX_DOC = 512
EPSILON = 1e-05
SQRT_HALF = 0.7071067811865476
INV_ROOT_TWO_PI = 0.3989422804014327
LOG2E = 1.4426950408889634
SCALE = HEAD ** (-0.5)
MIB = 2**20
BF16 = jnp.bfloat16
F32 = jnp.float32


def dot_nn(a, b):
    return jnp.dot(a, b, preferred_element_type=F32)


def dot_nt(a, b):
    return lax.dot_general(a, b, (((1,), (1,)), ((), ())), preferred_element_type=F32)


def dot_tn(a, b):
    return lax.dot_general(a, b, (((0,), (0,)), ((), ())), preferred_element_type=F32)


class Order:
    last = None


def call(
    name, body, grid, args, in_specs, outs, out_specs, scratch=(), flops=0, prefetch=0, after=(), aliases=None
):
    moved = sum(a.size * a.dtype.itemsize for a in args)
    moved += sum(math.prod(o.shape) * o.dtype.itemsize for o in outs)
    count = len(args)
    extra = [*after] + ([] if Order.last is None else [Order.last])

    def without_extra(*refs):
        body(*refs[:count], *refs[count + len(extra) :])

    got = pl.pallas_call(
        without_extra,
        grid_spec=pltpu.PrefetchScalarGridSpec(
            num_scalar_prefetch=prefetch,
            grid=grid,
            in_specs=list(in_specs) + [ANY] * len(extra),
            out_specs=out_specs,
            scratch_shapes=list(scratch),
        ),
        out_shape=outs,
        input_output_aliases=aliases or {},
        compiler_params=pltpu.CompilerParams(vmem_limit_bytes=60 * MIB),
        cost_estimate=pl.CostEstimate(flops=flops, bytes_accessed=moved, transcendentals=0),
        name=name,
    )(*args, *extra)
    fresh = [v for i, v in enumerate(got) if i not in (aliases or {}).values()]
    Order.last = min(fresh or got, key=lambda v: v.size)
    return got


def shape(dims, dtype):
    return jax.ShapeDtypeStruct(dims, dtype)


SMEM = pl.BlockSpec(memory_space=pltpu.SMEM)
ANY = pl.BlockSpec(memory_space=pl.ANY)


def gate(arrays, after):
    arrays = list(arrays)
    return call(
        "gate",
        lambda *refs: None,
        (1,),
        arrays,
        [ANY] * len(arrays),
        [shape(a.shape, a.dtype) for a in arrays],
        [ANY] * len(arrays),
        after=after,
        aliases={i: i for i in range(len(arrays))},
    )


def rows_of(block):
    return pl.BlockSpec(block, lambda i: (i, 0))


def cols_of(block):
    return pl.BlockSpec(block, lambda i: (0, i))


def fixed(block):
    return pl.BlockSpec(block, lambda i: (0,) * len(block))


def place_of(me, j, width):
    return pl.ds(pl.multiple_of((me ^ j) * width, width), width)


def start_all(copies):
    @pl.when(pl.program_id(0) == 0)
    def _():
        for one in copies:
            one.start()


def wait_all(copies):
    @pl.when(pl.program_id(0) == 0)
    def _():
        for one in copies:
            one.wait()


def row_blocks(me, n, width, source, target, sems, base):
    return [
        pltpu.make_async_copy(
            source.at[place_of(me, j, width), :],
            target.at[pl.ds(j * width, width), :],
            sems.at[base + j],
        )
        for j in range(n)
    ]


def col_blocks(me, n, width, source, target, sems, base):
    return [
        pltpu.make_async_copy(
            source.at[:, place_of(me, j, width)],
            target.at[:, pl.ds(j * width, width)],
            sems.at[base + j],
        )
        for j in range(n)
    ]


def stat_columns(first, second):
    lane = lax.broadcasted_iota(jnp.int32, (first.shape[0], 128), 1)
    return jnp.where(lane == 0, first, jnp.where(lane == 1, second, 0.0))


def fold_rows(values):
    return jnp.sum(values.reshape(values.shape[0] // 8, 8, values.shape[1]), 0)


def accumulate(ref, value):
    @pl.when(pl.program_id(0) == 0)
    def _():
        ref[...] = value

    @pl.when(pl.program_id(0) != 0)
    def _():
        ref[...] += value


def average_body(weights, history, wide, low):
    total = weights[0] * history[0].astype(F32)
    for j in range(1, history.shape[0]):
        total += weights[j] * history[j].astype(F32)
    wide[...] = total
    low[...] = total.astype(BF16)


def average(weights, history, row, length):
    count, _, width = history.shape
    tile = min(256, length)
    steps = length // tile
    return call(
        "average",
        average_body,
        (steps,),
        (weights, history),
        [SMEM, pl.BlockSpec((count, tile, width), lambda i: (0, row * steps + i, 0))],
        [shape((length, width), F32), shape((length, width), BF16)],
        [rows_of((tile, width))] * 2,
        flops=2 * count * length * width,
    )


def project_body(n, me, *refs):
    xs = refs[:n]
    gain, bias, cosine, sine, weight, qkv, normed, stat, held, sems = refs[n:]
    width = xs[0].shape[1]
    full = n * width
    heads = held.shape[1] // (3 * HEAD)
    copies = []
    for h in range(heads):
        part = pl.ds(3 * h * HEAD, 3 * HEAD)
        copies.append(pltpu.make_async_copy(weight.at[:, part], held.at[:, part], sems.at[h]))
    start_all(copies)
    total = square = 0.0
    for x in xs:
        value = x[...].astype(F32)
        total += jnp.sum(value, 1, keepdims=True)
        square += jnp.sum(value * value, 1, keepdims=True)
    mean = total / full
    inv = lax.rsqrt(square / full - mean * mean + EPSILON)
    stat[...] = stat_columns(mean, inv)
    for j, x in enumerate(xs):
        part = slice(j * width, (j + 1) * width)
        normed[:, place_of(me[0], j, width)] = (
            (x[...].astype(F32) - mean) * inv * gain[0:1, part] + bias[0:1, part]
        ).astype(BF16)
    for h in range(heads):
        wait_all(copies[h : h + 1])
        base = 3 * h * HEAD
        out = dot_nn(normed[...], held[:, base : base + 3 * HEAD])
        for s in range(2):
            v = out[:, s * HEAD : (s + 1) * HEAD]
            turned = v * cosine[...] + pltpu.roll(v, HEAD // 2, 1) * sine[...]
            qkv[:, base + s * HEAD : base + (s + 1) * HEAD] = turned.astype(BF16)
        qkv[:, base + 2 * HEAD : base + 3 * HEAD] = out[:, 2 * HEAD :].astype(BF16)


def project(me, xs, gain, bias, tables, weight):
    n, (length, width) = len(xs), xs[0].shape
    full, out = weight.shape
    tile = min(256, length)
    return call(
        "project",
        lambda *refs: project_body(n, *refs),
        (length // tile,),
        (me, *xs, gain, bias, *tables, weight),
        [SMEM]
        + [rows_of((tile, width))] * n
        + [fixed((8, full))] * 2
        + [rows_of((tile, HEAD))] * 2
        + [ANY],
        [shape((length, out), BF16), shape((length, full), BF16), shape((length, 128), F32)],
        [rows_of((tile, out)), rows_of((tile, full)), rows_of((tile, 128))],
        scratch=[pltpu.VMEM((full, out), BF16), pltpu.SemaphoreType.DMA((out // (3 * HEAD),))],
        flops=2 * length * full * out,
    )


def windows(length):
    block = min(256, length)
    for i in range(length // block):
        low = max(0, i * block - (MAX_DOC - 1)) // block * block
        yield slice(i * block, (i + 1) * block), slice(low, (i + 1) * block)


def score_mask(start, q_part, k_part):
    dims = (k_part.stop - k_part.start, q_part.stop - q_part.start)
    k_pos = lax.broadcasted_iota(jnp.int32, dims, 0) + k_part.start
    q_pos = lax.broadcasted_iota(jnp.int32, dims, 1) + q_part.start
    return (k_pos >= start[0:1, q_part]) & (k_pos <= q_pos)


def attend_body(start, qkv, out, logs):
    length = qkv.shape[0]
    value_t = qkv[:, 2 * HEAD :].T
    for q_part, k_part in windows(length):
        query, key = qkv[q_part, :HEAD], qkv[k_part, HEAD : 2 * HEAD]
        scores = dot_nt(key, query) * (SCALE * LOG2E)
        scores = jnp.where(score_mask(start, q_part, k_part), scores, -1e30)
        top = jnp.max(scores, 0, keepdims=True)
        probs = jnp.exp2(scores - top)
        total = jnp.sum(probs, 0, keepdims=True)
        logs[0, :, q_part] = jnp.broadcast_to(top + jnp.log2(total), (8, q_part.stop - q_part.start))
        got = dot_nn(value_t[:, k_part], probs.astype(BF16)) / total
        out[q_part, :] = got.T.astype(BF16)


def attend(start, qkv):
    length, width = qkv.shape
    heads = width // (3 * HEAD)
    return call(
        "attend",
        attend_body,
        (heads,),
        (start, qkv),
        [fixed((8, length)), cols_of((length, 3 * HEAD))],
        [shape((length, heads * HEAD), BF16), shape((heads, 8, length), F32)],
        [cols_of((length, HEAD)), pl.BlockSpec((1, 8, length), lambda i: (i, 0, 0))],
        flops=4 * length * 768 * HEAD * heads,
    )


def attend_back_body(start, cosine, sine, qkv, grad, logs, out, key_sum, value_sum):
    length = qkv.shape[0]
    key_t = qkv[:, HEAD : 2 * HEAD].T
    key_sum[...] = jnp.zeros_like(key_sum)
    value_sum[...] = jnp.zeros_like(value_sum)

    def turn_back(v, part):
        return (
            v * cosine[part, :] - pltpu.roll(v, HEAD // 2, 1) * sine[part, :]
        ).astype(BF16)

    for q_part, k_part in windows(length):
        query, key = qkv[q_part, :HEAD], qkv[k_part, HEAD : 2 * HEAD]
        value, g = qkv[k_part, 2 * HEAD :], grad[q_part, :]
        scores = dot_nt(key, query) * (SCALE * LOG2E) - logs[0, 0:1, q_part]
        probs = jnp.exp2(jnp.where(score_mask(start, q_part, k_part), scores, -1e30))
        prob_grad = dot_nt(value, g)
        mean = jnp.sum(prob_grad * probs, 0, keepdims=True)
        score_grad = (probs * (prob_grad - mean)).astype(BF16)
        value_sum[k_part, :] += dot_nn(probs.astype(BF16), g)
        key_sum[k_part, :] += dot_nn(score_grad, query)
        query_grad = dot_nn(key_t[:, k_part], score_grad) * SCALE
        out[q_part, :HEAD] = turn_back(query_grad.T, q_part)
    for q_part, _ in windows(length):
        out[q_part, HEAD : 2 * HEAD] = turn_back(key_sum[q_part, :] * SCALE, q_part)
        out[q_part, 2 * HEAD :] = value_sum[q_part, :].astype(BF16)


def attend_back(start, tables, qkv, grad, logs):
    length, width = qkv.shape
    heads = width // (3 * HEAD)
    return call(
        "attend_back",
        attend_back_body,
        (heads,),
        (start, *tables, qkv, grad, logs),
        [fixed((8, length))]
        + [fixed((length, HEAD))] * 2
        + [
            cols_of((length, 3 * HEAD)),
            cols_of((length, HEAD)),
            pl.BlockSpec((1, 8, length), lambda i: (i, 0, 0)),
        ],
        [shape((length, width), BF16)],
        [cols_of((length, 3 * HEAD))],
        scratch=[pltpu.VMEM((length, HEAD), F32)] * 2,
        flops=10 * length * 768 * HEAD * heads,
    )[0]


def feed_body(n, me, *refs):
    attended, xs, outs_w = refs[:n], refs[n : 2 * n], refs[2 * n : 3 * n]
    own, gain, bias, up_bias, up_weight, down_weight = refs[3 * n : 3 * n + 6]
    hidden, normed, stat, activated, slope = refs[3 * n + 6 : 3 * n + 11]
    parts = refs[3 * n + 11 : 4 * n + 11]
    out_held, up_held, down_held, joined, whole, sems = refs[4 * n + 11 :]
    width = xs[0].shape[1]
    full = n * width
    inner = up_held.shape[1]
    out_copies = []
    for j in range(n):
        for k in range(n):
            out_copies.append(
                pltpu.make_async_copy(
                    outs_w[k].at[:, place_of(me[0], j, width)],
                    out_held.at[pl.ds(k * width, width), pl.ds(j * width, width)],
                    sems.at[k * n + j],
                )
            )
    step = divisor(inner, 512)
    up_copies = []
    for c in range(inner // step):
        part = pl.ds(c * step, step)
        up_copies.append(
            pltpu.make_async_copy(up_weight.at[:, part], up_held.at[:, part], sems.at[n * n + n + c])
        )
    down_copies = col_blocks(me[0], n, width, down_weight, down_held, sems, n * n)
    start_all(out_copies + up_copies + down_copies)
    for j in range(n):
        joined[:, j * width : (j + 1) * width] = attended[j][...]
    total = square = 0.0
    for j in range(n):
        wait_all(out_copies[j * n : (j + 1) * n])
        part = slice(j * width, (j + 1) * width)
        base = own[...] if j == 0 else xs[j][...].astype(F32)
        value = base + dot_nn(joined[...], out_held[:, part])
        whole[:, part] = value
        if j == 0:
            hidden[...] = value
        total += jnp.sum(value, 1, keepdims=True)
        square += jnp.sum(value * value, 1, keepdims=True)
    mean = total / full
    inv = lax.rsqrt(square / full - mean * mean + EPSILON)
    stat[...] = stat_columns(mean, inv)
    for j in range(n):
        part = slice(j * width, (j + 1) * width)
        normed[:, place_of(me[0], j, width)] = (
            (whole[:, part] - mean) * inv * gain[0:1, part] + bias[0:1, part]
        ).astype(BF16)
    for c in range(inner // step):
        wait_all(up_copies[c : c + 1])
        part = slice(c * step, (c + 1) * step)
        up = dot_nn(normed[...], up_held[:, part]) + up_bias[0:1, part]
        half = 0.5 * (1.0 + lax.erf(up * SQRT_HALF))
        activated[:, part] = (up * half).astype(BF16)
        slope[:, part] = (half + up * INV_ROOT_TWO_PI * jnp.exp(-0.5 * up * up)).astype(BF16)
    for j in range(n):
        wait_all(down_copies[j : j + 1])
        parts[j][...] = dot_nn(
            activated[...], down_held[:, j * width : (j + 1) * width]
        ).astype(BF16)


def feed(me, attended, xs, outs_w, own, gain, bias, up_bias, up_weight, down_weight):
    n, (length, width) = len(xs), own.shape
    full, inner = up_weight.shape
    tile = min(256, length)
    got = call(
        "feed",
        lambda *refs: feed_body(n, *refs),
        (length // tile,),
        (me, *attended, *xs, *outs_w, own, gain, bias, up_bias, up_weight, down_weight),
        [SMEM]
        + [rows_of((tile, width))] * (2 * n)
        + [ANY] * n
        + [rows_of((tile, width))]
        + [fixed((8, full))] * 2
        + [fixed((8, inner))]
        + [ANY] * 2,
        [
            shape((length, width), F32),
            shape((length, full), BF16),
            shape((length, 128), F32),
            shape((length, inner), BF16),
            shape((length, inner), BF16),
        ]
        + [shape((length, width), BF16)] * n,
        [
            rows_of((tile, width)),
            rows_of((tile, full)),
            rows_of((tile, 128)),
            rows_of((tile, inner)),
            rows_of((tile, inner)),
        ]
        + [rows_of((tile, width))] * n,
        scratch=[
            pltpu.VMEM((full, full), BF16),
            pltpu.VMEM((full, inner), BF16),
            pltpu.VMEM((inner, full), BF16),
            pltpu.VMEM((tile, full), BF16),
            pltpu.VMEM((tile, full), F32),
            pltpu.SemaphoreType.DMA((n * n + n + inner // divisor(inner, 512),)),
        ],
        flops=2 * length * full * (full + 2 * inner),
    )
    return (*got[:5], got[5:])


def row_stats(total, weighted):
    return stat_columns(total, weighted).T[0:8, :]


def join_body(n, me, *refs):
    blocks, whole, sums = refs[:n], refs[n], refs[n + 1]
    width = blocks[0].shape[1]
    for j in range(n):
        whole[:, place_of(me[0], j, width)] = blocks[j][...]
    accumulate(sums, fold_rows(blocks[0][...].astype(F32)))


def join(me, blocks):
    n, (length, width) = len(blocks), blocks[0].shape
    tile = min(256, length)
    return call(
        "join",
        lambda *refs: join_body(n, *refs),
        (length // tile,),
        (me, *blocks),
        [SMEM] + [rows_of((tile, width))] * n,
        [shape((length, n * width), BF16), shape((8, width), F32)],
        [rows_of((tile, n * width)), fixed((8, width))],
    )


def feed_back_body(n, me, *refs):
    cot, slope, normed, gain, bias, up_weight, down_weight = refs[:7]
    up_grad, sums, up_bias_sum = refs[7:10]
    parts = refs[10 : n + 10]
    up_held, down_held, sems = refs[n + 10 :]
    width = parts[0].shape[1]
    inner = up_held.shape[1]
    step = divisor(inner, 512)
    steps = inner // step
    down_copies = []
    for c in range(steps):
        part = pl.ds(c * step, step)
        down_copies.append(
            pltpu.make_async_copy(down_weight.at[part, :], down_held.at[part, :], sems.at[n + c])
        )
    up_copies = row_blocks(me[0], n, width, up_weight, up_held, sems, 0)
    start_all(down_copies + up_copies)
    bias_parts = []
    for c in range(steps):
        wait_all(down_copies[c : c + 1])
        part = slice(c * step, (c + 1) * step)
        value = dot_nt(cot[...], down_held[part, :]) * slope[:, part].astype(F32)
        low = value.astype(BF16)
        up_grad[:, part] = low
        bias_parts.append(fold_rows(low.astype(F32)))
    accumulate(up_bias_sum, jnp.concatenate(bias_parts, 1))
    total = weighted = 0.0
    for j in range(n):
        wait_all(up_copies[j : j + 1])
        part = slice(j * width, (j + 1) * width)
        value = dot_nt(up_grad[...], up_held[part, :])
        parts[j][...] = value.astype(BF16)
        total += jnp.sum(value * gain[0:1, part], 1, keepdims=True)
        there = normed[:, place_of(me[0], j, width)].astype(F32)
        weighted += jnp.sum(value * (there - bias[0:1, part]), 1, keepdims=True)
    sums[...] = row_stats(total, weighted)


def feed_back(me, n, cot, slope, normed, gain, bias, up_weight, down_weight):
    length, full = cot.shape
    width = full // n
    inner = up_weight.shape[1]
    tile = min(256, length)
    got = call(
        "feed_back",
        lambda *refs: feed_back_body(n, *refs),
        (length // tile,),
        (me, cot, slope, normed, gain, bias, up_weight, down_weight),
        [SMEM]
        + [rows_of((tile, full)), rows_of((tile, inner)), rows_of((tile, full))]
        + [fixed((8, full))] * 2
        + [ANY] * 2,
        [shape((length, inner), BF16), shape((8, length), F32), shape((8, inner), F32)]
        + [shape((length, width), BF16)] * n,
        [rows_of((tile, inner)), cols_of((8, tile)), fixed((8, inner))]
        + [rows_of((tile, width))] * n,
        scratch=[
            pltpu.VMEM((full, inner), BF16),
            pltpu.VMEM((inner, full), BF16),
            pltpu.SemaphoreType.DMA((n + inner // divisor(inner, 512),)),
        ],
        flops=4 * length * full * inner,
    )
    return (*got[:3], got[3:])


def norm_back(refs, n_parts, source, stat, sums, gain, full):
    grad = refs[0][...].astype(F32)
    for ref in refs[1:n_parts]:
        grad += ref[...].astype(F32)
    columns = sums[...].T
    mean, inv = stat[:, 0:1], stat[:, 1:2]
    scaled = (source[...] - mean) * inv
    back = inv * (
        grad * gain[0:1, :] - columns[:, 0:1] * (1.0 / full) - scaled * (columns[:, 1:2] * (1.0 / full))
    )
    return back, fold_rows(grad * scaled), fold_rows(grad)


def hidden_back_body(k, full, *refs):
    parts = refs[:k]
    cot, hidden, stat, sums, gain, wide, low, gain_sum, bias_sum = refs[k:]
    back, gain_part, bias_part = norm_back(parts, k, hidden, stat, sums, gain, full)
    value = cot[...].astype(F32) + back
    wide[...] = value
    low[...] = value.astype(BF16)
    accumulate(gain_sum, gain_part)
    accumulate(bias_sum, bias_part)


def hidden_back(parts, cotangent, row, hidden, stat, sums, gain, full):
    k, (length, width) = len(parts), hidden.shape
    tile = min(256, length)
    steps = length // tile
    return call(
        "hidden_back",
        lambda *refs: hidden_back_body(k, full, *refs),
        (steps,),
        (*parts, cotangent, hidden, stat, sums, gain),
        [rows_of((tile, width))] * k
        + [
            pl.BlockSpec((tile, width), lambda i: (row * steps + i, 0)),
            rows_of((tile, width)),
            rows_of((tile, 128)),
            cols_of((8, tile)),
            fixed((8, width)),
        ],
        [shape((length, width), F32), shape((length, width), BF16)] + [shape((8, width), F32)] * 2,
        [rows_of((tile, width))] * 2 + [fixed((8, width))] * 2,
        flops=20 * length * width,
    )


def attended_back_body(n, me, *refs):
    grads = refs[:n]
    weight, joined, out = refs[n:]
    width = grads[0].shape[1]
    for j in range(n):
        joined[:, place_of(me[0], j, width)] = grads[j][...]
    out[...] = dot_nt(joined[...], weight[...]).astype(BF16)


def attended_back(me, grads, weight):
    n, (length, width) = len(grads), grads[0].shape
    rows, full = weight.shape
    tile = min(256, length)
    return call(
        "attended_back",
        lambda *refs: attended_back_body(n, *refs),
        (length // tile,),
        (me, *grads, weight),
        [SMEM] + [rows_of((tile, width))] * n + [fixed((rows, full))],
        [shape((length, full), BF16), shape((length, rows), BF16)],
        [rows_of((tile, full)), rows_of((tile, rows))],
        flops=2 * length * full * rows,
    )


def project_back_body(n, me, grad, normed, gain, bias, weight, sums, *refs):
    parts = refs[:n]
    held, sems = refs[n:]
    width = parts[0].shape[1]
    copies = row_blocks(me[0], n, width, weight, held, sems, 0)
    start_all(copies)
    total = weighted = 0.0
    for j in range(n):
        wait_all(copies[j : j + 1])
        part = slice(j * width, (j + 1) * width)
        value = dot_nt(grad[...], held[part, :])
        parts[j][...] = value.astype(BF16)
        total += jnp.sum(value * gain[0:1, part], 1, keepdims=True)
        there = normed[:, place_of(me[0], j, width)].astype(F32)
        weighted += jnp.sum(value * (there - bias[0:1, part]), 1, keepdims=True)
    sums[...] = row_stats(total, weighted)


def project_back(me, n, grad, normed, gain, bias, weight):
    length, out = grad.shape
    full = weight.shape[0]
    width = full // n
    tile = min(256, length)
    got = call(
        "project_back",
        lambda *refs: project_back_body(n, *refs),
        (length // tile,),
        (me, grad, normed, gain, bias, weight),
        [SMEM, rows_of((tile, out)), rows_of((tile, full))] + [fixed((8, full))] * 2 + [ANY],
        [shape((8, length), F32)] + [shape((length, width), BF16)] * n,
        [cols_of((8, tile))] + [rows_of((tile, width))] * n,
        scratch=[pltpu.VMEM((full, out), BF16), pltpu.SemaphoreType.DMA((n,))],
        flops=2 * length * full * out,
    )
    return got[0], got[1:]


def average_back_body(k, full, count, *refs):
    weights, parts = refs[0], refs[1 : k + 1]
    source, stat, sums, gain, hidden_grad, history = refs[k + 1 : k + 7]
    grad_history, depth_sum, gain_sum, bias_sum = refs[-4:]
    back, gain_part, bias_part = norm_back(parts, k, source, stat, sums, gain, full)
    value = hidden_grad[...] + back
    accumulate(gain_sum, gain_part)
    accumulate(bias_sum, bias_part)
    lanes = value.shape[1] // 128
    for j in range(count):
        grad_history[j] = (weights[j] * value).astype(BF16)
        product = fold_rows(value * history[j].astype(F32))
        folded = product[:, 0:128]
        for c in range(1, lanes):
            folded += product[:, c * 128 : (c + 1) * 128]
        accumulate(depth_sum.at[j], folded)


def average_back(weights, parts, source, stat, sums, gain, hidden_grad, history, row, made):
    k, (length, width) = len(parts), source.shape
    count = history.shape[0]
    tile = min(256, length)
    steps = length // tile
    full = gain[1]
    block = pl.BlockSpec((count, tile, width), lambda i: (0, row * steps + i, 0))
    args = (weights, *parts, source, stat, sums, gain[0], hidden_grad, history)
    specs = (
        [SMEM]
        + [rows_of((tile, width))] * (k + 1)
        + [rows_of((tile, 128)), cols_of((8, tile)), fixed((8, width)), rows_of((tile, width)), block]
    )
    more = {}
    if made is not None:
        more = {"aliases": {len(args): 0}}
        args, specs = (*args, made), specs + [ANY]
    return call(
        "average_back",
        lambda *refs: average_back_body(k, full, count, *refs),
        (steps,),
        args,
        specs,
        [shape(history.shape, BF16), shape((count, 8, 128), F32)] + [shape((8, width), F32)] * 2,
        [block, fixed((count, 8, 128))] + [fixed((8, width))] * 2,
        flops=6 * count * length * width,
        **more,
    )


def divisor(size, most):
    return max(d for d in range(128, most + 1, 128) if size % d == 0) if size > 128 else size


def weight_body(rows, *refs):
    out = refs[-1]
    total = dot_tn(refs[0][...], refs[rows][...])
    for r in range(1, rows):
        total += dot_tn(refs[r][...], refs[rows + r][...])
    out[...] = total.astype(BF16)


def weight_grad(lefts, rights):
    rows, (length, high), wide = len(lefts), lefts[0].shape, rights[0].shape[1]
    tall, across = divisor(high, 512), divisor(wide, 1024)
    return call(
        "weight_grad",
        lambda *refs: weight_body(rows, *refs),
        (high // tall, wide // across),
        (*lefts, *rights),
        [pl.BlockSpec((length, tall), lambda i, j: (0, i))] * rows
        + [pl.BlockSpec((length, across), lambda i, j: (0, j))] * rows,
        [shape((high, wide), BF16)],
        [pl.BlockSpec((tall, across), lambda i, j: (i, j))],
        flops=2 * rows * length * high * wide,
    )[0]


def tall_blocks_body(rows, count, group, *refs):
    lefts, rights = refs[: rows * count], refs[rows * count : rows * count + rows]
    out, turned = refs[-2:]
    high = lefts[0].shape[1]
    length = lefts[0].shape[0]

    @pl.when(pl.program_id(0) == 0)
    def _():
        for k in range(count):
            for r in range(rows):
                turned[k * high : (k + 1) * high, r * length : (r + 1) * length] = lefts[
                    k * rows + r
                ][...].T

    total = 0.0
    for r in range(rows):
        total += dot_nn(turned[:, r * length : (r + 1) * length], rights[r][...])
    out[...] = total.astype(BF16).reshape(out.shape)


def wide_blocks_body(rows, count, group, *refs):
    lefts, rights = refs[:rows], refs[rows : rows + rows * count]
    out = refs[-1]
    turned = [left[...].T for left in lefts]
    for k in range(count):
        total = 0.0
        for r in range(rows):
            total += dot_nn(turned[r], rights[k * rows + r][...])
        out[k] = total.astype(BF16)


class Spread:
    def __init__(self, lefts, rights, dim, bits, part=(0, 1)):
        self.lefts, self.rights, self.dim, self.bits, self.part = lefts, rights, dim, list(bits), part
        self.groups = lax.axis_size("dp")
        self.block = (lefts, rights)[dim][0].shape[1] // self.groups
        order = [0]
        for bit in reversed(self.bits):
            order = order + [e | bit for e in order]
        self.order = order

    def blocks(self, half):
        count = self.groups // 2
        which = self.order[half * count : (half + 1) * count]
        rows, length = len(self.lefts), self.lefts[0].shape[0]
        group = lax.axis_index("dp").astype(jnp.int32)[None]
        size, (index, pieces) = self.block, self.part
        stay = [
            pl.BlockSpec((length, size), lambda i, group, e=e: (0, group[0] ^ e))
            for e in which
            for _ in range(rows)
        ]
        other = self.rights if self.dim == 0 else self.lefts
        extent = other[0].shape[1] // pieces
        tile = divisor(extent, 512)
        steps = extent // tile
        move = [pl.BlockSpec((length, tile), lambda i, group: (0, index * steps + i))] * rows
        if self.dim == 0:
            args = (*(list(self.lefts) * count), *self.rights)
            specs = stay + move
            out, spec = (count, size, extent), pl.BlockSpec((count, size, tile), lambda i, group: (0, 0, i))
            body, scratch = tall_blocks_body, [pltpu.VMEM((count * size, rows * length), BF16)]
        else:
            args = (*self.lefts, *(list(self.rights) * count))
            specs = move + stay
            out, spec = (count, extent, size), pl.BlockSpec((count, tile, size), lambda i, group: (0, i, 0))
            body, scratch = wide_blocks_body, []
        return call(
            "weight_blocks",
            lambda *refs: body(rows, count, *refs),
            (steps,),
            (group, *args),
            specs,
            [shape(out, BF16)],
            [spec],
            scratch=scratch,
            flops=2 * rows * length * count * size * extent,
            prefetch=1,
        )[0]

    def send(self, value, step):
        bit = self.bits[step]
        return lax.ppermute(value, "dp", [(i, i ^ bit) for i in range(self.groups)])

    def first(self):
        self.coming = self.send(self.blocks(1), 0)
        self.step = 1

    def keep(self):
        self.held = self.blocks(0)

    def next(self):
        self.held, out = fold(self.held, self.coming)
        self.coming = self.send(out, self.step)
        self.step += 1

    def finish(self):
        return fold_last(self.held, self.coming)


def fold_body(held, came, keep, send):
    half = keep.shape[0]
    keep[...] = (held[:half].astype(F32) + came[:half].astype(F32)).astype(BF16)
    send[...] = (held[half:].astype(F32) + came[half:].astype(F32)).astype(BF16)


def fold(held, came):
    count, high, wide = held.shape
    tile = max(16, high // 4)
    full = pl.BlockSpec((count, tile, wide), lambda i: (0, i, 0))
    half = pl.BlockSpec((count // 2, tile, wide), lambda i: (0, i, 0))
    return call(
        "fold",
        fold_body,
        (high // tile,),
        (held, came),
        [full, full],
        [shape((count // 2, high, wide), BF16)] * 2,
        [half, half],
    )


def fold_last_body(held, came, out):
    out[...] = held[0].astype(F32) + came[0].astype(F32)


def fold_last(held, came):
    _, high, wide = held.shape
    tile = max(16, high // 4)
    spec = pl.BlockSpec((1, tile, wide), lambda i: (0, i, 0))
    return call(
        "fold_last",
        fold_last_body,
        (high // tile,),
        (held, came),
        [spec, spec],
        [shape((high, wide), F32)],
        [rows_of((tile, wide))],
    )[0]


def add_body(left, right, out):
    out[...] = (left[...].astype(F32) + right[...].astype(F32)).astype(BF16)


def add(left, right):
    length, width = left.shape
    tile = min(512, length)
    return call(
        "add",
        add_body,
        (length // tile,),
        (left, right),
        [rows_of((tile, width))] * 2,
        [shape((length, width), BF16)],
        [rows_of((tile, width))],
    )[0]


def output_body(k, *refs):
    parts, hidden, bias, out = refs[:k], refs[k], refs[k + 1], refs[-1]
    total = bias[0:1, :]
    for part in parts:
        total = total + part[...].astype(F32)
    out[...] = (hidden[...] + total).astype(BF16)


def output(parts, hidden, bias, row, rows, made):
    k, (length, width) = len(parts), hidden.shape
    tile = min(512, length)
    steps = length // tile
    args = (*parts, hidden, bias)
    specs = [rows_of((tile, width))] * (k + 1) + [fixed((8, width))]
    if made is not None:
        args, specs = (*args, made), specs + [ANY]
    return call(
        "output",
        lambda *refs: output_body(k, *refs),
        (steps,),
        args,
        specs,
        [shape((rows * length, width), BF16)],
        [pl.BlockSpec((tile, width), lambda i: (row * steps + i, 0))],
        aliases=None if made is None else {k + 2: 0},
    )[0]


class Ring:
    def __init__(self):
        self.n = lax.axis_size("mp")
        self.me = lax.axis_index("mp").astype(jnp.int32)
        self.pairs = self.n == 4
        self.core = [(i, i ^ 1) for i in range(self.n)]
        self.chip = [(i, i ^ 2) for i in range(self.n)]

    def over_core(self, value):
        return lax.ppermute(value, "mp", self.core)

    def over_chip(self, value):
        return lax.ppermute(value, "mp", self.chip)

    def gather(self, block):
        if self.pairs:
            sibling = self.over_core(block)
            across = self.over_chip(block)
            return [block, sibling, across, self.over_core(across)]
        every = lax.all_gather(block, "mp")
        return [
            lax.dynamic_index_in_dim(every, self.me ^ j, 0, keepdims=False) for j in range(self.n)
        ]

    def scatter_start(self, parts):
        if self.pairs:
            other, mine = self.over_core(parts[3]), self.over_core(parts[1])
            return (parts[0], mine, parts[2], other)
        return parts

    def scatter(self, parts):
        if self.pairs:
            return [parts[0], parts[1], self.over_chip(add(parts[2], parts[3]))]
        stacked = jnp.stack([part.astype(F32) for part in parts])
        ordered = jnp.take(stacked, self.me ^ jnp.arange(self.n), axis=0)
        return [lax.psum_scatter(ordered, "mp", scatter_dimension=0, tiled=False)]

    def total(self, value):
        if self.pairs:
            value = value + self.over_core(value)
            return value + self.over_chip(value)
        return lax.psum(value, "mp")

    def out_blocks(self, weight):
        rows = weight.shape[0]
        groups = lax.axis_size("dp")
        if self.pairs and rows % (16 * groups) == 0:
            size = rows // groups
            piece = lax.dynamic_slice_in_dim(weight, lax.axis_index("dp") * size, size, 0)
            across = lax.all_gather(self.over_chip(piece), "dp", axis=0, tiled=True)
            return [weight, self.over_core(weight), across, self.over_core(across)]
        return self.gather(weight)


def dp_total(vectors):
    groups = lax.axis_size("dp")
    sizes = [v.size for v in vectors]
    packed = jnp.concatenate(vectors)
    packed = jnp.pad(packed, (0, -packed.size % 1024)).reshape(-1, 128)
    bit = 1
    while bit < groups:
        packed = packed + lax.ppermute(packed, "dp", [(i, i ^ bit) for i in range(groups)])
        bit *= 2
    packed = packed.reshape(-1)
    ends = np.cumsum(sizes)
    return [packed[end - size : end] for end, size in zip(ends, sizes)]


def tables_of(length):
    half = HEAD // 2
    rate = np.exp(np.arange(half, dtype=np.float64) * (-math.log(10000.0) / half))
    angle = np.arange(length, dtype=np.float64)[:, None] * rate[None, :]
    cosine, sine = np.cos(angle), np.sin(angle)
    return (
        jnp.asarray(np.concatenate([cosine, cosine], 1), F32),
        jnp.asarray(np.concatenate([-sine, sine], 1), F32),
    )


def local(
    history,
    depth_weights,
    segment_ids,
    first_gain,
    first_bias,
    qkv_weight,
    out_weight,
    second_gain,
    second_bias,
    up_weight,
    up_bias,
    down_weight,
    down_bias,
    cotangent,
):
    ring = Ring()
    n = ring.n
    me = ring.me[None]
    width = history.shape[2]
    full = n * width
    row_count, length = segment_ids.shape
    rows = range(row_count)
    tables = tables_of(length)
    earlier = (segment_ids[:, None, :] < segment_ids[:, :, None]).astype(jnp.int32)
    starts = jnp.broadcast_to(jnp.sum(earlier, -1)[:, None, :], (row_count, 8, length))

    vectors = jnp.stack([first_gain, first_bias, second_gain, second_bias])
    vectors = jnp.concatenate(ring.gather(jnp.repeat(vectors, 8, 0)), 1)
    gain1, bias1, gain2, bias2 = (vectors[8 * i : 8 * i + 8] for i in range(4))
    own1, own2 = gain1[:, :width], gain2[:, :width]
    up_bias8 = jnp.broadcast_to(up_bias[None], (8, up_bias.shape[0]))

    down_bias8 = jnp.broadcast_to(down_bias[None], (8, width))
    groups = lax.axis_size("dp")
    spread = full % (128 * groups) == 0

    Order.last = None
    out_w = ring.out_blocks(out_weight)
    cot_rows = [lax.slice_in_dim(cotangent, r * length, (r + 1) * length) for r in rows]

    wide, low = zip(*[average(depth_weights, history, r, length) for r in rows])
    qkv, normed1, stat1, attended, logs, xs, heads = [], [], [], [], [], [], []
    waits = []
    for r in rows:
        block = low[r] if r == 0 else gate([low[r]], waits)[0]
        xs.append(ring.gather(block))
        waits = xs[r][1:]
    for r in rows:
        got = project(me, xs[r], gain1, bias1, tables, qkv_weight)
        qkv.append(got[0])
        normed1.append(got[1])
        stat1.append(got[2])
        got = attend(starts[r], qkv[r])
        attended.append(got[0])
        logs.append(got[1])
        heads.append(ring.gather(attended[r]))

    hidden, normed2, stat2, activated, slope, branch, cots = [], [], [], [], [], [], []
    for r in rows:
        cots.append(ring.gather(gate([cot_rows[r]], heads[r][1:] if r == 0 else [])[0]))
        got = feed(
            me, heads[r], xs[r], out_w, wide[r], gain2, bias2, up_bias8, up_weight, down_weight
        )
        hidden.append(got[0])
        normed2.append(got[1])
        stat2.append(got[2])
        activated.append(got[3])
        slope.append(got[4])
        branch.append(ring.scatter_start(got[5]))

    up_grad, parts2, sums2, up_bias_sum, down_bias_sum = [], [], [], 0.0, 0.0
    cot_full = []
    branch[0] = ring.scatter(branch[0])
    for r in rows:
        got = join(me, cots[r])
        cot_full.append(got[0])
        down_bias_sum += got[1]
    down = Spread(activated, cot_full, 1, (1, 2, 4)) if spread else None
    if spread:
        down.first()
    for r in rows:
        if r > 0:
            branch[r] = ring.scatter(branch[r])
    for r in rows:
        got = feed_back(
            me, n, cot_full[r], slope[r], normed2[r], gain2, bias2, up_weight, down_weight
        )
        up_grad.append(got[0])
        sums2.append(ring.total(got[1]))
        up_bias_sum += got[2]
        parts2.append(ring.scatter_start(got[3]))
        if r == 0 and spread:
            down.keep()
        if r == 0:
            parts2[r] = ring.scatter(parts2[r])
    up = []
    if spread:
        up = [
            Spread(normed2, up_grad, 0, (1, 2, 4), (0, 2)),
            Spread(normed2, up_grad, 0, (2, 4, 1), (1, 2)),
        ]
        up[1].first()
        up[0].first()
    for r in rows:
        if r > 0:
            parts2[r] = ring.scatter(parts2[r])

    hidden_grad, gain2_sum, bias2_sum, grads = [], 0.0, 0.0, []
    for r in rows:
        got = hidden_back(parts2[r], cotangent, r, hidden[r], stat2[r], sums2[r], own2, full)
        hidden_grad.append(got[0])
        gain2_sum += got[2]
        bias2_sum += got[3]
        grads.append(ring.gather(got[1]))
        if r == 0 and spread:
            up[1].keep()
            up[0].keep()
    if spread:
        down.next()

    grad_full, qkv_grad, parts1, sums1 = [], [], [], []
    for r in rows:
        got = attended_back(me, grads[r], out_weight)
        if r == 1:
            parts1[0] = ring.scatter(parts1[0])
        grad_full.append(got[0])
        qkv_grad.append(attend_back(starts[r], tables, qkv[r], got[1], logs[r]))
        if r == 1 and spread:
            up[1].next()
            down.next()
        sums, parts = project_back(me, n, qkv_grad[r], normed1[r], gain1, bias1, qkv_weight)
        sums1.append(ring.total(sums))
        parts1.append(ring.scatter_start(parts))

    if spread:
        qkv_w = [
            Spread(normed1, qkv_grad, 0, (1, 2, 4), (0, 2)),
            Spread(normed1, qkv_grad, 0, (2, 4, 1), (1, 2)),
        ]
        out = Spread(attended, grad_full, 1, (2, 4, 1))
        qkv_w[0].first()
        qkv_w[1].first()
    for r in rows:
        if r > 0 or row_count == 1:
            parts1[r] = ring.scatter(parts1[r])
    made = None
    if spread:
        out.first()
        qkv_w[0].keep()
        qkv_w[1].keep()
        out.keep()
        up[0].next()
    for r in rows:
        made = output(branch[r], hidden[r], down_bias8, r, row_count, made)

    grad_history, depth_sum, gain1_sum, bias1_sum = None, 0.0, 0.0, 0.0
    for r in rows:
        got = average_back(
            depth_weights,
            parts1[r],
            wide[r],
            stat1[r],
            sums1[r],
            (own1, full),
            hidden_grad[r],
            history,
            r,
            grad_history,
        )
        grad_history = got[0]
        depth_sum += got[1]
        gain1_sum += got[2]
        bias1_sum += got[3]
        if r == 0 and spread:
            up[1].next()
            up[0].next()

    if spread:
        down_total = down.finish()
        qkv_w[0].next()
        qkv_w[1].next()
        out.next()
        up_total = [up[0].finish(), up[1].finish()]
        qkv_w[0].next()
        qkv_w[1].next()
        out.next()
        out_total = out.finish()
        qkv_total = [qkv_w[0].finish(), qkv_w[1].finish()]
        up_total, qkv_total = jnp.concatenate(up_total, 1), jnp.concatenate(qkv_total, 1)
    else:
        down_total, up_total, out_total, qkv_total = (
            lax.psum_scatter(
                weight_grad(*pair), "dp", scatter_dimension=dim, tiled=True
            ).astype(F32)
            for pair, dim in (
                ((activated, cot_full), 1),
                ((normed2, up_grad), 0),
                ((attended, grad_full), 1),
                ((normed1, qkv_grad), 0),
            )
        )

    early = dp_total([jnp.sum(v, 0) for v in (up_bias_sum, down_bias_sum, gain2_sum, bias2_sum)])
    late = dp_total([jnp.sum(gain1_sum, 0), jnp.sum(bias1_sum, 0), jnp.sum(depth_sum, (1, 2))])
    depth_grad = ring.total(late[2])
    return (
        made,
        grad_history,
        depth_grad,
        late[0],
        late[1],
        qkv_total,
        out_total,
        early[2],
        early[3],
        up_total,
        early[0],
        down_total,
        early[1],
    )


def solution(mesh):
    placed = (
        P(None, "dp", "mp"),
        P(),
        P("dp", None),
        P("mp"),
        P("mp"),
        P(None, "mp"),
        P("mp", None),
        P("mp"),
        P("mp"),
        P(None, "mp"),
        P("mp"),
        P("mp", None),
        P("mp"),
        P("dp", "mp"),
    )
    return jax.shard_map(
        local,
        mesh=mesh,
        in_specs=placed,
        out_specs=(
            P("dp", "mp"),
            P(None, "dp", "mp"),
            P(),
            P("mp"),
            P("mp"),
            P("dp", "mp"),
            P("mp", "dp"),
            P("mp"),
            P("mp"),
            P("dp", "mp"),
            P("mp"),
            P("mp", "dp"),
            P("mp"),
        ),
        check_vma=False,
    )
```

```python
import math

import jax
import jax.numpy as jnp
import numpy as np
from jax import lax
from jax.experimental import pallas as pl
from jax.experimental.pallas import tpu as pltpu
from jax.sharding import PartitionSpec as P

HEAD = 128
MAX_DOC = 512
EPSILON = 1e-05
SQRT_HALF = 0.7071067811865476
INV_ROOT_TWO_PI = 0.3989422804014327
LOG2E = 1.4426950408889634
SCALE = HEAD ** (-0.5)
MIB = 2**20
BF16 = jnp.bfloat16
F32 = jnp.float32


def dot_nn(a, b):
    return jnp.dot(a, b, preferred_element_type=F32)


def dot_nt(a, b):
    return lax.dot_general(a, b, (((1,), (1,)), ((), ())), preferred_element_type=F32)


def dot_tn(a, b):
    return lax.dot_general(a, b, (((0,), (0,)), ((), ())), preferred_element_type=F32)


class Order:
    last = None


def call(
    name, body, grid, args, in_specs, outs, out_specs, scratch=(), prefetch=0, after=(), aliases=None
):
    count = len(args)
    extra = [*after]
    if Order.last is not None and not any(Order.last is a for a in args):
        extra.append(Order.last)

    def without_extra(*refs):
        body(*refs[:count], *refs[count + len(extra) :])

    got = pl.pallas_call(
        without_extra,
        grid_spec=pltpu.PrefetchScalarGridSpec(
            num_scalar_prefetch=prefetch,
            grid=grid,
            in_specs=list(in_specs) + [ANY] * len(extra),
            out_specs=out_specs,
            scratch_shapes=list(scratch),
        ),
        out_shape=outs,
        input_output_aliases=aliases or {},
        compiler_params=pltpu.CompilerParams(vmem_limit_bytes=60 * MIB),
        cost_estimate=pl.CostEstimate(flops=1, bytes_accessed=1, transcendentals=0),
        name=name,
    )(*args, *extra)
    fresh = [v for i, v in enumerate(got) if i not in (aliases or {}).values()]
    Order.last = min(fresh or got, key=lambda v: v.size)
    return got


def shape(dims, dtype):
    return jax.ShapeDtypeStruct(dims, dtype)


SMEM = pl.BlockSpec(memory_space=pltpu.SMEM)
ANY = pl.BlockSpec(memory_space=pl.ANY)


def gate(arrays, after=()):
    arrays = list(arrays)
    return call(
        "gate",
        lambda *refs: None,
        (1,),
        arrays,
        [ANY] * len(arrays),
        [shape(a.shape, a.dtype) for a in arrays],
        [ANY] * len(arrays),
        after=after,
        aliases={i: i for i in range(len(arrays))},
    )


def rows_of(block):
    return pl.BlockSpec(block, lambda i: (i, 0))


def cols_of(block):
    return pl.BlockSpec(block, lambda i: (0, i))


def fixed(block):
    return pl.BlockSpec(block, lambda i: (0,) * len(block))


def place_of(me, j, width):
    return pl.ds(pl.multiple_of((me ^ j) * width, width), width)


def with_weights(copies, work):
    @pl.when(pl.program_id(0) == 0)
    def _():
        for one in copies:
            one.start()

        def wait(some):
            for one in some:
                one.wait()

        work(wait)

    @pl.when(pl.program_id(0) != 0)
    def _():
        work(lambda some: None)


def row_blocks(me, n, width, source, target, sems, base):
    return [
        pltpu.make_async_copy(
            source.at[place_of(me, j, width), :],
            target.at[pl.ds(j * width, width), :],
            sems.at[base + j],
        )
        for j in range(n)
    ]


def col_blocks(me, n, width, source, target, sems, base):
    return [
        pltpu.make_async_copy(
            source.at[:, place_of(me, j, width)],
            target.at[:, pl.ds(j * width, width)],
            sems.at[base + j],
        )
        for j in range(n)
    ]


def stat_columns(first, second):
    lane = lax.broadcasted_iota(jnp.int32, (first.shape[0], 128), 1)
    return jnp.where(lane == 0, first, jnp.where(lane == 1, second, 0.0))


def fold_rows(values):
    return jnp.sum(values.reshape(values.shape[0] // 8, 8, values.shape[1]), 0)


def accumulate(ref, value):
    @pl.when(pl.program_id(0) == 0)
    def _():
        ref[...] = value

    @pl.when(pl.program_id(0) != 0)
    def _():
        ref[...] += value


def average_body(weights, history, wide, low):
    total = weights[0] * history[0].astype(F32)
    for j in range(1, history.shape[0]):
        total += weights[j] * history[j].astype(F32)
    wide[...] = total
    low[...] = total.astype(BF16)


def average(weights, history, row, length):
    count, _, width = history.shape
    tile = min(256, length)
    steps = length // tile
    return call(
        "average",
        average_body,
        (steps,),
        (weights, history),
        [SMEM, pl.BlockSpec((count, tile, width), lambda i: (0, row * steps + i, 0))],
        [shape((length, width), F32), shape((length, width), BF16)],
        [rows_of((tile, width))] * 2,
    )


def project_body(n, me, *refs):
    xs = refs[:n]
    gain, bias, cosine, sine, weight, qkv, normed, stat, held, joined, sems = refs[n:]
    width = xs[0].shape[1]
    full = n * width
    heads = held.shape[1] // (3 * HEAD)
    tile = xs[0].shape[0]
    sub = min(256, tile)
    copies = row_blocks(me[0], n, width, weight, held, sems, 0)

    def work(wait):
        for t in range(tile // sub):
            rows = slice(t * sub, (t + 1) * sub)
            total = square = 0.0
            for x in xs:
                value = x[rows, :].astype(F32)
                total += jnp.sum(value, 1, keepdims=True)
                square += jnp.sum(value * value, 1, keepdims=True)
            mean = total / full
            inv = lax.rsqrt(square / full - mean * mean + EPSILON)
            stat[rows, :] = stat_columns(mean, inv)
            for j, x in enumerate(xs):
                part = slice(j * width, (j + 1) * width)
                value = (x[rows, :].astype(F32) - mean) * inv * gain[0:1, part] + bias[0:1, part]
                joined[rows, part] = value.astype(BF16)
                normed[rows, place_of(me[0], j, width)] = value.astype(BF16)
            if t == 0:
                wait(copies)
            for h in range(heads):
                base = 3 * h * HEAD
                out = dot_nn(joined[rows, :], held[:, base : base + 3 * HEAD])
                for s in range(2):
                    v = out[:, s * HEAD : (s + 1) * HEAD]
                    turned = v * cosine[rows, :] + pltpu.roll(v, HEAD // 2, 1) * sine[rows, :]
                    qkv[rows, base + s * HEAD : base + (s + 1) * HEAD] = turned.astype(BF16)
                qkv[rows, base + 2 * HEAD : base + 3 * HEAD] = out[:, 2 * HEAD :].astype(BF16)

    with_weights(copies, work)


def project(me, xs, gain, bias, tables, weight):
    n, (length, width) = len(xs), xs[0].shape
    full, out = weight.shape
    tile = min(512, length)
    return call(
        "project",
        lambda *refs: project_body(n, *refs),
        (length // tile,),
        (me, *xs, gain, bias, *tables, weight),
        [SMEM]
        + [rows_of((tile, width))] * n
        + [fixed((8, full))] * 2
        + [rows_of((tile, HEAD))] * 2
        + [ANY],
        [shape((length, out), BF16), shape((length, full), BF16), shape((length, 128), F32)],
        [rows_of((tile, out)), rows_of((tile, full)), rows_of((tile, 128))],
        scratch=[
            pltpu.VMEM((full, out), BF16),
            pltpu.VMEM((tile, full), BF16),
            pltpu.SemaphoreType.DMA((n,)),
        ],
    )


def windows(length):
    block = min(256, length)
    for i in range(length // block):
        low = max(0, i * block - (MAX_DOC - 1)) // block * block
        yield slice(i * block, (i + 1) * block), slice(low, (i + 1) * block)


def score_mask(start, q_part, k_part):
    dims = (k_part.stop - k_part.start, q_part.stop - q_part.start)
    k_pos = lax.broadcasted_iota(jnp.int32, dims, 0) + k_part.start
    q_pos = lax.broadcasted_iota(jnp.int32, dims, 1) + q_part.start
    return (k_pos >= start[0:1, q_part]) & (k_pos <= q_pos)


def attend_body(start, qkv, out, logs):
    length = qkv.shape[0]
    value_t = qkv[:, 2 * HEAD :].T
    for q_part, k_part in windows(length):
        query, key = qkv[q_part, :HEAD], qkv[k_part, HEAD : 2 * HEAD]
        scores = dot_nt(key, query) * (SCALE * LOG2E)
        scores = jnp.where(score_mask(start, q_part, k_part), scores, -1e30)
        top = jnp.max(scores, 0, keepdims=True)
        probs = jnp.exp2(scores - top)
        total = jnp.sum(probs, 0, keepdims=True)
        logs[0, :, q_part] = jnp.broadcast_to(top + jnp.log2(total), (8, q_part.stop - q_part.start))
        got = dot_nn(value_t[:, k_part], probs.astype(BF16)) / total
        out[q_part, :] = got.T.astype(BF16)


def attend(start, qkv):
    length, width = qkv.shape
    heads = width // (3 * HEAD)
    return call(
        "attend",
        attend_body,
        (heads,),
        (start, qkv),
        [fixed((8, length)), cols_of((length, 3 * HEAD))],
        [shape((length, heads * HEAD), BF16), shape((heads, 8, length), F32)],
        [cols_of((length, HEAD)), pl.BlockSpec((1, 8, length), lambda i: (i, 0, 0))],
    )


def attend_back_body(start, cosine, sine, qkv, grad, logs, out, key_sum, value_sum):
    length = qkv.shape[0]
    key_t = qkv[:, HEAD : 2 * HEAD].T
    key_sum[...] = jnp.zeros_like(key_sum)
    value_sum[...] = jnp.zeros_like(value_sum)

    def turn_back(v, part):
        return (
            v * cosine[part, :] - pltpu.roll(v, HEAD // 2, 1) * sine[part, :]
        ).astype(BF16)

    for q_part, k_part in windows(length):
        query, key = qkv[q_part, :HEAD], qkv[k_part, HEAD : 2 * HEAD]
        value, g = qkv[k_part, 2 * HEAD :], grad[q_part, :]
        scores = dot_nt(key, query) * (SCALE * LOG2E) - logs[0, 0:1, q_part]
        probs = jnp.exp2(jnp.where(score_mask(start, q_part, k_part), scores, -1e30))
        prob_grad = dot_nt(value, g)
        mean = jnp.sum(prob_grad * probs, 0, keepdims=True)
        score_grad = (probs * (prob_grad - mean)).astype(BF16)
        value_sum[k_part, :] += dot_nn(probs.astype(BF16), g)
        key_sum[k_part, :] += dot_nn(score_grad, query)
        query_grad = dot_nn(key_t[:, k_part], score_grad) * SCALE
        out[q_part, :HEAD] = turn_back(query_grad.T, q_part)
    for q_part, _ in windows(length):
        out[q_part, HEAD : 2 * HEAD] = turn_back(key_sum[q_part, :] * SCALE, q_part)
        out[q_part, 2 * HEAD :] = value_sum[q_part, :].astype(BF16)


def attend_back(start, tables, qkv, grad, logs):
    length, width = qkv.shape
    heads = width // (3 * HEAD)
    return call(
        "attend_back",
        attend_back_body,
        (heads,),
        (start, *tables, qkv, grad, logs),
        [fixed((8, length))]
        + [fixed((length, HEAD))] * 2
        + [
            cols_of((length, 3 * HEAD)),
            cols_of((length, HEAD)),
            pl.BlockSpec((1, 8, length), lambda i: (i, 0, 0)),
        ],
        [shape((length, width), BF16)],
        [cols_of((length, 3 * HEAD))],
        scratch=[pltpu.VMEM((length, HEAD), F32)] * 2,
    )[0]


def feed_body(n, beside, me, *refs):
    attended, xs, outs_w = refs[:n], refs[n : 2 * n], refs[2 * n : 3 * n]
    own, gain, bias, up_bias, up_weight, down_weight = refs[3 * n : 3 * n + 6]
    extra = refs[3 * n + 6 : 3 * n + 6 + beside]
    refs = refs[3 * n + 6 + beside :]
    hidden, normed, stat, activated, slope = refs[:5]
    parts = refs[5 : n + 5]
    refs = refs[n + 5 :]
    if beside:
        put_beside(me, extra, *refs[:2])
        refs = refs[2:]
    out_held, up_held, down_held, joined, whole, sems = refs
    width = xs[0].shape[1]
    full = n * width
    inner = up_held.shape[1]
    out_copies = []
    for j in range(n):
        for k in range(n):
            out_copies.append(
                pltpu.make_async_copy(
                    outs_w[k].at[:, place_of(me[0], j, width)],
                    out_held.at[pl.ds(k * width, width), pl.ds(j * width, width)],
                    sems.at[j * n + k],
                )
            )
    up_copies = row_blocks(me[0], n, width, up_weight, up_held, sems, n * n)
    down_copies = col_blocks(me[0], n, width, down_weight, down_held, sems, n * n + n)

    def work(wait):
        for j in range(n):
            joined[:, j * width : (j + 1) * width] = attended[j][...]
        total = square = 0.0
        for j in range(n):
            wait(out_copies[j * n : (j + 1) * n])
            part = slice(j * width, (j + 1) * width)
            base = own[...] if j == 0 else xs[j][...].astype(F32)
            value = base + dot_nn(joined[...], out_held[:, part])
            whole[:, part] = value
            if j == 0:
                hidden[...] = value
            total += jnp.sum(value, 1, keepdims=True)
            square += jnp.sum(value * value, 1, keepdims=True)
        mean = total / full
        inv = lax.rsqrt(square / full - mean * mean + EPSILON)
        stat[...] = stat_columns(mean, inv)
        for j in range(n):
            part = slice(j * width, (j + 1) * width)
            value = ((whole[:, part] - mean) * inv * gain[0:1, part] + bias[0:1, part]).astype(BF16)
            joined[:, part] = value
            normed[:, place_of(me[0], j, width)] = value
        wait(up_copies)
        step = divisor(inner, 512)
        for c in range(inner // step):
            part = slice(c * step, (c + 1) * step)
            up = dot_nn(joined[...], up_held[:, part]) + up_bias[0:1, part]
            half = 0.5 * (1.0 + lax.erf(up * SQRT_HALF))
            activated[:, part] = (up * half).astype(BF16)
            slope[:, part] = (half + up * INV_ROOT_TWO_PI * jnp.exp(-0.5 * up * up)).astype(BF16)
        wait(down_copies)
        for j in range(n):
            parts[j][...] = dot_nn(
                activated[...], down_held[:, j * width : (j + 1) * width]
            ).astype(BF16)

    with_weights(out_copies + up_copies + down_copies, work)


def put_beside(me, blocks, whole, sums):
    width = blocks[0].shape[1]
    for j, block in enumerate(blocks):
        whole[:, place_of(me[0], j, width)] = block[...]
    accumulate(sums, fold_rows(blocks[0][...].astype(F32)))


def feed(me, attended, xs, outs_w, own, gain, bias, up_bias, up_weight, down_weight, beside=()):
    n, (length, width) = len(xs), own.shape
    full, inner = up_weight.shape
    tile = min(256, length)
    got = call(
        "feed",
        lambda *refs: feed_body(n, len(beside), *refs),
        (length // tile,),
        (me, *attended, *xs, *outs_w, own, gain, bias, up_bias, up_weight, down_weight, *beside),
        [SMEM]
        + [rows_of((tile, width))] * (2 * n)
        + [ANY] * n
        + [rows_of((tile, width))]
        + [fixed((8, full))] * 2
        + [fixed((8, inner))]
        + [ANY] * 2
        + [rows_of((tile, width))] * len(beside),
        [
            shape((length, width), F32),
            shape((length, full), BF16),
            shape((length, 128), F32),
            shape((length, inner), BF16),
            shape((length, inner), BF16),
        ]
        + [shape((length, width), BF16)] * n
        + ([shape((length, full), BF16), shape((8, width), F32)] if beside else []),
        [
            rows_of((tile, width)),
            rows_of((tile, full)),
            rows_of((tile, 128)),
            rows_of((tile, inner)),
            rows_of((tile, inner)),
        ]
        + [rows_of((tile, width))] * n
        + ([rows_of((tile, full)), fixed((8, width))] if beside else []),
        scratch=[
            pltpu.VMEM((full, full), BF16),
            pltpu.VMEM((full, inner), BF16),
            pltpu.VMEM((inner, full), BF16),
            pltpu.VMEM((tile, full), BF16),
            pltpu.VMEM((tile, full), F32),
            pltpu.SemaphoreType.DMA((n * n + 2 * n,)),
        ],
    )
    return (*got[:5], got[5 : n + 5], got[n + 5 :])


def row_stats(total, weighted):
    return stat_columns(total, weighted).T[0:8, :]


def beside(me, blocks):
    n, (length, width) = len(blocks), blocks[0].shape
    tile = min(256, length)
    return call(
        "beside",
        lambda me, *refs: put_beside(me, refs[:n], *refs[n:]),
        (length // tile,),
        (me, *blocks),
        [SMEM] + [rows_of((tile, width))] * n,
        [shape((length, n * width), BF16), shape((8, width), F32)],
        [rows_of((tile, n * width)), fixed((8, width))],
    )


def feed_back_body(n, beside, joined_in, me, *refs):
    cots, refs = refs[:joined_in], refs[joined_in:]
    slope, normed, gain, bias, up_weight, down_weight = refs[:6]
    extra, refs = refs[6 : 6 + beside], refs[6 + beside :]
    up_grad, sums, up_bias_sum = refs[:3]
    parts, refs = refs[3 : n + 3], refs[n + 3 :]
    if beside:
        put_beside(me, extra, *refs[:2])
        refs = refs[2:]
    up_held, down_held, sems = refs
    width = parts[0].shape[1]
    inner = up_held.shape[1]
    step = divisor(inner, 512)
    down_copies = [pltpu.make_async_copy(down_weight, down_held, sems.at[n])]
    up_copies = row_blocks(me[0], n, width, up_weight, up_held, sems, 0)
    cot = cots[0]

    def work(wait):
        wait(down_copies)
        bias_parts = []
        for c in range(inner // step):
            part = slice(c * step, (c + 1) * step)
            value = dot_nt(cot[...], down_held[part, :]) * slope[:, part].astype(F32)
            low = value.astype(BF16)
            up_grad[:, part] = low
            bias_parts.append(fold_rows(low.astype(F32)))
        accumulate(up_bias_sum, jnp.concatenate(bias_parts, 1))
        total = weighted = 0.0
        wait(up_copies)
        for j in range(n):
            part = slice(j * width, (j + 1) * width)
            value = dot_nt(up_grad[...], up_held[part, :])
            parts[j][...] = value.astype(BF16)
            total += jnp.sum(value * gain[0:1, part], 1, keepdims=True)
            there = normed[:, place_of(me[0], j, width)].astype(F32)
            weighted += jnp.sum(value * (there - bias[0:1, part]), 1, keepdims=True)
        sums[...] = row_stats(total, weighted)

    with_weights(down_copies + up_copies, work)


def feed_back(me, n, cot, slope, normed, gain, bias, up_weight, down_weight, beside=()):
    length, full = cot.shape
    width = full // n
    inner = up_weight.shape[1]
    tile = min(256, length)
    got = call(
        "feed_back",
        lambda *refs: feed_back_body(n, len(beside), 1, *refs),
        (length // tile,),
        (me, cot, slope, normed, gain, bias, up_weight, down_weight, *beside),
        [SMEM]
        + [rows_of((tile, full)), rows_of((tile, inner)), rows_of((tile, full))]
        + [fixed((8, full))] * 2
        + [ANY] * 2
        + [rows_of((tile, width))] * len(beside),
        [shape((length, inner), BF16), shape((8, length), F32), shape((8, inner), F32)]
        + [shape((length, width), BF16)] * n
        + ([shape((length, full), BF16), shape((8, width), F32)] if beside else []),
        [rows_of((tile, inner)), cols_of((8, tile)), fixed((8, inner))]
        + [rows_of((tile, width))] * n
        + ([rows_of((tile, full)), fixed((8, width))] if beside else []),
        scratch=[
            pltpu.VMEM((full, inner), BF16),
            pltpu.VMEM((inner, full), BF16),
            pltpu.SemaphoreType.DMA((n + 1,)),
        ],
    )
    return (*got[:3], got[3 : n + 3], got[n + 3 :])


def norm_back(refs, n_parts, source, stat, sums, gain, full):
    grad = refs[0][...].astype(F32)
    for ref in refs[1:n_parts]:
        grad += ref[...].astype(F32)
    columns = sum(one[...] for one in sums).T
    mean, inv = stat[:, 0:1], stat[:, 1:2]
    scaled = (source[...] - mean) * inv
    back = inv * (
        grad * gain[0:1, :] - columns[:, 0:1] * (1.0 / full) - scaled * (columns[:, 1:2] * (1.0 / full))
    )
    return back, fold_rows(grad * scaled), fold_rows(grad)


def hidden_back_body(k, m, full, *refs):
    parts, sums = refs[:k], refs[k : k + m]
    cot, hidden, stat, gain, wide, low, gain_sum, bias_sum = refs[k + m :]
    back, gain_part, bias_part = norm_back(parts, k, hidden, stat, sums, gain, full)
    value = cot[...].astype(F32) + back
    wide[...] = value
    low[...] = value.astype(BF16)
    accumulate(gain_sum, gain_part)
    accumulate(bias_sum, bias_part)


def hidden_back(parts, cotangent, row, hidden, stat, sums, gain, full):
    k, m, (length, width) = len(parts), len(sums), hidden.shape
    tile = min(256, length)
    steps = length // tile
    return call(
        "hidden_back",
        lambda *refs: hidden_back_body(k, m, full, *refs),
        (steps,),
        (*parts, *sums, cotangent, hidden, stat, gain),
        [rows_of((tile, width))] * k
        + [cols_of((8, tile))] * m
        + [
            pl.BlockSpec((tile, width), lambda i: (row * steps + i, 0)),
            rows_of((tile, width)),
            rows_of((tile, 128)),
            fixed((8, width)),
        ],
        [shape((length, width), F32), shape((length, width), BF16)] + [shape((8, width), F32)] * 2,
        [rows_of((tile, width))] * 2 + [fixed((8, width))] * 2,
    )


def attended_back_body(n, me, *refs):
    grads = refs[:n]
    weight, joined, out = refs[n:]
    width = grads[0].shape[1]
    for j in range(n):
        joined[:, place_of(me[0], j, width)] = grads[j][...]
    out[...] = dot_nt(joined[...], weight[...]).astype(BF16)


def attended_back(me, grads, weight):
    n, (length, width) = len(grads), grads[0].shape
    rows, full = weight.shape
    tile = min(256, length)
    return call(
        "attended_back",
        lambda *refs: attended_back_body(n, *refs),
        (length // tile,),
        (me, *grads, weight),
        [SMEM] + [rows_of((tile, width))] * n + [fixed((rows, full))],
        [shape((length, full), BF16), shape((length, rows), BF16)],
        [rows_of((tile, full)), rows_of((tile, rows))],
    )


def project_back_body(n, me, grad, normed, gain, bias, weight, sums, *refs):
    parts = refs[:n]
    held, sems = refs[n:]
    width = parts[0].shape[1]
    copies = row_blocks(me[0], n, width, weight, held, sems, 0)

    def work(wait):
        total = weighted = 0.0
        for j in range(n):
            wait(copies[j : j + 1])
            part = slice(j * width, (j + 1) * width)
            value = dot_nt(grad[...], held[part, :])
            parts[j][...] = value.astype(BF16)
            total += jnp.sum(value * gain[0:1, part], 1, keepdims=True)
            there = normed[:, place_of(me[0], j, width)].astype(F32)
            weighted += jnp.sum(value * (there - bias[0:1, part]), 1, keepdims=True)
        sums[...] = row_stats(total, weighted)

    with_weights(copies, work)


def project_back(me, n, grad, normed, gain, bias, weight):
    length, out = grad.shape
    full = weight.shape[0]
    width = full // n
    tile = min(256, length)
    got = call(
        "project_back",
        lambda *refs: project_back_body(n, *refs),
        (length // tile,),
        (me, grad, normed, gain, bias, weight),
        [SMEM, rows_of((tile, out)), rows_of((tile, full))] + [fixed((8, full))] * 2 + [ANY],
        [shape((8, length), F32)] + [shape((length, width), BF16)] * n,
        [cols_of((8, tile))] + [rows_of((tile, width))] * n,
        scratch=[pltpu.VMEM((full, out), BF16), pltpu.SemaphoreType.DMA((n,))],
    )
    return got[0], got[1:]


def average_back_body(k, m, full, count, *refs):
    weights, parts, sums = refs[0], refs[1 : k + 1], refs[k + 1 : k + m + 1]
    source, stat, gain, hidden_grad, history = refs[k + m + 1 : k + m + 6]
    grad_history, depth_sum, gain_sum, bias_sum = refs[-4:]
    back, gain_part, bias_part = norm_back(parts, k, source, stat, sums, gain, full)
    value = hidden_grad[...] + back
    accumulate(gain_sum, gain_part)
    accumulate(bias_sum, bias_part)
    lanes = value.shape[1] // 128
    for j in range(count):
        grad_history[j] = (weights[j] * value).astype(BF16)
        product = fold_rows(value * history[j].astype(F32))
        folded = product[:, 0:128]
        for c in range(1, lanes):
            folded += product[:, c * 128 : (c + 1) * 128]
        accumulate(depth_sum.at[j], folded)


def average_back(weights, parts, source, stat, sums, gain, hidden_grad, history, row, made):
    k, m, (length, width) = len(parts), len(sums), source.shape
    count = history.shape[0]
    tile = min(256, length)
    steps = length // tile
    full = gain[1]
    block = pl.BlockSpec((count, tile, width), lambda i: (0, row * steps + i, 0))
    args = (weights, *parts, *sums, source, stat, gain[0], hidden_grad, history)
    specs = (
        [SMEM]
        + [rows_of((tile, width))] * k
        + [cols_of((8, tile))] * m
        + [rows_of((tile, width)), rows_of((tile, 128)), fixed((8, width)), rows_of((tile, width)), block]
    )
    more = {}
    if made is not None:
        more = {"aliases": {len(args): 0}}
        args, specs = (*args, made), specs + [ANY]
    return call(
        "average_back",
        lambda *refs: average_back_body(k, m, full, count, *refs),
        (steps,),
        args,
        specs,
        [shape(history.shape, BF16), shape((count, 8, 128), F32)] + [shape((8, width), F32)] * 2,
        [block, fixed((count, 8, 128))] + [fixed((8, width))] * 2,
        **more,
    )


def divisor(size, most):
    return max(d for d in range(128, most + 1, 128) if size % d == 0) if size > 128 else size


def weight_body(rows, *refs):
    out = refs[-1]
    total = dot_tn(refs[0][...], refs[rows][...])
    for r in range(1, rows):
        total += dot_tn(refs[r][...], refs[rows + r][...])
    out[...] = total.astype(BF16)


def weight_grad(lefts, rights):
    rows, (length, high), wide = len(lefts), lefts[0].shape, rights[0].shape[1]
    tall, across = divisor(high, 512), divisor(wide, 1024)
    return call(
        "weight_grad",
        lambda *refs: weight_body(rows, *refs),
        (high // tall, wide // across),
        (*lefts, *rights),
        [pl.BlockSpec((length, tall), lambda i, j: (0, i))] * rows
        + [pl.BlockSpec((length, across), lambda i, j: (0, j))] * rows,
        [shape((high, wide), BF16)],
        [pl.BlockSpec((tall, across), lambda i, j: (i, j))],
    )[0]


def put_blocks(came, outs, k, value):
    if came is not None:
        value = value + came[k].astype(F32)
    per = outs[0].shape[0]
    outs[k // per][k % per] = value.astype(BF16)


def tall_blocks_body(rows, count, fused, group, *refs):
    lefts, rights = refs[: rows * count], refs[rows * count : rows * count + rows]
    refs = refs[rows * count + rows :]
    came, outs, turned = refs[0] if fused else None, refs[fused:-1], refs[-1]
    length, high = lefts[0].shape

    @pl.when(pl.program_id(0) == 0)
    def _():
        for k in range(count):
            for r in range(rows):
                turned[k * high : (k + 1) * high, r * length : (r + 1) * length] = lefts[
                    k * rows + r
                ][...].T

    for k in range(count):
        total = 0.0
        for r in range(rows):
            total += dot_nn(
                turned[k * high : (k + 1) * high, r * length : (r + 1) * length], rights[r][...]
            )
        put_blocks(came, outs, k, total)


def wide_blocks_body(rows, count, fused, group, *refs):
    lefts, rights = refs[:rows], refs[rows : rows + rows * count]
    refs = refs[rows + rows * count :]
    came, outs = refs[0] if fused else None, refs[fused:]
    turned = [left[...].T for left in lefts]
    for k in range(count):
        total = 0.0
        for r in range(rows):
            total += dot_nn(turned[r], rights[k * rows + r][...])
        put_blocks(came, outs, k, total)


class Spread:
    def __init__(self, lefts, rights, dim, bits, part=(0, 1)):
        self.lefts, self.rights, self.dim, self.bits, self.part = lefts, rights, dim, list(bits), part
        self.groups = lax.axis_size("dp")
        self.block = (lefts, rights)[dim][0].shape[1] // self.groups
        order = [0]
        for bit in reversed(self.bits):
            order = order + [e | bit for e in order]
        self.order = order

    def blocks(self, half, came=None):
        count = self.groups // 2
        which = self.order[half * count : (half + 1) * count]
        rows, length = len(self.lefts), self.lefts[0].shape[0]
        group = lax.axis_index("dp").astype(jnp.int32)[None]
        size, (index, pieces) = self.block, self.part
        stay = [
            pl.BlockSpec((length, size), lambda i, group, e=e: (0, group[0] ^ e))
            for e in which
            for _ in range(rows)
        ]
        other = self.rights if self.dim == 0 else self.lefts
        extent = other[0].shape[1] // pieces
        tile = divisor(extent, 512)
        steps = extent // tile
        move = [pl.BlockSpec((length, tile), lambda i, group: (0, index * steps + i))] * rows

        def blocked(number):
            if self.dim == 0:
                return (
                    shape((number, size, extent), BF16),
                    pl.BlockSpec((number, size, tile), lambda i, group: (0, 0, i)),
                )
            return (
                shape((number, extent, size), BF16),
                pl.BlockSpec((number, tile, size), lambda i, group: (0, i, 0)),
            )

        if self.dim == 0:
            args = (*(list(self.lefts) * count), *self.rights)
            specs = stay + move
            body, scratch = tall_blocks_body, [pltpu.VMEM((count * size, rows * length), BF16)]
        else:
            args = (*self.lefts, *(list(self.rights) * count))
            specs = move + stay
            body, scratch = wide_blocks_body, []
        outs = [blocked(count)]
        if came is not None:
            args, specs = (*args, came), specs + [blocked(count)[1]]
            outs = [blocked(count // 2)] * 2
        return call(
            "weight_blocks",
            lambda *refs: body(rows, count, came is not None, *refs),
            (steps,),
            (group, *args),
            specs,
            [one[0] for one in outs],
            [one[1] for one in outs],
            scratch=scratch,
            prefetch=1,
        )

    def send(self, value):
        bit = self.bits[self.step]
        self.step += 1
        self.coming = lax.ppermute(value, "dp", [(i, i ^ bit) for i in range(self.groups)])

    def first(self):
        self.step = 0
        self.send(self.blocks(1)[0])

    def keep(self):
        self.held = self.blocks(0)[0]

    def keep_added(self):
        self.held, out = self.blocks(0, self.coming)
        self.send(out)


def fold_body(count, *refs):
    for i in range(count):
        held, came, keep, send = refs[2 * i], refs[2 * i + 1], refs[2 * count + 2 * i], refs[2 * count + 2 * i + 1]
        half = keep.shape[0]
        keep[...] = (held[:half].astype(F32) + came[:half].astype(F32)).astype(BF16)
        send[...] = (held[half:].astype(F32) + came[half:].astype(F32)).astype(BF16)


def advance(*spreads):
    steps = 4
    args, specs, outs, out_specs = [], [], [], []
    for one in spreads:
        count, high, wide = one.held.shape
        args += [one.held, one.coming]
        specs += [pl.BlockSpec((count, high // steps, wide), lambda i: (0, i, 0))] * 2
        outs += [shape((count // 2, high, wide), BF16)] * 2
        out_specs += [pl.BlockSpec((count // 2, high // steps, wide), lambda i: (0, i, 0))] * 2
    got = call("fold", lambda *refs: fold_body(len(spreads), *refs), (steps,), args, specs, outs, out_specs)
    for i, one in enumerate(spreads):
        one.held = got[2 * i]
        one.send(got[2 * i + 1])


def finish_body(groups, *refs):
    outs = refs[len(refs) - len(groups) :]
    at = 0
    for out, group in zip(outs, groups):
        for first, wide in group:
            total = refs[at][0].astype(F32) + refs[at + 1][0].astype(F32)
            out[:, first : first + wide] = total
            at += 2


def finish(*groups):
    steps = 4
    args, specs, outs, out_specs, places = [], [], [], [], []
    for group in groups:
        first, place = 0, []
        for one in group:
            _, high, wide = one.held.shape
            args += [one.held, one.coming]
            specs += [pl.BlockSpec((1, high // steps, wide), lambda i: (0, i, 0))] * 2
            place.append((first, wide))
            first += wide
        outs.append(shape((high, first), F32))
        out_specs.append(rows_of((high // steps, first)))
        places.append(place)
    return call("finish", lambda *refs: finish_body(places, *refs), (steps,), args, specs, outs, out_specs)


def add_body(*refs):
    count = len(refs) // 3
    for left, right, out in zip(refs[:count], refs[count : 2 * count], refs[2 * count :]):
        out[...] = (left[...].astype(F32) + right[...].astype(F32)).astype(out.dtype)


def add(lefts, rights):
    steps = 2

    def spec(v):
        if v.dtype == BF16:
            return rows_of((v.shape[0] // steps, v.shape[1]))
        return cols_of((v.shape[0], v.shape[1] // steps))

    specs = [spec(v) for v in lefts]
    return call(
        "add", add_body, (steps,), (*lefts, *rights), specs * 2, [shape(v.shape, v.dtype) for v in lefts], specs
    )


def output_body(rows, steps, *refs):
    bias, out = refs[-2:]
    per = (len(refs) - 2) // rows
    for r in range(rows):

        @pl.when(pl.program_id(0) // steps == r)
        def _(r=r):
            total = bias[0:1, :]
            for part in refs[r * per + 1 : (r + 1) * per]:
                total = total + part[...].astype(F32)
            out[...] = (refs[r * per][...] + total).astype(BF16)


def output(parts, hidden, bias):
    rows, (length, width) = len(hidden), hidden[0].shape
    tile = min(512, length)
    steps = length // tile
    args, specs = [], []
    for r in range(rows):
        args += [hidden[r], *parts[r]]
        specs += [
            pl.BlockSpec((tile, width), lambda i, r=r: (jnp.clip(i - r * steps, 0, steps - 1), 0))
        ] * (1 + len(parts[r]))
    return call(
        "output",
        lambda *refs: output_body(rows, steps, *refs),
        (rows * steps,),
        (*args, bias),
        specs + [fixed((8, width))],
        [shape((rows * length, width), BF16)],
        [rows_of((tile, width))],
    )[0]


class Ring:
    def __init__(self):
        self.n = lax.axis_size("mp")
        self.me = lax.axis_index("mp").astype(jnp.int32)
        self.pairs = self.n == 4
        self.core = [(i, i ^ 1) for i in range(self.n)]
        self.chip = [(i, i ^ 2) for i in range(self.n)]

    def over_core(self, value):
        return lax.ppermute(value, "mp", self.core)

    def over_chip(self, value):
        return lax.ppermute(value, "mp", self.chip)

    def gather_start(self, block):
        if self.pairs:
            return [block, self.over_chip(block)]
        every = lax.all_gather(block, "mp")
        return [
            lax.dynamic_index_in_dim(every, self.me ^ j, 0, keepdims=False) for j in range(self.n)
        ]

    def gather_end(self, blocks, held=True):
        if self.pairs:
            block, across = gate(blocks) if held else blocks
            return [block, self.over_core(block), across, self.over_core(across)]
        return blocks

    def gather(self, block):
        return self.gather_end(self.gather_start(block), False)

    def scatter_start(self, parts, sums=None):
        extra = [] if sums is None else [sums]
        if self.pairs:
            sent = [parts[3], *extra, parts[1]]
            return [parts[2], *extra, parts[0]], [self.over_core(v) for v in sent]
        stacked = jnp.stack([part.astype(F32) for part in parts])
        ordered = jnp.take(stacked, self.me ^ jnp.arange(self.n), axis=0)
        total = lax.psum_scatter(ordered, "mp", scatter_dimension=0, tiled=False)
        return [total], [lax.psum(v, "mp") for v in extra]

    def scatter_end(self, state):
        if not self.pairs:
            return state
        got = add(*state)
        sums = list(got[1:-1])
        return [got[-1], self.over_chip(got[0])], sums + [self.over_chip(v) for v in sums]

    def total(self, value):
        if self.pairs:
            value = value + self.over_core(value)
            return value + self.over_chip(value)
        return lax.psum(value, "mp")

    def out_start(self, weight):
        rows, groups = weight.shape[0], lax.axis_size("dp")
        if self.pairs and rows % (16 * groups) == 0:
            size = rows // groups
            piece = lax.dynamic_slice_in_dim(weight, lax.axis_index("dp") * size, size, 0)
            return self.over_chip(piece)
        return None

    def out_middle(self, piece):
        return None if piece is None else lax.all_gather(gate([piece])[0], "dp", axis=0, tiled=True)

    def out_end(self, weight, across):
        if across is None:
            return lambda: self.gather(weight)
        sent = [self.over_core(weight), self.over_core(across)]

        def end():
            sibling, far = gate(sent)
            return [weight, sibling, across, far]

        return end


def dp_total(vectors):
    groups = lax.axis_size("dp")
    sizes = [v.size for v in vectors]
    packed = jnp.concatenate(vectors)
    packed = jnp.pad(packed, (0, -packed.size % 1024)).reshape(-1, 128)
    bit = 1
    while bit < groups:
        packed = packed + lax.ppermute(packed, "dp", [(i, i ^ bit) for i in range(groups)])
        bit *= 2
    packed = packed.reshape(-1)
    ends = np.cumsum(sizes)
    return [packed[end - size : end] for end, size in zip(ends, sizes)]


def tables_of(length):
    half = HEAD // 2
    rate = np.exp(np.arange(half, dtype=np.float64) * (-math.log(10000.0) / half))
    angle = np.arange(length, dtype=np.float64)[:, None] * rate[None, :]
    cosine, sine = np.cos(angle), np.sin(angle)
    return (
        jnp.asarray(np.concatenate([cosine, cosine], 1), F32),
        jnp.asarray(np.concatenate([-sine, sine], 1), F32),
    )


def local(
    history,
    depth_weights,
    segment_ids,
    first_gain,
    first_bias,
    qkv_weight,
    out_weight,
    second_gain,
    second_bias,
    up_weight,
    up_bias,
    down_weight,
    down_bias,
    cotangent,
):
    ring = Ring()
    n = ring.n
    me = ring.me[None]
    width = history.shape[2]
    full = n * width
    row_count, length = segment_ids.shape
    rows = range(row_count)
    tables = tables_of(length)
    earlier = (segment_ids[:, None, :] < segment_ids[:, :, None]).astype(jnp.int32)
    starts = jnp.broadcast_to(jnp.sum(earlier, -1)[:, None, :], (row_count, 8, length))

    vectors = jnp.stack([first_gain, first_bias, second_gain, second_bias])
    vectors = jnp.concatenate(ring.gather(jnp.repeat(vectors, 8, 0)), 1)
    gain1, bias1, gain2, bias2 = (vectors[8 * i : 8 * i + 8] for i in range(4))
    own1, own2 = gain1[:, :width], gain2[:, :width]
    up_bias8 = jnp.broadcast_to(up_bias[None], (8, up_bias.shape[0]))

    down_bias8 = jnp.broadcast_to(down_bias[None], (8, width))
    groups = lax.axis_size("dp")
    spread = full % (128 * groups) == 0 and groups >= 4
    last = row_count - 1

    Order.last = None
    piece = ring.out_start(out_weight)
    cot_rows = [lax.slice_in_dim(cotangent, r * length, (r + 1) * length) for r in rows]
    none = [None] * row_count
    wide, xs, qkv, normed1, stat1 = list(none), list(none), list(none), list(none), list(none)
    attended, logs, heads, cots, cot_full = list(none), list(none), list(none), list(none), list(none)
    hidden, normed2, stat2, activated, slope = (list(none) for _ in range(5))
    branch, up_grad, parts2, parts1 = list(none), list(none), list(none), list(none)
    hidden_grad, grads, grad_full, qkv_grad = list(none), list(none), list(none), list(none)
    up_bias_sum = down_bias_sum = gain2_sum = bias2_sum = 0.0

    low = list(none)
    for r in rows:
        wide[r], low[r] = average(depth_weights, history, r, length)
        if r == 0:
            xs[0] = ring.gather_start(low[0])
    across = ring.out_middle(piece)
    for r in rows:
        if r > 0:
            xs[r] = ring.gather_start(gate([low[r]], xs[r - 1][1:2])[0])
        if r == min(1, last):
            xs[0] = ring.gather_end(xs[0])
    out_w = ring.out_end(out_weight, across)
    for r in rows:
        if r > 0:
            xs[r] = ring.gather_end(xs[r])
        got = project(me, xs[r], gain1, bias1, tables, qkv_weight)
        qkv[r], normed1[r], stat1[r] = got
        if r > 0:
            heads[r - 1] = ring.gather_end(heads[r - 1])
        if r == last:
            out_w = out_w()
        attended[r], logs[r] = attend(starts[r], qkv[r])
        heads[r] = ring.gather_start(attended[r])

    for r in rows:
        cots[r] = ring.gather_start(gate([cot_rows[r]])[0])
        if r == last:
            heads[r] = ring.gather_end(heads[r])
        if r > 0:
            cots[r - 1] = ring.gather_end(cots[r - 1])
        got = feed(
            me,
            heads[r],
            xs[r],
            out_w,
            wide[r],
            gain2,
            bias2,
            up_bias8,
            up_weight,
            down_weight,
            cots[r - 1] if r > 0 else (),
        )
        hidden[r], normed2[r], stat2[r], activated[r], slope[r], parts, joined = got
        branch[r] = ring.scatter_start(parts)
        if r > 0:
            cot_full[r - 1], sums = joined
            down_bias_sum += sums

    cots[last] = ring.gather_end(cots[last])
    for r in range(last):
        branch[r] = ring.scatter_end(branch[r])[0]
    if row_count == 1:
        cot_full[0], sums = beside(me, cots[0])
        down_bias_sum += sums

    def back(r, more=()):
        return feed_back(
            me, n, cot_full[r], slope[r], normed2[r], gain2, bias2, up_weight, down_weight, more
        )

    def take(r, got):
        nonlocal up_bias_sum
        up_grad[r], sums, up_sum, parts, joined = got
        up_bias_sum += up_sum
        parts2[r] = ring.scatter_start(parts, sums)
        return joined

    joined = take(0, back(0, cots[last] if row_count > 1 else ()))
    if row_count > 1:
        cot_full[last], sums = joined
        down_bias_sum += sums
    branch[last] = ring.scatter_end(branch[last])[0]
    if spread:
        down = Spread(activated, cot_full, 1, (1, 2, 4))
        down.first()
    parts2[0] = ring.scatter_end(parts2[0])
    for r in rows[1:]:
        take(r, back(r))

    def hidden_step(r):
        nonlocal gain2_sum, bias2_sum
        parts, sums = parts2[r]
        hidden_grad[r], low_grad, gain_part, bias_part = hidden_back(
            parts, cotangent, r, hidden[r], stat2[r], sums, own2, full
        )
        gain2_sum += gain_part
        bias2_sum += bias_part
        grads[r] = ring.gather_start(low_grad)

    hidden_step(0)
    if spread:
        up = [
            Spread(normed2, up_grad, 0, (1, 2, 4), (0, 2)),
            Spread(normed2, up_grad, 0, (2, 4, 1), (1, 2)),
        ]
        up[1].first()
    for r in rows[1:]:
        parts2[r] = ring.scatter_end(parts2[r])
    if spread:
        up[0].first()
        down.keep()
    grads[0] = ring.gather_end(grads[0])

    for r in rows:
        grad_full[r], attended_grad = attended_back(me, grads[r], out_weight)
        qkv_grad[r] = attend_back(starts[r], tables, qkv[r], attended_grad, logs[r])
        if r < last:
            hidden_step(r + 1)
        sums, parts = project_back(me, n, qkv_grad[r], normed1[r], gain1, bias1, qkv_weight)
        parts1[r] = ring.scatter_start(parts, sums)
        if spread and r == 0:
            up[1].keep_added()
            advance(down)
        if r < last:
            grads[r + 1] = ring.gather_end(grads[r + 1])
            parts1[r] = ring.scatter_end(parts1[r])

    if spread:
        qkv_sum = [
            Spread(normed1, qkv_grad, 0, (1, 2, 4), (0, 2)),
            Spread(normed1, qkv_grad, 0, (2, 4, 1), (1, 2)),
        ]
        out_sum = Spread(attended, grad_full, 1, (2, 4, 1))
        qkv_sum[0].first()
    parts1[last] = ring.scatter_end(parts1[last])
    if spread:
        qkv_sum[1].first()
        out_sum.first()
        up[0].keep_added()
        advance(down, up[1])
        out_sum.keep()
    made = output(branch, hidden, down_bias8)

    grad_history, depth_sum, gain1_sum, bias1_sum = None, 0.0, 0.0, 0.0
    for r in rows:
        parts, sums = parts1[r]
        grad_history, depth_part, gain_part, bias_part = average_back(
            depth_weights,
            parts,
            wide[r],
            stat1[r],
            sums,
            (own1, full),
            hidden_grad[r],
            history,
            r,
            grad_history,
        )
        depth_sum += depth_part
        gain1_sum += gain_part
        bias1_sum += bias_part
        if r == 0 and spread:
            qkv_sum[0].keep_added()
            qkv_sum[1].keep_added()
            advance(up[0], out_sum)

    if spread:
        advance(qkv_sum[0], qkv_sum[1], out_sum)
        down_total, up_total, out_total, qkv_total = finish([down], up, [out_sum], qkv_sum)
    else:
        down_total, up_total, out_total, qkv_total = (
            lax.psum_scatter(
                weight_grad(*pair), "dp", scatter_dimension=dim, tiled=True
            ).astype(F32)
            for pair, dim in (
                ((activated, cot_full), 1),
                ((normed2, up_grad), 0),
                ((attended, grad_full), 1),
                ((normed1, qkv_grad), 0),
            )
        )

    sums = [up_bias_sum, down_bias_sum, gain2_sum, bias2_sum, gain1_sum, bias1_sum]
    depth_part = ring.total(jnp.sum(depth_sum, (1, 2)))
    sums = dp_total([jnp.sum(v, 0) for v in sums] + [depth_part])
    return (
        made,
        grad_history,
        sums[6],
        sums[4],
        sums[5],
        qkv_total,
        out_total,
        sums[2],
        sums[3],
        up_total,
        sums[0],
        down_total,
        sums[1],
    )


def solution(mesh):
    placed = (
        P(None, "dp", "mp"),
        P(),
        P("dp", None),
        P("mp"),
        P("mp"),
        P(None, "mp"),
        P("mp", None),
        P("mp"),
        P("mp"),
        P(None, "mp"),
        P("mp"),
        P("mp", None),
        P("mp"),
        P("dp", "mp"),
    )
    return jax.shard_map(
        local,
        mesh=mesh,
        in_specs=placed,
        out_specs=(
            P("dp", "mp"),
            P(None, "dp", "mp"),
            P(),
            P("mp"),
            P("mp"),
            P("dp", "mp"),
            P("mp", "dp"),
            P("mp"),
            P("mp"),
            P("dp", "mp"),
            P("mp"),
            P("mp", "dp"),
            P("mp"),
        ),
        check_vma=False,
    )
```

```python
import math

import jax
import jax.numpy as jnp
import numpy as np
from jax import lax
from jax.experimental import pallas as pl
from jax.experimental.pallas import tpu as pltpu
from jax.sharding import PartitionSpec as P

HEAD = 128
MAX_DOC = 512
EPSILON = 1e-05
SQRT_HALF = 0.7071067811865476
INV_ROOT_TWO_PI = 0.3989422804014327
LOG2E = 1.4426950408889634
SCALE = HEAD ** (-0.5)
MIB = 2**20
BF16 = jnp.bfloat16
F32 = jnp.float32


def dot_nn(a, b):
    return jnp.dot(a, b, preferred_element_type=F32)


def dot_nt(a, b):
    return lax.dot_general(a, b, (((1,), (1,)), ((), ())), preferred_element_type=F32)


def dot_tn(a, b):
    return lax.dot_general(a, b, (((0,), (0,)), ((), ())), preferred_element_type=F32)


class Order:
    last = None
    names = 0

    @staticmethod
    def name(remote):
        Order.names += remote
        return Order.names - 1 if remote else None


def call(
    name, body, grid, args, in_specs, outs, out_specs, scratch=(), prefetch=0, after=(), aliases=None, remote=False
):
    count = len(args)
    extra = [*after]
    if Order.last is not None and not any(Order.last is a for a in args):
        extra.append(Order.last)

    def without_extra(*refs):
        body(*refs[:count], *refs[count + len(extra) :])

    got = pl.pallas_call(
        without_extra,
        grid_spec=pltpu.PrefetchScalarGridSpec(
            num_scalar_prefetch=prefetch,
            grid=grid,
            in_specs=list(in_specs) + [ANY] * len(extra),
            out_specs=out_specs,
            scratch_shapes=list(scratch),
        ),
        out_shape=outs,
        input_output_aliases=aliases or {},
        compiler_params=pltpu.CompilerParams(
            vmem_limit_bytes=60 * MIB, collective_id=Order.name(remote), has_side_effects=remote
        ),
        cost_estimate=pl.CostEstimate(flops=10**12, bytes_accessed=10**8, transcendentals=0),
        name=name,
    )(*args, *extra)
    fresh = [v for i, v in enumerate(got) if i not in (aliases or {}).values()]
    Order.last = min(fresh or got, key=lambda v: v.size)
    return got


def shape(dims, dtype):
    return jax.ShapeDtypeStruct(dims, dtype)


def sent(dims, dtype):
    return pltpu.HBM(dims, dtype)


SMEM = pl.BlockSpec(memory_space=pltpu.SMEM)
ANY = pl.BlockSpec(memory_space=pl.ANY)


def gate(arrays, after=()):
    arrays = list(arrays)
    return call(
        "gate",
        lambda *refs: None,
        (1,),
        arrays,
        [ANY] * len(arrays),
        [shape(a.shape, a.dtype) for a in arrays],
        [ANY] * len(arrays),
        after=after,
        aliases={i: i for i in range(len(arrays))},
    )


def rows_of(block):
    return pl.BlockSpec(block, lambda i: (i, 0))


def cols_of(block):
    return pl.BlockSpec(block, lambda i: (0, i))


def fixed(block):
    return pl.BlockSpec(block, lambda i: (0,) * len(block))


def flip(me, j):
    there, bit = me, 1
    while bit <= j:
        if j & bit:
            there = there + bit * (1 - 2 * ((me // bit) % 2))
        bit *= 2
    return there


def place_of(me, j, width):
    return pl.ds(pl.multiple_of(flip(me, j) * width, width), width)


def greet():
    barrier = pltpu.get_barrier_semaphore()
    sibling = flip(lax.axis_index("mp"), 1)
    pl.semaphore_signal(
        barrier, inc=1, device_id={"mp": sibling}, device_id_type=pl.DeviceIdType.MESH
    )
    pl.semaphore_wait(barrier, 1)


def to_sibling(source, target, sems, at):
    return pltpu.make_async_remote_copy(
        src_ref=source,
        dst_ref=target,
        send_sem=sems.at[0, at],
        recv_sem=sems.at[1, at],
        device_id={"mp": flip(lax.axis_index("mp"), 1)},
        device_id_type=pl.DeviceIdType.MESH,
    )


class Gathered:
    def __init__(self, refs, pairs, steps):
        self.pairs, self.steps = pairs, steps
        self.blocks, self.whole = refs[:2] if pairs else refs, refs[2:4] if pairs else ()

    @staticmethod
    def specs(blocks, pairs, tile):
        width = blocks[0].shape[1]
        return [rows_of((tile, width))] * len(blocks) + ([ANY] * 2 if pairs else [])

    @staticmethod
    def scratch(blocks, pairs, steps):
        if not pairs:
            return []
        return [pltpu.VMEM((2, *blocks[0].shape), BF16), pltpu.SemaphoreType.DMA((2, 2 * steps))]

    def attach(self, refs):
        if self.pairs:
            self.came, self.sems = refs
        return self

    def copies(self, step):
        tile = self.blocks[0].shape[0]
        rows = pl.ds(pl.multiple_of(step * tile, tile), tile)
        return [
            to_sibling(self.whole[k].at[rows, :], self.came.at[k, rows, :], self.sems, 2 * step + k)
            for k in range(2)
        ]

    def start(self):
        if self.pairs:
            for step in range(self.steps):
                for one in self.copies(step):
                    one.start()

    def refs(self):
        if not self.pairs:
            return self.blocks
        step = pl.program_id(0)
        tile = self.blocks[0].shape[0]
        for one in self.copies(step):
            one.wait()
        rows = pl.ds(pl.multiple_of(step * tile, tile), tile)
        return [self.blocks[0], self.came.at[0, rows, :], self.blocks[1], self.came.at[1, rows, :]]


class Scattered:
    def __init__(self, pairs, n, steps, with_sums):
        self.pairs, self.n, self.steps, self.with_sums = pairs, n, steps, with_sums

    def outs(self, length, width):
        tile = length // self.steps
        if self.pairs:
            outs = [shape((length, width), BF16), sent((length, width), BF16)]
            specs = [fixed((length, width))] * 2
            if self.with_sums:
                outs, specs = outs + [sent((8, length), F32)], specs + [fixed((8, length))]
            return outs, specs
        outs, specs = [shape((length, width), BF16)] * self.n, [rows_of((tile, width))] * self.n
        if self.with_sums:
            outs, specs = outs + [shape((8, length), F32)], specs + [cols_of((8, tile))]
        return outs, specs

    def count(self):
        return (2 if self.pairs else self.n) + self.with_sums

    def scratch(self, length, width):
        if not self.pairs:
            return []
        tile = length // self.steps
        block = pltpu.VMEM((self.steps, 2, tile, width), BF16)
        made = [block, block, pltpu.VMEM((2, 2, tile, width), F32)]
        if self.with_sums:
            made += [pltpu.VMEM((self.steps, 8, tile), F32)] * 3
        return made + [pltpu.SemaphoreType.DMA((2, 3 * self.steps))]

    def attach(self, outs, scratch):
        self.out = outs
        if self.pairs:
            self.send, self.came, self.kept = scratch[:3]
            self.sums = scratch[3:-1]
            self.sems = scratch[-1]
        return self

    def copies(self, step):
        made = [
            to_sibling(self.send.at[step, k], self.came.at[step, k], self.sems, 3 * step + k)
            for k in range(2)
        ]
        if self.with_sums:
            made.append(to_sibling(self.sums[0].at[step], self.sums[1].at[step], self.sems, 3 * step + 2))
        return made

    def put(self, j, value):
        step = pl.program_id(0)
        if not self.pairs:
            self.out[j][...] = value.astype(BF16)
        elif j % 2:
            self.send[step, j // 2] = value.astype(BF16)
        else:
            self.kept[step % 2, j // 2] = value

    def take(self, step):
        tile = self.kept.shape[2]
        for one in self.copies(step):
            one.wait()
        rows = pl.ds(pl.multiple_of(step * tile, tile), tile)
        for k in range(2):
            total = self.kept[step % 2, k] + self.came[step, k].astype(F32)
            self.out[k][rows, :] = total.astype(BF16)
        if self.with_sums:
            self.out[2][:, rows] = self.sums[2][step] + self.sums[1][step]

    def finish(self, sums=None):
        if not self.pairs:
            if sums is not None:
                self.out[-1][...] = sums
            return
        step = pl.program_id(0)
        if sums is not None:
            self.sums[0][step] = sums
            self.sums[2][step] = sums
        for one in self.copies(step):
            one.start()

        @pl.when(step > 0)
        def _():
            self.take(step - 1)

        @pl.when(step == self.steps - 1)
        def _():
            self.take(step)


def with_weights(copies, work, remote=False, gathered=()):
    @pl.when(pl.program_id(0) == 0)
    def _():
        for one in copies:
            one.start()
        if remote:
            greet()
        for one in gathered:
            one.start()

        def wait(some):
            for one in some:
                one.wait()

        work(wait)

    @pl.when(pl.program_id(0) != 0)
    def _():
        work(lambda some: None)


def row_blocks(me, n, width, source, target, sems, base):
    return [
        pltpu.make_async_copy(
            source.at[place_of(me, j, width), :],
            target.at[pl.ds(j * width, width), :],
            sems.at[base + j],
        )
        for j in range(n)
    ]


def col_blocks(me, n, width, source, target, sems, base):
    return [
        pltpu.make_async_copy(
            source.at[:, place_of(me, j, width)],
            target.at[:, pl.ds(j * width, width)],
            sems.at[base + j],
        )
        for j in range(n)
    ]


def stat_columns(first, second):
    lane = lax.broadcasted_iota(jnp.int32, (first.shape[0], 128), 1)
    return jnp.where(lane == 0, first, jnp.where(lane == 1, second, 0.0))


def fold_rows(values):
    return jnp.sum(values.reshape(values.shape[0] // 8, 8, values.shape[1]), 0)


def accumulate(ref, value):
    @pl.when(pl.program_id(0) == 0)
    def _():
        ref[...] = value

    @pl.when(pl.program_id(0) != 0)
    def _():
        ref[...] += value


def average_body(weights, history, wide, low):
    total = weights[0] * history[0].astype(F32)
    for j in range(1, history.shape[0]):
        total += weights[j] * history[j].astype(F32)
    wide[...] = total
    low[...] = total.astype(BF16)


def average(weights, history, row, length):
    count, _, width = history.shape
    tile = min(256, length)
    steps = length // tile
    return call(
        "average",
        average_body,
        (steps,),
        (weights, history),
        [SMEM, pl.BlockSpec((count, tile, width), lambda i: (0, row * steps + i, 0))],
        [shape((length, width), F32), sent((length, width), BF16)],
        [rows_of((tile, width))] * 2,
    )


def project_body(n, pairs, steps, *refs):
    count = 4 if pairs else n
    x = Gathered(refs[:count], pairs, steps)
    gain, bias, cosine, sine, weight, qkv, normed, stat = refs[count : count + 8]
    refs = refs[count + 8 :]
    shared = refs[:2] if pairs else ()
    held, joined, sems, *more = refs[len(shared) :]
    x.attach(more)
    me = lax.axis_index("mp")
    tile, width = x.blocks[0].shape
    full = n * width
    heads = held.shape[1] // (3 * HEAD)
    sub = min(256, tile)
    copies = row_blocks(me, n, width, weight, held, sems, 0)

    def work(wait):
        xs = x.refs()
        for out, k in zip(shared, (1, 3)):
            out[...] = xs[k][...]
        for t in range(tile // sub):
            rows = slice(t * sub, (t + 1) * sub)
            total = square = 0.0
            for one in xs:
                value = one[rows, :].astype(F32)
                total += jnp.sum(value, 1, keepdims=True)
                square += jnp.sum(value * value, 1, keepdims=True)
            mean = total / full
            inv = lax.rsqrt(square / full - mean * mean + EPSILON)
            stat[rows, :] = stat_columns(mean, inv)
            for j, one in enumerate(xs):
                part = slice(j * width, (j + 1) * width)
                value = (one[rows, :].astype(F32) - mean) * inv * gain[0:1, part] + bias[0:1, part]
                joined[rows, part] = value.astype(BF16)
                normed[rows, place_of(me, j, width)] = value.astype(BF16)
            if t == 0:
                wait(copies)
            for h in range(heads):
                base = 3 * h * HEAD
                out = dot_nn(joined[rows, :], held[:, base : base + 3 * HEAD])
                for s in range(2):
                    v = out[:, s * HEAD : (s + 1) * HEAD]
                    turned = v * cosine[rows, :] + pltpu.roll(v, HEAD // 2, 1) * sine[rows, :]
                    qkv[rows, base + s * HEAD : base + (s + 1) * HEAD] = turned.astype(BF16)
                qkv[rows, base + 2 * HEAD : base + 3 * HEAD] = out[:, 2 * HEAD :].astype(BF16)

    with_weights(copies, work, pairs, [x])


def project(n, pairs, xs, gain, bias, tables, weight):
    length, width = xs[0].shape
    full, out = weight.shape
    tile = min(512, length)
    steps = length // tile
    got = call(
        "project",
        lambda *refs: project_body(n, pairs, steps, *refs),
        (steps,),
        (*xs, *(xs if pairs else ()), gain, bias, *tables, weight),
        Gathered.specs(xs, pairs, tile)
        + [fixed((8, full))] * 2
        + [rows_of((tile, HEAD))] * 2
        + [ANY],
        [shape((length, out), BF16), shape((length, full), BF16), shape((length, 128), F32)]
        + [shape((length, width), BF16)] * (2 * pairs),
        [rows_of((tile, out)), rows_of((tile, full)), rows_of((tile, 128))]
        + [rows_of((tile, width))] * (2 * pairs),
        scratch=[
            pltpu.VMEM((full, out), BF16),
            pltpu.VMEM((tile, full), BF16),
            pltpu.SemaphoreType.DMA((n,)),
        ]
        + Gathered.scratch(xs, pairs, steps),
        remote=pairs,
    )
    return *got[:3], [xs[0], got[3], xs[1], got[4]] if pairs else xs


def windows(length):
    block = min(256, length)
    for i in range(length // block):
        low = max(0, i * block - (MAX_DOC - 1)) // block * block
        yield slice(i * block, (i + 1) * block), slice(low, (i + 1) * block)


def score_mask(start, q_part, k_part):
    dims = (k_part.stop - k_part.start, q_part.stop - q_part.start)
    k_pos = lax.broadcasted_iota(jnp.int32, dims, 0) + k_part.start
    q_pos = lax.broadcasted_iota(jnp.int32, dims, 1) + q_part.start
    return (k_pos >= start[0:1, q_part]) & (k_pos <= q_pos)


def attend_body(start, qkv, out, logs):
    length = qkv.shape[0]
    value_t = qkv[:, 2 * HEAD :].T
    for q_part, k_part in windows(length):
        query, key = qkv[q_part, :HEAD], qkv[k_part, HEAD : 2 * HEAD]
        scores = dot_nt(key, query) * (SCALE * LOG2E)
        scores = jnp.where(score_mask(start, q_part, k_part), scores, -1e30)
        top = jnp.max(scores, 0, keepdims=True)
        probs = jnp.exp2(scores - top)
        total = jnp.sum(probs, 0, keepdims=True)
        logs[0, :, q_part] = jnp.broadcast_to(top + jnp.log2(total), (8, q_part.stop - q_part.start))
        got = dot_nn(value_t[:, k_part], probs.astype(BF16)) / total
        out[q_part, :] = got.T.astype(BF16)


def attend(start, qkv):
    length, width = qkv.shape
    heads = width // (3 * HEAD)
    return call(
        "attend",
        attend_body,
        (heads,),
        (start, qkv),
        [fixed((8, length)), cols_of((length, 3 * HEAD))],
        [sent((length, heads * HEAD), BF16), shape((heads, 8, length), F32)],
        [cols_of((length, HEAD)), pl.BlockSpec((1, 8, length), lambda i: (i, 0, 0))],
    )


def attend_back_body(start, cosine, sine, qkv, grad, logs, out, key_sum, value_sum):
    length = qkv.shape[0]
    key_t = qkv[:, HEAD : 2 * HEAD].T
    key_sum[...] = jnp.zeros_like(key_sum)
    value_sum[...] = jnp.zeros_like(value_sum)

    def turn_back(v, part):
        return (
            v * cosine[part, :] - pltpu.roll(v, HEAD // 2, 1) * sine[part, :]
        ).astype(BF16)

    for q_part, k_part in windows(length):
        query, key = qkv[q_part, :HEAD], qkv[k_part, HEAD : 2 * HEAD]
        value, g = qkv[k_part, 2 * HEAD :], grad[q_part, :]
        scores = dot_nt(key, query) * (SCALE * LOG2E) - logs[0, 0:1, q_part]
        probs = jnp.exp2(jnp.where(score_mask(start, q_part, k_part), scores, -1e30))
        prob_grad = dot_nt(value, g)
        mean = jnp.sum(prob_grad * probs, 0, keepdims=True)
        score_grad = (probs * (prob_grad - mean)).astype(BF16)
        value_sum[k_part, :] += dot_nn(probs.astype(BF16), g)
        key_sum[k_part, :] += dot_nn(score_grad, query)
        query_grad = dot_nn(key_t[:, k_part], score_grad) * SCALE
        out[q_part, :HEAD] = turn_back(query_grad.T, q_part)
    for q_part, _ in windows(length):
        out[q_part, HEAD : 2 * HEAD] = turn_back(key_sum[q_part, :] * SCALE, q_part)
        out[q_part, 2 * HEAD :] = value_sum[q_part, :].astype(BF16)


def attend_back(start, tables, qkv, grad, logs):
    length, width = qkv.shape
    heads = width // (3 * HEAD)
    return call(
        "attend_back",
        attend_back_body,
        (heads,),
        (start, *tables, qkv, grad, logs),
        [fixed((8, length))]
        + [fixed((length, HEAD))] * 2
        + [
            cols_of((length, 3 * HEAD)),
            cols_of((length, HEAD)),
            pl.BlockSpec((1, 8, length), lambda i: (i, 0, 0)),
        ],
        [shape((length, width), BF16)],
        [cols_of((length, 3 * HEAD))],
        scratch=[pltpu.VMEM((length, HEAD), F32)] * 2,
    )[0]


def feed_body(n, pairs, beside, steps, *refs):
    count = 4 if pairs else n
    attended = Gathered(refs[:count], pairs, steps)
    refs = refs[count:]
    xs, outs_w = refs[: n - 1], refs[n - 1 : 2 * n - 1]
    own, gain, bias, up_bias, up_weight, down_weight = refs[2 * n - 1 : 2 * n + 5]
    refs = refs[2 * n + 5 :]
    extra = None
    if beside:
        extra, refs = Gathered(refs[:count], pairs, steps), refs[count:]
    hidden, normed, stat, activated, slope = refs[:5]
    refs = refs[5:]
    parts = Scattered(pairs, n, steps, False)
    part_outs, refs = refs[: parts.count()], refs[parts.count() :]
    if beside:
        joined_outs, refs = refs[:2], refs[2:]
    out_held, up_held, down_held, joined, whole, sems, *refs = refs
    if pairs:
        attended.attach(refs[:2])
        if beside:
            extra.attach(refs[2:4])
        refs = refs[2 + 2 * beside :]
    parts.attach(part_outs, refs)
    me = lax.axis_index("mp")
    width = own.shape[1]
    full = n * width
    inner = up_held.shape[1]
    out_copies = []
    for j in range(n):
        for k in range(n):
            out_copies.append(
                pltpu.make_async_copy(
                    outs_w[k].at[:, place_of(me, j, width)],
                    out_held.at[pl.ds(k * width, width), pl.ds(j * width, width)],
                    sems.at[j * n + k],
                )
            )
    up_copies = row_blocks(me, n, width, up_weight, up_held, sems, n * n)
    down_copies = col_blocks(me, n, width, down_weight, down_held, sems, n * n + n)

    def work(wait):
        for j, one in enumerate(attended.refs()):
            joined[:, j * width : (j + 1) * width] = one[...]
        if beside:
            put_beside(me, extra.refs(), *joined_outs)
        total = square = 0.0
        for j in range(n):
            wait(out_copies[j * n : (j + 1) * n])
            part = slice(j * width, (j + 1) * width)
            base = own[...] if j == 0 else xs[j - 1][...].astype(F32)
            value = base + dot_nn(joined[...], out_held[:, part])
            whole[:, part] = value
            if j == 0:
                hidden[...] = value
            total += jnp.sum(value, 1, keepdims=True)
            square += jnp.sum(value * value, 1, keepdims=True)
        mean = total / full
        inv = lax.rsqrt(square / full - mean * mean + EPSILON)
        stat[...] = stat_columns(mean, inv)
        for j in range(n):
            part = slice(j * width, (j + 1) * width)
            value = ((whole[:, part] - mean) * inv * gain[0:1, part] + bias[0:1, part]).astype(BF16)
            joined[:, part] = value
            normed[:, place_of(me, j, width)] = value
        wait(up_copies)
        step = divisor(inner, 512)
        for c in range(inner // step):
            part = slice(c * step, (c + 1) * step)
            up = dot_nn(joined[...], up_held[:, part]) + up_bias[0:1, part]
            half = 0.5 * (1.0 + lax.erf(up * SQRT_HALF))
            activated[:, part] = (up * half).astype(BF16)
            slope[:, part] = (half + up * INV_ROOT_TWO_PI * jnp.exp(-0.5 * up * up)).astype(BF16)
        wait(down_copies)
        for j in range(n):
            parts.put(j, dot_nn(activated[...], down_held[:, j * width : (j + 1) * width]))

    with_weights(
        out_copies + up_copies + down_copies, work, pairs, [attended] + ([extra] if beside else [])
    )
    parts.finish()


def put_beside(me, blocks, whole, sums):
    width = blocks[0].shape[1]
    for j, block in enumerate(blocks):
        whole[:, place_of(me, j, width)] = block[...]
    accumulate(sums, fold_rows(blocks[0][...].astype(F32)))


def feed(
    n, pairs, attended, xs, outs_w, own, gain, bias, up_bias, up_weight, down_weight, beside=()
):
    length, width = own.shape
    full, inner = up_weight.shape
    tile = min(256, length)
    steps = length // tile
    parts = Scattered(pairs, n, steps, False)
    part_outs, part_specs = parts.outs(length, width)
    twice = tuple(attended) if pairs else ()
    extra = (*beside, *(beside if pairs else ()))
    got = call(
        "feed",
        lambda *refs: feed_body(n, pairs, bool(beside), steps, *refs),
        (steps,),
        (
            *attended,
            *twice,
            *xs[1:],
            *outs_w,
            own,
            gain,
            bias,
            up_bias,
            up_weight,
            down_weight,
            *extra,
        ),
        Gathered.specs(attended, pairs, tile)
        + [rows_of((tile, width))] * (n - 1)
        + [ANY] * n
        + [rows_of((tile, width))]
        + [fixed((8, full))] * 2
        + [fixed((8, inner))]
        + [ANY] * 2
        + (Gathered.specs(beside, pairs, tile) if beside else []),
        [
            shape((length, width), F32),
            shape((length, full), BF16),
            shape((length, 128), F32),
            shape((length, inner), BF16),
            shape((length, inner), BF16),
        ]
        + part_outs
        + ([shape((length, full), BF16), shape((8, width), F32)] if beside else []),
        [
            rows_of((tile, width)),
            rows_of((tile, full)),
            rows_of((tile, 128)),
            rows_of((tile, inner)),
            rows_of((tile, inner)),
        ]
        + part_specs
        + ([rows_of((tile, full)), fixed((8, width))] if beside else []),
        scratch=[
            pltpu.VMEM((full, full), BF16),
            pltpu.VMEM((full, inner), BF16),
            pltpu.VMEM((inner, full), BF16),
            pltpu.VMEM((tile, full), BF16),
            pltpu.VMEM((tile, full), F32),
            pltpu.SemaphoreType.DMA((n * n + 2 * n,)),
        ]
        + Gathered.scratch(attended, pairs, steps)
        + (Gathered.scratch(beside, pairs, steps) if beside else [])
        + parts.scratch(length, width),
        remote=pairs,
    )
    return (*got[:5], got[5 : 5 + parts.count()], got[5 + parts.count() :])


def row_stats(total, weighted):
    return stat_columns(total, weighted).T[0:8, :]


def norm_sums(parts, n, product, normed, gain, bias, me):
    width = gain.shape[1] // n
    total = weighted = 0.0
    for j in range(n):
        part = slice(j * width, (j + 1) * width)
        value = product(j)
        parts.put(j, value)
        total += jnp.sum(value * gain[0:1, part], 1, keepdims=True)
        there = normed[:, place_of(me, j, width)].astype(F32)
        weighted += jnp.sum(value * (there - bias[0:1, part]), 1, keepdims=True)
    return row_stats(total, weighted)


def feed_back_body(n, pairs, beside, steps, *refs):
    cot, slope, normed, gain, bias, up_weight, down_weight = refs[:7]
    refs = refs[7:]
    count = 4 if pairs else n
    extra = None
    if beside:
        extra, refs = Gathered(refs[:count], pairs, steps), refs[count:]
    up_grad, up_bias_sum = refs[:2]
    refs = refs[2:]
    parts = Scattered(pairs, n, steps, True)
    part_outs, refs = refs[: parts.count()], refs[parts.count() :]
    if beside:
        joined_outs, refs = refs[:2], refs[2:]
    up_held, down_held, row_sums, sems, *refs = refs
    if pairs and beside:
        extra.attach(refs[:2])
        refs = refs[2:]
    parts.attach(part_outs, refs)
    me = lax.axis_index("mp")
    inner = up_held.shape[1]
    width = gain.shape[1] // n
    step = divisor(inner, 512)
    down_copies = [pltpu.make_async_copy(down_weight, down_held, sems.at[n])]
    up_copies = row_blocks(me, n, width, up_weight, up_held, sems, 0)

    def work(wait):
        if beside:
            put_beside(me, extra.refs(), *joined_outs)
        wait(down_copies)
        bias_parts = []
        for c in range(inner // step):
            part = slice(c * step, (c + 1) * step)
            value = dot_nt(cot[...], down_held[part, :]) * slope[:, part].astype(F32)
            low = value.astype(BF16)
            up_grad[:, part] = low
            bias_parts.append(fold_rows(low.astype(F32)))
        accumulate(up_bias_sum, jnp.concatenate(bias_parts, 1))
        wait(up_copies)
        row_sums[...] = norm_sums(
            parts,
            n,
            lambda j: dot_nt(up_grad[...], up_held[j * width : (j + 1) * width, :]),
            normed,
            gain,
            bias,
            me,
        )

    with_weights(down_copies + up_copies, work, pairs, [extra] if beside else [])
    parts.finish(row_sums[...])


def feed_back(n, pairs, cot, slope, normed, gain, bias, up_weight, down_weight, beside=()):
    length, full = cot.shape
    width = full // n
    inner = up_weight.shape[1]
    tile = min(256, length)
    steps = length // tile
    parts = Scattered(pairs, n, steps, True)
    part_outs, part_specs = parts.outs(length, width)
    got = call(
        "feed_back",
        lambda *refs: feed_back_body(n, pairs, bool(beside), steps, *refs),
        (steps,),
        (
            cot,
            slope,
            normed,
            gain,
            bias,
            up_weight,
            down_weight,
            *beside,
            *(beside if pairs else ()),
        ),
        [rows_of((tile, full)), rows_of((tile, inner)), rows_of((tile, full))]
        + [fixed((8, full))] * 2
        + [ANY] * 2
        + (Gathered.specs(beside, pairs, tile) if beside else []),
        [shape((length, inner), BF16), shape((8, inner), F32)]
        + part_outs
        + ([shape((length, full), BF16), shape((8, width), F32)] if beside else []),
        [rows_of((tile, inner)), fixed((8, inner))]
        + part_specs
        + ([rows_of((tile, full)), fixed((8, width))] if beside else []),
        scratch=[
            pltpu.VMEM((full, inner), BF16),
            pltpu.VMEM((inner, full), BF16),
            pltpu.VMEM((8, tile), F32),
            pltpu.SemaphoreType.DMA((n + 1,)),
        ]
        + (Gathered.scratch(beside, pairs, steps) if beside else [])
        + parts.scratch(length, width),
        remote=pairs,
    )
    return (*got[:2], got[2 : 2 + parts.count()], got[2 + parts.count() :])


def norm_back(refs, n_parts, source, stat, sums, gain, full):
    grad = refs[0][...].astype(F32)
    for ref in refs[1:n_parts]:
        grad += ref[...].astype(F32)
    columns = sum(one[...] for one in sums).T
    mean, inv = stat[:, 0:1], stat[:, 1:2]
    scaled = (source[...] - mean) * inv
    back = inv * (
        grad * gain[0:1, :] - columns[:, 0:1] * (1.0 / full) - scaled * (columns[:, 1:2] * (1.0 / full))
    )
    return back, fold_rows(grad * scaled), fold_rows(grad)


def hidden_back_body(k, m, full, *refs):
    parts, sums = refs[:k], refs[k : k + m]
    cot, hidden, stat, gain, wide, low, gain_sum, bias_sum = refs[k + m :]
    back, gain_part, bias_part = norm_back(parts, k, hidden, stat, sums, gain, full)
    value = cot[...].astype(F32) + back
    wide[...] = value
    low[...] = value.astype(BF16)
    accumulate(gain_sum, gain_part)
    accumulate(bias_sum, bias_part)


def hidden_back(parts, cotangent, row, hidden, stat, sums, gain, full):
    k, m, (length, width) = len(parts), len(sums), hidden.shape
    tile = min(256, length)
    steps = length // tile
    return call(
        "hidden_back",
        lambda *refs: hidden_back_body(k, m, full, *refs),
        (steps,),
        (*parts, *sums, cotangent, hidden, stat, gain),
        [rows_of((tile, width))] * k
        + [cols_of((8, tile))] * m
        + [
            pl.BlockSpec((tile, width), lambda i: (row * steps + i, 0)),
            rows_of((tile, width)),
            rows_of((tile, 128)),
            fixed((8, width)),
        ],
        [shape((length, width), F32), sent((length, width), BF16)] + [shape((8, width), F32)] * 2,
        [rows_of((tile, width))] * 2 + [fixed((8, width))] * 2,
    )


def attended_back_body(n, pairs, steps, *refs):
    count = 4 if pairs else n
    grads = Gathered(refs[:count], pairs, steps)
    weight, joined, out, *more = refs[count:]
    grads.attach(more)
    me = lax.axis_index("mp")
    width = grads.blocks[0].shape[1]

    def work(wait):
        for j, one in enumerate(grads.refs()):
            joined[:, place_of(me, j, width)] = one[...]
        out[...] = dot_nt(joined[...], weight[...]).astype(BF16)

    with_weights([], work, pairs, [grads])


def attended_back(n, pairs, grads, weight):
    length, width = grads[0].shape
    rows, full = weight.shape
    tile = min(256, length)
    steps = length // tile
    return call(
        "attended_back",
        lambda *refs: attended_back_body(n, pairs, steps, *refs),
        (steps,),
        (*grads, *(grads if pairs else ()), weight),
        Gathered.specs(grads, pairs, tile) + [fixed((rows, full))],
        [shape((length, full), BF16), shape((length, rows), BF16)],
        [rows_of((tile, full)), rows_of((tile, rows))],
        scratch=Gathered.scratch(grads, pairs, steps),
        remote=pairs,
    )


def project_back_body(n, pairs, steps, grad, normed, gain, bias, weight, *refs):
    parts = Scattered(pairs, n, steps, True)
    part_outs, refs = refs[: parts.count()], refs[parts.count() :]
    held, row_sums, sems, *refs = refs
    parts.attach(part_outs, refs)
    me = lax.axis_index("mp")
    width = gain.shape[1] // n
    copies = row_blocks(me, n, width, weight, held, sems, 0)

    def work(wait):
        def product(j):
            wait(copies[j : j + 1])
            return dot_nt(grad[...], held[j * width : (j + 1) * width, :])

        row_sums[...] = norm_sums(parts, n, product, normed, gain, bias, me)

    with_weights(copies, work, pairs)
    parts.finish(row_sums[...])


def project_back(n, pairs, grad, normed, gain, bias, weight):
    length, out = grad.shape
    full = weight.shape[0]
    width = full // n
    tile = min(256, length)
    steps = length // tile
    parts = Scattered(pairs, n, steps, True)
    part_outs, part_specs = parts.outs(length, width)
    return call(
        "project_back",
        lambda *refs: project_back_body(n, pairs, steps, *refs),
        (steps,),
        (grad, normed, gain, bias, weight),
        [rows_of((tile, out)), rows_of((tile, full))] + [fixed((8, full))] * 2 + [ANY],
        part_outs,
        part_specs,
        scratch=[
            pltpu.VMEM((full, out), BF16),
            pltpu.VMEM((8, tile), F32),
            pltpu.SemaphoreType.DMA((n,)),
        ]
        + parts.scratch(length, width),
        remote=pairs,
    )


def average_back_body(k, m, full, count, *refs):
    weights, parts, sums = refs[0], refs[1 : k + 1], refs[k + 1 : k + m + 1]
    source, stat, gain, hidden_grad, history = refs[k + m + 1 : k + m + 6]
    grad_history, depth_sum, gain_sum, bias_sum = refs[-4:]
    back, gain_part, bias_part = norm_back(parts, k, source, stat, sums, gain, full)
    value = hidden_grad[...] + back
    accumulate(gain_sum, gain_part)
    accumulate(bias_sum, bias_part)
    lanes = value.shape[1] // 128
    for j in range(count):
        grad_history[j] = (weights[j] * value).astype(BF16)
        product = fold_rows(value * history[j].astype(F32))
        folded = product[:, 0:128]
        for c in range(1, lanes):
            folded += product[:, c * 128 : (c + 1) * 128]
        accumulate(depth_sum.at[j], folded)


def average_back(weights, parts, source, stat, sums, gain, hidden_grad, history, row, made):
    k, m, (length, width) = len(parts), len(sums), source.shape
    count = history.shape[0]
    tile = min(256, length)
    steps = length // tile
    full = gain[1]
    block = pl.BlockSpec((count, tile, width), lambda i: (0, row * steps + i, 0))
    args = (weights, *parts, *sums, source, stat, gain[0], hidden_grad, history)
    specs = (
        [SMEM]
        + [rows_of((tile, width))] * k
        + [cols_of((8, tile))] * m
        + [rows_of((tile, width)), rows_of((tile, 128)), fixed((8, width)), rows_of((tile, width)), block]
    )
    more = {}
    if made is not None:
        more = {"aliases": {len(args): 0}}
        args, specs = (*args, made), specs + [ANY]
    return call(
        "average_back",
        lambda *refs: average_back_body(k, m, full, count, *refs),
        (steps,),
        args,
        specs,
        [shape(history.shape, BF16), shape((count, 8, 128), F32)] + [shape((8, width), F32)] * 2,
        [block, fixed((count, 8, 128))] + [fixed((8, width))] * 2,
        **more,
    )


def divisor(size, most):
    return max(d for d in range(128, most + 1, 128) if size % d == 0) if size > 128 else size


def weight_body(rows, *refs):
    out = refs[-1]
    total = dot_tn(refs[0][...], refs[rows][...])
    for r in range(1, rows):
        total += dot_tn(refs[r][...], refs[rows + r][...])
    out[...] = total.astype(BF16)


def weight_grad(lefts, rights):
    rows, (length, high), wide = len(lefts), lefts[0].shape, rights[0].shape[1]
    tall, across = divisor(high, 512), divisor(wide, 1024)
    return call(
        "weight_grad",
        lambda *refs: weight_body(rows, *refs),
        (high // tall, wide // across),
        (*lefts, *rights),
        [pl.BlockSpec((length, tall), lambda i, j: (0, i))] * rows
        + [pl.BlockSpec((length, across), lambda i, j: (0, j))] * rows,
        [shape((high, wide), BF16)],
        [pl.BlockSpec((tall, across), lambda i, j: (i, j))],
    )[0]


def put_blocks(came, outs, k, value):
    if came is not None:
        value = value + came[k].astype(F32)
    per = outs[0].shape[0]
    outs[k // per][k % per] = value.astype(BF16)


def tall_blocks_body(rows, count, fused, group, *refs):
    lefts, rights = refs[: rows * count], refs[rows * count : rows * count + rows]
    refs = refs[rows * count + rows :]
    came, outs, turned = refs[0] if fused else None, refs[fused:-1], refs[-1]
    length, high = lefts[0].shape

    @pl.when(pl.program_id(0) == 0)
    def _():
        for k in range(count):
            for r in range(rows):
                turned[k * high : (k + 1) * high, r * length : (r + 1) * length] = lefts[
                    k * rows + r
                ][...].T

    for k in range(count):
        total = 0.0
        for r in range(rows):
            total += dot_nn(
                turned[k * high : (k + 1) * high, r * length : (r + 1) * length], rights[r][...]
            )
        put_blocks(came, outs, k, total)


def wide_blocks_body(rows, count, fused, group, *refs):
    lefts, rights = refs[:rows], refs[rows : rows + rows * count]
    refs = refs[rows + rows * count :]
    came, outs = refs[0] if fused else None, refs[fused:]
    turned = [left[...].T for left in lefts]
    for k in range(count):
        total = 0.0
        for r in range(rows):
            total += dot_nn(turned[r], rights[k * rows + r][...])
        put_blocks(came, outs, k, total)


class Spread:
    def __init__(self, lefts, rights, dim, bits, part=(0, 1)):
        self.lefts, self.rights, self.dim, self.bits, self.part = lefts, rights, dim, list(bits), part
        self.groups = lax.axis_size("dp")
        self.block = (lefts, rights)[dim][0].shape[1] // self.groups
        order = [0]
        for bit in reversed(self.bits):
            order = order + [e | bit for e in order]
        self.order = order

    def blocks(self, half, came=None):
        count = self.groups // 2
        which = self.order[half * count : (half + 1) * count]
        rows, length = len(self.lefts), self.lefts[0].shape[0]
        group = lax.axis_index("dp").astype(jnp.int32)[None]
        size, (index, pieces) = self.block, self.part
        stay = [
            pl.BlockSpec((length, size), lambda i, group, e=e: (0, group[0] ^ e))
            for e in which
            for _ in range(rows)
        ]
        other = self.rights if self.dim == 0 else self.lefts
        extent = other[0].shape[1] // pieces
        tile = divisor(extent, 512)
        steps = extent // tile
        move = [pl.BlockSpec((length, tile), lambda i, group: (0, index * steps + i))] * rows

        def blocked(number):
            if self.dim == 0:
                return (
                    sent((number, size, extent), BF16),
                    pl.BlockSpec((number, size, tile), lambda i, group: (0, 0, i)),
                )
            return (
                sent((number, extent, size), BF16),
                pl.BlockSpec((number, tile, size), lambda i, group: (0, i, 0)),
            )

        if self.dim == 0:
            args = (*(list(self.lefts) * count), *self.rights)
            specs = stay + move
            body, scratch = tall_blocks_body, [pltpu.VMEM((count * size, rows * length), BF16)]
        else:
            args = (*self.lefts, *(list(self.rights) * count))
            specs = move + stay
            body, scratch = wide_blocks_body, []
        outs = [blocked(count)]
        if came is not None:
            args, specs = (*args, came), specs + [blocked(count)[1]]
            outs = [blocked(count // 2)] * 2
        return call(
            "weight_blocks",
            lambda *refs: body(rows, count, came is not None, *refs),
            (steps,),
            (group, *args),
            specs,
            [one[0] for one in outs],
            [one[1] for one in outs],
            scratch=scratch,
            prefetch=1,
        )

    def send(self, value):
        bit = self.bits[self.step]
        self.step += 1
        self.coming = lax.ppermute(value, "dp", [(i, i ^ bit) for i in range(self.groups)])

    def first(self):
        self.step = 0
        self.send(self.blocks(1)[0])

    def keep(self):
        self.held = self.blocks(0)[0]

    def keep_added(self):
        self.held, out = self.blocks(0, self.coming)
        self.send(out)


def fold_body(count, *refs):
    for i in range(count):
        held, came, keep, send = refs[2 * i], refs[2 * i + 1], refs[2 * count + 2 * i], refs[2 * count + 2 * i + 1]
        half = keep.shape[0]
        keep[...] = (held[:half].astype(F32) + came[:half].astype(F32)).astype(BF16)
        send[...] = (held[half:].astype(F32) + came[half:].astype(F32)).astype(BF16)


def advance(*spreads):
    steps = 4
    args, specs, outs, out_specs = [], [], [], []
    for one in spreads:
        count, high, wide = one.held.shape
        args += [one.held, one.coming]
        specs += [pl.BlockSpec((count, high // steps, wide), lambda i: (0, i, 0))] * 2
        outs += [sent((count // 2, high, wide), BF16)] * 2
        out_specs += [pl.BlockSpec((count // 2, high // steps, wide), lambda i: (0, i, 0))] * 2
    got = call("fold", lambda *refs: fold_body(len(spreads), *refs), (steps,), args, specs, outs, out_specs)
    for i, one in enumerate(spreads):
        one.held = got[2 * i]
        one.send(got[2 * i + 1])


def finish_body(groups, *refs):
    outs = refs[len(refs) - len(groups) :]
    at = 0
    for out, group in zip(outs, groups):
        for first, wide in group:
            total = refs[at][0].astype(F32) + refs[at + 1][0].astype(F32)
            out[:, first : first + wide] = total
            at += 2


def finish(*groups):
    steps = 4
    args, specs, outs, out_specs, places = [], [], [], [], []
    for group in groups:
        first, place = 0, []
        for one in group:
            _, high, wide = one.held.shape
            args += [one.held, one.coming]
            specs += [pl.BlockSpec((1, high // steps, wide), lambda i: (0, i, 0))] * 2
            place.append((first, wide))
            first += wide
        outs.append(shape((high, first), F32))
        out_specs.append(rows_of((high // steps, first)))
        places.append(place)
    return call("finish", lambda *refs: finish_body(places, *refs), (steps,), args, specs, outs, out_specs)


def output_body(rows, steps, *refs):
    bias, out = refs[-2:]
    per = (len(refs) - 2) // rows
    for r in range(rows):

        @pl.when(pl.program_id(0) // steps == r)
        def _(r=r):
            total = bias[0:1, :]
            for part in refs[r * per + 1 : (r + 1) * per]:
                total = total + part[...].astype(F32)
            out[...] = (refs[r * per][...] + total).astype(BF16)


def output(parts, hidden, bias):
    rows, (length, width) = len(hidden), hidden[0].shape
    tile = min(512, length)
    steps = length // tile
    args, specs = [], []
    for r in range(rows):
        args += [hidden[r], *parts[r]]
        specs += [
            pl.BlockSpec((tile, width), lambda i, r=r: (jnp.clip(i - r * steps, 0, steps - 1), 0))
        ] * (1 + len(parts[r]))
    return call(
        "output",
        lambda *refs: output_body(rows, steps, *refs),
        (rows * steps,),
        (*args, bias),
        specs + [fixed((8, width))],
        [shape((rows * length, width), BF16)],
        [rows_of((tile, width))],
    )[0]


class Ring:
    def __init__(self):
        self.n = lax.axis_size("mp")
        self.me = lax.axis_index("mp").astype(jnp.int32)
        self.pairs = self.n == 4
        self.core = [(i, i ^ 1) for i in range(self.n)]
        self.chip = [(i, i ^ 2) for i in range(self.n)]

    def over_core(self, value):
        return lax.ppermute(value, "mp", self.core)

    def over_chip(self, value):
        return lax.ppermute(value, "mp", self.chip)

    def gather_start(self, block):
        if self.pairs:
            return [block, self.over_chip(block)]
        return self.gather(block)

    def gather(self, block):
        if self.pairs:
            across = self.over_chip(block)
            return [block, self.over_core(block), across, self.over_core(across)]
        every = lax.all_gather(block, "mp")
        return [
            lax.dynamic_index_in_dim(every, self.me ^ j, 0, keepdims=False) for j in range(self.n)
        ]

    def scatter(self, parts, sums=False):
        parts, extra = (parts[:-1], parts[-1:]) if sums else (parts, [])
        if self.pairs:
            return [parts[0], self.over_chip(parts[1])], [*extra, *map(self.over_chip, extra)]
        stacked = jnp.stack([part.astype(F32) for part in parts])
        ordered = jnp.take(stacked, self.me ^ jnp.arange(self.n), axis=0)
        total = lax.psum_scatter(ordered, "mp", scatter_dimension=0, tiled=False)
        return [total], [lax.psum(v, "mp") for v in extra]

    def total(self, value):
        if self.pairs:
            value = value + self.over_core(value)
            return value + self.over_chip(value)
        return lax.psum(value, "mp")

    def out_start(self, weight):
        rows, groups = weight.shape[0], lax.axis_size("dp")
        if self.pairs and rows % (16 * groups) == 0:
            size = rows // groups
            piece = lax.dynamic_slice_in_dim(weight, lax.axis_index("dp") * size, size, 0)
            return self.over_chip(piece)
        return None

    def out_middle(self, piece):
        return None if piece is None else lax.all_gather(piece, "dp", axis=0, tiled=True)

    def out_end(self, weight, across):
        if across is None:
            return self.gather(weight)
        across = gate([across])[0]
        return [weight, self.over_core(weight), across, self.over_core(across)]


def dp_total(vectors):
    groups = lax.axis_size("dp")
    sizes = [v.size for v in vectors]
    packed = jnp.concatenate(vectors)
    packed = jnp.pad(packed, (0, -packed.size % 1024)).reshape(-1, 128)
    bit = 1
    while bit < groups:
        packed = packed + lax.ppermute(packed, "dp", [(i, i ^ bit) for i in range(groups)])
        bit *= 2
    packed = packed.reshape(-1)
    ends = np.cumsum(sizes)
    return [packed[end - size : end] for end, size in zip(ends, sizes)]


def tables_of(length):
    half = HEAD // 2
    rate = np.exp(np.arange(half, dtype=np.float64) * (-math.log(10000.0) / half))
    angle = np.arange(length, dtype=np.float64)[:, None] * rate[None, :]
    cosine, sine = np.cos(angle), np.sin(angle)
    return (
        jnp.asarray(np.concatenate([cosine, cosine], 1), F32),
        jnp.asarray(np.concatenate([-sine, sine], 1), F32),
    )


def local(
    history,
    depth_weights,
    segment_ids,
    first_gain,
    first_bias,
    qkv_weight,
    out_weight,
    second_gain,
    second_bias,
    up_weight,
    up_bias,
    down_weight,
    down_bias,
    cotangent,
):
    ring = Ring()
    n = ring.n
    pairs = ring.pairs
    width = history.shape[2]
    full = n * width
    row_count, length = segment_ids.shape
    rows = range(row_count)
    tables = tables_of(length)
    earlier = (segment_ids[:, None, :] < segment_ids[:, :, None]).astype(jnp.int32)
    starts = jnp.broadcast_to(jnp.sum(earlier, -1)[:, None, :], (row_count, 8, length))

    up_bias8 = jnp.broadcast_to(up_bias[None], (8, up_bias.shape[0]))

    down_bias8 = jnp.broadcast_to(down_bias[None], (8, width))
    groups = lax.axis_size("dp")
    spread = full % (128 * groups) == 0 and groups >= 4
    last = row_count - 1

    Order.last, Order.names = None, 0
    vectors = jnp.stack([first_gain, first_bias, second_gain, second_bias])
    vectors = ring.gather_start(jnp.repeat(vectors, 8, 0))
    piece = ring.out_start(out_weight)
    cot_rows = [lax.slice_in_dim(cotangent, r * length, (r + 1) * length) for r in rows]
    none = [None] * row_count
    wide, low, xs, qkv, normed1, stat1 = (list(none) for _ in range(6))
    attended, logs, heads, cots, cot_full = (list(none) for _ in range(5))
    hidden, normed2, stat2, activated, slope = (list(none) for _ in range(5))
    branch, up_grad, parts2, parts1 = (list(none) for _ in range(4))
    hidden_grad, grads, grad_full, qkv_grad = (list(none) for _ in range(4))
    up_bias_sum = down_bias_sum = gain2_sum = bias2_sum = 0.0

    for r in rows:
        wide[r], low[r] = average(depth_weights, history, r, length)
        if r == 0:
            xs[0] = ring.gather_start(low[0])
            if pairs:
                vectors[1], piece = gate([vectors[1], piece])
                vectors = [
                    vectors[0],
                    ring.over_core(vectors[0]),
                    vectors[1],
                    ring.over_core(vectors[1]),
                ]
            across = ring.out_middle(piece)
    vectors = jnp.concatenate(vectors, 1)
    gain1, bias1, gain2, bias2 = (vectors[8 * i : 8 * i + 8] for i in range(4))
    own1, own2 = gain1[:, :width], gain2[:, :width]
    for r in rows[1:]:
        xs[r] = ring.gather_start(gate([low[r]], xs[r - 1][1:2])[0])
    for r in rows:
        qkv[r], normed1[r], stat1[r], xs[r] = project(
            n, pairs, xs[r], gain1, bias1, tables, qkv_weight
        )
        attended[r], logs[r] = attend(starts[r], qkv[r])
        heads[r] = ring.gather_start(attended[r])
        if r == 0:
            out_w = ring.out_end(out_weight, across)

    for r in rows:
        cots[r] = ring.gather_start(gate([cot_rows[r]])[0])
        got = feed(
            n,
            pairs,
            heads[r],
            xs[r],
            out_w,
            wide[r],
            gain2,
            bias2,
            up_bias8,
            up_weight,
            down_weight,
            cots[r - 1] if r > 0 else (),
        )
        hidden[r], normed2[r], stat2[r], activated[r], slope[r], parts, joined = got
        branch[r] = ring.scatter(parts)[0]
        if r > 0:
            cot_full[r - 1], sums = joined
            down_bias_sum += sums

    def back(r, more=()):
        return feed_back(
            n, pairs, cot_full[r], slope[r], normed2[r], gain2, bias2, up_weight, down_weight, more
        )

    def take(r, got):
        nonlocal up_bias_sum
        up_grad[r], up_sum, parts, joined = got
        up_bias_sum += up_sum
        parts2[r] = ring.scatter(parts, True)
        return joined

    cot_full[last], sums = take(0, back(0, cots[last]))
    down_bias_sum += sums
    if spread:
        down = Spread(activated, cot_full, 1, (1, 2, 4))
        down.first()
    if pairs:
        branch[0][1] = gate(branch[0][1:])[0]
    for r in rows[1:]:
        take(r, back(r))

    def hidden_step(r):
        nonlocal gain2_sum, bias2_sum
        parts, sums = parts2[r]
        hidden_grad[r], low_grad, gain_part, bias_part = hidden_back(
            parts, cotangent, r, hidden[r], stat2[r], sums, own2, full
        )
        gain2_sum += gain_part
        bias2_sum += bias_part
        grads[r] = ring.gather_start(low_grad)

    hidden_step(0)
    if spread:
        up = [
            Spread(normed2, up_grad, 0, (1, 2, 4), (0, 2)),
            Spread(normed2, up_grad, 0, (2, 4, 1), (1, 2)),
        ]
        up[1].first()
        if pairs:
            branch[last][1] = gate(branch[last][1:])[0]
        up[0].first()
        down.keep()

    for r in rows:
        grad_full[r], attended_grad = attended_back(n, pairs, grads[r], out_weight)
        if r < last:
            hidden_step(r + 1)
        qkv_grad[r] = attend_back(starts[r], tables, qkv[r], attended_grad, logs[r])
        parts = project_back(n, pairs, qkv_grad[r], normed1[r], gain1, bias1, qkv_weight)
        parts1[r] = ring.scatter(parts, True)
        if spread and r == 0:
            up[1].keep_added()
            advance(down)

    if spread:
        qkv_sum = [
            Spread(normed1, qkv_grad, 0, (1, 2, 4), (0, 2)),
            Spread(normed1, qkv_grad, 0, (2, 4, 1), (1, 2)),
        ]
        out_sum = Spread(attended, grad_full, 1, (2, 4, 1))
        qkv_sum[0].first()
        qkv_sum[1].first()
        out_sum.first()
        up[0].keep_added()
        advance(down, up[1])
        out_sum.keep()
    made = output(branch, hidden, down_bias8)

    grad_history, depth_sum, gain1_sum, bias1_sum = None, 0.0, 0.0, 0.0
    for r in rows:
        parts, sums = parts1[r]
        grad_history, depth_part, gain_part, bias_part = average_back(
            depth_weights,
            parts,
            wide[r],
            stat1[r],
            sums,
            (own1, full),
            hidden_grad[r],
            history,
            r,
            grad_history,
        )
        depth_sum += depth_part
        gain1_sum += gain_part
        bias1_sum += bias_part
        if r == 0 and spread:
            qkv_sum[0].keep_added()
            qkv_sum[1].keep_added()
            advance(up[0], out_sum)

    if spread:
        advance(qkv_sum[0], qkv_sum[1], out_sum)
        down_total, up_total, out_total, qkv_total = finish([down], up, [out_sum], qkv_sum)
    else:
        down_total, up_total, out_total, qkv_total = (
            lax.psum_scatter(
                weight_grad(*pair), "dp", scatter_dimension=dim, tiled=True
            ).astype(F32)
            for pair, dim in (
                ((activated, cot_full), 1),
                ((normed2, up_grad), 0),
                ((attended, grad_full), 1),
                ((normed1, qkv_grad), 0),
            )
        )

    sums = [up_bias_sum, down_bias_sum, gain2_sum, bias2_sum, gain1_sum, bias1_sum]
    depth_part = ring.total(jnp.sum(depth_sum, (1, 2)))
    sums = dp_total([jnp.sum(v, 0) for v in sums] + [depth_part])
    return (
        made,
        grad_history,
        sums[6],
        sums[4],
        sums[5],
        qkv_total,
        out_total,
        sums[2],
        sums[3],
        up_total,
        sums[0],
        down_total,
        sums[1],
    )


def solution(mesh):
    placed = (
        P(None, "dp", "mp"),
        P(),
        P("dp", None),
        P("mp"),
        P("mp"),
        P(None, "mp"),
        P("mp", None),
        P("mp"),
        P("mp"),
        P(None, "mp"),
        P("mp"),
        P("mp", None),
        P("mp"),
        P("dp", "mp"),
    )
    return jax.shard_map(
        local,
        mesh=mesh,
        in_specs=placed,
        out_specs=(
            P("dp", "mp"),
            P(None, "dp", "mp"),
            P(),
            P("mp"),
            P("mp"),
            P("dp", "mp"),
            P("mp", "dp"),
            P("mp"),
            P("mp"),
            P("dp", "mp"),
            P("mp"),
            P("mp", "dp"),
            P("mp"),
        ),
        check_vma=False,
    )
```

```python
import math

import jax
import jax.numpy as jnp
import numpy as np
from jax import lax
from jax.experimental import pallas as pl
from jax.experimental.pallas import tpu as pltpu
from jax.sharding import PartitionSpec as P

HEAD = 128
MAX_DOC = 512
EPSILON = 1e-05
SQRT_HALF = 0.7071067811865476
INV_ROOT_TWO_PI = 0.3989422804014327
LOG2E = 1.4426950408889634
SCALE = HEAD ** (-0.5)
MIB = 2**20
BF16 = jnp.bfloat16
F32 = jnp.float32


def dot_nn(a, b):
    return jnp.dot(a, b, preferred_element_type=F32)


def dot_nt(a, b):
    return lax.dot_general(a, b, (((1,), (1,)), ((), ())), preferred_element_type=F32)


def dot_tn(a, b):
    return lax.dot_general(a, b, (((0,), (0,)), ((), ())), preferred_element_type=F32)


class Order:
    last = None
    names = 0
    cost = 10**12

    @staticmethod
    def name(remote):
        Order.names += remote
        return Order.names - 1 if remote else None


def call(
    name, body, grid, args, in_specs, outs, out_specs, scratch=(), prefetch=0, after=(), aliases=None, remote=False
):
    count = len(args)
    extra = [*after]
    if Order.last is not None and not any(Order.last is a for a in args):
        extra.append(Order.last)

    def without_extra(*refs):
        body(*refs[:count], *refs[count + len(extra) :])

    got = pl.pallas_call(
        without_extra,
        grid_spec=pltpu.PrefetchScalarGridSpec(
            num_scalar_prefetch=prefetch,
            grid=grid,
            in_specs=list(in_specs) + [ANY] * len(extra),
            out_specs=out_specs,
            scratch_shapes=list(scratch),
        ),
        out_shape=outs,
        input_output_aliases=aliases or {},
        compiler_params=pltpu.CompilerParams(
            vmem_limit_bytes=60 * MIB, collective_id=Order.name(remote), has_side_effects=remote
        ),
        cost_estimate=pl.CostEstimate(flops=Order.cost, bytes_accessed=Order.cost // 10**4, transcendentals=0),
        name=name,
    )(*args, *extra)
    fresh = [v for i, v in enumerate(got) if i not in (aliases or {}).values()]
    Order.last = min(fresh or got, key=lambda v: v.size)
    return got


def shape(dims, dtype):
    return jax.ShapeDtypeStruct(dims, dtype)


def sent(dims, dtype):
    return pltpu.HBM(dims, dtype)


SMEM = pl.BlockSpec(memory_space=pltpu.SMEM)
ANY = pl.BlockSpec(memory_space=pl.ANY)


def gate(arrays, after=()):
    arrays = list(arrays)
    return call(
        "gate",
        lambda *refs: None,
        (1,),
        arrays,
        [ANY] * len(arrays),
        [shape(a.shape, a.dtype) for a in arrays],
        [ANY] * len(arrays),
        after=after,
        aliases={i: i for i in range(len(arrays))},
    )


def rows_of(block):
    return pl.BlockSpec(block, lambda i: (i, 0))


def cols_of(block):
    return pl.BlockSpec(block, lambda i: (0, i))


def fixed(block):
    return pl.BlockSpec(block, lambda i: (0,) * len(block))


def flip(me, j):
    there, bit = me, 1
    while bit <= j:
        if j & bit:
            there = there + bit * (1 - 2 * ((me // bit) % 2))
        bit *= 2
    return there


def place_of(me, j, width):
    return pl.ds(pl.multiple_of(flip(me, j) * width, width), width)


def greet():
    barrier = pltpu.get_barrier_semaphore()
    sibling = flip(lax.axis_index("mp"), 1)
    pl.semaphore_signal(
        barrier, inc=1, device_id={"mp": sibling}, device_id_type=pl.DeviceIdType.MESH
    )
    pl.semaphore_wait(barrier, 1)


def to_sibling(source, target, sems, at):
    return pltpu.make_async_remote_copy(
        src_ref=source,
        dst_ref=target,
        send_sem=sems.at[0, at],
        recv_sem=sems.at[1, at],
        device_id={"mp": flip(lax.axis_index("mp"), 1)},
        device_id_type=pl.DeviceIdType.MESH,
    )


class Gathered:
    def __init__(self, refs, pairs, steps):
        self.pairs, self.steps = pairs, steps
        self.blocks, self.whole = refs[:2] if pairs else refs, refs[2:4] if pairs else ()

    @staticmethod
    def specs(blocks, pairs, tile):
        width = blocks[0].shape[1]
        return [rows_of((tile, width))] * len(blocks) + ([ANY] * 2 if pairs else [])

    @staticmethod
    def scratch(blocks, pairs, steps):
        if not pairs:
            return []
        return [pltpu.VMEM((2, *blocks[0].shape), BF16), pltpu.SemaphoreType.DMA((2, 2 * steps))]

    def attach(self, refs):
        if self.pairs:
            self.came, self.sems = refs
        return self

    def copies(self, step):
        tile = self.blocks[0].shape[0]
        rows = pl.ds(pl.multiple_of(step * tile, tile), tile)
        return [
            to_sibling(self.whole[k].at[rows, :], self.came.at[k, rows, :], self.sems, 2 * step + k)
            for k in range(2)
        ]

    def start(self):
        if self.pairs:
            for step in range(self.steps):
                for one in self.copies(step):
                    one.start()

    def refs(self):
        if not self.pairs:
            return self.blocks
        step = pl.program_id(0)
        tile = self.blocks[0].shape[0]
        for one in self.copies(step):
            one.wait()
        rows = pl.ds(pl.multiple_of(step * tile, tile), tile)
        return [self.blocks[0], self.came.at[0, rows, :], self.blocks[1], self.came.at[1, rows, :]]


class Scattered:
    def __init__(self, pairs, n, steps, with_sums):
        self.pairs, self.n, self.steps, self.with_sums = pairs, n, steps, with_sums

    def outs(self, length, width):
        tile = length // self.steps
        if self.pairs:
            outs = [shape((length, width), BF16), sent((length, width), BF16)]
            specs = [fixed((length, width))] * 2
            if self.with_sums:
                outs, specs = outs + [sent((8, length), F32)], specs + [fixed((8, length))]
            return outs, specs
        outs, specs = [shape((length, width), BF16)] * self.n, [rows_of((tile, width))] * self.n
        if self.with_sums:
            outs, specs = outs + [shape((8, length), F32)], specs + [cols_of((8, tile))]
        return outs, specs

    def count(self):
        return (2 if self.pairs else self.n) + self.with_sums

    def scratch(self, length, width):
        if not self.pairs:
            return []
        tile = length // self.steps
        block = pltpu.VMEM((self.steps, 2, tile, width), BF16)
        made = [block, block, pltpu.VMEM((2, 2, tile, width), F32)]
        if self.with_sums:
            made += [pltpu.VMEM((self.steps, 8, tile), F32)] * 3
        return made + [pltpu.SemaphoreType.DMA((2, 3 * self.steps))]

    def attach(self, outs, scratch):
        self.out = outs
        if self.pairs:
            self.send, self.came, self.kept = scratch[:3]
            self.sums = scratch[3:-1]
            self.sems = scratch[-1]
        return self

    def copies(self, step):
        made = [
            to_sibling(self.send.at[step, k], self.came.at[step, k], self.sems, 3 * step + k)
            for k in range(2)
        ]
        if self.with_sums:
            made.append(to_sibling(self.sums[0].at[step], self.sums[1].at[step], self.sems, 3 * step + 2))
        return made

    def put(self, j, value):
        step = pl.program_id(0)
        if not self.pairs:
            self.out[j][...] = value.astype(BF16)
        elif j % 2:
            self.send[step, j // 2] = value.astype(BF16)
        else:
            self.kept[step % 2, j // 2] = value

    def take(self, step):
        tile = self.kept.shape[2]
        for one in self.copies(step):
            one.wait()
        rows = pl.ds(pl.multiple_of(step * tile, tile), tile)
        for k in range(2):
            total = self.kept[step % 2, k] + self.came[step, k].astype(F32)
            self.out[k][rows, :] = total.astype(BF16)
        if self.with_sums:
            self.out[2][:, rows] = self.sums[2][step] + self.sums[1][step]

    def finish(self, sums=None):
        if not self.pairs:
            if sums is not None:
                self.out[-1][...] = sums
            return
        step = pl.program_id(0)
        if sums is not None:
            self.sums[0][step] = sums
            self.sums[2][step] = sums
        for one in self.copies(step):
            one.start()

        @pl.when(step > 0)
        def _():
            self.take(step - 1)

        @pl.when(step == self.steps - 1)
        def _():
            self.take(step)


def with_weights(copies, work, remote=False, gathered=()):
    @pl.when(pl.program_id(0) == 0)
    def _():
        for one in copies:
            one.start()
        if remote:
            greet()
        for one in gathered:
            one.start()

        def wait(some):
            for one in some:
                one.wait()

        work(wait)

    @pl.when(pl.program_id(0) != 0)
    def _():
        work(lambda some: None)


def row_blocks(me, n, width, source, target, sems, base):
    return [
        pltpu.make_async_copy(
            source.at[place_of(me, j, width), :],
            target.at[pl.ds(j * width, width), :],
            sems.at[base + j],
        )
        for j in range(n)
    ]


def col_blocks(me, n, width, source, target, sems, base):
    return [
        pltpu.make_async_copy(
            source.at[:, place_of(me, j, width)],
            target.at[:, pl.ds(j * width, width)],
            sems.at[base + j],
        )
        for j in range(n)
    ]


def stat_columns(first, second):
    lane = lax.broadcasted_iota(jnp.int32, (first.shape[0], 128), 1)
    return jnp.where(lane == 0, first, jnp.where(lane == 1, second, 0.0))


def fold_rows(values):
    return jnp.sum(values.reshape(values.shape[0] // 8, 8, values.shape[1]), 0)


def accumulate(ref, value):
    @pl.when(pl.program_id(0) == 0)
    def _():
        ref[...] = value

    @pl.when(pl.program_id(0) != 0)
    def _():
        ref[...] += value


def average_body(weights, history, wide, low):
    chunk = min(32, wide.shape[0])
    for t in range(wide.shape[0] // chunk):
        rows = slice(t * chunk, (t + 1) * chunk)
        total = weights[0] * history[0, rows, :].astype(F32)
        for j in range(1, history.shape[0]):
            total += weights[j] * history[j, rows, :].astype(F32)
        wide[rows, :] = total
        low[rows, :] = total.astype(BF16)


def average(weights, history, row, length):
    count, _, width = history.shape
    tile = min(256, length)
    steps = length // tile
    return call(
        "average",
        average_body,
        (steps,),
        (weights, history),
        [SMEM, pl.BlockSpec((count, tile, width), lambda i: (0, row * steps + i, 0))],
        [shape((length, width), F32), sent((length, width), BF16)],
        [rows_of((tile, width))] * 2,
    )


def project_body(n, pairs, steps, *refs):
    count = 4 if pairs else n
    x = Gathered(refs[:count], pairs, steps)
    gain, bias, cosine, sine, weight, qkv, normed, stat = refs[count : count + 8]
    refs = refs[count + 8 :]
    shared = refs[:2] if pairs else ()
    held, joined, sems, *more = refs[len(shared) :]
    x.attach(more)
    me = lax.axis_index("mp")
    tile, width = x.blocks[0].shape
    full = n * width
    heads = held.shape[1] // (3 * HEAD)
    sub = min(256, tile)
    copies = row_blocks(me, n, width, weight, held, sems, 0)

    def work(wait):
        xs = x.refs()
        for out, k in zip(shared, (1, 3)):
            out[...] = xs[k][...]
        for t in range(tile // sub):
            rows = slice(t * sub, (t + 1) * sub)
            total = square = 0.0
            for one in xs:
                value = one[rows, :].astype(F32)
                total += jnp.sum(value, 1, keepdims=True)
                square += jnp.sum(value * value, 1, keepdims=True)
            mean = total / full
            inv = lax.rsqrt(square / full - mean * mean + EPSILON)
            stat[rows, :] = stat_columns(mean, inv)
            for j, one in enumerate(xs):
                part = slice(j * width, (j + 1) * width)
                value = (one[rows, :].astype(F32) - mean) * inv * gain[0:1, part] + bias[0:1, part]
                joined[rows, part] = value.astype(BF16)
                normed[rows, place_of(me, j, width)] = value.astype(BF16)
            if t == 0:
                wait(copies)
            for h in range(heads):
                base = 3 * h * HEAD
                out = dot_nn(joined[rows, :], held[:, base : base + 3 * HEAD])
                for s in range(2):
                    v = out[:, s * HEAD : (s + 1) * HEAD]
                    turned = v * cosine[rows, :] + pltpu.roll(v, HEAD // 2, 1) * sine[rows, :]
                    qkv[rows, base + s * HEAD : base + (s + 1) * HEAD] = turned.astype(BF16)
                qkv[rows, base + 2 * HEAD : base + 3 * HEAD] = out[:, 2 * HEAD :].astype(BF16)

    with_weights(copies, work, pairs, [x])


def project(n, pairs, xs, gain, bias, tables, weight):
    length, width = xs[0].shape
    full, out = weight.shape
    tile = min(512, length)
    steps = length // tile
    got = call(
        "project",
        lambda *refs: project_body(n, pairs, steps, *refs),
        (steps,),
        (*xs, *(xs if pairs else ()), gain, bias, *tables, weight),
        Gathered.specs(xs, pairs, tile)
        + [fixed((8, full))] * 2
        + [rows_of((tile, HEAD))] * 2
        + [ANY],
        [shape((length, out), BF16), shape((length, full), BF16), shape((length, 128), F32)]
        + [shape((length, width), BF16)] * (2 * pairs),
        [rows_of((tile, out)), rows_of((tile, full)), rows_of((tile, 128))]
        + [rows_of((tile, width))] * (2 * pairs),
        scratch=[
            pltpu.VMEM((full, out), BF16),
            pltpu.VMEM((tile, full), BF16),
            pltpu.SemaphoreType.DMA((n,)),
        ]
        + Gathered.scratch(xs, pairs, steps),
        remote=pairs,
    )
    return *got[:3], [xs[0], got[3], xs[1], got[4]] if pairs else xs


def windows(length):
    block = min(256, length)
    for i in range(length // block):
        low = max(0, i * block - (MAX_DOC - 1)) // block * block
        yield slice(i * block, (i + 1) * block), slice(low, (i + 1) * block)


def score_mask(start, q_part, k_part):
    dims = (k_part.stop - k_part.start, q_part.stop - q_part.start)
    k_pos = lax.broadcasted_iota(jnp.int32, dims, 0) + k_part.start
    q_pos = lax.broadcasted_iota(jnp.int32, dims, 1) + q_part.start
    return (k_pos >= start[0:1, q_part]) & (k_pos <= q_pos)


def attend_body(start, qkv, out, logs):
    length = qkv.shape[0]
    value_t = qkv[:, 2 * HEAD :].T
    for q_part, k_part in windows(length):
        query, key = qkv[q_part, :HEAD], qkv[k_part, HEAD : 2 * HEAD]
        scores = dot_nt(key, query) * (SCALE * LOG2E)
        scores = jnp.where(score_mask(start, q_part, k_part), scores, -1e30)
        top = jnp.max(scores, 0, keepdims=True)
        probs = jnp.exp2(scores - top)
        total = jnp.sum(probs, 0, keepdims=True)
        logs[0, :, q_part] = jnp.broadcast_to(top + jnp.log2(total), (8, q_part.stop - q_part.start))
        got = dot_nn(value_t[:, k_part], probs.astype(BF16)) / total
        out[q_part, :] = got.T.astype(BF16)


def attend(start, qkv):
    length, width = qkv.shape
    heads = width // (3 * HEAD)
    return call(
        "attend",
        attend_body,
        (heads,),
        (start, qkv),
        [fixed((8, length)), cols_of((length, 3 * HEAD))],
        [sent((length, heads * HEAD), BF16), shape((heads, 8, length), F32)],
        [cols_of((length, HEAD)), pl.BlockSpec((1, 8, length), lambda i: (i, 0, 0))],
    )


def attend_back_body(start, cosine, sine, qkv, grad, logs, out, key_sum, value_sum):
    length = qkv.shape[0]
    key_t = qkv[:, HEAD : 2 * HEAD].T
    key_sum[...] = jnp.zeros_like(key_sum)
    value_sum[...] = jnp.zeros_like(value_sum)

    def turn_back(v, part):
        return (
            v * cosine[part, :] - pltpu.roll(v, HEAD // 2, 1) * sine[part, :]
        ).astype(BF16)

    for q_part, k_part in windows(length):
        query, key = qkv[q_part, :HEAD], qkv[k_part, HEAD : 2 * HEAD]
        value, g = qkv[k_part, 2 * HEAD :], grad[q_part, :]
        scores = dot_nt(key, query) * (SCALE * LOG2E) - logs[0, 0:1, q_part]
        probs = jnp.exp2(jnp.where(score_mask(start, q_part, k_part), scores, -1e30))
        prob_grad = dot_nt(value, g)
        mean = jnp.sum(prob_grad * probs, 0, keepdims=True)
        score_grad = (probs * (prob_grad - mean)).astype(BF16)
        value_sum[k_part, :] += dot_nn(probs.astype(BF16), g)
        key_sum[k_part, :] += dot_nn(score_grad, query)
        query_grad = dot_nn(key_t[:, k_part], score_grad) * SCALE
        out[q_part, :HEAD] = turn_back(query_grad.T, q_part)
    for q_part, _ in windows(length):
        out[q_part, HEAD : 2 * HEAD] = turn_back(key_sum[q_part, :] * SCALE, q_part)
        out[q_part, 2 * HEAD :] = value_sum[q_part, :].astype(BF16)


def attend_back(start, tables, qkv, grad, logs):
    length, width = qkv.shape
    heads = width // (3 * HEAD)
    return call(
        "attend_back",
        attend_back_body,
        (heads,),
        (start, *tables, qkv, grad, logs),
        [fixed((8, length))]
        + [fixed((length, HEAD))] * 2
        + [
            cols_of((length, 3 * HEAD)),
            cols_of((length, HEAD)),
            pl.BlockSpec((1, 8, length), lambda i: (i, 0, 0)),
        ],
        [shape((length, width), BF16)],
        [cols_of((length, 3 * HEAD))],
        scratch=[pltpu.VMEM((length, HEAD), F32)] * 2,
    )[0]


def feed_body(n, pairs, steps, *refs):
    count = 4 if pairs else n
    attended = Gathered(refs[:count], pairs, steps)
    refs = refs[count:]
    xs, outs_w = refs[: n - 1], refs[n - 1 : 2 * n - 1]
    own, gain, bias, up_bias, up_weight, down_weight = refs[2 * n - 1 : 2 * n + 5]
    refs = refs[2 * n + 5 :]
    hidden, normed, stat, activated, slope = refs[:5]
    refs = refs[5:]
    parts = Scattered(pairs, n, steps, False)
    part_outs, refs = refs[: parts.count()], refs[parts.count() :]
    out_held, up_held, down_held, joined, whole, sems, *refs = refs
    if pairs:
        attended.attach(refs[:2])
        refs = refs[2:]
    parts.attach(part_outs, refs)
    me = lax.axis_index("mp")
    width = own.shape[1]
    full = n * width
    inner = up_held.shape[1]
    out_copies = []
    for j in range(n):
        for k in range(n):
            out_copies.append(
                pltpu.make_async_copy(
                    outs_w[k].at[:, place_of(me, j, width)],
                    out_held.at[pl.ds(k * width, width), pl.ds(j * width, width)],
                    sems.at[j * n + k],
                )
            )
    up_copies = row_blocks(me, n, width, up_weight, up_held, sems, n * n)
    down_copies = col_blocks(me, n, width, down_weight, down_held, sems, n * n + n)

    def work(wait):
        for j, one in enumerate(attended.refs()):
            joined[:, j * width : (j + 1) * width] = one[...]
        total = square = 0.0
        for j in range(n):
            wait(out_copies[j * n : (j + 1) * n])
            part = slice(j * width, (j + 1) * width)
            base = own[...] if j == 0 else xs[j - 1][...].astype(F32)
            value = base + dot_nn(joined[...], out_held[:, part])
            whole[:, part] = value
            if j == 0:
                hidden[...] = value
            total += jnp.sum(value, 1, keepdims=True)
            square += jnp.sum(value * value, 1, keepdims=True)
        mean = total / full
        inv = lax.rsqrt(square / full - mean * mean + EPSILON)
        stat[...] = stat_columns(mean, inv)
        for j in range(n):
            part = slice(j * width, (j + 1) * width)
            value = ((whole[:, part] - mean) * inv * gain[0:1, part] + bias[0:1, part]).astype(BF16)
            joined[:, part] = value
            normed[:, place_of(me, j, width)] = value
        wait(up_copies)
        step = divisor(inner, 512)
        for c in range(inner // step):
            part = slice(c * step, (c + 1) * step)
            up = dot_nn(joined[...], up_held[:, part]) + up_bias[0:1, part]
            half = 0.5 * (1.0 + lax.erf(up * SQRT_HALF))
            activated[:, part] = (up * half).astype(BF16)
            slope[:, part] = (half + up * INV_ROOT_TWO_PI * jnp.exp(-0.5 * up * up)).astype(BF16)
        wait(down_copies)
        for j in range(n):
            parts.put(j, dot_nn(activated[...], down_held[:, j * width : (j + 1) * width]))

    with_weights(out_copies + up_copies + down_copies, work, pairs, [attended])
    parts.finish()


def feed(n, pairs, attended, xs, outs_w, own, gain, bias, up_bias, up_weight, down_weight):
    length, width = own.shape
    full, inner = up_weight.shape
    tile = min(256, length)
    steps = length // tile
    parts = Scattered(pairs, n, steps, False)
    part_outs, part_specs = parts.outs(length, width)
    twice = tuple(attended) if pairs else ()
    got = call(
        "feed",
        lambda *refs: feed_body(n, pairs, steps, *refs),
        (steps,),
        (
            *attended,
            *twice,
            *xs[1:],
            *outs_w,
            own,
            gain,
            bias,
            up_bias,
            up_weight,
            down_weight,
        ),
        Gathered.specs(attended, pairs, tile)
        + [rows_of((tile, width))] * (n - 1)
        + [ANY] * n
        + [rows_of((tile, width))]
        + [fixed((8, full))] * 2
        + [fixed((8, inner))]
        + [ANY] * 2,
        [
            shape((length, width), F32),
            shape((length, full), BF16),
            shape((length, 128), F32),
            shape((length, inner), BF16),
            shape((length, inner), BF16),
        ]
        + part_outs,
        [
            rows_of((tile, width)),
            rows_of((tile, full)),
            rows_of((tile, 128)),
            rows_of((tile, inner)),
            rows_of((tile, inner)),
        ]
        + part_specs,
        scratch=[
            pltpu.VMEM((full, full), BF16),
            pltpu.VMEM((full, inner), BF16),
            pltpu.VMEM((inner, full), BF16),
            pltpu.VMEM((tile, full), BF16),
            pltpu.VMEM((tile, full), F32),
            pltpu.SemaphoreType.DMA((n * n + 2 * n,)),
        ]
        + Gathered.scratch(attended, pairs, steps)
        + parts.scratch(length, width),
        remote=pairs,
    )
    return (*got[:5], got[5:])


def row_stats(total, weighted):
    return stat_columns(total, weighted).T[0:8, :]


def norm_sums(parts, n, product, normed, gain, bias, me):
    width = gain.shape[1] // n
    total = weighted = 0.0
    for j in range(n):
        part = slice(j * width, (j + 1) * width)
        value = product(j)
        parts.put(j, value)
        total += jnp.sum(value * gain[0:1, part], 1, keepdims=True)
        there = normed[:, place_of(me, j, width)].astype(F32)
        weighted += jnp.sum(value * (there - bias[0:1, part]), 1, keepdims=True)
    return row_stats(total, weighted)


def feed_back_body(n, pairs, steps, held_in, passed, *refs):
    count = n if held_in or not pairs else 4
    cots, refs = Gathered(refs[:count], pairs and not held_in, steps), refs[count:]
    others = []
    for _ in range(passed):
        others.append(Gathered(refs[:4], pairs, steps))
        refs = refs[4:]
    slope, normed, gain, bias, up_weight, down_weight, up_grad, up_bias_sum, cot_sum = refs[:9]
    refs = refs[9:]
    parts = Scattered(pairs, n, steps, True)
    part_outs, refs = refs[: parts.count()], refs[parts.count() :]
    fetched = ([] if held_in or not pairs else [cots]) + others
    shared, refs = refs[: 2 * len(fetched)], refs[2 * len(fetched) :]
    up_held, down_held, joined, row_sums, sems, *refs = refs
    for one in fetched:
        one.attach(refs[:2])
        refs = refs[2:]
    parts.attach(part_outs, refs)
    me = lax.axis_index("mp")
    inner = up_held.shape[1]
    width = gain.shape[1] // n
    step = divisor(inner, 512)
    down_copies = col_blocks(me, n, width, down_weight, down_held, sems, n)
    up_copies = row_blocks(me, n, width, up_weight, up_held, sems, 0)

    def work(wait):
        blocks = cots.refs()
        for j, block in enumerate(blocks):
            joined[:, j * width : (j + 1) * width] = block[...]
        for i, one in enumerate(fetched):
            there = blocks if one is cots else one.refs()
            shared[2 * i][...] = there[1][...]
            shared[2 * i + 1][...] = there[3][...]
        accumulate(cot_sum, fold_rows(blocks[0][...].astype(F32)))
        wait(down_copies)
        bias_parts = []
        for c in range(inner // step):
            part = slice(c * step, (c + 1) * step)
            value = dot_nt(joined[...], down_held[part, :]) * slope[:, part].astype(F32)
            low = value.astype(BF16)
            up_grad[:, part] = low
            bias_parts.append(fold_rows(low.astype(F32)))
        accumulate(up_bias_sum, jnp.concatenate(bias_parts, 1))
        wait(up_copies)
        row_sums[...] = norm_sums(
            parts,
            n,
            lambda j: dot_nt(up_grad[...], up_held[j * width : (j + 1) * width, :]),
            normed,
            gain,
            bias,
            me,
        )

    with_weights(down_copies + up_copies, work, pairs, fetched)
    parts.finish(row_sums[...])


def feed_back(n, pairs, cots, others, slope, normed, gain, bias, up_weight, down_weight):
    length, full = normed.shape
    width = full // n
    inner = up_weight.shape[1]
    tile = min(256, length)
    steps = length // tile
    held_in = pairs and len(cots) == n
    others = others if pairs else []
    fetch = ([] if held_in or not pairs else [cots]) + others
    parts = Scattered(pairs, n, steps, True)
    part_outs, part_specs = parts.outs(length, width)
    args = [*cots, *(cots if pairs and not held_in else ())]
    specs = Gathered.specs(cots, pairs and not held_in, tile)
    for one in others:
        args += [*one, *one]
        specs += Gathered.specs(one, pairs, tile)
    got = call(
        "feed_back",
        lambda *refs: feed_back_body(n, pairs, steps, held_in, len(others), *refs),
        (steps,),
        (*args, slope, normed, gain, bias, up_weight, down_weight),
        specs
        + [rows_of((tile, inner)), rows_of((tile, full))]
        + [fixed((8, full))] * 2
        + [ANY] * 2,
        [shape((length, inner), BF16), shape((8, inner), F32), shape((8, width), F32)]
        + part_outs
        + [shape((length, width), BF16)] * (2 * len(fetch)),
        [rows_of((tile, inner)), fixed((8, inner)), fixed((8, width))]
        + part_specs
        + [rows_of((tile, width))] * (2 * len(fetch)),
        scratch=[
            pltpu.VMEM((full, inner), BF16),
            pltpu.VMEM((inner, full), BF16),
            pltpu.VMEM((tile, full), BF16),
            pltpu.VMEM((8, tile), F32),
            pltpu.SemaphoreType.DMA((2 * n,)),
        ]
        + sum([Gathered.scratch(one, pairs, steps) for one in fetch], [])
        + parts.scratch(length, width),
        remote=pairs,
    )
    got, shared = got[: 3 + parts.count()], got[3 + parts.count() :]
    blocks = [
        [one[0], shared[2 * i], one[1], shared[2 * i + 1]] for i, one in enumerate(fetch)
    ]
    return (*got[:3], got[3:], blocks)


def norm_back(refs, n_parts, source, stat, sums, gain, full):
    grad = refs[0][...].astype(F32)
    for ref in refs[1:n_parts]:
        grad += ref[...].astype(F32)
    columns = sum(one[...] for one in sums).T
    mean, inv = stat[:, 0:1], stat[:, 1:2]
    scaled = (source[...] - mean) * inv
    back = inv * (
        grad * gain[0:1, :] - columns[:, 0:1] * (1.0 / full) - scaled * (columns[:, 1:2] * (1.0 / full))
    )
    return back, fold_rows(grad * scaled), fold_rows(grad)


def hidden_back_body(k, m, full, *refs):
    parts, sums = refs[:k], refs[k : k + m]
    cot, hidden, stat, gain, wide, low, gain_sum, bias_sum = refs[k + m :]
    back, gain_part, bias_part = norm_back(parts, k, hidden, stat, sums, gain, full)
    value = cot[...].astype(F32) + back
    wide[...] = value
    low[...] = value.astype(BF16)
    accumulate(gain_sum, gain_part)
    accumulate(bias_sum, bias_part)


def hidden_back(parts, cotangent, row, hidden, stat, sums, gain, full):
    k, m, (length, width) = len(parts), len(sums), hidden.shape
    tile = min(256, length)
    steps = length // tile
    return call(
        "hidden_back",
        lambda *refs: hidden_back_body(k, m, full, *refs),
        (steps,),
        (*parts, *sums, cotangent, hidden, stat, gain),
        [rows_of((tile, width))] * k
        + [cols_of((8, tile))] * m
        + [
            pl.BlockSpec((tile, width), lambda i: (row * steps + i, 0)),
            rows_of((tile, width)),
            rows_of((tile, 128)),
            fixed((8, width)),
        ],
        [shape((length, width), F32), sent((length, width), BF16)] + [shape((8, width), F32)] * 2,
        [rows_of((tile, width))] * 2 + [fixed((8, width))] * 2,
    )


def attended_back_body(n, pairs, steps, *refs):
    count = 4 if pairs else n
    grads = Gathered(refs[:count], pairs, steps)
    weight, joined, out, *more = refs[count:]
    grads.attach(more)
    me = lax.axis_index("mp")
    width = grads.blocks[0].shape[1]

    def work(wait):
        for j, one in enumerate(grads.refs()):
            joined[:, place_of(me, j, width)] = one[...]
        out[...] = dot_nt(joined[...], weight[...]).astype(BF16)

    with_weights([], work, pairs, [grads])


def attended_back(n, pairs, grads, weight):
    length, width = grads[0].shape
    rows, full = weight.shape
    tile = min(256, length)
    steps = length // tile
    return call(
        "attended_back",
        lambda *refs: attended_back_body(n, pairs, steps, *refs),
        (steps,),
        (*grads, *(grads if pairs else ()), weight),
        Gathered.specs(grads, pairs, tile) + [fixed((rows, full))],
        [shape((length, full), BF16), shape((length, rows), BF16)],
        [rows_of((tile, full)), rows_of((tile, rows))],
        scratch=Gathered.scratch(grads, pairs, steps),
        remote=pairs,
    )


def project_back_body(n, pairs, steps, grad, normed, gain, bias, weight, *refs):
    parts = Scattered(pairs, n, steps, True)
    part_outs, refs = refs[: parts.count()], refs[parts.count() :]
    held, row_sums, sems, *refs = refs
    parts.attach(part_outs, refs)
    me = lax.axis_index("mp")
    width = gain.shape[1] // n
    copies = row_blocks(me, n, width, weight, held, sems, 0)

    def work(wait):
        def product(j):
            wait(copies[j : j + 1])
            return dot_nt(grad[...], held[j * width : (j + 1) * width, :])

        row_sums[...] = norm_sums(parts, n, product, normed, gain, bias, me)

    with_weights(copies, work, pairs)
    parts.finish(row_sums[...])


def project_back(n, pairs, grad, normed, gain, bias, weight):
    length, out = grad.shape
    full = weight.shape[0]
    width = full // n
    tile = min(256, length)
    steps = length // tile
    parts = Scattered(pairs, n, steps, True)
    part_outs, part_specs = parts.outs(length, width)
    return call(
        "project_back",
        lambda *refs: project_back_body(n, pairs, steps, *refs),
        (steps,),
        (grad, normed, gain, bias, weight),
        [rows_of((tile, out)), rows_of((tile, full))] + [fixed((8, full))] * 2 + [ANY],
        part_outs,
        part_specs,
        scratch=[
            pltpu.VMEM((full, out), BF16),
            pltpu.VMEM((8, tile), F32),
            pltpu.SemaphoreType.DMA((n,)),
        ]
        + parts.scratch(length, width),
        remote=pairs,
    )


def average_back_body(k, m, full, count, *refs):
    weights, parts, sums = refs[0], refs[1 : k + 1], refs[k + 1 : k + m + 1]
    source, stat, gain, hidden_grad, history = refs[k + m + 1 : k + m + 6]
    grad_history, depth_sum, gain_sum, bias_sum, held = refs[-5:]
    back, gain_part, bias_part = norm_back(parts, k, source, stat, sums, gain, full)
    held[...] = hidden_grad[...] + back
    accumulate(gain_sum, gain_part)
    accumulate(bias_sum, bias_part)
    lanes = held.shape[1] // 128
    chunk = min(32, held.shape[0])
    folded = [0.0] * count
    for t in range(held.shape[0] // chunk):
        rows = slice(t * chunk, (t + 1) * chunk)
        value = held[rows, :]
        for j in range(count):
            grad_history[j, rows, :] = (weights[j] * value).astype(BF16)
            product = fold_rows(value * history[j, rows, :].astype(F32))
            for c in range(lanes):
                folded[j] = folded[j] + product[:, c * 128 : (c + 1) * 128]
    for j in range(count):
        accumulate(depth_sum.at[j], folded[j])


def average_back(weights, parts, source, stat, sums, gain, hidden_grad, history, row, made):
    k, m, (length, width) = len(parts), len(sums), source.shape
    count = history.shape[0]
    tile = min(256, length)
    steps = length // tile
    full = gain[1]
    block = pl.BlockSpec((count, tile, width), lambda i: (0, row * steps + i, 0))
    args = (weights, *parts, *sums, source, stat, gain[0], hidden_grad, history)
    specs = (
        [SMEM]
        + [rows_of((tile, width))] * k
        + [cols_of((8, tile))] * m
        + [rows_of((tile, width)), rows_of((tile, 128)), fixed((8, width)), rows_of((tile, width)), block]
    )
    more = {}
    if made is not None:
        more = {"aliases": {len(args): 0}}
        args, specs = (*args, made), specs + [ANY]
    return call(
        "average_back",
        lambda *refs: average_back_body(k, m, full, count, *refs),
        (steps,),
        args,
        specs,
        [shape(history.shape, BF16), shape((count, 8, 128), F32)] + [shape((8, width), F32)] * 2,
        [block, fixed((count, 8, 128))] + [fixed((8, width))] * 2,
        scratch=[pltpu.VMEM((tile, width), F32)],
        **more,
    )


def divisor(size, most):
    return max(d for d in range(128, most + 1, 128) if size % d == 0) if size > 128 else size


def weight_body(rows, *refs):
    out = refs[-1]
    total = dot_tn(refs[0][...], refs[rows][...])
    for r in range(1, rows):
        total += dot_tn(refs[r][...], refs[rows + r][...])
    out[...] = total.astype(BF16)


def weight_grad(lefts, rights):
    rows, (length, high), wide = len(lefts), lefts[0].shape, rights[0].shape[1]
    tall, across = divisor(high, 1024), divisor(wide, 1024)
    return call(
        "weight_grad",
        lambda *refs: weight_body(rows, *refs),
        (high // tall, wide // across),
        (*lefts, *rights),
        [pl.BlockSpec((length, tall), lambda i, j: (0, i))] * rows
        + [pl.BlockSpec((length, across), lambda i, j: (0, j))] * rows,
        [shape((high, wide), BF16)],
        [pl.BlockSpec((tall, across), lambda i, j: (i, j))],
    )[0]


def weight_of_blocks_body(rows, n, me, *refs):
    lefts, rights, out = refs[:rows], refs[rows:-1], refs[-1]
    width = rights[0].shape[1]
    turned = [left[...].T for left in lefts]
    for j in range(n):
        total = 0.0
        for r in range(rows):
            total += dot_nn(turned[r], rights[r * n + j][...])
        out[:, place_of(me[0], j, width)] = total.astype(BF16)


def weight_of_blocks(me, lefts, rights):
    rows, n, (length, high) = len(lefts), len(rights[0]), lefts[0].shape
    width = rights[0][0].shape[1]
    tall = divisor(high, 512)
    return call(
        "weight_grad",
        lambda *refs: weight_of_blocks_body(rows, n, *refs),
        (high // tall,),
        (me, *lefts, *sum(rights, [])),
        [SMEM]
        + [pl.BlockSpec((length, tall), lambda i: (0, i))] * rows
        + [fixed((length, width))] * (rows * n),
        [shape((high, n * width), BF16)],
        [rows_of((tall, n * width))],
    )[0]


def put_blocks(came, outs, k, value):
    if came is not None:
        value = value + came[k].astype(F32)
    per = outs[0].shape[0]
    outs[k // per][k % per] = value.astype(BF16)


def tall_blocks_body(rows, count, fused, group, *refs):
    lefts, rights = refs[: rows * count], refs[rows * count : rows * count + rows]
    refs = refs[rows * count + rows :]
    came, outs, turned = refs[0] if fused else None, refs[fused:-1], refs[-1]
    length, high = lefts[0].shape

    @pl.when(pl.program_id(0) == 0)
    def _():
        for k in range(count):
            for r in range(rows):
                turned[k * high : (k + 1) * high, r * length : (r + 1) * length] = lefts[
                    k * rows + r
                ][...].T

    for k in range(count):
        total = 0.0
        for r in range(rows):
            total += dot_nn(
                turned[k * high : (k + 1) * high, r * length : (r + 1) * length], rights[r][...]
            )
        put_blocks(came, outs, k, total)


def wide_blocks_body(rows, count, fused, group, *refs):
    lefts, rights = refs[:rows], refs[rows : rows + rows * count]
    refs = refs[rows + rows * count :]
    came, outs = refs[0] if fused else None, refs[fused:]
    turned = [left[...].T for left in lefts]
    for k in range(count):
        total = 0.0
        for r in range(rows):
            total += dot_nn(turned[r], rights[k * rows + r][...])
        put_blocks(came, outs, k, total)


class Spread:
    def __init__(self, lefts, rights, dim, bits, part=(0, 1)):
        self.lefts, self.rights, self.dim, self.bits, self.part = lefts, rights, dim, list(bits), part
        self.groups = lax.axis_size("dp")
        self.block = (lefts, rights)[dim][0].shape[1] // self.groups
        order = [0]
        for bit in reversed(self.bits):
            order = order + [e | bit for e in order]
        self.order = order

    def blocks(self, half, came=None):
        count = self.groups // 2
        which = self.order[half * count : (half + 1) * count]
        rows, length = len(self.lefts), self.lefts[0].shape[0]
        group = lax.axis_index("dp").astype(jnp.int32)[None]
        size, (index, pieces) = self.block, self.part
        stay = [
            pl.BlockSpec((length, size), lambda i, group, e=e: (0, group[0] ^ e))
            for e in which
            for _ in range(rows)
        ]
        other = self.rights if self.dim == 0 else self.lefts
        extent = other[0].shape[1] // pieces
        tile = divisor(extent, 512)
        steps = extent // tile
        move = [pl.BlockSpec((length, tile), lambda i, group: (0, index * steps + i))] * rows

        def blocked(number):
            if self.dim == 0:
                return (
                    sent((number, size, extent), BF16),
                    pl.BlockSpec((number, size, tile), lambda i, group: (0, 0, i)),
                )
            return (
                sent((number, extent, size), BF16),
                pl.BlockSpec((number, tile, size), lambda i, group: (0, i, 0)),
            )

        if self.dim == 0:
            args = (*(list(self.lefts) * count), *self.rights)
            specs = stay + move
            body, scratch = tall_blocks_body, [pltpu.VMEM((count * size, rows * length), BF16)]
        else:
            args = (*self.lefts, *(list(self.rights) * count))
            specs = move + stay
            body, scratch = wide_blocks_body, []
        outs = [blocked(count)]
        if came is not None:
            args, specs = (*args, came), specs + [blocked(count)[1]]
            outs = [blocked(count // 2)] * 2
        return call(
            "weight_blocks",
            lambda *refs: body(rows, count, came is not None, *refs),
            (steps,),
            (group, *args),
            specs,
            [one[0] for one in outs],
            [one[1] for one in outs],
            scratch=scratch,
            prefetch=1,
        )

    def send(self, value):
        bit = self.bits[self.step]
        self.step += 1
        self.coming = lax.ppermute(value, "dp", [(i, i ^ bit) for i in range(self.groups)])

    def first(self):
        self.step = 0
        self.send(self.blocks(1)[0])

    def keep(self):
        self.held = self.blocks(0)[0]

    def keep_added(self):
        self.held, out = self.blocks(0, self.coming)
        self.send(out)


def fold_body(count, *refs):
    for i in range(count):
        held, came, keep, send = refs[2 * i], refs[2 * i + 1], refs[2 * count + 2 * i], refs[2 * count + 2 * i + 1]
        half = keep.shape[0]
        keep[...] = (held[:half].astype(F32) + came[:half].astype(F32)).astype(BF16)
        send[...] = (held[half:].astype(F32) + came[half:].astype(F32)).astype(BF16)


def advance(*spreads):
    steps = 4
    args, specs, outs, out_specs = [], [], [], []
    for one in spreads:
        count, high, wide = one.held.shape
        args += [one.held, one.coming]
        specs += [pl.BlockSpec((count, high // steps, wide), lambda i: (0, i, 0))] * 2
        outs += [sent((count // 2, high, wide), BF16)] * 2
        out_specs += [pl.BlockSpec((count // 2, high // steps, wide), lambda i: (0, i, 0))] * 2
    got = call("fold", lambda *refs: fold_body(len(spreads), *refs), (steps,), args, specs, outs, out_specs)
    for i, one in enumerate(spreads):
        one.held = got[2 * i]
        one.send(got[2 * i + 1])


def finish_body(groups, *refs):
    outs = refs[len(refs) - len(groups) :]
    at = 0
    for out, group in zip(outs, groups):
        for first, wide, count in group:
            total = refs[at][0].astype(F32)
            for ref in refs[at + 1 : at + count]:
                total += ref[0].astype(F32)
            out[:, first : first + wide] = total
            at += count


def finish(*groups):
    steps = 4
    args, specs, outs, out_specs, places = [], [], [], [], []
    for group in groups:
        first, place = 0, []
        for one in group:
            terms = [one.held, one.coming] if isinstance(one, Spread) else [one[None]]
            _, high, wide = terms[0].shape
            args += terms
            specs += [pl.BlockSpec((1, high // steps, wide), lambda i: (0, i, 0))] * len(terms)
            place.append((first, wide, len(terms)))
            first += wide
        outs.append(shape((high, first), F32))
        out_specs.append(rows_of((high // steps, first)))
        places.append(place)
    return call("finish", lambda *refs: finish_body(places, *refs), (steps,), args, specs, outs, out_specs)


def sums_body(groups, n, own, out, total, came, far, dp_sems, mp_sems):
    me = {"dp": lax.axis_index("dp"), "mp": lax.axis_index("mp")}
    peers = [("dp", b) for b in range(1, groups)] + [("mp", b) for b in range(1, n)]
    barrier = pltpu.get_barrier_semaphore()
    for axis, b in peers:
        pl.semaphore_signal(
            barrier, inc=1, device_id={axis: flip(me[axis], b)}, device_id_type=pl.DeviceIdType.MESH
        )
    pl.semaphore_wait(barrier, len(peers))

    def copy(axis, b, source, target, sems):
        return pltpu.make_async_remote_copy(
            src_ref=source,
            dst_ref=target.at[b - 1],
            send_sem=sems.at[0, b - 1],
            recv_sem=sems.at[1, b - 1],
            device_id={axis: flip(me[axis], b)},
            device_id_type=pl.DeviceIdType.MESH,
        )

    copies = [copy("dp", b, own, came, dp_sems) for b in range(1, groups)]
    for one in copies:
        one.start()
    for one in copies:
        one.wait()
    value = own[...]
    for b in range(groups - 1):
        value = value + came[b]
    out[...] = value
    total[...] = value[-8:]
    copies = [copy("mp", b, total, far, mp_sems) for b in range(1, n)]
    for one in copies:
        one.start()
    for one in copies:
        one.wait()
    value = total[...]
    for b in range(n - 1):
        value = value + far[b]
    out[-8:, :] = value


def sums(vectors, depth):
    groups, n = lax.axis_size("dp"), lax.axis_size("mp")
    sizes = [v.size for v in vectors]
    packed = jnp.concatenate(vectors)
    packed = jnp.pad(packed, (0, -packed.size % 1024)).reshape(-1, 128)
    packed = jnp.concatenate([packed, jnp.pad(depth[None], ((0, 7), (0, 128 - depth.size)))])
    high = packed.shape[0]
    got = call(
        "sums",
        lambda *refs: sums_body(groups, n, *refs),
        (1,),
        (packed,),
        [fixed((high, 128))],
        [shape((high, 128), F32)],
        [fixed((high, 128))],
        scratch=[
            pltpu.VMEM((8, 128), F32),
            pltpu.VMEM((groups - 1, high, 128), F32),
            pltpu.VMEM((n - 1, 8, 128), F32),
            pltpu.SemaphoreType.DMA((2, groups - 1)),
            pltpu.SemaphoreType.DMA((2, n - 1)),
        ],
        remote=True,
    )[0]
    flat = got.reshape(-1)
    ends = np.cumsum(sizes)
    return [flat[end - size : end] for end, size in zip(ends, sizes)], got[-8, : depth.size]


def output_body(rows, steps, *refs):
    bias, out = refs[-2:]
    per = (len(refs) - 2) // rows
    for r in range(rows):

        @pl.when(pl.program_id(0) // steps == r)
        def _(r=r):
            total = bias[0:1, :]
            for part in refs[r * per + 1 : (r + 1) * per]:
                total = total + part[...].astype(F32)
            out[...] = (refs[r * per][...] + total).astype(BF16)


def output(parts, hidden, bias):
    rows, (length, width) = len(hidden), hidden[0].shape
    tile = min(512, length)
    steps = length // tile
    args, specs = [], []
    for r in range(rows):
        args += [hidden[r], *parts[r]]
        specs += [
            pl.BlockSpec((tile, width), lambda i, r=r: (jnp.clip(i - r * steps, 0, steps - 1), 0))
        ] * (1 + len(parts[r]))
    return call(
        "output",
        lambda *refs: output_body(rows, steps, *refs),
        (rows * steps,),
        (*args, bias),
        specs + [fixed((8, width))],
        [shape((rows * length, width), BF16)],
        [rows_of((tile, width))],
    )[0]


class Ring:
    def __init__(self):
        self.n = lax.axis_size("mp")
        self.me = lax.axis_index("mp").astype(jnp.int32)
        self.pairs = self.n == 4
        self.core = [(i, i ^ 1) for i in range(self.n)]
        self.chip = [(i, i ^ 2) for i in range(self.n)]

    def over_core(self, value):
        return lax.ppermute(value, "mp", self.core)

    def over_chip(self, value):
        return lax.ppermute(value, "mp", self.chip)

    def gather_start(self, block):
        if self.pairs:
            return [block, self.over_chip(block)]
        return self.gather(block)

    def gather(self, block):
        if self.pairs:
            across = self.over_chip(block)
            return [block, self.over_core(block), across, self.over_core(across)]
        every = lax.all_gather(block, "mp")
        return [
            lax.dynamic_index_in_dim(every, self.me ^ j, 0, keepdims=False) for j in range(self.n)
        ]

    def scatter(self, parts, sums=False):
        parts, extra = (parts[:-1], parts[-1:]) if sums else (parts, [])
        if self.pairs:
            return [parts[0], self.over_chip(parts[1])], [*extra, *map(self.over_chip, extra)]
        stacked = jnp.stack([part.astype(F32) for part in parts])
        ordered = jnp.take(stacked, self.me ^ jnp.arange(self.n), axis=0)
        total = lax.psum_scatter(ordered, "mp", scatter_dimension=0, tiled=False)
        return [total], [lax.psum(v, "mp") for v in extra]

    def total(self, value):
        if self.pairs:
            value = value + self.over_core(value)
            return value + self.over_chip(value)
        return lax.psum(value, "mp")

    def out_start(self, weight):
        rows, groups = weight.shape[0], lax.axis_size("dp")
        if self.pairs and rows % (16 * groups) == 0:
            size = rows // groups
            piece = lax.dynamic_slice_in_dim(weight, lax.axis_index("dp") * size, size, 0)
            return self.over_chip(piece)
        return None

    def out_middle(self, piece):
        return None if piece is None else lax.all_gather(piece, "dp", axis=0, tiled=True)

    def out_end(self, weight, across):
        if across is None:
            return self.gather(weight)
        across = gate([across])[0]
        return [weight, self.over_core(weight), across, self.over_core(across)]


def tables_of(length):
    half = HEAD // 2
    rate = np.exp(np.arange(half, dtype=np.float64) * (-math.log(10000.0) / half))
    angle = np.arange(length, dtype=np.float64)[:, None] * rate[None, :]
    cosine, sine = np.cos(angle), np.sin(angle)
    return (
        jnp.asarray(np.concatenate([cosine, cosine], 1), F32),
        jnp.asarray(np.concatenate([-sine, sine], 1), F32),
    )


def local(
    history,
    depth_weights,
    segment_ids,
    first_gain,
    first_bias,
    qkv_weight,
    out_weight,
    second_gain,
    second_bias,
    up_weight,
    up_bias,
    down_weight,
    down_bias,
    cotangent,
):
    ring = Ring()
    n = ring.n
    pairs = ring.pairs
    width = history.shape[2]
    full = n * width
    row_count, length = segment_ids.shape
    rows = range(row_count)
    tables = tables_of(length)
    earlier = (segment_ids[:, None, :] < segment_ids[:, :, None]).astype(jnp.int32)
    starts = jnp.broadcast_to(jnp.sum(earlier, -1)[:, None, :], (row_count, 8, length))

    up_bias8 = jnp.broadcast_to(up_bias[None], (8, up_bias.shape[0]))

    down_bias8 = jnp.broadcast_to(down_bias[None], (8, width))
    groups = lax.axis_size("dp")
    spread = full % (128 * groups) == 0 and groups >= 4
    last = row_count - 1

    Order.last, Order.names, Order.cost = None, 0, 10**12
    vectors = jnp.stack([first_gain, first_bias, second_gain, second_bias])
    vectors = ring.gather_start(jnp.repeat(vectors, 8, 0))
    piece = ring.out_start(out_weight)
    cot_rows = [lax.slice_in_dim(cotangent, r * length, (r + 1) * length) for r in rows]
    none = [None] * row_count
    wide, low, xs, qkv, normed1, stat1 = (list(none) for _ in range(6))
    attended, logs, heads, cots = (list(none) for _ in range(4))
    hidden, normed2, stat2, activated, slope = (list(none) for _ in range(5))
    branch, up_grad, parts2, parts1 = (list(none) for _ in range(4))
    hidden_grad, grads, grad_full, qkv_grad = (list(none) for _ in range(4))
    up_bias_sum = down_bias_sum = gain2_sum = bias2_sum = 0.0

    for r in rows:
        wide[r], low[r] = average(depth_weights, history, r, length)
        if r == 0:
            xs[0] = ring.gather_start(low[0])
            if pairs:
                vectors[1], piece = gate([vectors[1], piece])
                vectors = [
                    vectors[0],
                    ring.over_core(vectors[0]),
                    vectors[1],
                    ring.over_core(vectors[1]),
                ]
            across = ring.out_middle(piece)
    vectors = jnp.concatenate(vectors, 1)
    gain1, bias1, gain2, bias2 = (vectors[8 * i : 8 * i + 8] for i in range(4))
    own1, own2 = gain1[:, :width], gain2[:, :width]
    for r in rows[1:]:
        xs[r] = ring.gather_start(gate([low[r]], xs[r - 1][1:2])[0])
    for r in rows:
        qkv[r], normed1[r], stat1[r], xs[r] = project(
            n, pairs, xs[r], gain1, bias1, tables, qkv_weight
        )
        attended[r], logs[r] = attend(starts[r], qkv[r])
        heads[r] = ring.gather_start(attended[r])
        if r == last:
            out_w = ring.out_end(out_weight, across)

    for r in rows:
        cots[r] = ring.gather_start(gate([cot_rows[r]])[0])
        got = feed(
            n,
            pairs,
            heads[r],
            xs[r],
            out_w,
            wide[r],
            gain2,
            bias2,
            up_bias8,
            up_weight,
            down_weight,
        )
        hidden[r], normed2[r], stat2[r], activated[r], slope[r], parts = got
        branch[r] = ring.scatter(parts)[0]

    def back(r, others):
        nonlocal up_bias_sum, down_bias_sum
        up_grad[r], up_sum, cot_sum, parts, blocks = feed_back(
            n, pairs, cots[r], others, slope[r], normed2[r], gain2, bias2, up_weight, down_weight
        )
        up_bias_sum += up_sum
        down_bias_sum += cot_sum
        parts2[r] = ring.scatter(parts, True)
        return blocks

    def spread_over_dp(value, dim):
        return lax.psum_scatter(value, "dp", scatter_dimension=dim, tiled=True)

    blocks = back(0, cots[1:])
    if pairs:
        cots = blocks
        branch[0][1] = gate(branch[0][1:])[0]
    down_sum = spread_over_dp(weight_of_blocks(ring.me[None], activated, cots), 1)
    for r in rows[1:]:
        back(r, [])

    def hidden_step(r):
        nonlocal gain2_sum, bias2_sum
        parts, row_sums = parts2[r]
        hidden_grad[r], low_grad, gain_part, bias_part = hidden_back(
            parts, cotangent, r, hidden[r], stat2[r], row_sums, own2, full
        )
        gain2_sum += gain_part
        bias2_sum += bias_part
        grads[r] = ring.gather_start(low_grad)

    hidden_step(0)
    up_sum = spread_over_dp(weight_grad(normed2, up_grad), 0)
    if pairs:
        branch[last][1] = gate(branch[last][1:])[0]

    for r in rows:
        grad_full[r], attended_grad = attended_back(n, pairs, grads[r], out_weight)
        if r < last:
            hidden_step(r + 1)
        Order.cost = 10**4 if r < last else 10**12
        qkv_grad[r] = attend_back(starts[r], tables, qkv[r], attended_grad, logs[r])
        Order.cost = 10**12
        if r == last and spread:
            qkv_sum = [
                Spread(normed1, qkv_grad, 0, (1, 2, 4), (0, 2)),
                Spread(normed1, qkv_grad, 0, (2, 4, 1), (1, 2)),
            ]
            qkv_sum[0].first()
            qkv_sum[1].first()
        parts = project_back(n, pairs, qkv_grad[r], normed1[r], gain1, bias1, qkv_weight)
        parts1[r] = ring.scatter(parts, True)

    if spread:
        out_sum = Spread(attended, grad_full, 1, (2, 4, 1))
        out_sum.first()
    if pairs:
        parts, row_sums = parts1[0]
        parts[1], row_sums[1] = gate([parts[1], row_sums[1]])
    down_sum = gate([down_sum])[0]
    made = output(branch, hidden, down_bias8)

    grad_history, depth_sum, gain1_sum, bias1_sum = None, 0.0, 0.0, 0.0
    for r in rows:
        parts, row_sums = parts1[r]
        grad_history, depth_part, gain_part, bias_part = average_back(
            depth_weights,
            parts,
            wide[r],
            stat1[r],
            row_sums,
            (own1, full),
            hidden_grad[r],
            history,
            r,
            grad_history,
        )
        depth_sum += depth_part
        gain1_sum += gain_part
        bias1_sum += bias_part
        if r == 0 and spread:
            qkv_sum[0].keep_added()
            qkv_sum[1].keep_added()
            out_sum.keep()

    Order.cost = 10**4
    vectors = [up_bias_sum, down_bias_sum, gain2_sum, bias2_sum, gain1_sum, bias1_sum]
    totals, depth_grad = sums([jnp.sum(v, 0) for v in vectors], jnp.sum(depth_sum, (1, 2)))
    if spread:
        advance(qkv_sum[0], qkv_sum[1], out_sum)
        advance(out_sum)
    else:
        qkv_sum = [spread_over_dp(weight_grad(normed1, qkv_grad), 0)]
        out_sum = spread_over_dp(weight_grad(attended, grad_full), 1)
    down_total, up_total, out_total, qkv_total = finish([down_sum], [up_sum], [out_sum], qkv_sum)
    return (
        made,
        grad_history,
        depth_grad,
        totals[4],
        totals[5],
        qkv_total,
        out_total,
        totals[2],
        totals[3],
        up_total,
        totals[0],
        down_total,
        totals[1],
    )


def solution(mesh):
    placed = (
        P(None, "dp", "mp"),
        P(),
        P("dp", None),
        P("mp"),
        P("mp"),
        P(None, "mp"),
        P("mp", None),
        P("mp"),
        P("mp"),
        P(None, "mp"),
        P("mp"),
        P("mp", None),
        P("mp"),
        P("dp", "mp"),
    )
    return jax.shard_map(
        local,
        mesh=mesh,
        in_specs=placed,
        out_specs=(
            P("dp", "mp"),
            P(None, "dp", "mp"),
            P(),
            P("mp"),
            P("mp"),
            P("dp", "mp"),
            P("mp", "dp"),
            P("mp"),
            P("mp"),
            P("dp", "mp"),
            P("mp"),
            P("mp", "dp"),
            P("mp"),
        ),
        check_vma=False,
    )
```

```python
import math

import jax
import jax.numpy as jnp
import numpy as np
from jax import lax
from jax.experimental import pallas as pl
from jax.experimental.pallas import tpu as pltpu
from jax.sharding import PartitionSpec as P

HEAD = 128
MAX_DOC = 512
EPSILON = 1e-05
SQRT_HALF = 0.7071067811865476
INV_ROOT_TWO_PI = 0.3989422804014327
LOG2E = 1.4426950408889634
SCALE = HEAD ** (-0.5)
MIB = 2**20
BF16 = jnp.bfloat16
F32 = jnp.float32


def dot_nn(a, b):
    return jnp.dot(a, b, preferred_element_type=F32)


def dot_nt(a, b):
    return lax.dot_general(a, b, (((1,), (1,)), ((), ())), preferred_element_type=F32)


def dot_tn(a, b):
    return lax.dot_general(a, b, (((0,), (0,)), ((), ())), preferred_element_type=F32)


LARGE, TINY = 10**12, 10**4


class Order:
    last = None
    names = 0
    cost = LARGE

    @staticmethod
    def name(remote):
        Order.names += remote
        return Order.names - 1 if remote else None


def call(
    name, body, grid, args, in_specs, outs, out_specs, scratch=(), prefetch=0, after=(), aliases=None, remote=False
):
    count = len(args)
    extra = [*after]
    if Order.last is not None and not any(Order.last is a for a in args):
        extra.append(Order.last)

    def without_extra(*refs):
        body(*refs[:count], *refs[count + len(extra) :])

    got = pl.pallas_call(
        without_extra,
        grid_spec=pltpu.PrefetchScalarGridSpec(
            num_scalar_prefetch=prefetch,
            grid=grid,
            in_specs=list(in_specs) + [ANY] * len(extra),
            out_specs=out_specs,
            scratch_shapes=list(scratch),
        ),
        out_shape=outs,
        input_output_aliases=aliases or {},
        compiler_params=pltpu.CompilerParams(
            vmem_limit_bytes=60 * MIB, collective_id=Order.name(remote), has_side_effects=remote
        ),
        cost_estimate=pl.CostEstimate(flops=Order.cost, bytes_accessed=Order.cost // 10**4, transcendentals=0),
        name=name,
    )(*args, *extra)
    fresh = [v for i, v in enumerate(got) if i not in (aliases or {}).values()]
    Order.last = min(fresh or got, key=lambda v: v.size)
    return got


def shape(dims, dtype):
    return jax.ShapeDtypeStruct(dims, dtype)


def sent(dims, dtype):
    return pltpu.HBM(dims, dtype)


SMEM = pl.BlockSpec(memory_space=pltpu.SMEM)
ANY = pl.BlockSpec(memory_space=pl.ANY)


def gate(arrays, after=()):
    arrays = list(arrays)
    return call(
        "gate",
        lambda *refs: None,
        (1,),
        arrays,
        [ANY] * len(arrays),
        [shape(a.shape, a.dtype) for a in arrays],
        [ANY] * len(arrays),
        after=after,
        aliases={i: i for i in range(len(arrays))},
    )


def rows_of(block):
    return pl.BlockSpec(block, lambda i: (i, 0))


def cols_of(block):
    return pl.BlockSpec(block, lambda i: (0, i))


def fixed(block):
    return pl.BlockSpec(block, lambda i: (0,) * len(block))


def flip(me, j):
    there, bit = me, 1
    while bit <= j:
        if j & bit:
            there = there + bit * (1 - 2 * ((me // bit) % 2))
        bit *= 2
    return there


def place_of(me, j, width):
    return pl.ds(pl.multiple_of(flip(me, j) * width, width), width)


def greet():
    barrier = pltpu.get_barrier_semaphore()
    sibling = flip(lax.axis_index("mp"), 1)
    pl.semaphore_signal(
        barrier, inc=1, device_id={"mp": sibling}, device_id_type=pl.DeviceIdType.MESH
    )
    pl.semaphore_wait(barrier, 1)


def to_sibling(source, target, sems, at):
    return pltpu.make_async_remote_copy(
        src_ref=source,
        dst_ref=target,
        send_sem=sems.at[0, at],
        recv_sem=sems.at[1, at],
        device_id={"mp": flip(lax.axis_index("mp"), 1)},
        device_id_type=pl.DeviceIdType.MESH,
    )


class Gathered:
    def __init__(self, refs, pairs, steps):
        self.pairs, self.steps = pairs, steps
        self.blocks, self.whole = refs[:2] if pairs else refs, refs[2:4] if pairs else ()

    @staticmethod
    def specs(blocks, pairs, tile):
        width = blocks[0].shape[1]
        return [rows_of((tile, width))] * len(blocks) + ([ANY] * 2 if pairs else [])

    @staticmethod
    def scratch(blocks, pairs, steps):
        if not pairs:
            return []
        return [pltpu.VMEM((2, *blocks[0].shape), BF16), pltpu.SemaphoreType.DMA((2, 2 * steps))]

    def attach(self, refs):
        if self.pairs:
            self.came, self.sems = refs
        return self

    def copies(self, step):
        tile = self.blocks[0].shape[0]
        rows = pl.ds(pl.multiple_of(step * tile, tile), tile)
        return [
            to_sibling(self.whole[k].at[rows, :], self.came.at[k, rows, :], self.sems, 2 * step + k)
            for k in range(2)
        ]

    def start(self):
        if self.pairs:
            for step in range(self.steps):
                for one in self.copies(step):
                    one.start()

    def refs(self):
        if not self.pairs:
            return self.blocks
        step = pl.program_id(0)
        tile = self.blocks[0].shape[0]
        for one in self.copies(step):
            one.wait()
        rows = pl.ds(pl.multiple_of(step * tile, tile), tile)
        return [self.blocks[0], self.came.at[0, rows, :], self.blocks[1], self.came.at[1, rows, :]]


class Scattered:
    def __init__(self, pairs, n, steps, with_sums):
        self.pairs, self.n, self.steps, self.with_sums = pairs, n, steps, with_sums

    def outs(self, length, width):
        tile = length // self.steps
        if self.pairs:
            outs = [shape((length, width), BF16), sent((length, width), BF16)]
            specs = [fixed((length, width))] * 2
            if self.with_sums:
                outs, specs = outs + [sent((8, length), F32)], specs + [fixed((8, length))]
            return outs, specs
        outs, specs = [shape((length, width), BF16)] * self.n, [rows_of((tile, width))] * self.n
        if self.with_sums:
            outs, specs = outs + [shape((8, length), F32)], specs + [cols_of((8, tile))]
        return outs, specs

    def count(self):
        return (2 if self.pairs else self.n) + self.with_sums

    def scratch(self, length, width):
        if not self.pairs:
            return []
        tile = length // self.steps
        block = pltpu.VMEM((self.steps, 2, tile, width), BF16)
        made = [block, block, pltpu.VMEM((2, 2, tile, width), F32)]
        if self.with_sums:
            made += [pltpu.VMEM((self.steps, 8, tile), F32)] * 3
        return made + [pltpu.SemaphoreType.DMA((2, 3 * self.steps))]

    def attach(self, outs, scratch):
        self.out = outs
        if self.pairs:
            self.send, self.came, self.kept = scratch[:3]
            self.sums = scratch[3:-1]
            self.sems = scratch[-1]
        return self

    def copies(self, step):
        made = [
            to_sibling(self.send.at[step, k], self.came.at[step, k], self.sems, 3 * step + k)
            for k in range(2)
        ]
        if self.with_sums:
            made.append(to_sibling(self.sums[0].at[step], self.sums[1].at[step], self.sems, 3 * step + 2))
        return made

    def put(self, j, value):
        step = pl.program_id(0)
        if not self.pairs:
            self.out[j][...] = value.astype(BF16)
        elif j % 2:
            self.send[step, j // 2] = value.astype(BF16)
        else:
            self.kept[step % 2, j // 2] = value

    def take(self, step):
        tile = self.kept.shape[2]
        for one in self.copies(step):
            one.wait()
        rows = pl.ds(pl.multiple_of(step * tile, tile), tile)
        for k in range(2):
            total = self.kept[step % 2, k] + self.came[step, k].astype(F32)
            self.out[k][rows, :] = total.astype(BF16)
        if self.with_sums:
            self.out[2][:, rows] = self.sums[2][step] + self.sums[1][step]

    def finish(self, sums=None):
        if not self.pairs:
            if sums is not None:
                self.out[-1][...] = sums
            return
        step = pl.program_id(0)
        if sums is not None:
            self.sums[0][step] = sums
            self.sums[2][step] = sums
        for one in self.copies(step):
            one.start()

        @pl.when(step > 0)
        def _():
            self.take(step - 1)

        @pl.when(step == self.steps - 1)
        def _():
            self.take(step)


def with_weights(copies, work, remote=False, gathered=()):
    @pl.when(pl.program_id(0) == 0)
    def _():
        for one in copies:
            one.start()
        if remote:
            greet()
        for one in gathered:
            one.start()

        def wait(some):
            for one in some:
                one.wait()

        work(wait)

    @pl.when(pl.program_id(0) != 0)
    def _():
        work(lambda some: None)


def row_blocks(me, n, width, source, target, sems, base):
    return [
        pltpu.make_async_copy(
            source.at[place_of(me, j, width), :],
            target.at[pl.ds(j * width, width), :],
            sems.at[base + j],
        )
        for j in range(n)
    ]


def col_blocks(me, n, width, source, target, sems, base):
    return [
        pltpu.make_async_copy(
            source.at[:, place_of(me, j, width)],
            target.at[:, pl.ds(j * width, width)],
            sems.at[base + j],
        )
        for j in range(n)
    ]


def stat_columns(first, second):
    lane = lax.broadcasted_iota(jnp.int32, (first.shape[0], 128), 1)
    return jnp.where(lane == 0, first, jnp.where(lane == 1, second, 0.0))


def fold_rows(values):
    return jnp.sum(values.reshape(values.shape[0] // 8, 8, values.shape[1]), 0)


def accumulate(ref, value):
    @pl.when(pl.program_id(0) == 0)
    def _():
        ref[...] = value

    @pl.when(pl.program_id(0) != 0)
    def _():
        ref[...] += value


def average_body(weights, history, wide, low):
    chunk = min(32, wide.shape[0])
    for t in range(wide.shape[0] // chunk):
        rows = slice(t * chunk, (t + 1) * chunk)
        total = weights[0] * history[0, rows, :].astype(F32)
        for j in range(1, history.shape[0]):
            total += weights[j] * history[j, rows, :].astype(F32)
        wide[rows, :] = total
        low[rows, :] = total.astype(BF16)


def average(weights, history, row, length):
    count, _, width = history.shape
    tile = min(256, length)
    steps = length // tile
    return call(
        "average",
        average_body,
        (steps,),
        (weights, history),
        [SMEM, pl.BlockSpec((count, tile, width), lambda i: (0, row * steps + i, 0))],
        [shape((length, width), F32), sent((length, width), BF16)],
        [rows_of((tile, width))] * 2,
    )


def project_body(n, pairs, steps, *refs):
    count = 4 if pairs else n
    x = Gathered(refs[:count], pairs, steps)
    gain, bias, cosine, sine, weight, qkv, normed, stat = refs[count : count + 8]
    refs = refs[count + 8 :]
    shared = refs[:2] if pairs else ()
    held, joined, sems, *more = refs[len(shared) :]
    x.attach(more)
    me = lax.axis_index("mp")
    tile, width = x.blocks[0].shape
    full = n * width
    heads = held.shape[1] // (3 * HEAD)
    sub = min(256, tile)
    copies = row_blocks(me, n, width, weight, held, sems, 0)

    def work(wait):
        xs = x.refs()
        for out, k in zip(shared, (1, 3)):
            out[...] = xs[k][...]
        for t in range(tile // sub):
            rows = slice(t * sub, (t + 1) * sub)
            total = square = 0.0
            for one in xs:
                value = one[rows, :].astype(F32)
                total += jnp.sum(value, 1, keepdims=True)
                square += jnp.sum(value * value, 1, keepdims=True)
            mean = total / full
            inv = lax.rsqrt(square / full - mean * mean + EPSILON)
            stat[rows, :] = stat_columns(mean, inv)
            for j, one in enumerate(xs):
                part = slice(j * width, (j + 1) * width)
                value = (one[rows, :].astype(F32) - mean) * inv * gain[0:1, part] + bias[0:1, part]
                joined[rows, part] = value.astype(BF16)
                normed[rows, place_of(me, j, width)] = value.astype(BF16)
            if t == 0:
                wait(copies)
            for h in range(heads):
                base = 3 * h * HEAD
                out = dot_nn(joined[rows, :], held[:, base : base + 3 * HEAD])
                for s in range(2):
                    v = out[:, s * HEAD : (s + 1) * HEAD]
                    turned = v * cosine[rows, :] + pltpu.roll(v, HEAD // 2, 1) * sine[rows, :]
                    qkv[rows, base + s * HEAD : base + (s + 1) * HEAD] = turned.astype(BF16)
                qkv[rows, base + 2 * HEAD : base + 3 * HEAD] = out[:, 2 * HEAD :].astype(BF16)

    with_weights(copies, work, pairs, [x])


def project(n, pairs, xs, gain, bias, tables, weight):
    length, width = xs[0].shape
    full, out = weight.shape
    tile = min(512, length)
    steps = length // tile
    got = call(
        "project",
        lambda *refs: project_body(n, pairs, steps, *refs),
        (steps,),
        (*xs, *(xs if pairs else ()), gain, bias, *tables, weight),
        Gathered.specs(xs, pairs, tile)
        + [fixed((8, full))] * 2
        + [rows_of((tile, HEAD))] * 2
        + [ANY],
        [shape((length, out), BF16), shape((length, full), BF16), shape((length, 128), F32)]
        + [shape((length, width), BF16)] * (2 * pairs),
        [rows_of((tile, out)), rows_of((tile, full)), rows_of((tile, 128))]
        + [rows_of((tile, width))] * (2 * pairs),
        scratch=[
            pltpu.VMEM((full, out), BF16),
            pltpu.VMEM((tile, full), BF16),
            pltpu.SemaphoreType.DMA((n,)),
        ]
        + Gathered.scratch(xs, pairs, steps),
        remote=pairs,
    )
    return *got[:3], [xs[0], got[3], xs[1], got[4]] if pairs else xs


def windows(length):
    block = min(256, length)
    for i in range(length // block):
        low = max(0, i * block - (MAX_DOC - 1)) // block * block
        yield slice(i * block, (i + 1) * block), slice(low, (i + 1) * block)


def score_mask(start, q_part, k_part):
    dims = (k_part.stop - k_part.start, q_part.stop - q_part.start)
    k_pos = lax.broadcasted_iota(jnp.int32, dims, 0) + k_part.start
    q_pos = lax.broadcasted_iota(jnp.int32, dims, 1) + q_part.start
    return (k_pos >= start[0:1, q_part]) & (k_pos <= q_pos)


def attend_body(start, qkv, out, logs):
    length = qkv.shape[0]
    value_t = qkv[:, 2 * HEAD :].T
    for q_part, k_part in windows(length):
        query, key = qkv[q_part, :HEAD], qkv[k_part, HEAD : 2 * HEAD]
        scores = dot_nt(key, query) * (SCALE * LOG2E)
        scores = jnp.where(score_mask(start, q_part, k_part), scores, -1e30)
        top = jnp.max(scores, 0, keepdims=True)
        probs = jnp.exp2(scores - top)
        total = jnp.sum(probs, 0, keepdims=True)
        logs[0, :, q_part] = jnp.broadcast_to(top + jnp.log2(total), (8, q_part.stop - q_part.start))
        got = dot_nn(value_t[:, k_part], probs.astype(BF16)) / total
        out[q_part, :] = got.T.astype(BF16)


def attend(start, qkv):
    length, width = qkv.shape
    heads = width // (3 * HEAD)
    return call(
        "attend",
        attend_body,
        (heads,),
        (start, qkv),
        [fixed((8, length)), cols_of((length, 3 * HEAD))],
        [sent((length, heads * HEAD), BF16), shape((heads, 8, length), F32)],
        [cols_of((length, HEAD)), pl.BlockSpec((1, 8, length), lambda i: (i, 0, 0))],
    )


def attend_back_body(start, cosine, sine, qkv, grad, logs, out, key_sum, value_sum):
    length = qkv.shape[0]
    key_t = qkv[:, HEAD : 2 * HEAD].T
    key_sum[...] = jnp.zeros_like(key_sum)
    value_sum[...] = jnp.zeros_like(value_sum)

    def turn_back(v, part):
        return (
            v * cosine[part, :] - pltpu.roll(v, HEAD // 2, 1) * sine[part, :]
        ).astype(BF16)

    for q_part, k_part in windows(length):
        query, key = qkv[q_part, :HEAD], qkv[k_part, HEAD : 2 * HEAD]
        value, g = qkv[k_part, 2 * HEAD :], grad[q_part, :]
        scores = dot_nt(key, query) * (SCALE * LOG2E) - logs[0, 0:1, q_part]
        probs = jnp.exp2(jnp.where(score_mask(start, q_part, k_part), scores, -1e30))
        prob_grad = dot_nt(value, g)
        mean = jnp.sum(prob_grad * probs, 0, keepdims=True)
        score_grad = (probs * (prob_grad - mean)).astype(BF16)
        value_sum[k_part, :] += dot_nn(probs.astype(BF16), g)
        key_sum[k_part, :] += dot_nn(score_grad, query)
        query_grad = dot_nn(key_t[:, k_part], score_grad) * SCALE
        out[q_part, :HEAD] = turn_back(query_grad.T, q_part)
    for q_part, _ in windows(length):
        out[q_part, HEAD : 2 * HEAD] = turn_back(key_sum[q_part, :] * SCALE, q_part)
        out[q_part, 2 * HEAD :] = value_sum[q_part, :].astype(BF16)


def attend_back(start, tables, qkv, grad, logs):
    length, width = qkv.shape
    heads = width // (3 * HEAD)
    return call(
        "attend_back",
        attend_back_body,
        (heads,),
        (start, *tables, qkv, grad, logs),
        [fixed((8, length))]
        + [fixed((length, HEAD))] * 2
        + [
            cols_of((length, 3 * HEAD)),
            cols_of((length, HEAD)),
            pl.BlockSpec((1, 8, length), lambda i: (i, 0, 0)),
        ],
        [shape((length, width), BF16)],
        [cols_of((length, 3 * HEAD))],
        scratch=[pltpu.VMEM((length, HEAD), F32)] * 2,
    )[0]


def feed_body(n, pairs, steps, *refs):
    count = 4 if pairs else n
    attended = Gathered(refs[:count], pairs, steps)
    refs = refs[count:]
    xs, outs_w = refs[: n - 1], refs[n - 1 : 2 * n - 1]
    own, gain, bias, up_bias, up_weight, down_weight = refs[2 * n - 1 : 2 * n + 5]
    refs = refs[2 * n + 5 :]
    hidden, normed, stat, activated, slope = refs[:5]
    refs = refs[5:]
    parts = Scattered(pairs, n, steps, False)
    part_outs, refs = refs[: parts.count()], refs[parts.count() :]
    out_held, up_held, down_held, joined, whole, sems, *refs = refs
    if pairs:
        attended.attach(refs[:2])
        refs = refs[2:]
    parts.attach(part_outs, refs)
    me = lax.axis_index("mp")
    width = own.shape[1]
    full = n * width
    inner = up_held.shape[1]
    out_copies = []
    for j in range(n):
        for k in range(n):
            out_copies.append(
                pltpu.make_async_copy(
                    outs_w[k].at[:, place_of(me, j, width)],
                    out_held.at[pl.ds(k * width, width), pl.ds(j * width, width)],
                    sems.at[j * n + k],
                )
            )
    up_copies = row_blocks(me, n, width, up_weight, up_held, sems, n * n)
    down_copies = col_blocks(me, n, width, down_weight, down_held, sems, n * n + n)

    def work(wait):
        for j, one in enumerate(attended.refs()):
            joined[:, j * width : (j + 1) * width] = one[...]
        total = square = 0.0
        for j in range(n):
            wait(out_copies[j * n : (j + 1) * n])
            part = slice(j * width, (j + 1) * width)
            base = own[...] if j == 0 else xs[j - 1][...].astype(F32)
            value = base + dot_nn(joined[...], out_held[:, part])
            whole[:, part] = value
            if j == 0:
                hidden[...] = value
            total += jnp.sum(value, 1, keepdims=True)
            square += jnp.sum(value * value, 1, keepdims=True)
        mean = total / full
        inv = lax.rsqrt(square / full - mean * mean + EPSILON)
        stat[...] = stat_columns(mean, inv)
        for j in range(n):
            part = slice(j * width, (j + 1) * width)
            value = ((whole[:, part] - mean) * inv * gain[0:1, part] + bias[0:1, part]).astype(BF16)
            joined[:, part] = value
            normed[:, place_of(me, j, width)] = value
        wait(up_copies)
        step = divisor(inner, 512)
        for c in range(inner // step):
            part = slice(c * step, (c + 1) * step)
            up = dot_nn(joined[...], up_held[:, part]) + up_bias[0:1, part]
            half = 0.5 * (1.0 + lax.erf(up * SQRT_HALF))
            activated[:, part] = (up * half).astype(BF16)
            slope[:, part] = (half + up * INV_ROOT_TWO_PI * jnp.exp(-0.5 * up * up)).astype(BF16)
        wait(down_copies)
        for j in range(n):
            parts.put(j, dot_nn(activated[...], down_held[:, j * width : (j + 1) * width]))

    with_weights(out_copies + up_copies + down_copies, work, pairs, [attended])
    parts.finish()


def feed(n, pairs, attended, xs, outs_w, own, gain, bias, up_bias, up_weight, down_weight):
    length, width = own.shape
    full, inner = up_weight.shape
    tile = min(256, length)
    steps = length // tile
    parts = Scattered(pairs, n, steps, False)
    part_outs, part_specs = parts.outs(length, width)
    twice = tuple(attended) if pairs else ()
    got = call(
        "feed",
        lambda *refs: feed_body(n, pairs, steps, *refs),
        (steps,),
        (
            *attended,
            *twice,
            *xs[1:],
            *outs_w,
            own,
            gain,
            bias,
            up_bias,
            up_weight,
            down_weight,
        ),
        Gathered.specs(attended, pairs, tile)
        + [rows_of((tile, width))] * (n - 1)
        + [ANY] * n
        + [rows_of((tile, width))]
        + [fixed((8, full))] * 2
        + [fixed((8, inner))]
        + [ANY] * 2,
        [
            shape((length, width), F32),
            shape((length, full), BF16),
            shape((length, 128), F32),
            shape((length, inner), BF16),
            shape((length, inner), BF16),
        ]
        + part_outs,
        [
            rows_of((tile, width)),
            rows_of((tile, full)),
            rows_of((tile, 128)),
            rows_of((tile, inner)),
            rows_of((tile, inner)),
        ]
        + part_specs,
        scratch=[
            pltpu.VMEM((full, full), BF16),
            pltpu.VMEM((full, inner), BF16),
            pltpu.VMEM((inner, full), BF16),
            pltpu.VMEM((tile, full), BF16),
            pltpu.VMEM((tile, full), F32),
            pltpu.SemaphoreType.DMA((n * n + 2 * n,)),
        ]
        + Gathered.scratch(attended, pairs, steps)
        + parts.scratch(length, width),
        remote=pairs,
    )
    return (*got[:5], got[5:])


def row_stats(total, weighted):
    return stat_columns(total, weighted).T[0:8, :]


def norm_sums(parts, n, product, normed, gain, bias, me):
    width = gain.shape[1] // n
    total = weighted = 0.0
    for j in range(n):
        part = slice(j * width, (j + 1) * width)
        value = product(j)
        parts.put(j, value)
        total += jnp.sum(value * gain[0:1, part], 1, keepdims=True)
        there = normed[:, place_of(me, j, width)].astype(F32)
        weighted += jnp.sum(value * (there - bias[0:1, part]), 1, keepdims=True)
    return row_stats(total, weighted)


def join_body(count, steps, *refs):
    gathered = [Gathered(refs[4 * i : 4 * i + 4], True, steps) for i in range(count)]
    outs, scratch = refs[4 * count : 5 * count], refs[5 * count :]
    for i, one in enumerate(gathered):
        one.attach(scratch[2 * i : 2 * i + 2])
    me = lax.axis_index("mp")

    def work(wait):
        for one, out in zip(gathered, outs):
            for j, block in enumerate(one.refs()):
                out[:, place_of(me, j, block.shape[1])] = block[...]

    with_weights([], work, True, gathered)


def join(gathered, full):
    length = gathered[0][0].shape[0]
    tile = min(256, length)
    steps = length // tile
    args, specs, scratch = [], [], []
    for one in gathered:
        args += [*one, *one]
        specs += Gathered.specs(one, True, tile)
        scratch += Gathered.scratch(one, True, steps)
    return call(
        "join",
        lambda *refs: join_body(len(gathered), steps, *refs),
        (steps,),
        args,
        specs,
        [shape((length, full), BF16)] * len(gathered),
        [rows_of((tile, full))] * len(gathered),
        scratch=scratch,
        remote=True,
    )


def feed_back_body(n, pairs, steps, *refs):
    cot, refs = refs[0], refs[1:]
    slope, normed, gain, bias, up_weight, down_weight, up_grad, up_bias_sum, cot_sum = refs[:9]
    refs = refs[9:]
    parts = Scattered(pairs, n, steps, True)
    part_outs, refs = refs[: parts.count()], refs[parts.count() :]
    up_held, down_held, row_sums, sems, *refs = refs
    parts.attach(part_outs, refs)
    me = lax.axis_index("mp")
    inner = up_held.shape[1]
    width = gain.shape[1] // n
    step = divisor(inner, 512)
    down_copies = [pltpu.make_async_copy(down_weight, down_held, sems.at[n])]
    up_copies = row_blocks(me, n, width, up_weight, up_held, sems, 0)

    def work(wait):
        accumulate(cot_sum, fold_rows(cot[:, place_of(me, 0, width)].astype(F32)))
        wait(down_copies)
        bias_parts = []
        for c in range(inner // step):
            part = slice(c * step, (c + 1) * step)
            value = dot_nt(cot[...], down_held[part, :]) * slope[:, part].astype(F32)
            low = value.astype(BF16)
            up_grad[:, part] = low
            bias_parts.append(fold_rows(low.astype(F32)))
        accumulate(up_bias_sum, jnp.concatenate(bias_parts, 1))
        wait(up_copies)
        row_sums[...] = norm_sums(
            parts,
            n,
            lambda j: dot_nt(up_grad[...], up_held[j * width : (j + 1) * width, :]),
            normed,
            gain,
            bias,
            me,
        )

    with_weights(down_copies + up_copies, work, pairs)
    parts.finish(row_sums[...])


def feed_back(n, pairs, cot, slope, normed, gain, bias, up_weight, down_weight):
    length, full = normed.shape
    width = full // n
    inner = up_weight.shape[1]
    tile = min(256, length)
    steps = length // tile
    parts = Scattered(pairs, n, steps, True)
    part_outs, part_specs = parts.outs(length, width)
    got = call(
        "feed_back",
        lambda *refs: feed_back_body(n, pairs, steps, *refs),
        (steps,),
        (cot, slope, normed, gain, bias, up_weight, down_weight),
        [rows_of((tile, full)), rows_of((tile, inner)), rows_of((tile, full))]
        + [fixed((8, full))] * 2
        + [ANY] * 2,
        [shape((length, inner), BF16), shape((8, inner), F32), shape((8, width), F32)] + part_outs,
        [rows_of((tile, inner)), fixed((8, inner)), fixed((8, width))] + part_specs,
        scratch=[
            pltpu.VMEM((full, inner), BF16),
            pltpu.VMEM((inner, full), BF16),
            pltpu.VMEM((8, tile), F32),
            pltpu.SemaphoreType.DMA((n + 1,)),
        ]
        + parts.scratch(length, width),
        remote=pairs,
    )
    return (*got[:3], got[3:])


def norm_back(refs, n_parts, source, stat, sums, gain, full):
    grad = refs[0][...].astype(F32)
    for ref in refs[1:n_parts]:
        grad += ref[...].astype(F32)
    columns = sum(one[...] for one in sums).T
    mean, inv = stat[:, 0:1], stat[:, 1:2]
    scaled = (source[...] - mean) * inv
    back = inv * (
        grad * gain[0:1, :] - columns[:, 0:1] * (1.0 / full) - scaled * (columns[:, 1:2] * (1.0 / full))
    )
    return back, fold_rows(grad * scaled), fold_rows(grad)


def hidden_back_body(k, m, full, *refs):
    parts, sums = refs[:k], refs[k : k + m]
    cot, hidden, stat, gain, wide, low, gain_sum, bias_sum = refs[k + m :]
    back, gain_part, bias_part = norm_back(parts, k, hidden, stat, sums, gain, full)
    value = cot[...].astype(F32) + back
    wide[...] = value
    low[...] = value.astype(BF16)
    accumulate(gain_sum, gain_part)
    accumulate(bias_sum, bias_part)


def hidden_back(parts, cotangent, row, hidden, stat, sums, gain, full):
    k, m, (length, width) = len(parts), len(sums), hidden.shape
    tile = min(256, length)
    steps = length // tile
    return call(
        "hidden_back",
        lambda *refs: hidden_back_body(k, m, full, *refs),
        (steps,),
        (*parts, *sums, cotangent, hidden, stat, gain),
        [rows_of((tile, width))] * k
        + [cols_of((8, tile))] * m
        + [
            pl.BlockSpec((tile, width), lambda i: (row * steps + i, 0)),
            rows_of((tile, width)),
            rows_of((tile, 128)),
            fixed((8, width)),
        ],
        [shape((length, width), F32), sent((length, width), BF16)] + [shape((8, width), F32)] * 2,
        [rows_of((tile, width))] * 2 + [fixed((8, width))] * 2,
    )


def attended_back_body(n, pairs, steps, *refs):
    count = 4 if pairs else n
    grads = Gathered(refs[:count], pairs, steps)
    weight, joined, out, *more = refs[count:]
    grads.attach(more)
    me = lax.axis_index("mp")
    width = grads.blocks[0].shape[1]

    def work(wait):
        for j, one in enumerate(grads.refs()):
            joined[:, place_of(me, j, width)] = one[...]
        out[...] = dot_nt(joined[...], weight[...]).astype(BF16)

    with_weights([], work, pairs, [grads])


def attended_back(n, pairs, grads, weight):
    length, width = grads[0].shape
    rows, full = weight.shape
    tile = min(256, length)
    steps = length // tile
    return call(
        "attended_back",
        lambda *refs: attended_back_body(n, pairs, steps, *refs),
        (steps,),
        (*grads, *(grads if pairs else ()), weight),
        Gathered.specs(grads, pairs, tile) + [fixed((rows, full))],
        [shape((length, full), BF16), shape((length, rows), BF16)],
        [rows_of((tile, full)), rows_of((tile, rows))],
        scratch=Gathered.scratch(grads, pairs, steps),
        remote=pairs,
    )


def project_back_body(n, pairs, steps, grad, normed, gain, bias, weight, *refs):
    parts = Scattered(pairs, n, steps, True)
    part_outs, refs = refs[: parts.count()], refs[parts.count() :]
    held, row_sums, sems, *refs = refs
    parts.attach(part_outs, refs)
    me = lax.axis_index("mp")
    width = gain.shape[1] // n
    copies = row_blocks(me, n, width, weight, held, sems, 0)

    def work(wait):
        def product(j):
            wait(copies[j : j + 1])
            return dot_nt(grad[...], held[j * width : (j + 1) * width, :])

        row_sums[...] = norm_sums(parts, n, product, normed, gain, bias, me)

    with_weights(copies, work, pairs)
    parts.finish(row_sums[...])


def project_back(n, pairs, grad, normed, gain, bias, weight):
    length, out = grad.shape
    full = weight.shape[0]
    width = full // n
    tile = min(256, length)
    steps = length // tile
    parts = Scattered(pairs, n, steps, True)
    part_outs, part_specs = parts.outs(length, width)
    return call(
        "project_back",
        lambda *refs: project_back_body(n, pairs, steps, *refs),
        (steps,),
        (grad, normed, gain, bias, weight),
        [rows_of((tile, out)), rows_of((tile, full))] + [fixed((8, full))] * 2 + [ANY],
        part_outs,
        part_specs,
        scratch=[
            pltpu.VMEM((full, out), BF16),
            pltpu.VMEM((8, tile), F32),
            pltpu.SemaphoreType.DMA((n,)),
        ]
        + parts.scratch(length, width),
        remote=pairs,
    )


def average_back_body(k, m, full, count, *refs):
    weights, parts, sums = refs[0], refs[1 : k + 1], refs[k + 1 : k + m + 1]
    source, stat, gain, hidden_grad, history = refs[k + m + 1 : k + m + 6]
    grad_history, depth_sum, gain_sum, bias_sum, held = refs[-5:]
    back, gain_part, bias_part = norm_back(parts, k, source, stat, sums, gain, full)
    held[...] = hidden_grad[...] + back
    accumulate(gain_sum, gain_part)
    accumulate(bias_sum, bias_part)
    lanes = held.shape[1] // 128
    chunk = min(32, held.shape[0])
    folded = [0.0] * count
    for t in range(held.shape[0] // chunk):
        rows = slice(t * chunk, (t + 1) * chunk)
        value = held[rows, :]
        for j in range(count):
            grad_history[j, rows, :] = (weights[j] * value).astype(BF16)
            product = fold_rows(value * history[j, rows, :].astype(F32))
            for c in range(lanes):
                folded[j] = folded[j] + product[:, c * 128 : (c + 1) * 128]
    for j in range(count):
        accumulate(depth_sum.at[j], folded[j])


def average_back(weights, parts, source, stat, sums, gain, hidden_grad, history, row, made):
    k, m, (length, width) = len(parts), len(sums), source.shape
    count = history.shape[0]
    tile = min(256, length)
    steps = length // tile
    full = gain[1]
    block = pl.BlockSpec((count, tile, width), lambda i: (0, row * steps + i, 0))
    args = (weights, *parts, *sums, source, stat, gain[0], hidden_grad, history)
    specs = (
        [SMEM]
        + [rows_of((tile, width))] * k
        + [cols_of((8, tile))] * m
        + [rows_of((tile, width)), rows_of((tile, 128)), fixed((8, width)), rows_of((tile, width)), block]
    )
    more = {}
    if made is not None:
        more = {"aliases": {len(args): 0}}
        args, specs = (*args, made), specs + [ANY]
    return call(
        "average_back",
        lambda *refs: average_back_body(k, m, full, count, *refs),
        (steps,),
        args,
        specs,
        [shape(history.shape, BF16), shape((count, 8, 128), F32)] + [shape((8, width), F32)] * 2,
        [block, fixed((count, 8, 128))] + [fixed((8, width))] * 2,
        scratch=[pltpu.VMEM((tile, width), F32)],
        **more,
    )


def divisor(size, most):
    return max(d for d in range(128, most + 1, 128) if size % d == 0) if size > 128 else size


def weight_body(rows, *refs):
    out = refs[-1]
    total = dot_tn(refs[0][...], refs[rows][...])
    for r in range(1, rows):
        total += dot_tn(refs[r][...], refs[rows + r][...])
    out[...] = total.astype(BF16)


def weight_grad(lefts, rights):
    rows, (length, high), wide = len(lefts), lefts[0].shape, rights[0].shape[1]
    tall, across = divisor(high, 1024), divisor(wide, 1024)
    return call(
        "weight_grad",
        lambda *refs: weight_body(rows, *refs),
        (high // tall, wide // across),
        (*lefts, *rights),
        [pl.BlockSpec((length, tall), lambda i, j: (0, i))] * rows
        + [pl.BlockSpec((length, across), lambda i, j: (0, j))] * rows,
        [shape((high, wide), BF16)],
        [pl.BlockSpec((tall, across), lambda i, j: (i, j))],
    )[0]


def put_blocks(came, outs, k, value):
    if came is not None:
        value = value + came[k].astype(F32)
    per = outs[0].shape[0]
    outs[k // per][k % per] = value.astype(BF16)


def tall_blocks_body(rows, count, fused, group, *refs):
    lefts, rights = refs[: rows * count], refs[rows * count : rows * count + rows]
    refs = refs[rows * count + rows :]
    came, outs, turned = refs[0] if fused else None, refs[fused:-1], refs[-1]
    length, high = lefts[0].shape

    @pl.when(pl.program_id(0) == 0)
    def _():
        for k in range(count):
            for r in range(rows):
                turned[k * high : (k + 1) * high, r * length : (r + 1) * length] = lefts[
                    k * rows + r
                ][...].T

    for k in range(count):
        total = 0.0
        for r in range(rows):
            total += dot_nn(
                turned[k * high : (k + 1) * high, r * length : (r + 1) * length], rights[r][...]
            )
        put_blocks(came, outs, k, total)


def wide_blocks_body(rows, count, fused, group, *refs):
    lefts, rights = refs[:rows], refs[rows : rows + rows * count]
    refs = refs[rows + rows * count :]
    came, outs = refs[0] if fused else None, refs[fused:]
    turned = [left[...].T for left in lefts]
    for k in range(count):
        total = 0.0
        for r in range(rows):
            total += dot_nn(turned[r], rights[k * rows + r][...])
        put_blocks(came, outs, k, total)


class Spread:
    def __init__(self, lefts, rights, dim, bits, part=(0, 1)):
        self.lefts, self.rights, self.dim, self.bits, self.part = lefts, rights, dim, list(bits), part
        self.groups = lax.axis_size("dp")
        self.block = (lefts, rights)[dim][0].shape[1] // self.groups
        order = [0]
        for bit in reversed(self.bits):
            order = order + [e | bit for e in order]
        self.order = order

    def blocks(self, half, came=None):
        count = self.groups // 2
        which = self.order[half * count : (half + 1) * count]
        rows, length = len(self.lefts), self.lefts[0].shape[0]
        group = lax.axis_index("dp").astype(jnp.int32)[None]
        size, (index, pieces) = self.block, self.part
        stay = [
            pl.BlockSpec((length, size), lambda i, group, e=e: (0, group[0] ^ e))
            for e in which
            for _ in range(rows)
        ]
        other = self.rights if self.dim == 0 else self.lefts
        extent = other[0].shape[1] // pieces
        tile = divisor(extent, 512)
        steps = extent // tile
        move = [pl.BlockSpec((length, tile), lambda i, group: (0, index * steps + i))] * rows

        def blocked(number):
            if self.dim == 0:
                return (
                    sent((number, size, extent), BF16),
                    pl.BlockSpec((number, size, tile), lambda i, group: (0, 0, i)),
                )
            return (
                sent((number, extent, size), BF16),
                pl.BlockSpec((number, tile, size), lambda i, group: (0, i, 0)),
            )

        if self.dim == 0:
            args = (*(list(self.lefts) * count), *self.rights)
            specs = stay + move
            body, scratch = tall_blocks_body, [pltpu.VMEM((count * size, rows * length), BF16)]
        else:
            args = (*self.lefts, *(list(self.rights) * count))
            specs = move + stay
            body, scratch = wide_blocks_body, []
        outs = [blocked(count)]
        if came is not None:
            args, specs = (*args, came), specs + [blocked(count)[1]]
            outs = [blocked(count // 2)] * 2
        return call(
            "weight_blocks",
            lambda *refs: body(rows, count, came is not None, *refs),
            (steps,),
            (group, *args),
            specs,
            [one[0] for one in outs],
            [one[1] for one in outs],
            scratch=scratch,
            prefetch=1,
        )

    def send(self, value):
        bit = self.bits[self.step]
        self.step += 1
        self.coming = lax.ppermute(value, "dp", [(i, i ^ bit) for i in range(self.groups)])

    def first(self):
        self.step = 0
        self.send(self.blocks(1)[0])

    def keep(self):
        self.held = self.blocks(0)[0]

    def keep_added(self):
        self.held, out = self.blocks(0, self.coming)
        self.send(out)


def fold_body(count, *refs):
    for i in range(count):
        held, came, keep, send = refs[2 * i], refs[2 * i + 1], refs[2 * count + 2 * i], refs[2 * count + 2 * i + 1]
        half = keep.shape[0]
        keep[...] = (held[:half].astype(F32) + came[:half].astype(F32)).astype(BF16)
        send[...] = (held[half:].astype(F32) + came[half:].astype(F32)).astype(BF16)


def advance(*spreads):
    steps = 4
    args, specs, outs, out_specs = [], [], [], []
    for one in spreads:
        count, high, wide = one.held.shape
        args += [one.held, one.coming]
        specs += [pl.BlockSpec((count, high // steps, wide), lambda i: (0, i, 0))] * 2
        outs += [sent((count // 2, high, wide), BF16)] * 2
        out_specs += [pl.BlockSpec((count // 2, high // steps, wide), lambda i: (0, i, 0))] * 2
    got = call("fold", lambda *refs: fold_body(len(spreads), *refs), (steps,), args, specs, outs, out_specs)
    for i, one in enumerate(spreads):
        one.held = got[2 * i]
        one.send(got[2 * i + 1])


def finish_body(groups, *refs):
    outs = refs[len(refs) - len(groups) :]
    at = 0
    for out, group in zip(outs, groups):
        for first, wide, count in group:
            total = refs[at][0].astype(F32)
            for ref in refs[at + 1 : at + count]:
                total += ref[0].astype(F32)
            out[:, first : first + wide] = total
            at += count


def finish(*groups):
    steps = 4
    args, specs, outs, out_specs, places = [], [], [], [], []
    for group in groups:
        first, place = 0, []
        for one in group:
            terms = [one.held, one.coming] if isinstance(one, Spread) else [one[None]]
            _, high, wide = terms[0].shape
            args += terms
            specs += [pl.BlockSpec((1, high // steps, wide), lambda i: (0, i, 0))] * len(terms)
            place.append((first, wide, len(terms)))
            first += wide
        outs.append(shape((high, first), F32))
        out_specs.append(rows_of((high // steps, first)))
        places.append(place)
    return call("finish", lambda *refs: finish_body(places, *refs), (steps,), args, specs, outs, out_specs)


def sums_body(groups, n, own, out, total, came, far, dp_sems, mp_sems):
    me = {"dp": lax.axis_index("dp"), "mp": lax.axis_index("mp")}
    peers = [("dp", b) for b in range(1, groups)] + [("mp", b) for b in range(1, n)]
    barrier = pltpu.get_barrier_semaphore()
    for axis, b in peers:
        pl.semaphore_signal(
            barrier, inc=1, device_id={axis: flip(me[axis], b)}, device_id_type=pl.DeviceIdType.MESH
        )
    pl.semaphore_wait(barrier, len(peers))

    def copy(axis, b, source, target, sems):
        return pltpu.make_async_remote_copy(
            src_ref=source,
            dst_ref=target.at[b - 1],
            send_sem=sems.at[0, b - 1],
            recv_sem=sems.at[1, b - 1],
            device_id={axis: flip(me[axis], b)},
            device_id_type=pl.DeviceIdType.MESH,
        )

    copies = [copy("dp", b, own, came, dp_sems) for b in range(1, groups)]
    for one in copies:
        one.start()
    for one in copies:
        one.wait()
    value = own[...]
    for b in range(groups - 1):
        value = value + came[b]
    out[...] = value
    total[...] = value[-8:]
    copies = [copy("mp", b, total, far, mp_sems) for b in range(1, n)]
    for one in copies:
        one.start()
    for one in copies:
        one.wait()
    value = total[...]
    for b in range(n - 1):
        value = value + far[b]
    out[-8:, :] = value


def sums(vectors, depth):
    groups, n = lax.axis_size("dp"), lax.axis_size("mp")
    sizes = [v.size for v in vectors]
    packed = jnp.concatenate(vectors)
    packed = jnp.pad(packed, (0, -packed.size % 1024)).reshape(-1, 128)
    packed = jnp.concatenate([packed, jnp.pad(depth[None], ((0, 7), (0, 128 - depth.size)))])
    high = packed.shape[0]
    got = call(
        "sums",
        lambda *refs: sums_body(groups, n, *refs),
        (1,),
        (packed,),
        [fixed((high, 128))],
        [shape((high, 128), F32)],
        [fixed((high, 128))],
        scratch=[
            pltpu.VMEM((8, 128), F32),
            pltpu.VMEM((groups - 1, high, 128), F32),
            pltpu.VMEM((n - 1, 8, 128), F32),
            pltpu.SemaphoreType.DMA((2, groups - 1)),
            pltpu.SemaphoreType.DMA((2, n - 1)),
        ],
        remote=True,
    )[0]
    flat = got.reshape(-1)
    ends = np.cumsum(sizes)
    return [flat[end - size : end] for end, size in zip(ends, sizes)], got[-8, : depth.size]


def output_body(rows, steps, *refs):
    bias, out = refs[-2:]
    per = (len(refs) - 2) // rows
    for r in range(rows):

        @pl.when(pl.program_id(0) // steps == r)
        def _(r=r):
            total = bias[0:1, :]
            for part in refs[r * per + 1 : (r + 1) * per]:
                total = total + part[...].astype(F32)
            out[...] = (refs[r * per][...] + total).astype(BF16)


def output(parts, hidden, bias):
    rows, (length, width) = len(hidden), hidden[0].shape
    tile = min(512, length)
    steps = length // tile
    args, specs = [], []
    for r in range(rows):
        args += [hidden[r], *parts[r]]
        specs += [
            pl.BlockSpec((tile, width), lambda i, r=r: (jnp.clip(i - r * steps, 0, steps - 1), 0))
        ] * (1 + len(parts[r]))
    return call(
        "output",
        lambda *refs: output_body(rows, steps, *refs),
        (rows * steps,),
        (*args, bias),
        specs + [fixed((8, width))],
        [shape((rows * length, width), BF16)],
        [rows_of((tile, width))],
    )[0]


class Ring:
    def __init__(self):
        self.n = lax.axis_size("mp")
        self.me = lax.axis_index("mp").astype(jnp.int32)
        self.pairs = self.n == 4
        self.core = [(i, i ^ 1) for i in range(self.n)]
        self.chip = [(i, i ^ 2) for i in range(self.n)]

    def over_core(self, value):
        return lax.ppermute(value, "mp", self.core)

    def over_chip(self, value):
        return lax.ppermute(value, "mp", self.chip)

    def gather_start(self, block):
        if self.pairs:
            return [block, self.over_chip(block)]
        return self.gather(block)

    def gather(self, block):
        if self.pairs:
            across = self.over_chip(block)
            return [block, self.over_core(block), across, self.over_core(across)]
        every = lax.all_gather(block, "mp")
        return [
            lax.dynamic_index_in_dim(every, self.me ^ j, 0, keepdims=False) for j in range(self.n)
        ]

    def scatter(self, parts, sums=False):
        parts, extra = (parts[:-1], parts[-1:]) if sums else (parts, [])
        if self.pairs:
            return [parts[0], self.over_chip(parts[1])], [*extra, *map(self.over_chip, extra)]
        stacked = jnp.stack([part.astype(F32) for part in parts])
        ordered = jnp.take(stacked, self.me ^ jnp.arange(self.n), axis=0)
        total = lax.psum_scatter(ordered, "mp", scatter_dimension=0, tiled=False)
        return [total], [lax.psum(v, "mp") for v in extra]

    def total(self, value):
        if self.pairs:
            value = value + self.over_core(value)
            return value + self.over_chip(value)
        return lax.psum(value, "mp")

    def out_start(self, weight):
        rows, groups = weight.shape[0], lax.axis_size("dp")
        if self.pairs and rows % (16 * groups) == 0:
            size = rows // groups
            piece = lax.dynamic_slice_in_dim(weight, lax.axis_index("dp") * size, size, 0)
            return self.over_chip(piece)
        return None

    def out_middle(self, piece):
        return None if piece is None else lax.all_gather(piece, "dp", axis=0, tiled=True)

    def out_end(self, weight, across):
        if across is None:
            return self.gather(weight)
        across = gate([across])[0]
        return [weight, self.over_core(weight), across, self.over_core(across)]


def tables_of(length):
    half = HEAD // 2
    rate = np.exp(np.arange(half, dtype=np.float64) * (-math.log(10000.0) / half))
    angle = np.arange(length, dtype=np.float64)[:, None] * rate[None, :]
    cosine, sine = np.cos(angle), np.sin(angle)
    return (
        jnp.asarray(np.concatenate([cosine, cosine], 1), F32),
        jnp.asarray(np.concatenate([-sine, sine], 1), F32),
    )


def local(
    history,
    depth_weights,
    segment_ids,
    first_gain,
    first_bias,
    qkv_weight,
    out_weight,
    second_gain,
    second_bias,
    up_weight,
    up_bias,
    down_weight,
    down_bias,
    cotangent,
):
    ring = Ring()
    n = ring.n
    pairs = ring.pairs
    width = history.shape[2]
    full = n * width
    row_count, length = segment_ids.shape
    rows = range(row_count)
    tables = tables_of(length)
    earlier = (segment_ids[:, None, :] < segment_ids[:, :, None]).astype(jnp.int32)
    starts = jnp.broadcast_to(jnp.sum(earlier, -1)[:, None, :], (row_count, 8, length))

    up_bias8 = jnp.broadcast_to(up_bias[None], (8, up_bias.shape[0]))

    down_bias8 = jnp.broadcast_to(down_bias[None], (8, width))
    groups = lax.axis_size("dp")
    spread = full % (128 * groups) == 0 and groups >= 4
    last = row_count - 1

    Order.last, Order.names, Order.cost = None, 0, LARGE
    vectors = jnp.stack([first_gain, first_bias, second_gain, second_bias])
    vectors = ring.gather_start(jnp.repeat(vectors, 8, 0))
    piece = ring.out_start(out_weight)
    cot_rows = [lax.slice_in_dim(cotangent, r * length, (r + 1) * length) for r in rows]
    none = [None] * row_count
    wide, low, xs, qkv, normed1, stat1 = (list(none) for _ in range(6))
    attended, logs, heads, cots = (list(none) for _ in range(4))
    hidden, normed2, stat2, activated, slope = (list(none) for _ in range(5))
    branch, up_grad, parts2, parts1 = (list(none) for _ in range(4))
    hidden_grad, grads, grad_full, qkv_grad = (list(none) for _ in range(4))
    up_bias_sum = down_bias_sum = gain2_sum = bias2_sum = 0.0

    for r in rows:
        wide[r], low[r] = average(depth_weights, history, r, length)
        if r == 0:
            xs[0] = ring.gather_start(low[0])
            if pairs:
                vectors[1], piece = gate([vectors[1], piece])
                vectors = [
                    vectors[0],
                    ring.over_core(vectors[0]),
                    vectors[1],
                    ring.over_core(vectors[1]),
                ]
            across = ring.out_middle(piece)
    vectors = jnp.concatenate(vectors, 1)
    gain1, bias1, gain2, bias2 = (vectors[8 * i : 8 * i + 8] for i in range(4))
    own1, own2 = gain1[:, :width], gain2[:, :width]
    for r in rows[1:]:
        xs[r] = ring.gather_start(gate([low[r]], xs[r - 1][1:2])[0])
    for r in rows:
        qkv[r], normed1[r], stat1[r], xs[r] = project(
            n, pairs, xs[r], gain1, bias1, tables, qkv_weight
        )
        attended[r], logs[r] = attend(starts[r], qkv[r])
        heads[r] = ring.gather_start(attended[r])
        if r == last:
            out_w = ring.out_end(out_weight, across)

    for r in rows:
        cots[r] = ring.gather_start(gate([cot_rows[r]])[0])
        got = feed(
            n,
            pairs,
            heads[r],
            xs[r],
            out_w,
            wide[r],
            gain2,
            bias2,
            up_bias8,
            up_weight,
            down_weight,
        )
        hidden[r], normed2[r], stat2[r], activated[r], slope[r], parts = got
        branch[r] = ring.scatter(parts)[0]

    def spread_over_dp(value, dim):
        return lax.psum_scatter(value, "dp", scatter_dimension=dim, tiled=True)

    if pairs:
        cot_full = join(cots, full)
        branch[0][1] = gate(branch[0][1:])[0]
    else:
        cot_full = [lax.all_gather(v, "mp", axis=1, tiled=True) for v in cot_rows]
    if spread:
        down_sum = Spread(activated, cot_full, 1, (1, 2, 4))
        down_sum.first()

    for r in rows:
        up_grad[r], up_sum, cot_sum, parts = feed_back(
            n, pairs, cot_full[r], slope[r], normed2[r], gain2, bias2, up_weight, down_weight
        )
        up_bias_sum += up_sum
        down_bias_sum += cot_sum
        parts2[r] = ring.scatter(parts, True)
        if r == 0 and pairs:
            branch[last][1] = gate(branch[last][1:])[0]

    def hidden_step(r):
        nonlocal gain2_sum, bias2_sum
        parts, row_sums = parts2[r]
        hidden_grad[r], low_grad, gain_part, bias_part = hidden_back(
            parts, cotangent, r, hidden[r], stat2[r], row_sums, own2, full
        )
        gain2_sum += gain_part
        bias2_sum += bias_part
        grads[r] = ring.gather_start(low_grad)

    hidden_step(0)
    if spread:
        up_sum = Spread(normed2, up_grad, 0, (1, 2, 4))
        up_sum.first()

        down_sum.keep_added()

    for r in rows:
        grad_full[r], attended_grad = attended_back(n, pairs, grads[r], out_weight)
        if r < last:
            hidden_step(r + 1)
        qkv_grad[r] = attend_back(starts[r], tables, qkv[r], attended_grad, logs[r])
        if r == last and spread:
            advance(down_sum)
            qkv_sum = Spread(normed1, qkv_grad, 0, (1, 2, 4))
            qkv_sum.first()
        if r > 0 and pairs:
            parts, row_sums = parts1[r - 1]
            parts[1], row_sums[1] = gate([parts[1], row_sums[1]])
        parts = project_back(n, pairs, qkv_grad[r], normed1[r], gain1, bias1, qkv_weight)
        parts1[r] = ring.scatter(parts, True)

    if spread:
        up_sum.keep_added()
        out_sum = Spread(attended, grad_full, 1, (1, 2, 4))
        out_sum.first()
    made = output(branch, hidden, down_bias8)

    grad_history, depth_sum, gain1_sum, bias1_sum = None, 0.0, 0.0, 0.0
    for r in rows:
        parts, row_sums = parts1[r]
        grad_history, depth_part, gain_part, bias_part = average_back(
            depth_weights,
            parts,
            wide[r],
            stat1[r],
            row_sums,
            (own1, full),
            hidden_grad[r],
            history,
            r,
            grad_history,
        )
        depth_sum += depth_part
        gain1_sum += gain_part
        bias1_sum += bias_part
        if r == 0:
            if pairs:
                parts, row_sums = parts1[last]
                parts[1], row_sums[1] = gate([parts[1], row_sums[1]])
            if spread:
                qkv_sum.keep_added()

    if spread:
        down_sum.coming = gate([down_sum.coming])[0]
        advance(up_sum)
        out_sum.keep_added()
        advance(qkv_sum, out_sum)
    else:
        qkv_sum = spread_over_dp(weight_grad(normed1, qkv_grad), 0)
        out_sum = spread_over_dp(weight_grad(attended, grad_full), 1)
        down_sum = spread_over_dp(weight_grad(activated, cot_full), 1)
        up_sum = spread_over_dp(weight_grad(normed2, up_grad), 0)
    down_total, up_total, out_total, qkv_total = finish([down_sum], [up_sum], [out_sum], [qkv_sum])
    vectors = [up_bias_sum, down_bias_sum, gain2_sum, bias2_sum, gain1_sum, bias1_sum]
    totals, depth_grad = sums([jnp.sum(v, 0) for v in vectors], jnp.sum(depth_sum, (1, 2)))
    return (
        made,
        grad_history,
        depth_grad,
        totals[4],
        totals[5],
        qkv_total,
        out_total,
        totals[2],
        totals[3],
        up_total,
        totals[0],
        down_total,
        totals[1],
    )


def solution(mesh):
    placed = (
        P(None, "dp", "mp"),
        P(),
        P("dp", None),
        P("mp"),
        P("mp"),
        P(None, "mp"),
        P("mp", None),
        P("mp"),
        P("mp"),
        P(None, "mp"),
        P("mp"),
        P("mp", None),
        P("mp"),
        P("dp", "mp"),
    )
    return jax.shard_map(
        local,
        mesh=mesh,
        in_specs=placed,
        out_specs=(
            P("dp", "mp"),
            P(None, "dp", "mp"),
            P(),
            P("mp"),
            P("mp"),
            P("dp", "mp"),
            P("mp", "dp"),
            P("mp"),
            P("mp"),
            P("dp", "mp"),
            P("mp"),
            P("mp", "dp"),
            P("mp"),
        ),
        check_vma=False,
    )
```

```python
import math

import jax
import jax.numpy as jnp
import numpy as np
from jax import lax
from jax.experimental import pallas as pl
from jax.experimental.pallas import tpu as pltpu
from jax.sharding import PartitionSpec as P

HEAD = 128
MAX_DOC = 512
EPSILON = 1e-05
SQRT_HALF = 0.7071067811865476
INV_ROOT_TWO_PI = 0.3989422804014327
LOG2E = 1.4426950408889634
SCALE = HEAD ** (-0.5)
MIB = 2**20
BF16 = jnp.bfloat16
F32 = jnp.float32


def dot_nn(a, b):
    return jnp.dot(a, b, preferred_element_type=F32)


def dot_nt(a, b):
    return lax.dot_general(a, b, (((1,), (1,)), ((), ())), preferred_element_type=F32)


def dot_tn(a, b):
    return lax.dot_general(a, b, (((0,), (0,)), ((), ())), preferred_element_type=F32)


LARGE, TINY = 10**12, 10**4


class Order:
    last = None
    names = 0
    cost = LARGE

    @staticmethod
    def name(remote):
        Order.names += remote
        return Order.names - 1 if remote else None


def call(
    name, body, grid, args, in_specs, outs, out_specs, scratch=(), prefetch=0, after=(), aliases=None, remote=False
):
    count = len(args)
    extra = [*after]
    if Order.last is not None and not any(Order.last is a for a in args):
        extra.append(Order.last)

    def without_extra(*refs):
        body(*refs[:count], *refs[count + len(extra) :])

    got = pl.pallas_call(
        without_extra,
        grid_spec=pltpu.PrefetchScalarGridSpec(
            num_scalar_prefetch=prefetch,
            grid=grid,
            in_specs=list(in_specs) + [ANY] * len(extra),
            out_specs=out_specs,
            scratch_shapes=list(scratch),
        ),
        out_shape=outs,
        input_output_aliases=aliases or {},
        compiler_params=pltpu.CompilerParams(
            vmem_limit_bytes=60 * MIB, collective_id=Order.name(remote), has_side_effects=remote
        ),
        cost_estimate=pl.CostEstimate(flops=Order.cost, bytes_accessed=Order.cost // 10**4, transcendentals=0),
        name=name,
    )(*args, *extra)
    fresh = [v for i, v in enumerate(got) if i not in (aliases or {}).values()]
    Order.last = min(fresh or got, key=lambda v: v.size)
    return got


def shape(dims, dtype):
    return jax.ShapeDtypeStruct(dims, dtype)


def sent(dims, dtype):
    return pltpu.HBM(dims, dtype)


SMEM = pl.BlockSpec(memory_space=pltpu.SMEM)
ANY = pl.BlockSpec(memory_space=pl.ANY)


def gate(arrays, after=()):
    arrays = list(arrays)
    return call(
        "gate",
        lambda *refs: None,
        (1,),
        arrays,
        [ANY] * len(arrays),
        [shape(a.shape, a.dtype) for a in arrays],
        [ANY] * len(arrays),
        after=after,
        aliases={i: i for i in range(len(arrays))},
    )


def rows_of(block):
    return pl.BlockSpec(block, lambda i: (i, 0))


def cols_of(block):
    return pl.BlockSpec(block, lambda i: (0, i))


def fixed(block):
    return pl.BlockSpec(block, lambda i: (0,) * len(block))


def flip(me, j):
    there, bit = me, 1
    while bit <= j:
        if j & bit:
            there = there + bit * (1 - 2 * ((me // bit) % 2))
        bit *= 2
    return there


def place_of(me, j, width):
    return pl.ds(pl.multiple_of(flip(me, j) * width, width), width)


def greet():
    barrier = pltpu.get_barrier_semaphore()
    sibling = flip(lax.axis_index("mp"), 1)
    pl.semaphore_signal(
        barrier, inc=1, device_id={"mp": sibling}, device_id_type=pl.DeviceIdType.MESH
    )
    pl.semaphore_wait(barrier, 1)


def to_sibling(source, target, sems, at):
    return pltpu.make_async_remote_copy(
        src_ref=source,
        dst_ref=target,
        send_sem=sems.at[0, at],
        recv_sem=sems.at[1, at],
        device_id={"mp": flip(lax.axis_index("mp"), 1)},
        device_id_type=pl.DeviceIdType.MESH,
    )


class Gathered:
    def __init__(self, refs, pairs, steps):
        self.pairs, self.steps = pairs, steps
        self.blocks, self.whole = refs[:2] if pairs else refs, refs[2:4] if pairs else ()

    @staticmethod
    def specs(blocks, pairs, tile):
        width = blocks[0].shape[1]
        return [rows_of((tile, width))] * len(blocks) + ([ANY] * 2 if pairs else [])

    @staticmethod
    def scratch(blocks, pairs, steps):
        if not pairs:
            return []
        return [pltpu.VMEM((2, *blocks[0].shape), BF16), pltpu.SemaphoreType.DMA((2, 2 * steps))]

    def attach(self, refs):
        if self.pairs:
            self.came, self.sems = refs
        return self

    def copies(self, step):
        tile = self.blocks[0].shape[0]
        rows = pl.ds(pl.multiple_of(step * tile, tile), tile)
        return [
            to_sibling(self.whole[k].at[rows, :], self.came.at[k, rows, :], self.sems, 2 * step + k)
            for k in range(2)
        ]

    def start(self):
        if self.pairs:
            for step in range(self.steps):
                for one in self.copies(step):
                    one.start()

    def refs(self):
        if not self.pairs:
            return self.blocks
        step = pl.program_id(0)
        tile = self.blocks[0].shape[0]
        for one in self.copies(step):
            one.wait()
        rows = pl.ds(pl.multiple_of(step * tile, tile), tile)
        return [self.blocks[0], self.came.at[0, rows, :], self.blocks[1], self.came.at[1, rows, :]]


EXTRA = 16


def pack(sums, width):
    rows = []
    for s in range(2):
        rest = sums[s : s + 1, :]
        for _ in range(3):
            piece = rest.astype(BF16).astype(F32)
            rest = rest - piece
            rows += [piece[:, h : h + width] for h in range(0, sums.shape[1], width)]
    assert len(rows) <= EXTRA
    rows += [jnp.zeros((1, width), F32)] * (EXTRA - len(rows))
    return jnp.concatenate(rows).astype(BF16)


def unpack(packed, target):
    width = packed.shape[1]
    per = target.shape[1] // width
    value = packed[...].astype(F32)
    for s in range(2):
        for h in range(per):
            at = [(3 * s + p) * per + h for p in range(3)]
            total = value[at[0] : at[0] + 1] + value[at[1] : at[1] + 1] + value[at[2] : at[2] + 1]
            target[s : s + 1, h * width : (h + 1) * width] = total


class Scattered:
    def __init__(self, pairs, n, steps, with_sums):
        self.pairs, self.n, self.steps, self.with_sums = pairs, n, steps, with_sums

    def outs(self, length, width):
        tile = length // self.steps
        if self.pairs:
            high = length + EXTRA * self.with_sums
            outs = [shape((length, width), BF16), sent((high, width), BF16)]
            specs = [fixed((length, width)), fixed((high, width))]
            if self.with_sums:
                outs, specs = outs + [shape((8, length), F32)], specs + [fixed((8, length))]
            return outs, specs
        outs, specs = [shape((length, width), BF16)] * self.n, [rows_of((tile, width))] * self.n
        if self.with_sums:
            outs, specs = outs + [shape((8, length), F32)], specs + [cols_of((8, tile))]
        return outs, specs

    def count(self):
        return (2 if self.pairs else self.n) + self.with_sums

    def scratch(self, length, width):
        if not self.pairs:
            return []
        tile = length // self.steps
        block = pltpu.VMEM((self.steps, 2, tile, width), BF16)
        made = [block, block, pltpu.VMEM((2, 2, tile, width), F32)]
        if self.with_sums:
            made += [pltpu.VMEM((self.steps, 8, tile), F32)] * 3
        return made + [pltpu.SemaphoreType.DMA((2, 3 * self.steps))]

    def attach(self, outs, scratch):
        self.out = outs
        if self.pairs:
            self.send, self.came, self.kept = scratch[:3]
            self.sums = scratch[3:-1]
            self.sems = scratch[-1]
        return self

    def copies(self, step):
        made = [
            to_sibling(self.send.at[step, k], self.came.at[step, k], self.sems, 3 * step + k)
            for k in range(2)
        ]
        if self.with_sums:
            made.append(to_sibling(self.sums[0].at[step], self.sums[1].at[step], self.sems, 3 * step + 2))
        return made

    def put(self, j, value):
        step = pl.program_id(0)
        if not self.pairs:
            self.out[j][...] = value.astype(BF16)
        elif j % 2:
            self.send[step, j // 2] = value.astype(BF16)
        else:
            self.kept[step % 2, j // 2] = value

    def take(self, step):
        tile = self.kept.shape[2]
        for one in self.copies(step):
            one.wait()
        rows = pl.ds(pl.multiple_of(step * tile, tile), tile)
        for k in range(2):
            total = self.kept[step % 2, k] + self.came[step, k].astype(F32)
            self.out[k][rows, :] = total.astype(BF16)
        if self.with_sums:
            self.out[2][:, rows] = self.sums[2][step] + self.sums[1][step]

    def finish(self, sums=None):
        if not self.pairs:
            if sums is not None:
                self.out[-1][...] = sums
            return
        step = pl.program_id(0)
        if sums is not None:
            self.sums[0][step] = sums
            self.sums[2][step] = sums
        for one in self.copies(step):
            one.start()

        @pl.when(step > 0)
        def _():
            self.take(step - 1)

        @pl.when(step == self.steps - 1)
        def _():
            self.take(step)
            if self.with_sums:
                length, width = self.out[0].shape
                self.out[1][length:, :] = pack(self.out[2][...], width)


def with_weights(copies, work, remote=False, gathered=()):
    @pl.when(pl.program_id(0) == 0)
    def _():
        for one in copies:
            one.start()
        if remote:
            greet()
        for one in gathered:
            one.start()

        def wait(some):
            for one in some:
                one.wait()

        work(wait)

    @pl.when(pl.program_id(0) != 0)
    def _():
        work(lambda some: None)


def row_blocks(me, n, width, source, target, sems, base):
    return [
        pltpu.make_async_copy(
            source.at[place_of(me, j, width), :],
            target.at[pl.ds(j * width, width), :],
            sems.at[base + j],
        )
        for j in range(n)
    ]


def col_blocks(me, n, width, source, target, sems, base):
    return [
        pltpu.make_async_copy(
            source.at[:, place_of(me, j, width)],
            target.at[:, pl.ds(j * width, width)],
            sems.at[base + j],
        )
        for j in range(n)
    ]


def stat_columns(first, second):
    lane = lax.broadcasted_iota(jnp.int32, (first.shape[0], 128), 1)
    return jnp.where(lane == 0, first, jnp.where(lane == 1, second, 0.0))


def fold_rows(values):
    return jnp.sum(values.reshape(values.shape[0] // 8, 8, values.shape[1]), 0)


def accumulate(ref, value):
    @pl.when(pl.program_id(0) == 0)
    def _():
        ref[...] = value

    @pl.when(pl.program_id(0) != 0)
    def _():
        ref[...] += value


def average_body(weights, history, wide, low):
    chunk = min(32, wide.shape[0])
    for t in range(wide.shape[0] // chunk):
        rows = slice(t * chunk, (t + 1) * chunk)
        total = weights[0] * history[0, rows, :].astype(F32)
        for j in range(1, history.shape[0]):
            total += weights[j] * history[j, rows, :].astype(F32)
        wide[rows, :] = total
        low[rows, :] = total.astype(BF16)


def average(weights, history, row, length):
    count, _, width = history.shape
    tile = min(256, length)
    steps = length // tile
    return call(
        "average",
        average_body,
        (steps,),
        (weights, history),
        [SMEM, pl.BlockSpec((count, tile, width), lambda i: (0, row * steps + i, 0))],
        [shape((length, width), F32), sent((length, width), BF16)],
        [rows_of((tile, width))] * 2,
    )


def project_body(n, pairs, steps, *refs):
    count = 4 if pairs else n
    x = Gathered(refs[:count], pairs, steps)
    gain, bias, cosine, sine, weight, qkv, normed, stat = refs[count : count + 8]
    refs = refs[count + 8 :]
    shared = refs[:2] if pairs else ()
    held, joined, sems, *more = refs[len(shared) :]
    x.attach(more)
    me = lax.axis_index("mp")
    tile, width = x.blocks[0].shape
    full = n * width
    heads = held.shape[1] // (3 * HEAD)
    sub = min(256, tile)
    copies = row_blocks(me, n, width, weight, held, sems, 0)

    def work(wait):
        xs = x.refs()
        for out, k in zip(shared, (1, 3)):
            out[...] = xs[k][...]
        for t in range(tile // sub):
            rows = slice(t * sub, (t + 1) * sub)
            total = square = 0.0
            for one in xs:
                value = one[rows, :].astype(F32)
                total += jnp.sum(value, 1, keepdims=True)
                square += jnp.sum(value * value, 1, keepdims=True)
            mean = total / full
            inv = lax.rsqrt(square / full - mean * mean + EPSILON)
            stat[rows, :] = stat_columns(mean, inv)
            for j, one in enumerate(xs):
                part = slice(j * width, (j + 1) * width)
                value = (one[rows, :].astype(F32) - mean) * inv * gain[0:1, part] + bias[0:1, part]
                joined[rows, part] = value.astype(BF16)
                normed[rows, place_of(me, j, width)] = value.astype(BF16)
            if t == 0:
                wait(copies)
            for h in range(heads):
                base = 3 * h * HEAD
                out = dot_nn(joined[rows, :], held[:, base : base + 3 * HEAD])
                for s in range(2):
                    v = out[:, s * HEAD : (s + 1) * HEAD]
                    turned = v * cosine[rows, :] + pltpu.roll(v, HEAD // 2, 1) * sine[rows, :]
                    qkv[rows, base + s * HEAD : base + (s + 1) * HEAD] = turned.astype(BF16)
                qkv[rows, base + 2 * HEAD : base + 3 * HEAD] = out[:, 2 * HEAD :].astype(BF16)

    with_weights(copies, work, pairs, [x])


def project(n, pairs, xs, gain, bias, tables, weight):
    length, width = xs[0].shape
    full, out = weight.shape
    tile = min(512, length)
    steps = length // tile
    got = call(
        "project",
        lambda *refs: project_body(n, pairs, steps, *refs),
        (steps,),
        (*xs, *(xs if pairs else ()), gain, bias, *tables, weight),
        Gathered.specs(xs, pairs, tile)
        + [fixed((8, full))] * 2
        + [rows_of((tile, HEAD))] * 2
        + [ANY],
        [shape((length, out), BF16), shape((length, full), BF16), shape((length, 128), F32)]
        + [shape((length, width), BF16)] * (2 * pairs),
        [rows_of((tile, out)), rows_of((tile, full)), rows_of((tile, 128))]
        + [rows_of((tile, width))] * (2 * pairs),
        scratch=[
            pltpu.VMEM((full, out), BF16),
            pltpu.VMEM((tile, full), BF16),
            pltpu.SemaphoreType.DMA((n,)),
        ]
        + Gathered.scratch(xs, pairs, steps),
        remote=pairs,
    )
    return *got[:3], [xs[0], got[3], xs[1], got[4]] if pairs else xs


def windows(length):
    block = min(256, length)
    for i in range(length // block):
        low = max(0, i * block - (MAX_DOC - 1)) // block * block
        yield slice(i * block, (i + 1) * block), slice(low, (i + 1) * block)


def score_mask(start, q_part, k_part):
    dims = (k_part.stop - k_part.start, q_part.stop - q_part.start)
    k_pos = lax.broadcasted_iota(jnp.int32, dims, 0) + k_part.start
    q_pos = lax.broadcasted_iota(jnp.int32, dims, 1) + q_part.start
    return (k_pos >= start[0:1, q_part]) & (k_pos <= q_pos)


def attend_body(start, qkv, out, logs):
    length = qkv.shape[0]
    value_t = qkv[:, 2 * HEAD :].T
    for q_part, k_part in windows(length):
        query, key = qkv[q_part, :HEAD], qkv[k_part, HEAD : 2 * HEAD]
        scores = dot_nt(key, query) * (SCALE * LOG2E)
        scores = jnp.where(score_mask(start, q_part, k_part), scores, -1e30)
        top = jnp.max(scores, 0, keepdims=True)
        probs = jnp.exp2(scores - top)
        total = jnp.sum(probs, 0, keepdims=True)
        logs[0, :, q_part] = jnp.broadcast_to(top + jnp.log2(total), (8, q_part.stop - q_part.start))
        got = dot_nn(value_t[:, k_part], probs.astype(BF16)) / total
        out[q_part, :] = got.T.astype(BF16)


def attend(start, qkv):
    length, width = qkv.shape
    heads = width // (3 * HEAD)
    return call(
        "attend",
        attend_body,
        (heads,),
        (start, qkv),
        [fixed((8, length)), cols_of((length, 3 * HEAD))],
        [sent((length, heads * HEAD), BF16), shape((heads, 8, length), F32)],
        [cols_of((length, HEAD)), pl.BlockSpec((1, 8, length), lambda i: (i, 0, 0))],
    )


def attend_back_body(start, cosine, sine, qkv, grad, logs, out, key_sum, value_sum):
    length = qkv.shape[0]
    key_t = qkv[:, HEAD : 2 * HEAD].T
    key_sum[...] = jnp.zeros_like(key_sum)
    value_sum[...] = jnp.zeros_like(value_sum)

    def turn_back(v, part):
        return (
            v * cosine[part, :] - pltpu.roll(v, HEAD // 2, 1) * sine[part, :]
        ).astype(BF16)

    for q_part, k_part in windows(length):
        query, key = qkv[q_part, :HEAD], qkv[k_part, HEAD : 2 * HEAD]
        value, g = qkv[k_part, 2 * HEAD :], grad[q_part, :]
        scores = dot_nt(key, query) * (SCALE * LOG2E) - logs[0, 0:1, q_part]
        probs = jnp.exp2(jnp.where(score_mask(start, q_part, k_part), scores, -1e30))
        prob_grad = dot_nt(value, g)
        mean = jnp.sum(prob_grad * probs, 0, keepdims=True)
        score_grad = (probs * (prob_grad - mean)).astype(BF16)
        value_sum[k_part, :] += dot_nn(probs.astype(BF16), g)
        key_sum[k_part, :] += dot_nn(score_grad, query)
        query_grad = dot_nn(key_t[:, k_part], score_grad) * SCALE
        out[q_part, :HEAD] = turn_back(query_grad.T, q_part)
    for q_part, _ in windows(length):
        out[q_part, HEAD : 2 * HEAD] = turn_back(key_sum[q_part, :] * SCALE, q_part)
        out[q_part, 2 * HEAD :] = value_sum[q_part, :].astype(BF16)


def attend_back(start, tables, qkv, grad, logs):
    length, width = qkv.shape
    heads = width // (3 * HEAD)
    return call(
        "attend_back",
        attend_back_body,
        (heads,),
        (start, *tables, qkv, grad, logs),
        [fixed((8, length))]
        + [fixed((length, HEAD))] * 2
        + [
            cols_of((length, 3 * HEAD)),
            cols_of((length, HEAD)),
            pl.BlockSpec((1, 8, length), lambda i: (i, 0, 0)),
        ],
        [shape((length, width), BF16)],
        [cols_of((length, 3 * HEAD))],
        scratch=[pltpu.VMEM((length, HEAD), F32)] * 2,
    )[0]


def feed_body(n, pairs, steps, *refs):
    count = 4 if pairs else n
    attended = Gathered(refs[:count], pairs, steps)
    refs = refs[count:]
    xs, outs_w = refs[: n - 1], refs[n - 1 : 2 * n - 1]
    own, gain, bias, up_bias, up_weight, down_weight = refs[2 * n - 1 : 2 * n + 5]
    refs = refs[2 * n + 5 :]
    hidden, normed, stat, activated, slope = refs[:5]
    refs = refs[5:]
    parts = Scattered(pairs, n, steps, False)
    part_outs, refs = refs[: parts.count()], refs[parts.count() :]
    out_held, up_held, down_held, joined, whole, sems, *refs = refs
    if pairs:
        attended.attach(refs[:2])
        refs = refs[2:]
    parts.attach(part_outs, refs)
    me = lax.axis_index("mp")
    width = own.shape[1]
    full = n * width
    inner = up_held.shape[1]
    out_copies = []
    for j in range(n):
        for k in range(n):
            out_copies.append(
                pltpu.make_async_copy(
                    outs_w[k].at[:, place_of(me, j, width)],
                    out_held.at[pl.ds(k * width, width), pl.ds(j * width, width)],
                    sems.at[j * n + k],
                )
            )
    up_copies = row_blocks(me, n, width, up_weight, up_held, sems, n * n)
    down_copies = col_blocks(me, n, width, down_weight, down_held, sems, n * n + n)

    def work(wait):
        for j, one in enumerate(attended.refs()):
            joined[:, j * width : (j + 1) * width] = one[...]
        total = square = 0.0
        for j in range(n):
            wait(out_copies[j * n : (j + 1) * n])
            part = slice(j * width, (j + 1) * width)
            base = own[...] if j == 0 else xs[j - 1][...].astype(F32)
            value = base + dot_nn(joined[...], out_held[:, part])
            whole[:, part] = value
            if j == 0:
                hidden[...] = value
            total += jnp.sum(value, 1, keepdims=True)
            square += jnp.sum(value * value, 1, keepdims=True)
        mean = total / full
        inv = lax.rsqrt(square / full - mean * mean + EPSILON)
        stat[...] = stat_columns(mean, inv)
        for j in range(n):
            part = slice(j * width, (j + 1) * width)
            value = ((whole[:, part] - mean) * inv * gain[0:1, part] + bias[0:1, part]).astype(BF16)
            joined[:, part] = value
            normed[:, place_of(me, j, width)] = value
        wait(up_copies)
        step = divisor(inner, 512)
        for c in range(inner // step):
            part = slice(c * step, (c + 1) * step)
            up = dot_nn(joined[...], up_held[:, part]) + up_bias[0:1, part]
            half = 0.5 * (1.0 + lax.erf(up * SQRT_HALF))
            activated[:, part] = (up * half).astype(BF16)
            slope[:, part] = (half + up * INV_ROOT_TWO_PI * jnp.exp(-0.5 * up * up)).astype(BF16)
        wait(down_copies)
        for j in range(n):
            parts.put(j, dot_nn(activated[...], down_held[:, j * width : (j + 1) * width]))

    with_weights(out_copies + up_copies + down_copies, work, pairs, [attended])
    parts.finish()


def feed(n, pairs, attended, xs, outs_w, own, gain, bias, up_bias, up_weight, down_weight):
    length, width = own.shape
    full, inner = up_weight.shape
    tile = min(256, length)
    steps = length // tile
    parts = Scattered(pairs, n, steps, False)
    part_outs, part_specs = parts.outs(length, width)
    twice = tuple(attended) if pairs else ()
    got = call(
        "feed",
        lambda *refs: feed_body(n, pairs, steps, *refs),
        (steps,),
        (
            *attended,
            *twice,
            *xs[1:],
            *outs_w,
            own,
            gain,
            bias,
            up_bias,
            up_weight,
            down_weight,
        ),
        Gathered.specs(attended, pairs, tile)
        + [rows_of((tile, width))] * (n - 1)
        + [ANY] * n
        + [rows_of((tile, width))]
        + [fixed((8, full))] * 2
        + [fixed((8, inner))]
        + [ANY] * 2,
        [
            shape((length, width), F32),
            shape((length, full), BF16),
            shape((length, 128), F32),
            shape((length, inner), BF16),
            shape((length, inner), BF16),
        ]
        + part_outs,
        [
            rows_of((tile, width)),
            rows_of((tile, full)),
            rows_of((tile, 128)),
            rows_of((tile, inner)),
            rows_of((tile, inner)),
        ]
        + part_specs,
        scratch=[
            pltpu.VMEM((full, full), BF16),
            pltpu.VMEM((full, inner), BF16),
            pltpu.VMEM((inner, full), BF16),
            pltpu.VMEM((tile, full), BF16),
            pltpu.VMEM((tile, full), F32),
            pltpu.SemaphoreType.DMA((n * n + 2 * n,)),
        ]
        + Gathered.scratch(attended, pairs, steps)
        + parts.scratch(length, width),
        remote=pairs,
    )
    return (*got[:5], got[5:])


def row_stats(total, weighted):
    return stat_columns(total, weighted).T[0:8, :]


def norm_sums(parts, n, product, normed, gain, bias, me):
    width = gain.shape[1] // n
    total = weighted = 0.0
    for j in range(n):
        part = slice(j * width, (j + 1) * width)
        value = product(j)
        parts.put(j, value)
        total += jnp.sum(value * gain[0:1, part], 1, keepdims=True)
        there = normed[:, place_of(me, j, width)].astype(F32)
        weighted += jnp.sum(value * (there - bias[0:1, part]), 1, keepdims=True)
    return row_stats(total, weighted)


def join_body(count, steps, *refs):
    gathered = [Gathered(refs[4 * i : 4 * i + 4], True, steps) for i in range(count)]
    outs, scratch = refs[4 * count : 5 * count], refs[5 * count :]
    for i, one in enumerate(gathered):
        one.attach(scratch[2 * i : 2 * i + 2])
    me = lax.axis_index("mp")

    def work(wait):
        for one, out in zip(gathered, outs):
            for j, block in enumerate(one.refs()):
                out[:, place_of(me, j, block.shape[1])] = block[...]

    with_weights([], work, True, gathered)


def join(gathered, full):
    length = gathered[0][0].shape[0]
    tile = min(256, length)
    steps = length // tile
    args, specs, scratch = [], [], []
    for one in gathered:
        args += [*one, *one]
        specs += Gathered.specs(one, True, tile)
        scratch += Gathered.scratch(one, True, steps)
    return call(
        "join",
        lambda *refs: join_body(len(gathered), steps, *refs),
        (steps,),
        args,
        specs,
        [shape((length, full), BF16)] * len(gathered),
        [rows_of((tile, full))] * len(gathered),
        scratch=scratch,
        remote=True,
    )


def feed_back_body(n, pairs, steps, *refs):
    cot, refs = refs[0], refs[1:]
    slope, normed, gain, bias, up_weight, down_weight, up_grad, up_bias_sum, cot_sum = refs[:9]
    refs = refs[9:]
    parts = Scattered(pairs, n, steps, True)
    part_outs, refs = refs[: parts.count()], refs[parts.count() :]
    up_held, down_held, row_sums, sems, *refs = refs
    parts.attach(part_outs, refs)
    me = lax.axis_index("mp")
    inner = up_held.shape[1]
    width = gain.shape[1] // n
    step = divisor(inner, 512)
    down_copies = [pltpu.make_async_copy(down_weight, down_held, sems.at[n])]
    up_copies = row_blocks(me, n, width, up_weight, up_held, sems, 0)

    def work(wait):
        accumulate(cot_sum, fold_rows(cot[:, place_of(me, 0, width)].astype(F32)))
        wait(down_copies)
        bias_parts = []
        for c in range(inner // step):
            part = slice(c * step, (c + 1) * step)
            value = dot_nt(cot[...], down_held[part, :]) * slope[:, part].astype(F32)
            low = value.astype(BF16)
            up_grad[:, part] = low
            bias_parts.append(fold_rows(low.astype(F32)))
        accumulate(up_bias_sum, jnp.concatenate(bias_parts, 1))
        wait(up_copies)
        row_sums[...] = norm_sums(
            parts,
            n,
            lambda j: dot_nt(up_grad[...], up_held[j * width : (j + 1) * width, :]),
            normed,
            gain,
            bias,
            me,
        )

    with_weights(down_copies + up_copies, work, pairs)
    parts.finish(row_sums[...])


def feed_back(n, pairs, cot, slope, normed, gain, bias, up_weight, down_weight):
    length, full = normed.shape
    width = full // n
    inner = up_weight.shape[1]
    tile = min(256, length)
    steps = length // tile
    parts = Scattered(pairs, n, steps, True)
    part_outs, part_specs = parts.outs(length, width)
    got = call(
        "feed_back",
        lambda *refs: feed_back_body(n, pairs, steps, *refs),
        (steps,),
        (cot, slope, normed, gain, bias, up_weight, down_weight),
        [rows_of((tile, full)), rows_of((tile, inner)), rows_of((tile, full))]
        + [fixed((8, full))] * 2
        + [ANY] * 2,
        [shape((length, inner), BF16), shape((8, inner), F32), shape((8, width), F32)] + part_outs,
        [rows_of((tile, inner)), fixed((8, inner)), fixed((8, width))] + part_specs,
        scratch=[
            pltpu.VMEM((full, inner), BF16),
            pltpu.VMEM((inner, full), BF16),
            pltpu.VMEM((8, tile), F32),
            pltpu.SemaphoreType.DMA((n + 1,)),
        ]
        + parts.scratch(length, width),
        remote=pairs,
    )
    return (*got[:3], got[3:])


def norm_back(refs, n_parts, source, stat, sums, gain, full):
    grad = refs[0][...].astype(F32)
    for ref in refs[1:n_parts]:
        grad += ref[...].astype(F32)
    columns = sums[0][...]
    if len(sums) > 1:
        packed, far = sums[1:]

        @pl.when(pl.program_id(0) == 0)
        def _():
            far[...] = jnp.zeros_like(far)
            unpack(packed, far)

        tile = refs[0].shape[0]
        columns += far[:, pl.ds(pl.multiple_of(pl.program_id(0) * tile, tile), tile)]
    columns = columns.T
    mean, inv = stat[:, 0:1], stat[:, 1:2]
    scaled = (source[...] - mean) * inv
    back = inv * (
        grad * gain[0:1, :] - columns[:, 0:1] * (1.0 / full) - scaled * (columns[:, 1:2] * (1.0 / full))
    )
    return back, fold_rows(grad * scaled), fold_rows(grad)


def sum_specs(sums, tile, length):
    far = [pl.BlockSpec((EXTRA, v.shape[1]), lambda i: (length // EXTRA, 0)) for v in sums[1:]]
    return [cols_of((8, tile)), *far]


def hidden_back_body(k, m, full, *refs):
    parts, sums = refs[:k], refs[k : k + m]
    cot, hidden, stat, gain, wide, low, gain_sum, bias_sum, *more = refs[k + m :]
    sums = (*sums, *more)
    back, gain_part, bias_part = norm_back(parts, k, hidden, stat, sums, gain, full)
    value = cot[...].astype(F32) + back
    wide[...] = value
    low[...] = value.astype(BF16)
    accumulate(gain_sum, gain_part)
    accumulate(bias_sum, bias_part)


def hidden_back(parts, cotangent, row, hidden, stat, sums, gain, full):
    k, m, (length, width) = len(parts), len(sums), hidden.shape
    tile = min(256, length)
    steps = length // tile
    return call(
        "hidden_back",
        lambda *refs: hidden_back_body(k, m, full, *refs),
        (steps,),
        (*parts, *sums, cotangent, hidden, stat, gain),
        [rows_of((tile, width))] * k
        + sum_specs(sums, tile, length)
        + [
            pl.BlockSpec((tile, width), lambda i: (row * steps + i, 0)),
            rows_of((tile, width)),
            rows_of((tile, 128)),
            fixed((8, width)),
        ],
        [shape((length, width), F32), sent((length, width), BF16)] + [shape((8, width), F32)] * 2,
        [rows_of((tile, width))] * 2 + [fixed((8, width))] * 2,
        scratch=[pltpu.VMEM((8, length), F32)] * (m - 1),
    )


def attended_back_body(n, pairs, steps, *refs):
    count = 4 if pairs else n
    grads = Gathered(refs[:count], pairs, steps)
    weight, joined, out, *more = refs[count:]
    grads.attach(more)
    me = lax.axis_index("mp")
    width = grads.blocks[0].shape[1]

    def work(wait):
        for j, one in enumerate(grads.refs()):
            joined[:, place_of(me, j, width)] = one[...]
        out[...] = dot_nt(joined[...], weight[...]).astype(BF16)

    with_weights([], work, pairs, [grads])


def attended_back(n, pairs, grads, weight):
    length, width = grads[0].shape
    rows, full = weight.shape
    tile = min(256, length)
    steps = length // tile
    return call(
        "attended_back",
        lambda *refs: attended_back_body(n, pairs, steps, *refs),
        (steps,),
        (*grads, *(grads if pairs else ()), weight),
        Gathered.specs(grads, pairs, tile) + [fixed((rows, full))],
        [shape((length, full), BF16), shape((length, rows), BF16)],
        [rows_of((tile, full)), rows_of((tile, rows))],
        scratch=Gathered.scratch(grads, pairs, steps),
        remote=pairs,
    )


def project_back_body(n, pairs, steps, grad, normed, gain, bias, weight, *refs):
    parts = Scattered(pairs, n, steps, True)
    part_outs, refs = refs[: parts.count()], refs[parts.count() :]
    held, row_sums, sems, *refs = refs
    parts.attach(part_outs, refs)
    me = lax.axis_index("mp")
    width = gain.shape[1] // n
    copies = row_blocks(me, n, width, weight, held, sems, 0)

    def work(wait):
        def product(j):
            wait(copies[j : j + 1])
            return dot_nt(grad[...], held[j * width : (j + 1) * width, :])

        row_sums[...] = norm_sums(parts, n, product, normed, gain, bias, me)

    with_weights(copies, work, pairs)
    parts.finish(row_sums[...])


def project_back(n, pairs, grad, normed, gain, bias, weight):
    length, out = grad.shape
    full = weight.shape[0]
    width = full // n
    tile = min(256, length)
    steps = length // tile
    parts = Scattered(pairs, n, steps, True)
    part_outs, part_specs = parts.outs(length, width)
    return call(
        "project_back",
        lambda *refs: project_back_body(n, pairs, steps, *refs),
        (steps,),
        (grad, normed, gain, bias, weight),
        [rows_of((tile, out)), rows_of((tile, full))] + [fixed((8, full))] * 2 + [ANY],
        part_outs,
        part_specs,
        scratch=[
            pltpu.VMEM((full, out), BF16),
            pltpu.VMEM((8, tile), F32),
            pltpu.SemaphoreType.DMA((n,)),
        ]
        + parts.scratch(length, width),
        remote=pairs,
    )


def average_back_body(k, m, full, count, *refs):
    weights, parts, sums = refs[0], refs[1 : k + 1], refs[k + 1 : k + m + 1]
    source, stat, gain, hidden_grad, history = refs[k + m + 1 : k + m + 6]
    refs, more = (refs[:-1], refs[-1:]) if m > 1 else (refs, ())
    sums = (*sums, *more)
    grad_history, depth_sum, gain_sum, bias_sum, held = refs[-5:]
    back, gain_part, bias_part = norm_back(parts, k, source, stat, sums, gain, full)
    held[...] = hidden_grad[...] + back
    accumulate(gain_sum, gain_part)
    accumulate(bias_sum, bias_part)
    lanes = held.shape[1] // 128
    chunk = min(32, held.shape[0])
    folded = [0.0] * count
    for t in range(held.shape[0] // chunk):
        rows = slice(t * chunk, (t + 1) * chunk)
        value = held[rows, :]
        for j in range(count):
            grad_history[j, rows, :] = (weights[j] * value).astype(BF16)
            product = fold_rows(value * history[j, rows, :].astype(F32))
            for c in range(lanes):
                folded[j] = folded[j] + product[:, c * 128 : (c + 1) * 128]
    for j in range(count):
        accumulate(depth_sum.at[j], folded[j])


def average_back(weights, parts, source, stat, sums, gain, hidden_grad, history, row, made):
    k, m, (length, width) = len(parts), len(sums), source.shape
    count = history.shape[0]
    tile = min(256, length)
    steps = length // tile
    full = gain[1]
    block = pl.BlockSpec((count, tile, width), lambda i: (0, row * steps + i, 0))
    args = (weights, *parts, *sums, source, stat, gain[0], hidden_grad, history)
    specs = (
        [SMEM]
        + [rows_of((tile, width))] * k
        + sum_specs(sums, tile, length)
        + [rows_of((tile, width)), rows_of((tile, 128)), fixed((8, width)), rows_of((tile, width)), block]
    )
    more = {}
    if made is not None:
        more = {"aliases": {len(args): 0}}
        args, specs = (*args, made), specs + [ANY]
    return call(
        "average_back",
        lambda *refs: average_back_body(k, m, full, count, *refs),
        (steps,),
        args,
        specs,
        [shape(history.shape, BF16), shape((count, 8, 128), F32)] + [shape((8, width), F32)] * 2,
        [block, fixed((count, 8, 128))] + [fixed((8, width))] * 2,
        scratch=[pltpu.VMEM((tile, width), F32)] + [pltpu.VMEM((8, length), F32)] * (m - 1),
        **more,
    )


def divisor(size, most):
    return max(d for d in range(128, most + 1, 128) if size % d == 0) if size > 128 else size


def weight_body(rows, *refs):
    out = refs[-1]
    total = dot_tn(refs[0][...], refs[rows][...])
    for r in range(1, rows):
        total += dot_tn(refs[r][...], refs[rows + r][...])
    out[...] = total.astype(BF16)


def weight_grad(lefts, rights):
    rows, (length, high), wide = len(lefts), lefts[0].shape, rights[0].shape[1]
    tall, across = divisor(high, 1024), divisor(wide, 1024)
    return call(
        "weight_grad",
        lambda *refs: weight_body(rows, *refs),
        (high // tall, wide // across),
        (*lefts, *rights),
        [pl.BlockSpec((length, tall), lambda i, j: (0, i))] * rows
        + [pl.BlockSpec((length, across), lambda i, j: (0, j))] * rows,
        [shape((high, wide), BF16)],
        [pl.BlockSpec((tall, across), lambda i, j: (i, j))],
    )[0]


def put_blocks(came, outs, k, value):
    if came is not None:
        value = value + came[k].astype(F32)
    per = outs[0].shape[0]
    outs[k // per][k % per] = value.astype(BF16)


def tall_blocks_body(rows, count, fused, group, *refs):
    lefts, rights = refs[: rows * count], refs[rows * count : rows * count + rows]
    refs = refs[rows * count + rows :]
    came, outs, turned = refs[0] if fused else None, refs[fused:-1], refs[-1]
    length, high = lefts[0].shape

    @pl.when(pl.program_id(0) == 0)
    def _():
        for k in range(count):
            for r in range(rows):
                turned[k * high : (k + 1) * high, r * length : (r + 1) * length] = lefts[
                    k * rows + r
                ][...].T

    for k in range(count):
        total = 0.0
        for r in range(rows):
            total += dot_nn(
                turned[k * high : (k + 1) * high, r * length : (r + 1) * length], rights[r][...]
            )
        put_blocks(came, outs, k, total)


def wide_blocks_body(rows, count, fused, group, *refs):
    lefts, rights = refs[:rows], refs[rows : rows + rows * count]
    refs = refs[rows + rows * count :]
    came, outs = refs[0] if fused else None, refs[fused:]
    turned = [left[...].T for left in lefts]
    for k in range(count):
        total = 0.0
        for r in range(rows):
            total += dot_nn(turned[r], rights[k * rows + r][...])
        put_blocks(came, outs, k, total)


class Spread:
    def __init__(self, lefts, rights, dim, bits, part=(0, 1)):
        self.lefts, self.rights, self.dim, self.bits, self.part = lefts, rights, dim, list(bits), part
        self.groups = lax.axis_size("dp")
        self.block = (lefts, rights)[dim][0].shape[1] // self.groups
        order = [0]
        for bit in reversed(self.bits):
            order = order + [e | bit for e in order]
        self.order = order

    def blocks(self, half, came=None):
        count = self.groups // 2
        which = self.order[half * count : (half + 1) * count]
        rows, length = len(self.lefts), self.lefts[0].shape[0]
        group = lax.axis_index("dp").astype(jnp.int32)[None]
        size, (index, pieces) = self.block, self.part
        stay = [
            pl.BlockSpec((length, size), lambda i, group, e=e: (0, group[0] ^ e))
            for e in which
            for _ in range(rows)
        ]
        other = self.rights if self.dim == 0 else self.lefts
        extent = other[0].shape[1] // pieces
        tile = divisor(extent, 512)
        steps = extent // tile
        move = [pl.BlockSpec((length, tile), lambda i, group: (0, index * steps + i))] * rows

        def blocked(number):
            if self.dim == 0:
                return (
                    sent((number, size, extent), BF16),
                    pl.BlockSpec((number, size, tile), lambda i, group: (0, 0, i)),
                )
            return (
                sent((number, extent, size), BF16),
                pl.BlockSpec((number, tile, size), lambda i, group: (0, i, 0)),
            )

        if self.dim == 0:
            args = (*(list(self.lefts) * count), *self.rights)
            specs = stay + move
            body, scratch = tall_blocks_body, [pltpu.VMEM((count * size, rows * length), BF16)]
        else:
            args = (*self.lefts, *(list(self.rights) * count))
            specs = move + stay
            body, scratch = wide_blocks_body, []
        outs = [blocked(count)]
        if came is not None:
            args, specs = (*args, came), specs + [blocked(count)[1]]
            outs = [blocked(count // 2)] * 2
        return call(
            "weight_blocks",
            lambda *refs: body(rows, count, came is not None, *refs),
            (steps,),
            (group, *args),
            specs,
            [one[0] for one in outs],
            [one[1] for one in outs],
            scratch=scratch,
            prefetch=1,
        )

    def send(self, value):
        bit = self.bits[self.step]
        self.step += 1
        self.coming = lax.ppermute(value, "dp", [(i, i ^ bit) for i in range(self.groups)])

    def first(self):
        self.step = 0
        self.send(self.blocks(1)[0])

    def keep(self):
        self.held = self.blocks(0)[0]

    def keep_added(self):
        self.held, out = self.blocks(0, self.coming)
        self.send(out)


def fold_body(count, *refs):
    for i in range(count):
        held, came, keep, send = refs[2 * i], refs[2 * i + 1], refs[2 * count + 2 * i], refs[2 * count + 2 * i + 1]
        half = keep.shape[0]
        keep[...] = (held[:half].astype(F32) + came[:half].astype(F32)).astype(BF16)
        send[...] = (held[half:].astype(F32) + came[half:].astype(F32)).astype(BF16)


def advance(*spreads):
    steps = 4
    args, specs, outs, out_specs = [], [], [], []
    for one in spreads:
        count, high, wide = one.held.shape
        args += [one.held, one.coming]
        specs += [pl.BlockSpec((count, high // steps, wide), lambda i: (0, i, 0))] * 2
        outs += [sent((count // 2, high, wide), BF16)] * 2
        out_specs += [pl.BlockSpec((count // 2, high // steps, wide), lambda i: (0, i, 0))] * 2
    got = call("fold", lambda *refs: fold_body(len(spreads), *refs), (steps,), args, specs, outs, out_specs)
    for i, one in enumerate(spreads):
        one.held = got[2 * i]
        one.send(got[2 * i + 1])


def finish_body(groups, *refs):
    outs = refs[len(refs) - len(groups) :]
    at = 0
    for out, group in zip(outs, groups):
        for first, wide, count in group:
            total = refs[at][0].astype(F32)
            for ref in refs[at + 1 : at + count]:
                total += ref[0].astype(F32)
            out[:, first : first + wide] = total
            at += count


def finish(*groups):
    steps = 4
    args, specs, outs, out_specs, places = [], [], [], [], []
    for group in groups:
        first, place = 0, []
        for one in group:
            terms = [one.held, one.coming] if isinstance(one, Spread) else [one[None]]
            _, high, wide = terms[0].shape
            args += terms
            specs += [pl.BlockSpec((1, high // steps, wide), lambda i: (0, i, 0))] * len(terms)
            place.append((first, wide, len(terms)))
            first += wide
        outs.append(shape((high, first), F32))
        out_specs.append(rows_of((high // steps, first)))
        places.append(place)
    return call("finish", lambda *refs: finish_body(places, *refs), (steps,), args, specs, outs, out_specs)


def sums_body(groups, n, own, out, total, came, far, dp_sems, mp_sems):
    me = {"dp": lax.axis_index("dp"), "mp": lax.axis_index("mp")}
    peers = [("dp", b) for b in range(1, groups)] + [("mp", b) for b in range(1, n)]
    barrier = pltpu.get_barrier_semaphore()
    for axis, b in peers:
        pl.semaphore_signal(
            barrier, inc=1, device_id={axis: flip(me[axis], b)}, device_id_type=pl.DeviceIdType.MESH
        )
    pl.semaphore_wait(barrier, len(peers))

    def copy(axis, b, source, target, sems):
        return pltpu.make_async_remote_copy(
            src_ref=source,
            dst_ref=target.at[b - 1],
            send_sem=sems.at[0, b - 1],
            recv_sem=sems.at[1, b - 1],
            device_id={axis: flip(me[axis], b)},
            device_id_type=pl.DeviceIdType.MESH,
        )

    copies = [copy("dp", b, own, came, dp_sems) for b in range(1, groups)]
    for one in copies:
        one.start()
    for one in copies:
        one.wait()
    value = own[...]
    for b in range(groups - 1):
        value = value + came[b]
    out[...] = value
    total[...] = value[-8:]
    copies = [copy("mp", b, total, far, mp_sems) for b in range(1, n)]
    for one in copies:
        one.start()
    for one in copies:
        one.wait()
    value = total[...]
    for b in range(n - 1):
        value = value + far[b]
    out[-8:, :] = value


def sums(vectors, depth):
    groups, n = lax.axis_size("dp"), lax.axis_size("mp")
    sizes = [v.size for v in vectors]
    packed = jnp.concatenate(vectors)
    packed = jnp.pad(packed, (0, -packed.size % 1024)).reshape(-1, 128)
    packed = jnp.concatenate([packed, jnp.pad(depth[None], ((0, 7), (0, 128 - depth.size)))])
    high = packed.shape[0]
    got = call(
        "sums",
        lambda *refs: sums_body(groups, n, *refs),
        (1,),
        (packed,),
        [fixed((high, 128))],
        [shape((high, 128), F32)],
        [fixed((high, 128))],
        scratch=[
            pltpu.VMEM((8, 128), F32),
            pltpu.VMEM((groups - 1, high, 128), F32),
            pltpu.VMEM((n - 1, 8, 128), F32),
            pltpu.SemaphoreType.DMA((2, groups - 1)),
            pltpu.SemaphoreType.DMA((2, n - 1)),
        ],
        remote=True,
    )[0]
    flat = got.reshape(-1)
    ends = np.cumsum(sizes)
    return [flat[end - size : end] for end, size in zip(ends, sizes)], got[-8, : depth.size]


def output_body(rows, steps, *refs):
    bias, out = refs[-2:]
    per = (len(refs) - 2) // rows
    for r in range(rows):

        @pl.when(pl.program_id(0) // steps == r)
        def _(r=r):
            total = bias[0:1, :]
            for part in refs[r * per + 1 : (r + 1) * per]:
                total = total + part[...].astype(F32)
            out[...] = (refs[r * per][...] + total).astype(BF16)


def output(parts, hidden, bias):
    rows, (length, width) = len(hidden), hidden[0].shape
    tile = min(512, length)
    steps = length // tile
    args, specs = [], []
    for r in range(rows):
        args += [hidden[r], *parts[r]]
        specs += [
            pl.BlockSpec((tile, width), lambda i, r=r: (jnp.clip(i - r * steps, 0, steps - 1), 0))
        ] * (1 + len(parts[r]))
    return call(
        "output",
        lambda *refs: output_body(rows, steps, *refs),
        (rows * steps,),
        (*args, bias),
        specs + [fixed((8, width))],
        [shape((rows * length, width), BF16)],
        [rows_of((tile, width))],
    )[0]


class Ring:
    def __init__(self):
        self.n = lax.axis_size("mp")
        self.me = lax.axis_index("mp").astype(jnp.int32)
        self.pairs = self.n == 4
        self.core = [(i, i ^ 1) for i in range(self.n)]
        self.chip = [(i, i ^ 2) for i in range(self.n)]

    def over_core(self, value):
        return lax.ppermute(value, "mp", self.core)

    def over_chip(self, value):
        return lax.ppermute(value, "mp", self.chip)

    def gather_start(self, block):
        if self.pairs:
            return [block, self.over_chip(block)]
        return self.gather(block)

    def gather(self, block):
        if self.pairs:
            across = self.over_chip(block)
            return [block, self.over_core(block), across, self.over_core(across)]
        every = lax.all_gather(block, "mp")
        return [
            lax.dynamic_index_in_dim(every, self.me ^ j, 0, keepdims=False) for j in range(self.n)
        ]

    def scatter(self, parts, sums=False):
        parts, extra = (parts[:-1], parts[-1:]) if sums else (parts, [])
        if self.pairs:
            came = self.over_chip(parts[1])
            return [parts[0], came], [*extra, came] if sums else []
        stacked = jnp.stack([part.astype(F32) for part in parts])
        ordered = jnp.take(stacked, self.me ^ jnp.arange(self.n), axis=0)
        total = lax.psum_scatter(ordered, "mp", scatter_dimension=0, tiled=False)
        return [total], [lax.psum(v, "mp") for v in extra]

    def total(self, value):
        if self.pairs:
            value = value + self.over_core(value)
            return value + self.over_chip(value)
        return lax.psum(value, "mp")

    def out_start(self, weight):
        rows, groups = weight.shape[0], lax.axis_size("dp")
        if self.pairs and rows % (16 * groups) == 0:
            size = rows // groups
            piece = lax.dynamic_slice_in_dim(weight, lax.axis_index("dp") * size, size, 0)
            return self.over_chip(piece)
        return None

    def out_middle(self, piece):
        return None if piece is None else lax.all_gather(piece, "dp", axis=0, tiled=True)

    def out_end(self, weight, across):
        if across is None:
            return self.gather(weight)
        across = gate([across])[0]
        return [weight, self.over_core(weight), across, self.over_core(across)]


def tables_of(length):
    half = HEAD // 2
    rate = np.exp(np.arange(half, dtype=np.float64) * (-math.log(10000.0) / half))
    angle = np.arange(length, dtype=np.float64)[:, None] * rate[None, :]
    cosine, sine = np.cos(angle), np.sin(angle)
    return (
        jnp.asarray(np.concatenate([cosine, cosine], 1), F32),
        jnp.asarray(np.concatenate([-sine, sine], 1), F32),
    )


def local(
    history,
    depth_weights,
    segment_ids,
    first_gain,
    first_bias,
    qkv_weight,
    out_weight,
    second_gain,
    second_bias,
    up_weight,
    up_bias,
    down_weight,
    down_bias,
    cotangent,
):
    ring = Ring()
    n = ring.n
    pairs = ring.pairs
    width = history.shape[2]
    full = n * width
    row_count, length = segment_ids.shape
    rows = range(row_count)
    tables = tables_of(length)
    earlier = (segment_ids[:, None, :] < segment_ids[:, :, None]).astype(jnp.int32)
    starts = jnp.broadcast_to(jnp.sum(earlier, -1)[:, None, :], (row_count, 8, length))

    up_bias8 = jnp.broadcast_to(up_bias[None], (8, up_bias.shape[0]))

    down_bias8 = jnp.broadcast_to(down_bias[None], (8, width))
    groups = lax.axis_size("dp")
    spread = full % (128 * groups) == 0 and groups >= 4
    last = row_count - 1

    Order.last, Order.names, Order.cost = None, 0, LARGE
    vectors = jnp.stack([first_gain, first_bias, second_gain, second_bias])
    vectors = ring.gather_start(jnp.repeat(vectors, 8, 0))
    piece = ring.out_start(out_weight)
    cot_rows = [lax.slice_in_dim(cotangent, r * length, (r + 1) * length) for r in rows]
    none = [None] * row_count
    wide, low, xs, qkv, normed1, stat1 = (list(none) for _ in range(6))
    attended, logs, heads, cots = (list(none) for _ in range(4))
    hidden, normed2, stat2, activated, slope = (list(none) for _ in range(5))
    branch, up_grad, parts2, parts1 = (list(none) for _ in range(4))
    hidden_grad, grads, grad_full, qkv_grad = (list(none) for _ in range(4))
    up_bias_sum = down_bias_sum = gain2_sum = bias2_sum = 0.0

    for r in rows:
        wide[r], low[r] = average(depth_weights, history, r, length)
        if r == 0:
            xs[0] = ring.gather_start(low[0])
            if pairs:
                vectors[1], piece = gate([vectors[1], piece])
                vectors = [
                    vectors[0],
                    ring.over_core(vectors[0]),
                    vectors[1],
                    ring.over_core(vectors[1]),
                ]
            across = ring.out_middle(piece)
    vectors = jnp.concatenate(vectors, 1)
    gain1, bias1, gain2, bias2 = (vectors[8 * i : 8 * i + 8] for i in range(4))
    own1, own2 = gain1[:, :width], gain2[:, :width]
    for r in rows[1:]:
        xs[r] = ring.gather_start(gate([low[r]], xs[r - 1][1:2])[0])
    for r in rows:
        qkv[r], normed1[r], stat1[r], xs[r] = project(
            n, pairs, xs[r], gain1, bias1, tables, qkv_weight
        )
        attended[r], logs[r] = attend(starts[r], qkv[r])
        heads[r] = ring.gather_start(attended[r])
        if r == last:
            out_w = ring.out_end(out_weight, across)

    for r in rows:
        cots[r] = ring.gather_start(gate([cot_rows[r]])[0])
        got = feed(
            n,
            pairs,
            heads[r],
            xs[r],
            out_w,
            wide[r],
            gain2,
            bias2,
            up_bias8,
            up_weight,
            down_weight,
        )
        hidden[r], normed2[r], stat2[r], activated[r], slope[r], parts = got
        branch[r] = ring.scatter(parts)[0]

    def spread_over_dp(value, dim):
        return lax.psum_scatter(value, "dp", scatter_dimension=dim, tiled=True)

    if pairs:
        cot_full = join(cots, full)
        branch[0][1] = gate(branch[0][1:])[0]
    else:
        cot_full = [lax.all_gather(v, "mp", axis=1, tiled=True) for v in cot_rows]
    if spread:
        down_sum = Spread(activated, cot_full, 1, (1, 2, 4))
        down_sum.first()

    for r in rows:
        up_grad[r], up_sum, cot_sum, parts = feed_back(
            n, pairs, cot_full[r], slope[r], normed2[r], gain2, bias2, up_weight, down_weight
        )
        up_bias_sum += up_sum
        down_bias_sum += cot_sum
        parts2[r] = ring.scatter(parts, True)
        if r == 0 and pairs:
            branch[last][1] = gate(branch[last][1:])[0]

    def hidden_step(r):
        nonlocal gain2_sum, bias2_sum
        parts, row_sums = parts2[r]
        hidden_grad[r], low_grad, gain_part, bias_part = hidden_back(
            parts, cotangent, r, hidden[r], stat2[r], row_sums, own2, full
        )
        gain2_sum += gain_part
        bias2_sum += bias_part
        grads[r] = ring.gather_start(low_grad)

    hidden_step(0)
    if spread:
        up_sum = Spread(normed2, up_grad, 0, (1, 2, 4))
        up_sum.first()

        down_sum.keep_added()

    for r in rows:
        grad_full[r], attended_grad = attended_back(n, pairs, grads[r], out_weight)
        if r < last:
            hidden_step(r + 1)
        qkv_grad[r] = attend_back(starts[r], tables, qkv[r], attended_grad, logs[r])
        if r == last and spread:
            advance(down_sum)
            qkv_sum = [
                Spread(normed1, qkv_grad, 0, (1, 2, 4), (0, 2)),
                Spread(normed1, qkv_grad, 0, (1, 2, 4), (1, 2)),
            ]
            qkv_sum[0].first()
            up_sum.keep_added()
            qkv_sum[1].first()
        if r > 0 and pairs:
            parts, row_sums = parts1[r - 1]
            parts[1] = row_sums[1] = gate([parts[1]])[0]
        parts = project_back(n, pairs, qkv_grad[r], normed1[r], gain1, bias1, qkv_weight)
        parts1[r] = ring.scatter(parts, True)

    if spread:
        down_sum.coming = gate([down_sum.coming])[0]
        out_sum = Spread(attended, grad_full, 1, (1, 2, 4))
        out_sum.first()
    made = output(branch, hidden, down_bias8)

    grad_history, depth_sum, gain1_sum, bias1_sum = None, 0.0, 0.0, 0.0
    for r in rows:
        parts, row_sums = parts1[r]
        grad_history, depth_part, gain_part, bias_part = average_back(
            depth_weights,
            parts,
            wide[r],
            stat1[r],
            row_sums,
            (own1, full),
            hidden_grad[r],
            history,
            r,
            grad_history,
        )
        depth_sum += depth_part
        gain1_sum += gain_part
        bias1_sum += bias_part
        if r == 0:
            if pairs:
                parts, row_sums = parts1[last]
                parts[1] = row_sums[1] = gate([parts[1]])[0]
            if spread:
                qkv_sum[0].keep_added()
                advance(up_sum)

    Order.cost = TINY
    vectors = [up_bias_sum, down_bias_sum, gain2_sum, bias2_sum, gain1_sum, bias1_sum]
    vectors, depth_part = [jnp.sum(v, 0) for v in vectors], jnp.sum(depth_sum, (1, 2))
    if spread:
        qkv_sum[1].keep_added()
        out_sum.keep_added()
        up_sum.coming = gate([up_sum.coming])[0]
        advance(qkv_sum[0])
        advance(qkv_sum[1], out_sum)
    else:
        qkv_sum = [spread_over_dp(weight_grad(normed1, qkv_grad), 0)]
        out_sum = spread_over_dp(weight_grad(attended, grad_full), 1)
        down_sum = spread_over_dp(weight_grad(activated, cot_full), 1)
        up_sum = spread_over_dp(weight_grad(normed2, up_grad), 0)
    down_total, up_total, out_total, qkv_total = finish([down_sum], [up_sum], [out_sum], qkv_sum)
    totals, depth_grad = sums(vectors, depth_part)
    return (
        made,
        grad_history,
        depth_grad,
        totals[4],
        totals[5],
        qkv_total,
        out_total,
        totals[2],
        totals[3],
        up_total,
        totals[0],
        down_total,
        totals[1],
    )


def solution(mesh):
    placed = (
        P(None, "dp", "mp"),
        P(),
        P("dp", None),
        P("mp"),
        P("mp"),
        P(None, "mp"),
        P("mp", None),
        P("mp"),
        P("mp"),
        P(None, "mp"),
        P("mp"),
        P("mp", None),
        P("mp"),
        P("dp", "mp"),
    )
    return jax.shard_map(
        local,
        mesh=mesh,
        in_specs=placed,
        out_specs=(
            P("dp", "mp"),
            P(None, "dp", "mp"),
            P(),
            P("mp"),
            P("mp"),
            P("dp", "mp"),
            P("mp", "dp"),
            P("mp"),
            P("mp"),
            P("dp", "mp"),
            P("mp"),
            P("mp", "dp"),
            P("mp"),
        ),
        check_vma=False,
    )
```

```python
import math

import jax
import jax.numpy as jnp
import numpy as np
from jax import lax
from jax.experimental import pallas as pl
from jax.experimental.pallas import tpu as pltpu
from jax.sharding import PartitionSpec as P

HEAD = 128
MAX_DOC = 512
EPSILON = 1e-05
SQRT_HALF = 0.7071067811865476
INV_ROOT_TWO_PI = 0.3989422804014327
LOG2E = 1.4426950408889634
SCALE = HEAD ** (-0.5)
MIB = 2**20
BF16 = jnp.bfloat16
F32 = jnp.float32


def dot_nn(a, b):
    return jnp.dot(a, b, preferred_element_type=F32)


def dot_nt(a, b):
    return lax.dot_general(a, b, (((1,), (1,)), ((), ())), preferred_element_type=F32)


def dot_tn(a, b):
    return lax.dot_general(a, b, (((0,), (0,)), ((), ())), preferred_element_type=F32)


LARGE, TINY = 10**12, 10**4


class Order:
    last = None
    names = 0
    cost = LARGE

    @staticmethod
    def name(remote):
        Order.names += remote
        return Order.names - 1 if remote else None


def call(
    name, body, grid, args, in_specs, outs, out_specs, scratch=(), prefetch=0, after=(), aliases=None, remote=False
):
    count = len(args)
    extra = [*after]
    if Order.last is not None and not any(Order.last is a for a in args):
        extra.append(Order.last)

    def without_extra(*refs):
        body(*refs[:count], *refs[count + len(extra) :])

    got = pl.pallas_call(
        without_extra,
        grid_spec=pltpu.PrefetchScalarGridSpec(
            num_scalar_prefetch=prefetch,
            grid=grid,
            in_specs=list(in_specs) + [ANY] * len(extra),
            out_specs=out_specs,
            scratch_shapes=list(scratch),
        ),
        out_shape=outs,
        input_output_aliases=aliases or {},
        compiler_params=pltpu.CompilerParams(
            vmem_limit_bytes=60 * MIB, collective_id=Order.name(remote), has_side_effects=remote
        ),
        cost_estimate=pl.CostEstimate(flops=Order.cost, bytes_accessed=Order.cost // 10**4, transcendentals=0),
        name=name,
    )(*args, *extra)
    fresh = [v for i, v in enumerate(got) if i not in (aliases or {}).values()]
    Order.last = min(fresh or got, key=lambda v: v.size)
    return got


def shape(dims, dtype):
    return jax.ShapeDtypeStruct(dims, dtype)


def sent(dims, dtype):
    return pltpu.HBM(dims, dtype)


SMEM = pl.BlockSpec(memory_space=pltpu.SMEM)
ANY = pl.BlockSpec(memory_space=pl.ANY)


def gate(arrays, after=()):
    arrays = list(arrays)
    return call(
        "gate",
        lambda *refs: None,
        (1,),
        arrays,
        [ANY] * len(arrays),
        [shape(a.shape, a.dtype) for a in arrays],
        [ANY] * len(arrays),
        after=after,
        aliases={i: i for i in range(len(arrays))},
    )


def rows_of(block):
    return pl.BlockSpec(block, lambda i: (i, 0))


def cols_of(block):
    return pl.BlockSpec(block, lambda i: (0, i))


def fixed(block):
    return pl.BlockSpec(block, lambda i: (0,) * len(block))


def flip(me, j):
    there, bit = me, 1
    while bit <= j:
        if j & bit:
            there = there + bit * (1 - 2 * ((me // bit) % 2))
        bit *= 2
    return there


def place_of(me, j, width):
    return pl.ds(pl.multiple_of(flip(me, j) * width, width), width)


def greet():
    barrier = pltpu.get_barrier_semaphore()
    sibling = flip(lax.axis_index("mp"), 1)
    pl.semaphore_signal(
        barrier, inc=1, device_id={"mp": sibling}, device_id_type=pl.DeviceIdType.MESH
    )
    pl.semaphore_wait(barrier, 1)


def to_sibling(source, target, sems, at):
    return pltpu.make_async_remote_copy(
        src_ref=source,
        dst_ref=target,
        send_sem=sems.at[0, at],
        recv_sem=sems.at[1, at],
        device_id={"mp": flip(lax.axis_index("mp"), 1)},
        device_id_type=pl.DeviceIdType.MESH,
    )


class Gathered:
    def __init__(self, refs, pairs, steps):
        self.pairs, self.steps = pairs, steps
        self.blocks, self.whole = refs[:2] if pairs else refs, refs[2:4] if pairs else ()

    @staticmethod
    def specs(blocks, pairs, tile):
        width = blocks[0].shape[1]
        return [rows_of((tile, width))] * len(blocks) + ([ANY] * 2 if pairs else [])

    @staticmethod
    def scratch(blocks, pairs, steps):
        if not pairs:
            return []
        return [pltpu.VMEM((2, *blocks[0].shape), BF16), pltpu.SemaphoreType.DMA((2, 2 * steps))]

    def attach(self, refs):
        if self.pairs:
            self.came, self.sems = refs
        return self

    def copies(self, step):
        tile = self.blocks[0].shape[0]
        rows = pl.ds(pl.multiple_of(step * tile, tile), tile)
        return [
            to_sibling(self.whole[k].at[rows, :], self.came.at[k, rows, :], self.sems, 2 * step + k)
            for k in range(2)
        ]

    def start(self):
        if self.pairs:
            for step in range(self.steps):
                for one in self.copies(step):
                    one.start()

    def refs(self):
        if not self.pairs:
            return self.blocks
        step = pl.program_id(0)
        tile = self.blocks[0].shape[0]
        for one in self.copies(step):
            one.wait()
        rows = pl.ds(pl.multiple_of(step * tile, tile), tile)
        return [self.blocks[0], self.came.at[0, rows, :], self.blocks[1], self.came.at[1, rows, :]]


EXTRA = 16


def pack(sums, width):
    rows = []
    for s in range(2):
        rest = sums[s : s + 1, :]
        for _ in range(3):
            piece = rest.astype(BF16).astype(F32)
            rest = rest - piece
            rows += [piece[:, h : h + width] for h in range(0, sums.shape[1], width)]
    assert len(rows) <= EXTRA
    rows += [jnp.zeros((1, width), F32)] * (EXTRA - len(rows))
    return jnp.concatenate(rows).astype(BF16)


def unpack(packed, target):
    width = packed.shape[1]
    per = target.shape[1] // width
    value = packed[...].astype(F32)
    for s in range(2):
        for h in range(per):
            at = [(3 * s + p) * per + h for p in range(3)]
            total = value[at[0] : at[0] + 1] + value[at[1] : at[1] + 1] + value[at[2] : at[2] + 1]
            target[s : s + 1, h * width : (h + 1) * width] = total


class Scattered:
    def __init__(self, pairs, n, steps, with_sums):
        self.pairs, self.n, self.steps, self.with_sums = pairs, n, steps, with_sums

    def outs(self, length, width):
        tile = length // self.steps
        if self.pairs:
            high = length + EXTRA * self.with_sums
            outs = [shape((length, width), BF16), sent((high, width), BF16)]
            specs = [fixed((length, width)), fixed((high, width))]
            if self.with_sums:
                outs, specs = outs + [shape((8, length), F32)], specs + [fixed((8, length))]
            return outs, specs
        outs, specs = [shape((length, width), BF16)] * self.n, [rows_of((tile, width))] * self.n
        if self.with_sums:
            outs, specs = outs + [shape((8, length), F32)], specs + [cols_of((8, tile))]
        return outs, specs

    def count(self):
        return (2 if self.pairs else self.n) + self.with_sums

    def scratch(self, length, width):
        if not self.pairs:
            return []
        tile = length // self.steps
        block = pltpu.VMEM((self.steps, 2, tile, width), BF16)
        made = [block, block, pltpu.VMEM((2, 2, tile, width), F32)]
        if self.with_sums:
            made += [pltpu.VMEM((self.steps, 8, tile), F32)] * 3
        return made + [pltpu.SemaphoreType.DMA((2, 3 * self.steps))]

    def attach(self, outs, scratch):
        self.out = outs
        if self.pairs:
            self.send, self.came, self.kept = scratch[:3]
            self.sums = scratch[3:-1]
            self.sems = scratch[-1]
        return self

    def copies(self, step):
        made = [
            to_sibling(self.send.at[step, k], self.came.at[step, k], self.sems, 3 * step + k)
            for k in range(2)
        ]
        if self.with_sums:
            made.append(to_sibling(self.sums[0].at[step], self.sums[1].at[step], self.sems, 3 * step + 2))
        return made

    def put(self, j, value):
        step = pl.program_id(0)
        if not self.pairs:
            self.out[j][...] = value.astype(BF16)
        elif j % 2:
            self.send[step, j // 2] = value.astype(BF16)
        else:
            self.kept[step % 2, j // 2] = value

    def take(self, step):
        tile = self.kept.shape[2]
        for one in self.copies(step):
            one.wait()
        rows = pl.ds(pl.multiple_of(step * tile, tile), tile)
        for k in range(2):
            total = self.kept[step % 2, k] + self.came[step, k].astype(F32)
            self.out[k][rows, :] = total.astype(BF16)
        if self.with_sums:
            self.out[2][:, rows] = self.sums[2][step] + self.sums[1][step]

    def finish(self, sums=None):
        if not self.pairs:
            if sums is not None:
                self.out[-1][...] = sums
            return
        step = pl.program_id(0)
        if sums is not None:
            self.sums[0][step] = sums
            self.sums[2][step] = sums
        for one in self.copies(step):
            one.start()

        @pl.when(step > 0)
        def _():
            self.take(step - 1)

        @pl.when(step == self.steps - 1)
        def _():
            self.take(step)
            if self.with_sums:
                length, width = self.out[0].shape
                self.out[1][length:, :] = pack(self.out[2][...], width)


def with_weights(copies, work, remote=False, gathered=()):
    @pl.when(pl.program_id(0) == 0)
    def _():
        for one in copies:
            one.start()
        if remote:
            greet()
        for one in gathered:
            one.start()

        def wait(some):
            for one in some:
                one.wait()

        work(wait)

    @pl.when(pl.program_id(0) != 0)
    def _():
        work(lambda some: None)


def row_blocks(me, n, width, source, target, sems, base):
    return [
        pltpu.make_async_copy(
            source.at[place_of(me, j, width), :],
            target.at[pl.ds(j * width, width), :],
            sems.at[base + j],
        )
        for j in range(n)
    ]


def col_blocks(me, n, width, source, target, sems, base):
    return [
        pltpu.make_async_copy(
            source.at[:, place_of(me, j, width)],
            target.at[:, pl.ds(j * width, width)],
            sems.at[base + j],
        )
        for j in range(n)
    ]


def stat_columns(first, second):
    lane = lax.broadcasted_iota(jnp.int32, (first.shape[0], 128), 1)
    return jnp.where(lane == 0, first, jnp.where(lane == 1, second, 0.0))


def fold_rows(values):
    return jnp.sum(values.reshape(values.shape[0] // 8, 8, values.shape[1]), 0)


def accumulate(ref, value):
    @pl.when(pl.program_id(0) == 0)
    def _():
        ref[...] = value

    @pl.when(pl.program_id(0) != 0)
    def _():
        ref[...] += value


def average_body(weights, history, wide, low):
    chunk = min(32, wide.shape[0])
    for t in range(wide.shape[0] // chunk):
        rows = slice(t * chunk, (t + 1) * chunk)
        total = weights[0] * history[0, rows, :].astype(F32)
        for j in range(1, history.shape[0]):
            total += weights[j] * history[j, rows, :].astype(F32)
        wide[rows, :] = total
        low[rows, :] = total.astype(BF16)


def average(weights, history, row, length):
    count, _, width = history.shape
    tile = min(256, length)
    steps = length // tile
    return call(
        "average",
        average_body,
        (steps,),
        (weights, history),
        [SMEM, pl.BlockSpec((count, tile, width), lambda i: (0, row * steps + i, 0))],
        [shape((length, width), F32), sent((length, width), BF16)],
        [rows_of((tile, width))] * 2,
    )


def project_body(n, pairs, steps, *refs):
    count = 4 if pairs else n
    x = Gathered(refs[:count], pairs, steps)
    gain, bias, cosine, sine, weight, qkv, normed, stat = refs[count : count + 8]
    refs = refs[count + 8 :]
    shared = refs[:2] if pairs else ()
    held, joined, sems, *more = refs[len(shared) :]
    x.attach(more)
    me = lax.axis_index("mp")
    tile, width = x.blocks[0].shape
    full = n * width
    heads = held.shape[1] // (3 * HEAD)
    sub = min(256, tile)
    copies = row_blocks(me, n, width, weight, held, sems, 0)

    def work(wait):
        xs = x.refs()
        for out, k in zip(shared, (1, 3)):
            out[...] = xs[k][...]
        for t in range(tile // sub):
            rows = slice(t * sub, (t + 1) * sub)
            total = square = 0.0
            for one in xs:
                value = one[rows, :].astype(F32)
                total += jnp.sum(value, 1, keepdims=True)
                square += jnp.sum(value * value, 1, keepdims=True)
            mean = total / full
            inv = lax.rsqrt(square / full - mean * mean + EPSILON)
            stat[rows, :] = stat_columns(mean, inv)
            for j, one in enumerate(xs):
                part = slice(j * width, (j + 1) * width)
                value = (one[rows, :].astype(F32) - mean) * inv * gain[0:1, part] + bias[0:1, part]
                joined[rows, part] = value.astype(BF16)
                normed[rows, place_of(me, j, width)] = value.astype(BF16)
            if t == 0:
                wait(copies)
            for h in range(heads):
                base = 3 * h * HEAD
                out = dot_nn(joined[rows, :], held[:, base : base + 3 * HEAD])
                for s in range(2):
                    v = out[:, s * HEAD : (s + 1) * HEAD]
                    turned = v * cosine[rows, :] + pltpu.roll(v, HEAD // 2, 1) * sine[rows, :]
                    qkv[rows, base + s * HEAD : base + (s + 1) * HEAD] = turned.astype(BF16)
                qkv[rows, base + 2 * HEAD : base + 3 * HEAD] = out[:, 2 * HEAD :].astype(BF16)

    with_weights(copies, work, pairs, [x])


def project(n, pairs, xs, gain, bias, tables, weight):
    length, width = xs[0].shape
    full, out = weight.shape
    tile = min(512, length)
    steps = length // tile
    got = call(
        "project",
        lambda *refs: project_body(n, pairs, steps, *refs),
        (steps,),
        (*xs, *(xs if pairs else ()), gain, bias, *tables, weight),
        Gathered.specs(xs, pairs, tile)
        + [fixed((8, full))] * 2
        + [rows_of((tile, HEAD))] * 2
        + [ANY],
        [shape((length, out), BF16), shape((length, full), BF16), shape((length, 128), F32)]
        + [shape((length, width), BF16)] * (2 * pairs),
        [rows_of((tile, out)), rows_of((tile, full)), rows_of((tile, 128))]
        + [rows_of((tile, width))] * (2 * pairs),
        scratch=[
            pltpu.VMEM((full, out), BF16),
            pltpu.VMEM((tile, full), BF16),
            pltpu.SemaphoreType.DMA((n,)),
        ]
        + Gathered.scratch(xs, pairs, steps),
        remote=pairs,
    )
    return *got[:3], [xs[0], got[3], xs[1], got[4]] if pairs else xs


def windows(length):
    block = min(256, length)
    for i in range(length // block):
        low = max(0, i * block - (MAX_DOC - 1)) // block * block
        yield slice(i * block, (i + 1) * block), slice(low, (i + 1) * block)


def score_mask(start, q_part, k_part):
    dims = (k_part.stop - k_part.start, q_part.stop - q_part.start)
    k_pos = lax.broadcasted_iota(jnp.int32, dims, 0) + k_part.start
    q_pos = lax.broadcasted_iota(jnp.int32, dims, 1) + q_part.start
    return (k_pos >= start[0:1, q_part]) & (k_pos <= q_pos)


def attend_body(start, qkv, out, logs):
    length = qkv.shape[0]
    value_t = qkv[:, 2 * HEAD :].T
    for q_part, k_part in windows(length):
        query, key = qkv[q_part, :HEAD], qkv[k_part, HEAD : 2 * HEAD]
        scores = dot_nt(key, query) * (SCALE * LOG2E)
        scores = jnp.where(score_mask(start, q_part, k_part), scores, -1e30)
        top = jnp.max(scores, 0, keepdims=True)
        probs = jnp.exp2(scores - top)
        total = jnp.sum(probs, 0, keepdims=True)
        logs[0, :, q_part] = jnp.broadcast_to(top + jnp.log2(total), (8, q_part.stop - q_part.start))
        got = dot_nn(value_t[:, k_part], probs.astype(BF16)) / total
        out[q_part, :] = got.T.astype(BF16)


def attend(start, qkv):
    length, width = qkv.shape
    heads = width // (3 * HEAD)
    return call(
        "attend",
        attend_body,
        (heads,),
        (start, qkv),
        [fixed((8, length)), cols_of((length, 3 * HEAD))],
        [sent((length, heads * HEAD), BF16), shape((heads, 8, length), F32)],
        [cols_of((length, HEAD)), pl.BlockSpec((1, 8, length), lambda i: (i, 0, 0))],
    )


def attend_back_body(start, cosine, sine, qkv, grad, logs, out, key_sum, value_sum):
    length = qkv.shape[0]
    key_t = qkv[:, HEAD : 2 * HEAD].T
    key_sum[...] = jnp.zeros_like(key_sum)
    value_sum[...] = jnp.zeros_like(value_sum)

    def turn_back(v, part):
        return (
            v * cosine[part, :] - pltpu.roll(v, HEAD // 2, 1) * sine[part, :]
        ).astype(BF16)

    for q_part, k_part in windows(length):
        query, key = qkv[q_part, :HEAD], qkv[k_part, HEAD : 2 * HEAD]
        value, g = qkv[k_part, 2 * HEAD :], grad[q_part, :]
        scores = dot_nt(key, query) * (SCALE * LOG2E) - logs[0, 0:1, q_part]
        probs = jnp.exp2(jnp.where(score_mask(start, q_part, k_part), scores, -1e30))
        prob_grad = dot_nt(value, g)
        mean = jnp.sum(prob_grad * probs, 0, keepdims=True)
        score_grad = (probs * (prob_grad - mean)).astype(BF16)
        value_sum[k_part, :] += dot_nn(probs.astype(BF16), g)
        key_sum[k_part, :] += dot_nn(score_grad, query)
        query_grad = dot_nn(key_t[:, k_part], score_grad) * SCALE
        out[q_part, :HEAD] = turn_back(query_grad.T, q_part)
    for q_part, _ in windows(length):
        out[q_part, HEAD : 2 * HEAD] = turn_back(key_sum[q_part, :] * SCALE, q_part)
        out[q_part, 2 * HEAD :] = value_sum[q_part, :].astype(BF16)


def attend_back(start, tables, qkv, grad, logs):
    length, width = qkv.shape
    heads = width // (3 * HEAD)
    return call(
        "attend_back",
        attend_back_body,
        (heads,),
        (start, *tables, qkv, grad, logs),
        [fixed((8, length))]
        + [fixed((length, HEAD))] * 2
        + [
            cols_of((length, 3 * HEAD)),
            cols_of((length, HEAD)),
            pl.BlockSpec((1, 8, length), lambda i: (i, 0, 0)),
        ],
        [shape((length, width), BF16)],
        [cols_of((length, 3 * HEAD))],
        scratch=[pltpu.VMEM((length, HEAD), F32)] * 2,
    )[0]


def feed_body(n, pairs, steps, *refs):
    count = 4 if pairs else n
    attended = Gathered(refs[:count], pairs, steps)
    refs = refs[count:]
    xs, outs_w = refs[: n - 1], refs[n - 1 : 2 * n - 1]
    own, gain, bias, up_bias, up_weight, down_weight = refs[2 * n - 1 : 2 * n + 5]
    refs = refs[2 * n + 5 :]
    hidden, normed, stat, activated, slope = refs[:5]
    refs = refs[5:]
    parts = Scattered(pairs, n, steps, False)
    part_outs, refs = refs[: parts.count()], refs[parts.count() :]
    out_held, up_held, down_held, joined, whole, sems, *refs = refs
    if pairs:
        attended.attach(refs[:2])
        refs = refs[2:]
    parts.attach(part_outs, refs)
    me = lax.axis_index("mp")
    width = own.shape[1]
    full = n * width
    inner = up_held.shape[1]
    out_copies = []
    for j in range(n):
        for k in range(n):
            out_copies.append(
                pltpu.make_async_copy(
                    outs_w[k].at[:, place_of(me, j, width)],
                    out_held.at[pl.ds(k * width, width), pl.ds(j * width, width)],
                    sems.at[j * n + k],
                )
            )
    up_copies = row_blocks(me, n, width, up_weight, up_held, sems, n * n)
    down_copies = col_blocks(me, n, width, down_weight, down_held, sems, n * n + n)

    def work(wait):
        for j, one in enumerate(attended.refs()):
            joined[:, j * width : (j + 1) * width] = one[...]
        total = square = 0.0
        for j in range(n):
            wait(out_copies[j * n : (j + 1) * n])
            part = slice(j * width, (j + 1) * width)
            base = own[...] if j == 0 else xs[j - 1][...].astype(F32)
            value = base + dot_nn(joined[...], out_held[:, part])
            whole[:, part] = value
            if j == 0:
                hidden[...] = value
            total += jnp.sum(value, 1, keepdims=True)
            square += jnp.sum(value * value, 1, keepdims=True)
        mean = total / full
        inv = lax.rsqrt(square / full - mean * mean + EPSILON)
        stat[...] = stat_columns(mean, inv)
        for j in range(n):
            part = slice(j * width, (j + 1) * width)
            value = ((whole[:, part] - mean) * inv * gain[0:1, part] + bias[0:1, part]).astype(BF16)
            joined[:, part] = value
            normed[:, place_of(me, j, width)] = value
        wait(up_copies)
        step = divisor(inner, 512)
        for c in range(inner // step):
            part = slice(c * step, (c + 1) * step)
            up = dot_nn(joined[...], up_held[:, part]) + up_bias[0:1, part]
            half = 0.5 * (1.0 + lax.erf(up * SQRT_HALF))
            activated[:, part] = (up * half).astype(BF16)
            slope[:, part] = (half + up * INV_ROOT_TWO_PI * jnp.exp(-0.5 * up * up)).astype(BF16)
        wait(down_copies)
        for j in range(n):
            parts.put(j, dot_nn(activated[...], down_held[:, j * width : (j + 1) * width]))

    with_weights(out_copies + up_copies + down_copies, work, pairs, [attended])
    parts.finish()


def feed(n, pairs, attended, xs, outs_w, own, gain, bias, up_bias, up_weight, down_weight):
    length, width = own.shape
    full, inner = up_weight.shape
    tile = min(256, length)
    steps = length // tile
    parts = Scattered(pairs, n, steps, False)
    part_outs, part_specs = parts.outs(length, width)
    twice = tuple(attended) if pairs else ()
    got = call(
        "feed",
        lambda *refs: feed_body(n, pairs, steps, *refs),
        (steps,),
        (
            *attended,
            *twice,
            *xs[1:],
            *outs_w,
            own,
            gain,
            bias,
            up_bias,
            up_weight,
            down_weight,
        ),
        Gathered.specs(attended, pairs, tile)
        + [rows_of((tile, width))] * (n - 1)
        + [ANY] * n
        + [rows_of((tile, width))]
        + [fixed((8, full))] * 2
        + [fixed((8, inner))]
        + [ANY] * 2,
        [
            shape((length, width), F32),
            shape((length, full), BF16),
            shape((length, 128), F32),
            shape((length, inner), BF16),
            shape((length, inner), BF16),
        ]
        + part_outs,
        [
            rows_of((tile, width)),
            rows_of((tile, full)),
            rows_of((tile, 128)),
            rows_of((tile, inner)),
            rows_of((tile, inner)),
        ]
        + part_specs,
        scratch=[
            pltpu.VMEM((full, full), BF16),
            pltpu.VMEM((full, inner), BF16),
            pltpu.VMEM((inner, full), BF16),
            pltpu.VMEM((tile, full), BF16),
            pltpu.VMEM((tile, full), F32),
            pltpu.SemaphoreType.DMA((n * n + 2 * n,)),
        ]
        + Gathered.scratch(attended, pairs, steps)
        + parts.scratch(length, width),
        remote=pairs,
    )
    return (*got[:5], got[5:])


def row_stats(total, weighted):
    return stat_columns(total, weighted).T[0:8, :]


def norm_sums(parts, n, product, normed, gain, bias, me):
    width = gain.shape[1] // n
    total = weighted = 0.0
    for j in range(n):
        part = slice(j * width, (j + 1) * width)
        value = product(j)
        parts.put(j, value)
        total += jnp.sum(value * gain[0:1, part], 1, keepdims=True)
        there = normed[:, place_of(me, j, width)].astype(F32)
        weighted += jnp.sum(value * (there - bias[0:1, part]), 1, keepdims=True)
    return row_stats(total, weighted)


def join_body(count, steps, *refs):
    gathered = [Gathered(refs[4 * i : 4 * i + 4], True, steps) for i in range(count)]
    outs, scratch = refs[4 * count : 5 * count], refs[5 * count :]
    for i, one in enumerate(gathered):
        one.attach(scratch[2 * i : 2 * i + 2])
    me = lax.axis_index("mp")

    def work(wait):
        for one, out in zip(gathered, outs):
            for j, block in enumerate(one.refs()):
                out[:, place_of(me, j, block.shape[1])] = block[...]

    with_weights([], work, True, gathered)


def join(gathered, full):
    length = gathered[0][0].shape[0]
    tile = min(256, length)
    steps = length // tile
    args, specs, scratch = [], [], []
    for one in gathered:
        args += [*one, *one]
        specs += Gathered.specs(one, True, tile)
        scratch += Gathered.scratch(one, True, steps)
    return call(
        "join",
        lambda *refs: join_body(len(gathered), steps, *refs),
        (steps,),
        args,
        specs,
        [shape((length, full), BF16)] * len(gathered),
        [rows_of((tile, full))] * len(gathered),
        scratch=scratch,
        remote=True,
    )


def feed_back_body(n, pairs, steps, *refs):
    cot, refs = refs[0], refs[1:]
    slope, normed, gain, bias, up_weight, down_weight, up_grad, up_bias_sum, cot_sum = refs[:9]
    refs = refs[9:]
    parts = Scattered(pairs, n, steps, True)
    part_outs, refs = refs[: parts.count()], refs[parts.count() :]
    up_held, down_held, row_sums, sems, *refs = refs
    parts.attach(part_outs, refs)
    me = lax.axis_index("mp")
    inner = up_held.shape[1]
    width = gain.shape[1] // n
    step = divisor(inner, 512)
    down_copies = [pltpu.make_async_copy(down_weight, down_held, sems.at[n])]
    up_copies = row_blocks(me, n, width, up_weight, up_held, sems, 0)

    def work(wait):
        accumulate(cot_sum, fold_rows(cot[:, place_of(me, 0, width)].astype(F32)))
        wait(down_copies)
        bias_parts = []
        for c in range(inner // step):
            part = slice(c * step, (c + 1) * step)
            value = dot_nt(cot[...], down_held[part, :]) * slope[:, part].astype(F32)
            low = value.astype(BF16)
            up_grad[:, part] = low
            bias_parts.append(fold_rows(low.astype(F32)))
        accumulate(up_bias_sum, jnp.concatenate(bias_parts, 1))
        wait(up_copies)
        row_sums[...] = norm_sums(
            parts,
            n,
            lambda j: dot_nt(up_grad[...], up_held[j * width : (j + 1) * width, :]),
            normed,
            gain,
            bias,
            me,
        )

    with_weights(down_copies + up_copies, work, pairs)
    parts.finish(row_sums[...])


def feed_back(n, pairs, cot, slope, normed, gain, bias, up_weight, down_weight):
    length, full = normed.shape
    width = full // n
    inner = up_weight.shape[1]
    tile = min(256, length)
    steps = length // tile
    parts = Scattered(pairs, n, steps, True)
    part_outs, part_specs = parts.outs(length, width)
    got = call(
        "feed_back",
        lambda *refs: feed_back_body(n, pairs, steps, *refs),
        (steps,),
        (cot, slope, normed, gain, bias, up_weight, down_weight),
        [rows_of((tile, full)), rows_of((tile, inner)), rows_of((tile, full))]
        + [fixed((8, full))] * 2
        + [ANY] * 2,
        [shape((length, inner), BF16), shape((8, inner), F32), shape((8, width), F32)] + part_outs,
        [rows_of((tile, inner)), fixed((8, inner)), fixed((8, width))] + part_specs,
        scratch=[
            pltpu.VMEM((full, inner), BF16),
            pltpu.VMEM((inner, full), BF16),
            pltpu.VMEM((8, tile), F32),
            pltpu.SemaphoreType.DMA((n + 1,)),
        ]
        + parts.scratch(length, width),
        remote=pairs,
    )
    return (*got[:3], got[3:])


def norm_back(refs, n_parts, source, stat, sums, gain, full):
    grad = refs[0][...].astype(F32)
    for ref in refs[1:n_parts]:
        grad += ref[...].astype(F32)
    columns = sums[0][...]
    if len(sums) > 1:
        packed, far = sums[1:]

        @pl.when(pl.program_id(0) == 0)
        def _():
            far[...] = jnp.zeros_like(far)
            unpack(packed, far)

        tile = refs[0].shape[0]
        columns += far[:, pl.ds(pl.multiple_of(pl.program_id(0) * tile, tile), tile)]
    columns = columns.T
    mean, inv = stat[:, 0:1], stat[:, 1:2]
    scaled = (source[...] - mean) * inv
    back = inv * (
        grad * gain[0:1, :] - columns[:, 0:1] * (1.0 / full) - scaled * (columns[:, 1:2] * (1.0 / full))
    )
    return back, fold_rows(grad * scaled), fold_rows(grad)


def sum_specs(sums, tile, length):
    far = [pl.BlockSpec((EXTRA, v.shape[1]), lambda i: (length // EXTRA, 0)) for v in sums[1:]]
    return [cols_of((8, tile)), *far]


def hidden_back_body(k, m, full, *refs):
    parts, sums = refs[:k], refs[k : k + m]
    cot, hidden, stat, gain, wide, low, gain_sum, bias_sum, *more = refs[k + m :]
    sums = (*sums, *more)
    back, gain_part, bias_part = norm_back(parts, k, hidden, stat, sums, gain, full)
    value = cot[...].astype(F32) + back
    wide[...] = value
    low[...] = value.astype(BF16)
    accumulate(gain_sum, gain_part)
    accumulate(bias_sum, bias_part)


def hidden_back(parts, cotangent, row, hidden, stat, sums, gain, full):
    k, m, (length, width) = len(parts), len(sums), hidden.shape
    tile = min(256, length)
    steps = length // tile
    return call(
        "hidden_back",
        lambda *refs: hidden_back_body(k, m, full, *refs),
        (steps,),
        (*parts, *sums, cotangent, hidden, stat, gain),
        [rows_of((tile, width))] * k
        + sum_specs(sums, tile, length)
        + [
            pl.BlockSpec((tile, width), lambda i: (row * steps + i, 0)),
            rows_of((tile, width)),
            rows_of((tile, 128)),
            fixed((8, width)),
        ],
        [shape((length, width), F32), sent((length, width), BF16)] + [shape((8, width), F32)] * 2,
        [rows_of((tile, width))] * 2 + [fixed((8, width))] * 2,
        scratch=[pltpu.VMEM((8, length), F32)] * (m - 1),
    )


def attended_back_body(n, pairs, steps, *refs):
    count = 4 if pairs else n
    grads = Gathered(refs[:count], pairs, steps)
    weight, joined, out, *more = refs[count:]
    grads.attach(more)
    me = lax.axis_index("mp")
    width = grads.blocks[0].shape[1]

    def work(wait):
        for j, one in enumerate(grads.refs()):
            joined[:, place_of(me, j, width)] = one[...]
        out[...] = dot_nt(joined[...], weight[...]).astype(BF16)

    with_weights([], work, pairs, [grads])


def attended_back(n, pairs, grads, weight):
    length, width = grads[0].shape
    rows, full = weight.shape
    tile = min(256, length)
    steps = length // tile
    return call(
        "attended_back",
        lambda *refs: attended_back_body(n, pairs, steps, *refs),
        (steps,),
        (*grads, *(grads if pairs else ()), weight),
        Gathered.specs(grads, pairs, tile) + [fixed((rows, full))],
        [shape((length, full), BF16), shape((length, rows), BF16)],
        [rows_of((tile, full)), rows_of((tile, rows))],
        scratch=Gathered.scratch(grads, pairs, steps),
        remote=pairs,
    )


def project_back_body(n, pairs, steps, grad, normed, gain, bias, weight, *refs):
    parts = Scattered(pairs, n, steps, True)
    part_outs, refs = refs[: parts.count()], refs[parts.count() :]
    held, row_sums, sems, *refs = refs
    parts.attach(part_outs, refs)
    me = lax.axis_index("mp")
    width = gain.shape[1] // n
    copies = row_blocks(me, n, width, weight, held, sems, 0)

    def work(wait):
        def product(j):
            wait(copies[j : j + 1])
            return dot_nt(grad[...], held[j * width : (j + 1) * width, :])

        row_sums[...] = norm_sums(parts, n, product, normed, gain, bias, me)

    with_weights(copies, work, pairs)
    parts.finish(row_sums[...])


def project_back(n, pairs, grad, normed, gain, bias, weight):
    length, out = grad.shape
    full = weight.shape[0]
    width = full // n
    tile = min(256, length)
    steps = length // tile
    parts = Scattered(pairs, n, steps, True)
    part_outs, part_specs = parts.outs(length, width)
    return call(
        "project_back",
        lambda *refs: project_back_body(n, pairs, steps, *refs),
        (steps,),
        (grad, normed, gain, bias, weight),
        [rows_of((tile, out)), rows_of((tile, full))] + [fixed((8, full))] * 2 + [ANY],
        part_outs,
        part_specs,
        scratch=[
            pltpu.VMEM((full, out), BF16),
            pltpu.VMEM((8, tile), F32),
            pltpu.SemaphoreType.DMA((n,)),
        ]
        + parts.scratch(length, width),
        remote=pairs,
    )


def average_back_body(k, m, full, count, *refs):
    weights, parts, sums = refs[0], refs[1 : k + 1], refs[k + 1 : k + m + 1]
    source, stat, gain, hidden_grad, history = refs[k + m + 1 : k + m + 6]
    refs, more = (refs[:-1], refs[-1:]) if m > 1 else (refs, ())
    sums = (*sums, *more)
    grad_history, depth_sum, gain_sum, bias_sum, held = refs[-5:]
    back, gain_part, bias_part = norm_back(parts, k, source, stat, sums, gain, full)
    held[...] = hidden_grad[...] + back
    accumulate(gain_sum, gain_part)
    accumulate(bias_sum, bias_part)
    lanes = held.shape[1] // 128
    chunk = min(32, held.shape[0])
    folded = [0.0] * count
    for t in range(held.shape[0] // chunk):
        rows = slice(t * chunk, (t + 1) * chunk)
        value = held[rows, :]
        for j in range(count):
            grad_history[j, rows, :] = (weights[j] * value).astype(BF16)
            product = fold_rows(value * history[j, rows, :].astype(F32))
            for c in range(lanes):
                folded[j] = folded[j] + product[:, c * 128 : (c + 1) * 128]
    for j in range(count):
        accumulate(depth_sum.at[j], folded[j])


def average_back(weights, parts, source, stat, sums, gain, hidden_grad, history, row, made):
    k, m, (length, width) = len(parts), len(sums), source.shape
    count = history.shape[0]
    tile = min(256, length)
    steps = length // tile
    full = gain[1]
    block = pl.BlockSpec((count, tile, width), lambda i: (0, row * steps + i, 0))
    args = (weights, *parts, *sums, source, stat, gain[0], hidden_grad, history)
    specs = (
        [SMEM]
        + [rows_of((tile, width))] * k
        + sum_specs(sums, tile, length)
        + [rows_of((tile, width)), rows_of((tile, 128)), fixed((8, width)), rows_of((tile, width)), block]
    )
    more = {}
    if made is not None:
        more = {"aliases": {len(args): 0}}
        args, specs = (*args, made), specs + [ANY]
    return call(
        "average_back",
        lambda *refs: average_back_body(k, m, full, count, *refs),
        (steps,),
        args,
        specs,
        [shape(history.shape, BF16), shape((count, 8, 128), F32)] + [shape((8, width), F32)] * 2,
        [block, fixed((count, 8, 128))] + [fixed((8, width))] * 2,
        scratch=[pltpu.VMEM((tile, width), F32)] + [pltpu.VMEM((8, length), F32)] * (m - 1),
        **more,
    )


def divisor(size, most):
    return max(d for d in range(128, most + 1, 128) if size % d == 0) if size > 128 else size


def weight_body(rows, *refs):
    out = refs[-1]
    total = dot_tn(refs[0][...], refs[rows][...])
    for r in range(1, rows):
        total += dot_tn(refs[r][...], refs[rows + r][...])
    out[...] = total.astype(BF16)


def weight_grad(lefts, rights):
    rows, (length, high), wide = len(lefts), lefts[0].shape, rights[0].shape[1]
    tall, across = divisor(high, 1024), divisor(wide, 1024)
    return call(
        "weight_grad",
        lambda *refs: weight_body(rows, *refs),
        (high // tall, wide // across),
        (*lefts, *rights),
        [pl.BlockSpec((length, tall), lambda i, j: (0, i))] * rows
        + [pl.BlockSpec((length, across), lambda i, j: (0, j))] * rows,
        [shape((high, wide), BF16)],
        [pl.BlockSpec((tall, across), lambda i, j: (i, j))],
    )[0]


def put_blocks(came, outs, k, value):
    if came is not None:
        value = value + came[k].astype(F32)
    per = outs[0].shape[0]
    outs[k // per][k % per] = value.astype(BF16)


def tall_blocks_body(rows, count, fused, group, *refs):
    lefts, rights = refs[: rows * count], refs[rows * count : rows * count + rows]
    refs = refs[rows * count + rows :]
    came, outs, turned = refs[0] if fused else None, refs[fused:-1], refs[-1]
    length, high = lefts[0].shape

    @pl.when(pl.program_id(0) == 0)
    def _():
        for k in range(count):
            for r in range(rows):
                turned[k * high : (k + 1) * high, r * length : (r + 1) * length] = lefts[
                    k * rows + r
                ][...].T

    for k in range(count):
        total = 0.0
        for r in range(rows):
            total += dot_nn(
                turned[k * high : (k + 1) * high, r * length : (r + 1) * length], rights[r][...]
            )
        put_blocks(came, outs, k, total)


def wide_blocks_body(rows, count, fused, group, *refs):
    lefts, rights = refs[:rows], refs[rows : rows + rows * count]
    refs = refs[rows + rows * count :]
    came, outs = refs[0] if fused else None, refs[fused:]
    turned = [left[...].T for left in lefts]
    for k in range(count):
        total = 0.0
        for r in range(rows):
            total += dot_nn(turned[r], rights[k * rows + r][...])
        put_blocks(came, outs, k, total)


class Spread:
    def __init__(self, lefts, rights, dim, bits, part=(0, 1)):
        self.lefts, self.rights, self.dim, self.bits, self.part = lefts, rights, dim, list(bits), part
        self.groups = lax.axis_size("dp")
        self.block = (lefts, rights)[dim][0].shape[1] // self.groups
        order = [0]
        for bit in reversed(self.bits):
            order = order + [e | bit for e in order]
        self.order = order

    def blocks(self, half, came=None):
        count = self.groups // 2
        which = self.order[half * count : (half + 1) * count]
        rows, length = len(self.lefts), self.lefts[0].shape[0]
        group = lax.axis_index("dp").astype(jnp.int32)[None]
        size, (index, pieces) = self.block, self.part
        stay = [
            pl.BlockSpec((length, size), lambda i, group, e=e: (0, group[0] ^ e))
            for e in which
            for _ in range(rows)
        ]
        other = self.rights if self.dim == 0 else self.lefts
        extent = other[0].shape[1] // pieces
        tile = divisor(extent, 512)
        steps = extent // tile
        move = [pl.BlockSpec((length, tile), lambda i, group: (0, index * steps + i))] * rows

        def blocked(number):
            if self.dim == 0:
                return (
                    sent((number, size, extent), BF16),
                    pl.BlockSpec((number, size, tile), lambda i, group: (0, 0, i)),
                )
            return (
                sent((number, extent, size), BF16),
                pl.BlockSpec((number, tile, size), lambda i, group: (0, i, 0)),
            )

        if self.dim == 0:
            args = (*(list(self.lefts) * count), *self.rights)
            specs = stay + move
            body, scratch = tall_blocks_body, [pltpu.VMEM((count * size, rows * length), BF16)]
        else:
            args = (*self.lefts, *(list(self.rights) * count))
            specs = move + stay
            body, scratch = wide_blocks_body, []
        outs = [blocked(count)]
        if came is not None:
            args, specs = (*args, came), specs + [blocked(count)[1]]
            outs = [blocked(count // 2)] * 2
        return call(
            "weight_blocks",
            lambda *refs: body(rows, count, came is not None, *refs),
            (steps,),
            (group, *args),
            specs,
            [one[0] for one in outs],
            [one[1] for one in outs],
            scratch=scratch,
            prefetch=1,
        )

    def send(self, value):
        bit = self.bits[self.step]
        self.step += 1
        self.coming = lax.ppermute(value, "dp", [(i, i ^ bit) for i in range(self.groups)])

    def first(self):
        self.step = 0
        self.send(self.blocks(1)[0])

    def keep(self):
        self.held = self.blocks(0)[0]

    def keep_added(self):
        self.held, out = self.blocks(0, self.coming)
        self.send(out)


def fold_body(count, *refs):
    for i in range(count):
        held, came, keep, send = refs[2 * i], refs[2 * i + 1], refs[2 * count + 2 * i], refs[2 * count + 2 * i + 1]
        half = keep.shape[0]
        keep[...] = (held[:half].astype(F32) + came[:half].astype(F32)).astype(BF16)
        send[...] = (held[half:].astype(F32) + came[half:].astype(F32)).astype(BF16)


def advance(*spreads):
    steps = 4
    args, specs, outs, out_specs = [], [], [], []
    for one in spreads:
        count, high, wide = one.held.shape
        args += [one.held, one.coming]
        specs += [pl.BlockSpec((count, high // steps, wide), lambda i: (0, i, 0))] * 2
        outs += [sent((count // 2, high, wide), BF16)] * 2
        out_specs += [pl.BlockSpec((count // 2, high // steps, wide), lambda i: (0, i, 0))] * 2
    got = call("fold", lambda *refs: fold_body(len(spreads), *refs), (steps,), args, specs, outs, out_specs)
    for i, one in enumerate(spreads):
        one.held = got[2 * i]
        one.send(got[2 * i + 1])


def finish_body(groups, *refs):
    outs = refs[len(refs) - len(groups) :]
    at = 0
    for out, group in zip(outs, groups):
        for first, wide, count in group:
            total = refs[at][0].astype(F32)
            for ref in refs[at + 1 : at + count]:
                total += ref[0].astype(F32)
            out[:, first : first + wide] = total
            at += count


def finish(*groups):
    steps = 4
    args, specs, outs, out_specs, places = [], [], [], [], []
    for group in groups:
        first, place = 0, []
        for one in group:
            terms = [one.held, one.coming] if isinstance(one, Spread) else [one[None]]
            _, high, wide = terms[0].shape
            args += terms
            specs += [pl.BlockSpec((1, high // steps, wide), lambda i: (0, i, 0))] * len(terms)
            place.append((first, wide, len(terms)))
            first += wide
        outs.append(shape((high, first), F32))
        out_specs.append(rows_of((high // steps, first)))
        places.append(place)
    return call("finish", lambda *refs: finish_body(places, *refs), (steps,), args, specs, outs, out_specs)


def sums_body(groups, n, own, out, total, came, far, dp_sems, mp_sems):
    me = {"dp": lax.axis_index("dp"), "mp": lax.axis_index("mp")}
    peers = [("dp", b) for b in range(1, groups)] + [("mp", b) for b in range(1, n)]
    barrier = pltpu.get_barrier_semaphore()
    for axis, b in peers:
        pl.semaphore_signal(
            barrier, inc=1, device_id={axis: flip(me[axis], b)}, device_id_type=pl.DeviceIdType.MESH
        )
    pl.semaphore_wait(barrier, len(peers))

    def copy(axis, b, source, target, sems):
        return pltpu.make_async_remote_copy(
            src_ref=source,
            dst_ref=target.at[b - 1],
            send_sem=sems.at[0, b - 1],
            recv_sem=sems.at[1, b - 1],
            device_id={axis: flip(me[axis], b)},
            device_id_type=pl.DeviceIdType.MESH,
        )

    copies = [copy("dp", b, own, came, dp_sems) for b in range(1, groups)]
    for one in copies:
        one.start()
    for one in copies:
        one.wait()
    value = own[...]
    for b in range(groups - 1):
        value = value + came[b]
    out[...] = value
    total[...] = value[-8:]
    copies = [copy("mp", b, total, far, mp_sems) for b in range(1, n)]
    for one in copies:
        one.start()
    for one in copies:
        one.wait()
    value = total[...]
    for b in range(n - 1):
        value = value + far[b]
    out[-8:, :] = value


def sums(vectors, depth):
    groups, n = lax.axis_size("dp"), lax.axis_size("mp")
    sizes = [v.size for v in vectors]
    packed = jnp.concatenate(vectors)
    packed = jnp.pad(packed, (0, -packed.size % 1024)).reshape(-1, 128)
    packed = jnp.concatenate([packed, jnp.pad(depth[None], ((0, 7), (0, 128 - depth.size)))])
    high = packed.shape[0]
    got = call(
        "sums",
        lambda *refs: sums_body(groups, n, *refs),
        (1,),
        (packed,),
        [fixed((high, 128))],
        [shape((high, 128), F32)],
        [fixed((high, 128))],
        scratch=[
            pltpu.VMEM((8, 128), F32),
            pltpu.VMEM((groups - 1, high, 128), F32),
            pltpu.VMEM((n - 1, 8, 128), F32),
            pltpu.SemaphoreType.DMA((2, groups - 1)),
            pltpu.SemaphoreType.DMA((2, n - 1)),
        ],
        remote=True,
    )[0]
    flat = got.reshape(-1)
    ends = np.cumsum(sizes)
    return [flat[end - size : end] for end, size in zip(ends, sizes)], got[-8, : depth.size]


def output_body(rows, steps, *refs):
    bias, out = refs[-2:]
    per = (len(refs) - 2) // rows
    for r in range(rows):

        @pl.when(pl.program_id(0) // steps == r)
        def _(r=r):
            total = bias[0:1, :]
            for part in refs[r * per + 1 : (r + 1) * per]:
                total = total + part[...].astype(F32)
            out[...] = (refs[r * per][...] + total).astype(BF16)


def output(parts, hidden, bias):
    rows, (length, width) = len(hidden), hidden[0].shape
    tile = min(512, length)
    steps = length // tile
    args, specs = [], []
    for r in range(rows):
        args += [hidden[r], *parts[r]]
        specs += [
            pl.BlockSpec((tile, width), lambda i, r=r: (jnp.clip(i - r * steps, 0, steps - 1), 0))
        ] * (1 + len(parts[r]))
    return call(
        "output",
        lambda *refs: output_body(rows, steps, *refs),
        (rows * steps,),
        (*args, bias),
        specs + [fixed((8, width))],
        [shape((rows * length, width), BF16)],
        [rows_of((tile, width))],
    )[0]


class Ring:
    def __init__(self):
        self.n = lax.axis_size("mp")
        self.me = lax.axis_index("mp").astype(jnp.int32)
        self.pairs = self.n == 4
        self.core = [(i, i ^ 1) for i in range(self.n)]
        self.chip = [(i, i ^ 2) for i in range(self.n)]

    def over_core(self, value):
        return lax.ppermute(value, "mp", self.core)

    def over_chip(self, value):
        return lax.ppermute(value, "mp", self.chip)

    def gather_start(self, block):
        if self.pairs:
            return [block, self.over_chip(block)]
        return self.gather(block)

    def gather(self, block):
        if self.pairs:
            across = self.over_chip(block)
            return [block, self.over_core(block), across, self.over_core(across)]
        every = lax.all_gather(block, "mp")
        return [
            lax.dynamic_index_in_dim(every, self.me ^ j, 0, keepdims=False) for j in range(self.n)
        ]

    def scatter(self, parts, sums=False):
        parts, extra = (parts[:-1], parts[-1:]) if sums else (parts, [])
        if self.pairs:
            came = self.over_chip(parts[1])
            return [parts[0], came], [*extra, came] if sums else []
        stacked = jnp.stack([part.astype(F32) for part in parts])
        ordered = jnp.take(stacked, self.me ^ jnp.arange(self.n), axis=0)
        total = lax.psum_scatter(ordered, "mp", scatter_dimension=0, tiled=False)
        return [total], [lax.psum(v, "mp") for v in extra]

    def total(self, value):
        if self.pairs:
            value = value + self.over_core(value)
            return value + self.over_chip(value)
        return lax.psum(value, "mp")

    def out_start(self, weight):
        rows, groups = weight.shape[0], lax.axis_size("dp")
        if self.pairs and rows % (16 * groups) == 0:
            size = rows // groups
            piece = lax.dynamic_slice_in_dim(weight, lax.axis_index("dp") * size, size, 0)
            return self.over_chip(piece)
        return None

    def out_middle(self, piece):
        return None if piece is None else lax.all_gather(piece, "dp", axis=0, tiled=True)

    def out_end(self, weight, across):
        if across is None:
            return self.gather(weight)
        across = gate([across])[0]
        return [weight, self.over_core(weight), across, self.over_core(across)]


def tables_of(length):
    half = HEAD // 2
    rate = np.exp(np.arange(half, dtype=np.float64) * (-math.log(10000.0) / half))
    angle = np.arange(length, dtype=np.float64)[:, None] * rate[None, :]
    cosine, sine = np.cos(angle), np.sin(angle)
    return (
        jnp.asarray(np.concatenate([cosine, cosine], 1), F32),
        jnp.asarray(np.concatenate([-sine, sine], 1), F32),
    )


def local(
    history,
    depth_weights,
    segment_ids,
    first_gain,
    first_bias,
    qkv_weight,
    out_weight,
    second_gain,
    second_bias,
    up_weight,
    up_bias,
    down_weight,
    down_bias,
    cotangent,
):
    ring = Ring()
    n = ring.n
    pairs = ring.pairs
    width = history.shape[2]
    full = n * width
    row_count, length = segment_ids.shape
    rows = range(row_count)
    tables = tables_of(length)
    earlier = (segment_ids[:, None, :] < segment_ids[:, :, None]).astype(jnp.int32)
    starts = jnp.broadcast_to(jnp.sum(earlier, -1)[:, None, :], (row_count, 8, length))

    up_bias8 = jnp.broadcast_to(up_bias[None], (8, up_bias.shape[0]))

    down_bias8 = jnp.broadcast_to(down_bias[None], (8, width))
    groups = lax.axis_size("dp")
    spread = full % (128 * groups) == 0 and groups >= 4
    last = row_count - 1

    Order.last, Order.names, Order.cost = None, 0, LARGE
    vectors = jnp.stack([first_gain, first_bias, second_gain, second_bias])
    vectors = ring.gather_start(jnp.repeat(vectors, 8, 0))
    piece = ring.out_start(out_weight)
    cot_rows = [lax.slice_in_dim(cotangent, r * length, (r + 1) * length) for r in rows]
    none = [None] * row_count
    wide, low, xs, qkv, normed1, stat1 = (list(none) for _ in range(6))
    attended, logs, heads, cots = (list(none) for _ in range(4))
    hidden, normed2, stat2, activated, slope = (list(none) for _ in range(5))
    branch, up_grad, parts2, parts1 = (list(none) for _ in range(4))
    hidden_grad, grads, grad_full, qkv_grad = (list(none) for _ in range(4))
    up_bias_sum = down_bias_sum = gain2_sum = bias2_sum = 0.0

    for r in rows:
        wide[r], low[r] = average(depth_weights, history, r, length)
        if r == 0:
            xs[0] = ring.gather_start(low[0])
            if pairs:
                vectors[1], piece = gate([vectors[1], piece])
                vectors = [
                    vectors[0],
                    ring.over_core(vectors[0]),
                    vectors[1],
                    ring.over_core(vectors[1]),
                ]
            across = ring.out_middle(piece)
    vectors = jnp.concatenate(vectors, 1)
    gain1, bias1, gain2, bias2 = (vectors[8 * i : 8 * i + 8] for i in range(4))
    own1, own2 = gain1[:, :width], gain2[:, :width]
    for r in rows[1:]:
        xs[r] = ring.gather_start(gate([low[r]], xs[r - 1][1:2])[0])
    for r in rows:
        qkv[r], normed1[r], stat1[r], xs[r] = project(
            n, pairs, xs[r], gain1, bias1, tables, qkv_weight
        )
        attended[r], logs[r] = attend(starts[r], qkv[r])
        heads[r] = ring.gather_start(attended[r])
        if r == last:
            out_w = ring.out_end(out_weight, across)

    for r in rows:
        cots[r] = ring.gather_start(gate([cot_rows[r]])[0])
        got = feed(
            n,
            pairs,
            heads[r],
            xs[r],
            out_w,
            wide[r],
            gain2,
            bias2,
            up_bias8,
            up_weight,
            down_weight,
        )
        hidden[r], normed2[r], stat2[r], activated[r], slope[r], parts = got
        branch[r] = ring.scatter(parts)[0]

    def spread_over_dp(value, dim):
        return lax.psum_scatter(value, "dp", scatter_dimension=dim, tiled=True)

    if pairs:
        cot_full = join(cots, full)
        branch[0][1] = gate(branch[0][1:])[0]
    else:
        cot_full = [lax.all_gather(v, "mp", axis=1, tiled=True) for v in cot_rows]
    down_sum = spread_over_dp(weight_grad(activated, cot_full), 1)

    for r in rows:
        up_grad[r], up_sum, cot_sum, parts = feed_back(
            n, pairs, cot_full[r], slope[r], normed2[r], gain2, bias2, up_weight, down_weight
        )
        up_bias_sum += up_sum
        down_bias_sum += cot_sum
        parts2[r] = ring.scatter(parts, True)
        if r == 0 and pairs:
            branch[last][1] = gate(branch[last][1:])[0]

    def hidden_step(r):
        nonlocal gain2_sum, bias2_sum
        parts, row_sums = parts2[r]
        hidden_grad[r], low_grad, gain_part, bias_part = hidden_back(
            parts, cotangent, r, hidden[r], stat2[r], row_sums, own2, full
        )
        gain2_sum += gain_part
        bias2_sum += bias_part
        grads[r] = ring.gather_start(low_grad)

    hidden_step(0)
    if spread:
        up_sum = Spread(normed2, up_grad, 0, (1, 2, 4))
        up_sum.first()
    made = output(branch, hidden, down_bias8)
    for r in rows[1:]:
        hidden_step(r)

    for r in rows:
        grad_full[r], attended_grad = attended_back(n, pairs, grads[r], out_weight)
        qkv_grad[r] = attend_back(starts[r], tables, qkv[r], attended_grad, logs[r])
        if r == last and spread:
            qkv_sum = [
                Spread(normed1, qkv_grad, 0, (1, 2, 4), (0, 2)),
                Spread(normed1, qkv_grad, 0, (1, 2, 4), (1, 2)),
            ]
            qkv_sum[0].first()
        if r > 0 and pairs:
            parts, row_sums = parts1[r - 1]
            parts[1] = row_sums[1] = gate([parts[1]])[0]
        parts = project_back(n, pairs, qkv_grad[r], normed1[r], gain1, bias1, qkv_weight)
        parts1[r] = ring.scatter(parts, True)

    if spread:
        down_sum = gate([down_sum])[0]
        up_sum.keep_added()
        qkv_sum[1].first()
        out_sum = Spread(attended, grad_full, 1, (1, 2, 4))
        out_sum.first()

    grad_history, depth_sum, gain1_sum, bias1_sum = None, 0.0, 0.0, 0.0
    for r in rows:
        parts, row_sums = parts1[r]
        grad_history, depth_part, gain_part, bias_part = average_back(
            depth_weights,
            parts,
            wide[r],
            stat1[r],
            row_sums,
            (own1, full),
            hidden_grad[r],
            history,
            r,
            grad_history,
        )
        depth_sum += depth_part
        gain1_sum += gain_part
        bias1_sum += bias_part
        if r == 0:
            if pairs:
                parts, row_sums = parts1[last]
                parts[1] = row_sums[1] = gate([parts[1]])[0]
            if spread:
                qkv_sum[0].keep_added()
                advance(up_sum)

    Order.cost = TINY
    vectors = [up_bias_sum, down_bias_sum, gain2_sum, bias2_sum, gain1_sum, bias1_sum]
    vectors, depth_part = [jnp.sum(v, 0) for v in vectors], jnp.sum(depth_sum, (1, 2))
    if spread:
        qkv_sum[1].keep_added()
        out_sum.keep_added()
        up_sum.coming = gate([up_sum.coming])[0]
        advance(qkv_sum[0])
        totals, depth_grad = sums(vectors, depth_part)
        advance(qkv_sum[1], out_sum)
    else:
        qkv_sum = [spread_over_dp(weight_grad(normed1, qkv_grad), 0)]
        out_sum = spread_over_dp(weight_grad(attended, grad_full), 1)
        up_sum = spread_over_dp(weight_grad(normed2, up_grad), 0)
        totals, depth_grad = sums(vectors, depth_part)
    down_total, up_total, out_total, qkv_total = finish([down_sum], [up_sum], [out_sum], qkv_sum)
    return (
        made,
        grad_history,
        depth_grad,
        totals[4],
        totals[5],
        qkv_total,
        out_total,
        totals[2],
        totals[3],
        up_total,
        totals[0],
        down_total,
        totals[1],
    )


def solution(mesh):
    placed = (
        P(None, "dp", "mp"),
        P(),
        P("dp", None),
        P("mp"),
        P("mp"),
        P(None, "mp"),
        P("mp", None),
        P("mp"),
        P("mp"),
        P(None, "mp"),
        P("mp"),
        P("mp", None),
        P("mp"),
        P("dp", "mp"),
    )
    return jax.shard_map(
        local,
        mesh=mesh,
        in_specs=placed,
        out_specs=(
            P("dp", "mp"),
            P(None, "dp", "mp"),
            P(),
            P("mp"),
            P("mp"),
            P("dp", "mp"),
            P("mp", "dp"),
            P("mp"),
            P("mp"),
            P("dp", "mp"),
            P("mp"),
            P("mp", "dp"),
            P("mp"),
        ),
        check_vma=False,
    )
```

```python
import math

import jax
import jax.numpy as jnp
import numpy as np
from jax import lax
from jax.experimental import pallas as pl
from jax.experimental.pallas import tpu as pltpu
from jax.sharding import PartitionSpec as P

HEAD = 128
MAX_DOC = 512
EPSILON = 1e-05
SQRT_HALF = 0.7071067811865476
INV_ROOT_TWO_PI = 0.3989422804014327
LOG2E = 1.4426950408889634
SCALE = HEAD ** (-0.5)
MIB = 2**20
BF16 = jnp.bfloat16
F32 = jnp.float32


def dot_nn(a, b):
    return jnp.dot(a, b, preferred_element_type=F32)


def dot_nt(a, b):
    return lax.dot_general(a, b, (((1,), (1,)), ((), ())), preferred_element_type=F32)


def dot_tn(a, b):
    return lax.dot_general(a, b, (((0,), (0,)), ((), ())), preferred_element_type=F32)


LARGE, TINY = 10**12, 10**4


class Order:
    last = None
    names = 0
    cost = LARGE

    @staticmethod
    def name(remote):
        Order.names += remote
        return Order.names - 1 if remote else None


def call(
    name, body, grid, args, in_specs, outs, out_specs, scratch=(), prefetch=0, after=(), aliases=None, remote=False
):
    count = len(args)
    extra = [*after]
    if Order.last is not None and not any(Order.last is a for a in args):
        extra.append(Order.last)

    def without_extra(*refs):
        body(*refs[:count], *refs[count + len(extra) :])

    got = pl.pallas_call(
        without_extra,
        grid_spec=pltpu.PrefetchScalarGridSpec(
            num_scalar_prefetch=prefetch,
            grid=grid,
            in_specs=list(in_specs) + [ANY] * len(extra),
            out_specs=out_specs,
            scratch_shapes=list(scratch),
        ),
        out_shape=outs,
        input_output_aliases=aliases or {},
        compiler_params=pltpu.CompilerParams(
            vmem_limit_bytes=60 * MIB, collective_id=Order.name(remote), has_side_effects=remote
        ),
        cost_estimate=pl.CostEstimate(flops=Order.cost, bytes_accessed=Order.cost // 10**4, transcendentals=0),
        name=name,
    )(*args, *extra)
    fresh = [v for i, v in enumerate(got) if i not in (aliases or {}).values()]
    Order.last = min(fresh or got, key=lambda v: v.size)
    return got


def shape(dims, dtype):
    return jax.ShapeDtypeStruct(dims, dtype)


def sent(dims, dtype):
    return pltpu.HBM(dims, dtype)


SMEM = pl.BlockSpec(memory_space=pltpu.SMEM)
ANY = pl.BlockSpec(memory_space=pl.ANY)


def gate(arrays, after=()):
    arrays = list(arrays)
    return call(
        "gate",
        lambda *refs: None,
        (1,),
        arrays,
        [ANY] * len(arrays),
        [shape(a.shape, a.dtype) for a in arrays],
        [ANY] * len(arrays),
        after=after,
        aliases={i: i for i in range(len(arrays))},
    )


def rows_of(block):
    return pl.BlockSpec(block, lambda i: (i, 0))


def cols_of(block):
    return pl.BlockSpec(block, lambda i: (0, i))


def fixed(block):
    return pl.BlockSpec(block, lambda i: (0,) * len(block))


def flip(me, j):
    there, bit = me, 1
    while bit <= j:
        if j & bit:
            there = there + bit * (1 - 2 * ((me // bit) % 2))
        bit *= 2
    return there


def place_of(me, j, width):
    return pl.ds(pl.multiple_of(flip(me, j) * width, width), width)


def greet():
    barrier = pltpu.get_barrier_semaphore()
    sibling = flip(lax.axis_index("mp"), 1)
    pl.semaphore_signal(
        barrier, inc=1, device_id={"mp": sibling}, device_id_type=pl.DeviceIdType.MESH
    )
    pl.semaphore_wait(barrier, 1)


def to_sibling(source, target, sems, at):
    return pltpu.make_async_remote_copy(
        src_ref=source,
        dst_ref=target,
        send_sem=sems.at[0, at],
        recv_sem=sems.at[1, at],
        device_id={"mp": flip(lax.axis_index("mp"), 1)},
        device_id_type=pl.DeviceIdType.MESH,
    )


class Gathered:
    def __init__(self, refs, pairs, steps):
        self.pairs, self.steps = pairs, steps
        self.blocks, self.whole = refs[:2] if pairs else refs, refs[2:4] if pairs else ()

    @staticmethod
    def specs(blocks, pairs, tile):
        width = blocks[0].shape[1]
        return [rows_of((tile, width))] * len(blocks) + ([ANY] * 2 if pairs else [])

    @staticmethod
    def scratch(blocks, pairs, steps):
        if not pairs:
            return []
        return [pltpu.VMEM((2, *blocks[0].shape), BF16), pltpu.SemaphoreType.DMA((2, 2 * steps))]

    def attach(self, refs):
        if self.pairs:
            self.came, self.sems = refs
        return self

    def copies(self, step):
        tile = self.blocks[0].shape[0]
        rows = pl.ds(pl.multiple_of(step * tile, tile), tile)
        return [
            to_sibling(self.whole[k].at[rows, :], self.came.at[k, rows, :], self.sems, 2 * step + k)
            for k in range(2)
        ]

    def start(self):
        if self.pairs:
            for step in range(self.steps):
                for one in self.copies(step):
                    one.start()

    def refs(self):
        if not self.pairs:
            return self.blocks
        step = pl.program_id(0)
        tile = self.blocks[0].shape[0]
        for one in self.copies(step):
            one.wait()
        rows = pl.ds(pl.multiple_of(step * tile, tile), tile)
        return [self.blocks[0], self.came.at[0, rows, :], self.blocks[1], self.came.at[1, rows, :]]


EXTRA = 16


def pack(sums, width):
    rows = []
    for s in range(2):
        rest = sums[s : s + 1, :]
        for _ in range(3):
            piece = rest.astype(BF16).astype(F32)
            rest = rest - piece
            rows += [piece[:, h : h + width] for h in range(0, sums.shape[1], width)]
    assert len(rows) <= EXTRA
    rows += [jnp.zeros((1, width), F32)] * (EXTRA - len(rows))
    return jnp.concatenate(rows).astype(BF16)


def unpack(packed, target):
    width = packed.shape[1]
    per = target.shape[1] // width
    value = packed[...].astype(F32)
    for s in range(2):
        for h in range(per):
            at = [(3 * s + p) * per + h for p in range(3)]
            total = value[at[0] : at[0] + 1] + value[at[1] : at[1] + 1] + value[at[2] : at[2] + 1]
            target[s : s + 1, h * width : (h + 1) * width] = total


class Scattered:
    def __init__(self, pairs, n, steps, with_sums):
        self.pairs, self.n, self.steps, self.with_sums = pairs, n, steps, with_sums

    def outs(self, length, width):
        tile = length // self.steps
        if self.pairs:
            high = length + EXTRA * self.with_sums
            outs = [shape((length, width), BF16), sent((high, width), BF16)]
            specs = [fixed((length, width)), fixed((high, width))]
            if self.with_sums:
                outs, specs = outs + [shape((8, length), F32)], specs + [fixed((8, length))]
            return outs, specs
        outs, specs = [shape((length, width), BF16)] * self.n, [rows_of((tile, width))] * self.n
        if self.with_sums:
            outs, specs = outs + [shape((8, length), F32)], specs + [cols_of((8, tile))]
        return outs, specs

    def count(self):
        return (2 if self.pairs else self.n) + self.with_sums

    def scratch(self, length, width):
        if not self.pairs:
            return []
        tile = length // self.steps
        block = pltpu.VMEM((self.steps, 2, tile, width), BF16)
        made = [block, block, pltpu.VMEM((2, 2, tile, width), F32)]
        if self.with_sums:
            made += [pltpu.VMEM((self.steps, 8, tile), F32)] * 3
        return made + [pltpu.SemaphoreType.DMA((2, 3 * self.steps))]

    def attach(self, outs, scratch):
        self.out = outs
        if self.pairs:
            self.send, self.came, self.kept = scratch[:3]
            self.sums = scratch[3:-1]
            self.sems = scratch[-1]
        return self

    def copies(self, step):
        made = [
            to_sibling(self.send.at[step, k], self.came.at[step, k], self.sems, 3 * step + k)
            for k in range(2)
        ]
        if self.with_sums:
            made.append(to_sibling(self.sums[0].at[step], self.sums[1].at[step], self.sems, 3 * step + 2))
        return made

    def put(self, j, value):
        step = pl.program_id(0)
        if not self.pairs:
            self.out[j][...] = value.astype(BF16)
        elif j % 2:
            self.send[step, j // 2] = value.astype(BF16)
        else:
            self.kept[step % 2, j // 2] = value

    def take(self, step):
        tile = self.kept.shape[2]
        for one in self.copies(step):
            one.wait()
        rows = pl.ds(pl.multiple_of(step * tile, tile), tile)
        for k in range(2):
            total = self.kept[step % 2, k] + self.came[step, k].astype(F32)
            self.out[k][rows, :] = total.astype(BF16)
        if self.with_sums:
            self.out[2][:, rows] = self.sums[2][step] + self.sums[1][step]

    def finish(self, sums=None):
        if not self.pairs:
            if sums is not None:
                self.out[-1][...] = sums
            return
        step = pl.program_id(0)
        if sums is not None:
            self.sums[0][step] = sums
            self.sums[2][step] = sums
        for one in self.copies(step):
            one.start()

        @pl.when(step > 0)
        def _():
            self.take(step - 1)

        @pl.when(step == self.steps - 1)
        def _():
            self.take(step)
            if self.with_sums:
                length, width = self.out[0].shape
                self.out[1][length:, :] = pack(self.out[2][...], width)


def with_weights(copies, work, remote=False, gathered=()):
    @pl.when(pl.program_id(0) == 0)
    def _():
        for one in copies:
            one.start()
        if remote:
            greet()
        for one in gathered:
            one.start()

        def wait(some):
            for one in some:
                one.wait()

        work(wait)

    @pl.when(pl.program_id(0) != 0)
    def _():
        work(lambda some: None)


def row_blocks(me, n, width, source, target, sems, base):
    return [
        pltpu.make_async_copy(
            source.at[place_of(me, j, width), :],
            target.at[pl.ds(j * width, width), :],
            sems.at[base + j],
        )
        for j in range(n)
    ]


def col_blocks(me, n, width, source, target, sems, base):
    return [
        pltpu.make_async_copy(
            source.at[:, place_of(me, j, width)],
            target.at[:, pl.ds(j * width, width)],
            sems.at[base + j],
        )
        for j in range(n)
    ]


def stat_columns(first, second):
    lane = lax.broadcasted_iota(jnp.int32, (first.shape[0], 128), 1)
    return jnp.where(lane == 0, first, jnp.where(lane == 1, second, 0.0))


def fold_rows(values):
    return jnp.sum(values.reshape(values.shape[0] // 8, 8, values.shape[1]), 0)


def accumulate(ref, value):
    @pl.when(pl.program_id(0) == 0)
    def _():
        ref[...] = value

    @pl.when(pl.program_id(0) != 0)
    def _():
        ref[...] += value


def average_body(weights, history, wide, low):
    chunk = min(32, wide.shape[0])
    for t in range(wide.shape[0] // chunk):
        rows = slice(t * chunk, (t + 1) * chunk)
        total = weights[0] * history[0, rows, :].astype(F32)
        for j in range(1, history.shape[0]):
            total += weights[j] * history[j, rows, :].astype(F32)
        wide[rows, :] = total
        low[rows, :] = total.astype(BF16)


def average(weights, history, row, length):
    count, _, width = history.shape
    tile = min(256, length)
    steps = length // tile
    return call(
        "average",
        average_body,
        (steps,),
        (weights, history),
        [SMEM, pl.BlockSpec((count, tile, width), lambda i: (0, row * steps + i, 0))],
        [shape((length, width), F32), sent((length, width), BF16)],
        [rows_of((tile, width))] * 2,
    )


def project_body(n, pairs, steps, *refs):
    count = 4 if pairs else n
    x = Gathered(refs[:count], pairs, steps)
    gain, bias, cosine, sine, weight, qkv, normed, stat = refs[count : count + 8]
    refs = refs[count + 8 :]
    shared = refs[:2] if pairs else ()
    held, joined, sems, *more = refs[len(shared) :]
    x.attach(more)
    me = lax.axis_index("mp")
    tile, width = x.blocks[0].shape
    full = n * width
    heads = held.shape[1] // (3 * HEAD)
    sub = min(256, tile)
    copies = row_blocks(me, n, width, weight, held, sems, 0)

    def work(wait):
        xs = x.refs()
        for out, k in zip(shared, (1, 3)):
            out[...] = xs[k][...]
        for t in range(tile // sub):
            rows = slice(t * sub, (t + 1) * sub)
            total = square = 0.0
            for one in xs:
                value = one[rows, :].astype(F32)
                total += jnp.sum(value, 1, keepdims=True)
                square += jnp.sum(value * value, 1, keepdims=True)
            mean = total / full
            inv = lax.rsqrt(square / full - mean * mean + EPSILON)
            stat[rows, :] = stat_columns(mean, inv)
            for j, one in enumerate(xs):
                part = slice(j * width, (j + 1) * width)
                value = (one[rows, :].astype(F32) - mean) * inv * gain[0:1, part] + bias[0:1, part]
                joined[rows, part] = value.astype(BF16)
                normed[rows, place_of(me, j, width)] = value.astype(BF16)
            if t == 0:
                wait(copies)
            for h in range(heads):
                base = 3 * h * HEAD
                out = dot_nn(joined[rows, :], held[:, base : base + 3 * HEAD])
                for s in range(2):
                    v = out[:, s * HEAD : (s + 1) * HEAD]
                    turned = v * cosine[rows, :] + pltpu.roll(v, HEAD // 2, 1) * sine[rows, :]
                    qkv[rows, base + s * HEAD : base + (s + 1) * HEAD] = turned.astype(BF16)
                qkv[rows, base + 2 * HEAD : base + 3 * HEAD] = out[:, 2 * HEAD :].astype(BF16)

    with_weights(copies, work, pairs, [x])


def project(n, pairs, xs, gain, bias, tables, weight):
    length, width = xs[0].shape
    full, out = weight.shape
    tile = min(512, length)
    steps = length // tile
    got = call(
        "project",
        lambda *refs: project_body(n, pairs, steps, *refs),
        (steps,),
        (*xs, *(xs if pairs else ()), gain, bias, *tables, weight),
        Gathered.specs(xs, pairs, tile)
        + [fixed((8, full))] * 2
        + [rows_of((tile, HEAD))] * 2
        + [ANY],
        [shape((length, out), BF16), shape((length, full), BF16), shape((length, 128), F32)]
        + [shape((length, width), BF16)] * (2 * pairs),
        [rows_of((tile, out)), rows_of((tile, full)), rows_of((tile, 128))]
        + [rows_of((tile, width))] * (2 * pairs),
        scratch=[
            pltpu.VMEM((full, out), BF16),
            pltpu.VMEM((tile, full), BF16),
            pltpu.SemaphoreType.DMA((n,)),
        ]
        + Gathered.scratch(xs, pairs, steps),
        remote=pairs,
    )
    return *got[:3], [xs[0], got[3], xs[1], got[4]] if pairs else xs


def windows(length):
    block = min(256, length)
    for i in range(length // block):
        low = max(0, i * block - (MAX_DOC - 1)) // block * block
        yield slice(i * block, (i + 1) * block), slice(low, (i + 1) * block)


def score_mask(start, q_part, k_part):
    dims = (k_part.stop - k_part.start, q_part.stop - q_part.start)
    k_pos = lax.broadcasted_iota(jnp.int32, dims, 0) + k_part.start
    q_pos = lax.broadcasted_iota(jnp.int32, dims, 1) + q_part.start
    return (k_pos >= start[0:1, q_part]) & (k_pos <= q_pos)


def attend_body(start, qkv, out, logs):
    length = qkv.shape[0]
    value_t = qkv[:, 2 * HEAD :].T
    for q_part, k_part in windows(length):
        query, key = qkv[q_part, :HEAD], qkv[k_part, HEAD : 2 * HEAD]
        scores = dot_nt(key, query) * (SCALE * LOG2E)
        scores = jnp.where(score_mask(start, q_part, k_part), scores, -1e30)
        top = jnp.max(scores, 0, keepdims=True)
        probs = jnp.exp2(scores - top)
        total = jnp.sum(probs, 0, keepdims=True)
        logs[0, :, q_part] = jnp.broadcast_to(top + jnp.log2(total), (8, q_part.stop - q_part.start))
        got = dot_nn(value_t[:, k_part], probs.astype(BF16)) / total
        out[q_part, :] = got.T.astype(BF16)


def attend(start, qkv):
    length, width = qkv.shape
    heads = width // (3 * HEAD)
    return call(
        "attend",
        attend_body,
        (heads,),
        (start, qkv),
        [fixed((8, length)), cols_of((length, 3 * HEAD))],
        [sent((length, heads * HEAD), BF16), shape((heads, 8, length), F32)],
        [cols_of((length, HEAD)), pl.BlockSpec((1, 8, length), lambda i: (i, 0, 0))],
    )


def attend_back_body(start, cosine, sine, qkv, grad, logs, out, key_sum, value_sum):
    length = qkv.shape[0]
    key_t = qkv[:, HEAD : 2 * HEAD].T
    key_sum[...] = jnp.zeros_like(key_sum)
    value_sum[...] = jnp.zeros_like(value_sum)

    def turn_back(v, part):
        return (
            v * cosine[part, :] - pltpu.roll(v, HEAD // 2, 1) * sine[part, :]
        ).astype(BF16)

    for q_part, k_part in windows(length):
        query, key = qkv[q_part, :HEAD], qkv[k_part, HEAD : 2 * HEAD]
        value, g = qkv[k_part, 2 * HEAD :], grad[q_part, :]
        scores = dot_nt(key, query) * (SCALE * LOG2E) - logs[0, 0:1, q_part]
        probs = jnp.exp2(jnp.where(score_mask(start, q_part, k_part), scores, -1e30))
        prob_grad = dot_nt(value, g)
        mean = jnp.sum(prob_grad * probs, 0, keepdims=True)
        score_grad = (probs * (prob_grad - mean)).astype(BF16)
        value_sum[k_part, :] += dot_nn(probs.astype(BF16), g)
        key_sum[k_part, :] += dot_nn(score_grad, query)
        query_grad = dot_nn(key_t[:, k_part], score_grad) * SCALE
        out[q_part, :HEAD] = turn_back(query_grad.T, q_part)
    for q_part, _ in windows(length):
        out[q_part, HEAD : 2 * HEAD] = turn_back(key_sum[q_part, :] * SCALE, q_part)
        out[q_part, 2 * HEAD :] = value_sum[q_part, :].astype(BF16)


def attend_back(start, tables, qkv, grad, logs):
    length, width = qkv.shape
    heads = width // (3 * HEAD)
    return call(
        "attend_back",
        attend_back_body,
        (heads,),
        (start, *tables, qkv, grad, logs),
        [fixed((8, length))]
        + [fixed((length, HEAD))] * 2
        + [
            cols_of((length, 3 * HEAD)),
            cols_of((length, HEAD)),
            pl.BlockSpec((1, 8, length), lambda i: (i, 0, 0)),
        ],
        [shape((length, width), BF16)],
        [cols_of((length, 3 * HEAD))],
        scratch=[pltpu.VMEM((length, HEAD), F32)] * 2,
    )[0]


def feed_body(n, pairs, steps, *refs):
    count = 4 if pairs else n
    attended = Gathered(refs[:count], pairs, steps)
    refs = refs[count:]
    xs, outs_w = refs[: n - 1], refs[n - 1 : 2 * n - 1]
    own, gain, bias, up_bias, up_weight, down_weight = refs[2 * n - 1 : 2 * n + 5]
    refs = refs[2 * n + 5 :]
    hidden, normed, stat, activated, slope = refs[:5]
    refs = refs[5:]
    parts = Scattered(pairs, n, steps, False)
    part_outs, refs = refs[: parts.count()], refs[parts.count() :]
    out_held, up_held, down_held, joined, whole, sems, *refs = refs
    if pairs:
        attended.attach(refs[:2])
        refs = refs[2:]
    parts.attach(part_outs, refs)
    me = lax.axis_index("mp")
    width = own.shape[1]
    full = n * width
    inner = up_held.shape[1]
    out_copies = []
    for j in range(n):
        for k in range(n):
            out_copies.append(
                pltpu.make_async_copy(
                    outs_w[k].at[:, place_of(me, j, width)],
                    out_held.at[pl.ds(k * width, width), pl.ds(j * width, width)],
                    sems.at[j * n + k],
                )
            )
    up_copies = row_blocks(me, n, width, up_weight, up_held, sems, n * n)
    down_copies = col_blocks(me, n, width, down_weight, down_held, sems, n * n + n)

    def work(wait):
        for j, one in enumerate(attended.refs()):
            joined[:, j * width : (j + 1) * width] = one[...]
        total = square = 0.0
        for j in range(n):
            wait(out_copies[j * n : (j + 1) * n])
            part = slice(j * width, (j + 1) * width)
            base = own[...] if j == 0 else xs[j - 1][...].astype(F32)
            value = base + dot_nn(joined[...], out_held[:, part])
            whole[:, part] = value
            if j == 0:
                hidden[...] = value
            total += jnp.sum(value, 1, keepdims=True)
            square += jnp.sum(value * value, 1, keepdims=True)
        mean = total / full
        inv = lax.rsqrt(square / full - mean * mean + EPSILON)
        stat[...] = stat_columns(mean, inv)
        for j in range(n):
            part = slice(j * width, (j + 1) * width)
            value = ((whole[:, part] - mean) * inv * gain[0:1, part] + bias[0:1, part]).astype(BF16)
            joined[:, part] = value
            normed[:, place_of(me, j, width)] = value
        wait(up_copies)
        step = divisor(inner, 512)
        for c in range(inner // step):
            part = slice(c * step, (c + 1) * step)
            up = dot_nn(joined[...], up_held[:, part]) + up_bias[0:1, part]
            half = 0.5 * (1.0 + lax.erf(up * SQRT_HALF))
            activated[:, part] = (up * half).astype(BF16)
            slope[:, part] = (half + up * INV_ROOT_TWO_PI * jnp.exp(-0.5 * up * up)).astype(BF16)
        wait(down_copies)
        for j in range(n):
            parts.put(j, dot_nn(activated[...], down_held[:, j * width : (j + 1) * width]))

    with_weights(out_copies + up_copies + down_copies, work, pairs, [attended])
    parts.finish()


def feed(n, pairs, attended, xs, outs_w, own, gain, bias, up_bias, up_weight, down_weight):
    length, width = own.shape
    full, inner = up_weight.shape
    tile = min(256, length)
    steps = length // tile
    parts = Scattered(pairs, n, steps, False)
    part_outs, part_specs = parts.outs(length, width)
    twice = tuple(attended) if pairs else ()
    got = call(
        "feed",
        lambda *refs: feed_body(n, pairs, steps, *refs),
        (steps,),
        (
            *attended,
            *twice,
            *xs[1:],
            *outs_w,
            own,
            gain,
            bias,
            up_bias,
            up_weight,
            down_weight,
        ),
        Gathered.specs(attended, pairs, tile)
        + [rows_of((tile, width))] * (n - 1)
        + [ANY] * n
        + [rows_of((tile, width))]
        + [fixed((8, full))] * 2
        + [fixed((8, inner))]
        + [ANY] * 2,
        [
            shape((length, width), F32),
            shape((length, full), BF16),
            shape((length, 128), F32),
            shape((length, inner), BF16),
            shape((length, inner), BF16),
        ]
        + part_outs,
        [
            rows_of((tile, width)),
            rows_of((tile, full)),
            rows_of((tile, 128)),
            rows_of((tile, inner)),
            rows_of((tile, inner)),
        ]
        + part_specs,
        scratch=[
            pltpu.VMEM((full, full), BF16),
            pltpu.VMEM((full, inner), BF16),
            pltpu.VMEM((inner, full), BF16),
            pltpu.VMEM((tile, full), BF16),
            pltpu.VMEM((tile, full), F32),
            pltpu.SemaphoreType.DMA((n * n + 2 * n,)),
        ]
        + Gathered.scratch(attended, pairs, steps)
        + parts.scratch(length, width),
        remote=pairs,
    )
    return (*got[:5], got[5:])


def row_stats(total, weighted):
    return stat_columns(total, weighted).T[0:8, :]


def norm_sums(parts, n, product, normed, gain, bias, me):
    width = gain.shape[1] // n
    total = weighted = 0.0
    for j in range(n):
        part = slice(j * width, (j + 1) * width)
        value = product(j)
        parts.put(j, value)
        total += jnp.sum(value * gain[0:1, part], 1, keepdims=True)
        there = normed[:, place_of(me, j, width)].astype(F32)
        weighted += jnp.sum(value * (there - bias[0:1, part]), 1, keepdims=True)
    return row_stats(total, weighted)


def join_body(count, steps, *refs):
    gathered = [Gathered(refs[4 * i : 4 * i + 4], True, steps) for i in range(count)]
    outs, scratch = refs[4 * count : 5 * count], refs[5 * count :]
    for i, one in enumerate(gathered):
        one.attach(scratch[2 * i : 2 * i + 2])
    me = lax.axis_index("mp")

    def work(wait):
        for one, out in zip(gathered, outs):
            for j, block in enumerate(one.refs()):
                out[:, place_of(me, j, block.shape[1])] = block[...]

    with_weights([], work, True, gathered)


def join(gathered, full):
    length = gathered[0][0].shape[0]
    tile = min(256, length)
    steps = length // tile
    args, specs, scratch = [], [], []
    for one in gathered:
        args += [*one, *one]
        specs += Gathered.specs(one, True, tile)
        scratch += Gathered.scratch(one, True, steps)
    return call(
        "join",
        lambda *refs: join_body(len(gathered), steps, *refs),
        (steps,),
        args,
        specs,
        [shape((length, full), BF16)] * len(gathered),
        [rows_of((tile, full))] * len(gathered),
        scratch=scratch,
        remote=True,
    )


def feed_back_body(n, pairs, steps, *refs):
    cot, refs = refs[0], refs[1:]
    slope, normed, gain, bias, up_weight, down_weight, up_grad, up_bias_sum, cot_sum = refs[:9]
    refs = refs[9:]
    parts = Scattered(pairs, n, steps, True)
    part_outs, refs = refs[: parts.count()], refs[parts.count() :]
    up_held, down_held, row_sums, sems, *refs = refs
    parts.attach(part_outs, refs)
    me = lax.axis_index("mp")
    inner = up_held.shape[1]
    width = gain.shape[1] // n
    step = divisor(inner, 512)
    down_copies = [pltpu.make_async_copy(down_weight, down_held, sems.at[n])]
    up_copies = row_blocks(me, n, width, up_weight, up_held, sems, 0)

    def work(wait):
        accumulate(cot_sum, fold_rows(cot[:, place_of(me, 0, width)].astype(F32)))
        wait(down_copies)
        bias_parts = []
        for c in range(inner // step):
            part = slice(c * step, (c + 1) * step)
            value = dot_nt(cot[...], down_held[part, :]) * slope[:, part].astype(F32)
            low = value.astype(BF16)
            up_grad[:, part] = low
            bias_parts.append(fold_rows(low.astype(F32)))
        accumulate(up_bias_sum, jnp.concatenate(bias_parts, 1))
        wait(up_copies)
        row_sums[...] = norm_sums(
            parts,
            n,
            lambda j: dot_nt(up_grad[...], up_held[j * width : (j + 1) * width, :]),
            normed,
            gain,
            bias,
            me,
        )

    with_weights(down_copies + up_copies, work, pairs)
    parts.finish(row_sums[...])


def feed_back(n, pairs, cot, slope, normed, gain, bias, up_weight, down_weight):
    length, full = normed.shape
    width = full // n
    inner = up_weight.shape[1]
    tile = min(256, length)
    steps = length // tile
    parts = Scattered(pairs, n, steps, True)
    part_outs, part_specs = parts.outs(length, width)
    got = call(
        "feed_back",
        lambda *refs: feed_back_body(n, pairs, steps, *refs),
        (steps,),
        (cot, slope, normed, gain, bias, up_weight, down_weight),
        [rows_of((tile, full)), rows_of((tile, inner)), rows_of((tile, full))]
        + [fixed((8, full))] * 2
        + [ANY] * 2,
        [shape((length, inner), BF16), shape((8, inner), F32), shape((8, width), F32)] + part_outs,
        [rows_of((tile, inner)), fixed((8, inner)), fixed((8, width))] + part_specs,
        scratch=[
            pltpu.VMEM((full, inner), BF16),
            pltpu.VMEM((inner, full), BF16),
            pltpu.VMEM((8, tile), F32),
            pltpu.SemaphoreType.DMA((n + 1,)),
        ]
        + parts.scratch(length, width),
        remote=pairs,
    )
    return (*got[:3], got[3:])


def norm_back(refs, n_parts, source, stat, sums, gain, full):
    grad = refs[0][...].astype(F32)
    for ref in refs[1:n_parts]:
        grad += ref[...].astype(F32)
    columns = sums[0][...]
    if len(sums) > 1:
        packed, far = sums[1:]

        @pl.when(pl.program_id(0) == 0)
        def _():
            far[...] = jnp.zeros_like(far)
            unpack(packed, far)

        tile = refs[0].shape[0]
        columns += far[:, pl.ds(pl.multiple_of(pl.program_id(0) * tile, tile), tile)]
    columns = columns.T
    mean, inv = stat[:, 0:1], stat[:, 1:2]
    scaled = (source[...] - mean) * inv
    back = inv * (
        grad * gain[0:1, :] - columns[:, 0:1] * (1.0 / full) - scaled * (columns[:, 1:2] * (1.0 / full))
    )
    return back, fold_rows(grad * scaled), fold_rows(grad)


def sum_specs(sums, tile, length):
    far = [pl.BlockSpec((EXTRA, v.shape[1]), lambda i: (length // EXTRA, 0)) for v in sums[1:]]
    return [cols_of((8, tile)), *far]


def hidden_back_body(k, m, full, *refs):
    parts, sums = refs[:k], refs[k : k + m]
    cot, hidden, stat, gain, wide, low, gain_sum, bias_sum, *more = refs[k + m :]
    sums = (*sums, *more)
    back, gain_part, bias_part = norm_back(parts, k, hidden, stat, sums, gain, full)
    value = cot[...].astype(F32) + back
    wide[...] = value
    low[...] = value.astype(BF16)
    accumulate(gain_sum, gain_part)
    accumulate(bias_sum, bias_part)


def hidden_back(parts, cotangent, row, hidden, stat, sums, gain, full):
    k, m, (length, width) = len(parts), len(sums), hidden.shape
    tile = min(256, length)
    steps = length // tile
    return call(
        "hidden_back",
        lambda *refs: hidden_back_body(k, m, full, *refs),
        (steps,),
        (*parts, *sums, cotangent, hidden, stat, gain),
        [rows_of((tile, width))] * k
        + sum_specs(sums, tile, length)
        + [
            pl.BlockSpec((tile, width), lambda i: (row * steps + i, 0)),
            rows_of((tile, width)),
            rows_of((tile, 128)),
            fixed((8, width)),
        ],
        [shape((length, width), F32), sent((length, width), BF16)] + [shape((8, width), F32)] * 2,
        [rows_of((tile, width))] * 2 + [fixed((8, width))] * 2,
        scratch=[pltpu.VMEM((8, length), F32)] * (m - 1),
    )


def attended_back_body(n, pairs, steps, *refs):
    count = 4 if pairs else n
    grads = Gathered(refs[:count], pairs, steps)
    weight, joined, out, *more = refs[count:]
    grads.attach(more)
    me = lax.axis_index("mp")
    width = grads.blocks[0].shape[1]

    def work(wait):
        for j, one in enumerate(grads.refs()):
            joined[:, place_of(me, j, width)] = one[...]
        out[...] = dot_nt(joined[...], weight[...]).astype(BF16)

    with_weights([], work, pairs, [grads])


def attended_back(n, pairs, grads, weight):
    length, width = grads[0].shape
    rows, full = weight.shape
    tile = min(256, length)
    steps = length // tile
    return call(
        "attended_back",
        lambda *refs: attended_back_body(n, pairs, steps, *refs),
        (steps,),
        (*grads, *(grads if pairs else ()), weight),
        Gathered.specs(grads, pairs, tile) + [fixed((rows, full))],
        [shape((length, full), BF16), shape((length, rows), BF16)],
        [rows_of((tile, full)), rows_of((tile, rows))],
        scratch=Gathered.scratch(grads, pairs, steps),
        remote=pairs,
    )


def project_back_body(n, pairs, steps, grad, normed, gain, bias, weight, *refs):
    parts = Scattered(pairs, n, steps, True)
    part_outs, refs = refs[: parts.count()], refs[parts.count() :]
    held, row_sums, sems, *refs = refs
    parts.attach(part_outs, refs)
    me = lax.axis_index("mp")
    width = gain.shape[1] // n
    copies = row_blocks(me, n, width, weight, held, sems, 0)

    def work(wait):
        def product(j):
            wait(copies[j : j + 1])
            return dot_nt(grad[...], held[j * width : (j + 1) * width, :])

        row_sums[...] = norm_sums(parts, n, product, normed, gain, bias, me)

    with_weights(copies, work, pairs)
    parts.finish(row_sums[...])


def project_back(n, pairs, grad, normed, gain, bias, weight):
    length, out = grad.shape
    full = weight.shape[0]
    width = full // n
    tile = min(256, length)
    steps = length // tile
    parts = Scattered(pairs, n, steps, True)
    part_outs, part_specs = parts.outs(length, width)
    return call(
        "project_back",
        lambda *refs: project_back_body(n, pairs, steps, *refs),
        (steps,),
        (grad, normed, gain, bias, weight),
        [rows_of((tile, out)), rows_of((tile, full))] + [fixed((8, full))] * 2 + [ANY],
        part_outs,
        part_specs,
        scratch=[
            pltpu.VMEM((full, out), BF16),
            pltpu.VMEM((8, tile), F32),
            pltpu.SemaphoreType.DMA((n,)),
        ]
        + parts.scratch(length, width),
        remote=pairs,
    )


def average_back_body(k, m, full, count, *refs):
    weights, parts, sums = refs[0], refs[1 : k + 1], refs[k + 1 : k + m + 1]
    source, stat, gain, hidden_grad, history = refs[k + m + 1 : k + m + 6]
    refs, more = (refs[:-1], refs[-1:]) if m > 1 else (refs, ())
    sums = (*sums, *more)
    grad_history, depth_sum, gain_sum, bias_sum, held = refs[-5:]
    back, gain_part, bias_part = norm_back(parts, k, source, stat, sums, gain, full)
    held[...] = hidden_grad[...] + back
    accumulate(gain_sum, gain_part)
    accumulate(bias_sum, bias_part)
    lanes = held.shape[1] // 128
    chunk = min(32, held.shape[0])
    folded = [0.0] * count
    for t in range(held.shape[0] // chunk):
        rows = slice(t * chunk, (t + 1) * chunk)
        value = held[rows, :]
        for j in range(count):
            grad_history[j, rows, :] = (weights[j] * value).astype(BF16)
            product = fold_rows(value * history[j, rows, :].astype(F32))
            for c in range(lanes):
                folded[j] = folded[j] + product[:, c * 128 : (c + 1) * 128]
    for j in range(count):
        accumulate(depth_sum.at[j], folded[j])


def average_back(weights, parts, source, stat, sums, gain, hidden_grad, history, row, made):
    k, m, (length, width) = len(parts), len(sums), source.shape
    count = history.shape[0]
    tile = min(256, length)
    steps = length // tile
    full = gain[1]
    block = pl.BlockSpec((count, tile, width), lambda i: (0, row * steps + i, 0))
    args = (weights, *parts, *sums, source, stat, gain[0], hidden_grad, history)
    specs = (
        [SMEM]
        + [rows_of((tile, width))] * k
        + sum_specs(sums, tile, length)
        + [rows_of((tile, width)), rows_of((tile, 128)), fixed((8, width)), rows_of((tile, width)), block]
    )
    more = {}
    if made is not None:
        more = {"aliases": {len(args): 0}}
        args, specs = (*args, made), specs + [ANY]
    return call(
        "average_back",
        lambda *refs: average_back_body(k, m, full, count, *refs),
        (steps,),
        args,
        specs,
        [shape(history.shape, BF16), shape((count, 8, 128), F32)] + [shape((8, width), F32)] * 2,
        [block, fixed((count, 8, 128))] + [fixed((8, width))] * 2,
        scratch=[pltpu.VMEM((tile, width), F32)] + [pltpu.VMEM((8, length), F32)] * (m - 1),
        **more,
    )


def divisor(size, most):
    return max(d for d in range(128, most + 1, 128) if size % d == 0) if size > 128 else size


def weight_body(rows, *refs):
    out = refs[-1]
    total = dot_tn(refs[0][...], refs[rows][...])
    for r in range(1, rows):
        total += dot_tn(refs[r][...], refs[rows + r][...])
    out[...] = total.astype(BF16)


def weight_grad(lefts, rights):
    rows, (length, high), wide = len(lefts), lefts[0].shape, rights[0].shape[1]
    tall, across = divisor(high, 1024), divisor(wide, 1024)
    return call(
        "weight_grad",
        lambda *refs: weight_body(rows, *refs),
        (high // tall, wide // across),
        (*lefts, *rights),
        [pl.BlockSpec((length, tall), lambda i, j: (0, i))] * rows
        + [pl.BlockSpec((length, across), lambda i, j: (0, j))] * rows,
        [shape((high, wide), BF16)],
        [pl.BlockSpec((tall, across), lambda i, j: (i, j))],
    )[0]


def put_blocks(came, outs, k, value):
    if came is not None:
        value = value + came[k].astype(F32)
    per = outs[0].shape[0]
    outs[k // per][k % per] = value.astype(BF16)


def tall_blocks_body(rows, count, fused, group, *refs):
    lefts, rights = refs[: rows * count], refs[rows * count : rows * count + rows]
    refs = refs[rows * count + rows :]
    came, outs, turned = refs[0] if fused else None, refs[fused:-1], refs[-1]
    length, high = lefts[0].shape

    @pl.when(pl.program_id(0) == 0)
    def _():
        for k in range(count):
            for r in range(rows):
                turned[k * high : (k + 1) * high, r * length : (r + 1) * length] = lefts[
                    k * rows + r
                ][...].T

    for k in range(count):
        total = 0.0
        for r in range(rows):
            total += dot_nn(
                turned[k * high : (k + 1) * high, r * length : (r + 1) * length], rights[r][...]
            )
        put_blocks(came, outs, k, total)


def wide_blocks_body(rows, count, fused, group, *refs):
    lefts, rights = refs[:rows], refs[rows : rows + rows * count]
    refs = refs[rows + rows * count :]
    came, outs = refs[0] if fused else None, refs[fused:]
    turned = [left[...].T for left in lefts]
    for k in range(count):
        total = 0.0
        for r in range(rows):
            total += dot_nn(turned[r], rights[k * rows + r][...])
        put_blocks(came, outs, k, total)


class Spread:
    def __init__(self, lefts, rights, dim, bits, part=(0, 1)):
        self.lefts, self.rights, self.dim, self.bits, self.part = lefts, rights, dim, list(bits), part
        self.groups = lax.axis_size("dp")
        self.block = (lefts, rights)[dim][0].shape[1] // self.groups
        order = [0]
        for bit in reversed(self.bits):
            order = order + [e | bit for e in order]
        self.order = order

    def blocks(self, half, came=None):
        count = self.groups // 2
        which = self.order[half * count : (half + 1) * count]
        rows, length = len(self.lefts), self.lefts[0].shape[0]
        group = lax.axis_index("dp").astype(jnp.int32)[None]
        size, (index, pieces) = self.block, self.part
        stay = [
            pl.BlockSpec((length, size), lambda i, group, e=e: (0, group[0] ^ e))
            for e in which
            for _ in range(rows)
        ]
        other = self.rights if self.dim == 0 else self.lefts
        extent = other[0].shape[1] // pieces
        tile = divisor(extent, 512)
        steps = extent // tile
        move = [pl.BlockSpec((length, tile), lambda i, group: (0, index * steps + i))] * rows

        def blocked(number):
            if self.dim == 0:
                return (
                    sent((number, size, extent), BF16),
                    pl.BlockSpec((number, size, tile), lambda i, group: (0, 0, i)),
                )
            return (
                sent((number, extent, size), BF16),
                pl.BlockSpec((number, tile, size), lambda i, group: (0, i, 0)),
            )

        if self.dim == 0:
            args = (*(list(self.lefts) * count), *self.rights)
            specs = stay + move
            body, scratch = tall_blocks_body, [pltpu.VMEM((count * size, rows * length), BF16)]
        else:
            args = (*self.lefts, *(list(self.rights) * count))
            specs = move + stay
            body, scratch = wide_blocks_body, []
        outs = [blocked(count)]
        if came is not None:
            args, specs = (*args, came), specs + [blocked(count)[1]]
            outs = [blocked(count // 2)] * 2
        return call(
            "weight_blocks",
            lambda *refs: body(rows, count, came is not None, *refs),
            (steps,),
            (group, *args),
            specs,
            [one[0] for one in outs],
            [one[1] for one in outs],
            scratch=scratch,
            prefetch=1,
        )

    def send(self, value):
        bit = self.bits[self.step]
        self.step += 1
        self.coming = lax.ppermute(value, "dp", [(i, i ^ bit) for i in range(self.groups)])

    def first(self):
        self.step = 0
        self.send(self.blocks(1)[0])

    def keep(self):
        self.held = self.blocks(0)[0]

    def keep_added(self):
        self.held, out = self.blocks(0, self.coming)
        self.send(out)


def fold_body(count, *refs):
    for i in range(count):
        held, came, keep, send = refs[2 * i], refs[2 * i + 1], refs[2 * count + 2 * i], refs[2 * count + 2 * i + 1]
        half = keep.shape[0]
        keep[...] = (held[:half].astype(F32) + came[:half].astype(F32)).astype(BF16)
        send[...] = (held[half:].astype(F32) + came[half:].astype(F32)).astype(BF16)


def advance(*spreads):
    steps = 4
    args, specs, outs, out_specs = [], [], [], []
    for one in spreads:
        count, high, wide = one.held.shape
        args += [one.held, one.coming]
        specs += [pl.BlockSpec((count, high // steps, wide), lambda i: (0, i, 0))] * 2
        outs += [sent((count // 2, high, wide), BF16)] * 2
        out_specs += [pl.BlockSpec((count // 2, high // steps, wide), lambda i: (0, i, 0))] * 2
    got = call("fold", lambda *refs: fold_body(len(spreads), *refs), (steps,), args, specs, outs, out_specs)
    for i, one in enumerate(spreads):
        one.held = got[2 * i]
        one.send(got[2 * i + 1])


def finish_body(groups, *refs):
    outs = refs[len(refs) - len(groups) :]
    at = 0
    for out, group in zip(outs, groups):
        for first, wide, count in group:
            total = refs[at][0].astype(F32)
            for ref in refs[at + 1 : at + count]:
                total += ref[0].astype(F32)
            out[:, first : first + wide] = total
            at += count


def finish(*groups):
    steps = 4
    args, specs, outs, out_specs, places = [], [], [], [], []
    for group in groups:
        first, place = 0, []
        for one in group:
            terms = [one.held, one.coming] if isinstance(one, Spread) else [one[None]]
            _, high, wide = terms[0].shape
            args += terms
            specs += [pl.BlockSpec((1, high // steps, wide), lambda i: (0, i, 0))] * len(terms)
            place.append((first, wide, len(terms)))
            first += wide
        outs.append(shape((high, first), F32))
        out_specs.append(rows_of((high // steps, first)))
        places.append(place)
    return call("finish", lambda *refs: finish_body(places, *refs), (steps,), args, specs, outs, out_specs)


def sums_body(groups, n, own, out, total, came, far, dp_sems, mp_sems):
    me = {"dp": lax.axis_index("dp"), "mp": lax.axis_index("mp")}
    peers = [("dp", b) for b in range(1, groups)] + [("mp", b) for b in range(1, n)]
    barrier = pltpu.get_barrier_semaphore()
    for axis, b in peers:
        pl.semaphore_signal(
            barrier, inc=1, device_id={axis: flip(me[axis], b)}, device_id_type=pl.DeviceIdType.MESH
        )
    pl.semaphore_wait(barrier, len(peers))

    def copy(axis, b, source, target, sems):
        return pltpu.make_async_remote_copy(
            src_ref=source,
            dst_ref=target.at[b - 1],
            send_sem=sems.at[0, b - 1],
            recv_sem=sems.at[1, b - 1],
            device_id={axis: flip(me[axis], b)},
            device_id_type=pl.DeviceIdType.MESH,
        )

    copies = [copy("dp", b, own, came, dp_sems) for b in range(1, groups)]
    for one in copies:
        one.start()
    for one in copies:
        one.wait()
    value = own[...]
    for b in range(groups - 1):
        value = value + came[b]
    out[...] = value
    total[...] = value[-8:]
    copies = [copy("mp", b, total, far, mp_sems) for b in range(1, n)]
    for one in copies:
        one.start()
    for one in copies:
        one.wait()
    value = total[...]
    for b in range(n - 1):
        value = value + far[b]
    out[-8:, :] = value


def sums(vectors, depth):
    groups, n = lax.axis_size("dp"), lax.axis_size("mp")
    sizes = [v.size for v in vectors]
    packed = jnp.concatenate(vectors)
    packed = jnp.pad(packed, (0, -packed.size % 1024)).reshape(-1, 128)
    packed = jnp.concatenate([packed, jnp.pad(depth[None], ((0, 7), (0, 128 - depth.size)))])
    high = packed.shape[0]
    got = call(
        "sums",
        lambda *refs: sums_body(groups, n, *refs),
        (1,),
        (packed,),
        [fixed((high, 128))],
        [shape((high, 128), F32)],
        [fixed((high, 128))],
        scratch=[
            pltpu.VMEM((8, 128), F32),
            pltpu.VMEM((groups - 1, high, 128), F32),
            pltpu.VMEM((n - 1, 8, 128), F32),
            pltpu.SemaphoreType.DMA((2, groups - 1)),
            pltpu.SemaphoreType.DMA((2, n - 1)),
        ],
        remote=True,
    )[0]
    flat = got.reshape(-1)
    ends = np.cumsum(sizes)
    return [flat[end - size : end] for end, size in zip(ends, sizes)], got[-8, : depth.size]


def output_body(rows, steps, *refs):
    bias, out = refs[-2:]
    per = (len(refs) - 2) // rows
    for r in range(rows):

        @pl.when(pl.program_id(0) // steps == r)
        def _(r=r):
            total = bias[0:1, :]
            for part in refs[r * per + 1 : (r + 1) * per]:
                total = total + part[...].astype(F32)
            out[...] = (refs[r * per][...] + total).astype(BF16)


def output(parts, hidden, bias):
    rows, (length, width) = len(hidden), hidden[0].shape
    tile = min(512, length)
    steps = length // tile
    args, specs = [], []
    for r in range(rows):
        args += [hidden[r], *parts[r]]
        specs += [
            pl.BlockSpec((tile, width), lambda i, r=r: (jnp.clip(i - r * steps, 0, steps - 1), 0))
        ] * (1 + len(parts[r]))
    return call(
        "output",
        lambda *refs: output_body(rows, steps, *refs),
        (rows * steps,),
        (*args, bias),
        specs + [fixed((8, width))],
        [shape((rows * length, width), BF16)],
        [rows_of((tile, width))],
    )[0]


class Ring:
    def __init__(self):
        self.n = lax.axis_size("mp")
        self.me = lax.axis_index("mp").astype(jnp.int32)
        self.pairs = self.n == 4
        self.core = [(i, i ^ 1) for i in range(self.n)]
        self.chip = [(i, i ^ 2) for i in range(self.n)]

    def over_core(self, value):
        return lax.ppermute(value, "mp", self.core)

    def over_chip(self, value):
        return lax.ppermute(value, "mp", self.chip)

    def gather_start(self, block):
        if self.pairs:
            return [block, self.over_chip(block)]
        return self.gather(block)

    def gather(self, block):
        if self.pairs:
            across = self.over_chip(block)
            return [block, self.over_core(block), across, self.over_core(across)]
        every = lax.all_gather(block, "mp")
        return [
            lax.dynamic_index_in_dim(every, self.me ^ j, 0, keepdims=False) for j in range(self.n)
        ]

    def scatter(self, parts, sums=False):
        parts, extra = (parts[:-1], parts[-1:]) if sums else (parts, [])
        if self.pairs:
            came = self.over_chip(parts[1])
            return [parts[0], came], [*extra, came] if sums else []
        stacked = jnp.stack([part.astype(F32) for part in parts])
        ordered = jnp.take(stacked, self.me ^ jnp.arange(self.n), axis=0)
        total = lax.psum_scatter(ordered, "mp", scatter_dimension=0, tiled=False)
        return [total], [lax.psum(v, "mp") for v in extra]

    def total(self, value):
        if self.pairs:
            value = value + self.over_core(value)
            return value + self.over_chip(value)
        return lax.psum(value, "mp")

    def out_start(self, weight):
        rows, groups = weight.shape[0], lax.axis_size("dp")
        if self.pairs and rows % (16 * groups) == 0:
            size = rows // groups
            piece = lax.dynamic_slice_in_dim(weight, lax.axis_index("dp") * size, size, 0)
            return self.over_chip(piece)
        return None

    def out_middle(self, piece):
        return None if piece is None else lax.all_gather(piece, "dp", axis=0, tiled=True)

    def out_end(self, weight, across):
        if across is None:
            return self.gather(weight)
        across = gate([across])[0]
        return [weight, self.over_core(weight), across, self.over_core(across)]


def tables_of(length):
    half = HEAD // 2
    rate = np.exp(np.arange(half, dtype=np.float64) * (-math.log(10000.0) / half))
    angle = np.arange(length, dtype=np.float64)[:, None] * rate[None, :]
    cosine, sine = np.cos(angle), np.sin(angle)
    return (
        jnp.asarray(np.concatenate([cosine, cosine], 1), F32),
        jnp.asarray(np.concatenate([-sine, sine], 1), F32),
    )


def local(
    history,
    depth_weights,
    segment_ids,
    first_gain,
    first_bias,
    qkv_weight,
    out_weight,
    second_gain,
    second_bias,
    up_weight,
    up_bias,
    down_weight,
    down_bias,
    cotangent,
):
    ring = Ring()
    n = ring.n
    pairs = ring.pairs
    width = history.shape[2]
    full = n * width
    row_count, length = segment_ids.shape
    rows = range(row_count)
    tables = tables_of(length)
    earlier = (segment_ids[:, None, :] < segment_ids[:, :, None]).astype(jnp.int32)
    starts = jnp.broadcast_to(jnp.sum(earlier, -1)[:, None, :], (row_count, 8, length))

    up_bias8 = jnp.broadcast_to(up_bias[None], (8, up_bias.shape[0]))

    down_bias8 = jnp.broadcast_to(down_bias[None], (8, width))
    groups = lax.axis_size("dp")
    spread = full % (128 * groups) == 0 and groups >= 4
    last = row_count - 1

    Order.last, Order.names, Order.cost = None, 0, LARGE
    vectors = jnp.stack([first_gain, first_bias, second_gain, second_bias])
    vectors = ring.gather_start(jnp.repeat(vectors, 8, 0))
    piece = ring.out_start(out_weight)
    cot_rows = [lax.slice_in_dim(cotangent, r * length, (r + 1) * length) for r in rows]
    none = [None] * row_count
    wide, low, xs, qkv, normed1, stat1 = (list(none) for _ in range(6))
    attended, logs, heads, cots = (list(none) for _ in range(4))
    hidden, normed2, stat2, activated, slope = (list(none) for _ in range(5))
    branch, up_grad, parts2, parts1 = (list(none) for _ in range(4))
    hidden_grad, grads, grad_full, qkv_grad = (list(none) for _ in range(4))
    up_bias_sum = down_bias_sum = gain2_sum = bias2_sum = 0.0

    for r in rows:
        wide[r], low[r] = average(depth_weights, history, r, length)
        if r == 0:
            xs[0] = ring.gather_start(low[0])
            if pairs:
                vectors[1], piece = gate([vectors[1], piece])
                vectors = [
                    vectors[0],
                    ring.over_core(vectors[0]),
                    vectors[1],
                    ring.over_core(vectors[1]),
                ]
            across = ring.out_middle(piece)
    vectors = jnp.concatenate(vectors, 1)
    gain1, bias1, gain2, bias2 = (vectors[8 * i : 8 * i + 8] for i in range(4))
    own1, own2 = gain1[:, :width], gain2[:, :width]
    for r in rows[1:]:
        xs[r] = ring.gather_start(gate([low[r]], xs[r - 1][1:2])[0])
    for r in rows:
        qkv[r], normed1[r], stat1[r], xs[r] = project(
            n, pairs, xs[r], gain1, bias1, tables, qkv_weight
        )
        attended[r], logs[r] = attend(starts[r], qkv[r])
        heads[r] = ring.gather_start(attended[r])
        if r == last:
            out_w = ring.out_end(out_weight, across)

    for r in rows:
        cots[r] = ring.gather_start(gate([cot_rows[r]])[0])
        got = feed(
            n,
            pairs,
            heads[r],
            xs[r],
            out_w,
            wide[r],
            gain2,
            bias2,
            up_bias8,
            up_weight,
            down_weight,
        )
        hidden[r], normed2[r], stat2[r], activated[r], slope[r], parts = got
        branch[r] = ring.scatter(parts)[0]

    def spread_over_dp(value, dim):
        return lax.psum_scatter(value, "dp", scatter_dimension=dim, tiled=True)

    if pairs:
        cot_full = join(cots, full)
        branch[0][1] = gate(branch[0][1:])[0]
    else:
        cot_full = [lax.all_gather(v, "mp", axis=1, tiled=True) for v in cot_rows]
    down_sum = spread_over_dp(weight_grad(activated, cot_full), 1)

    for r in rows:
        up_grad[r], up_sum, cot_sum, parts = feed_back(
            n, pairs, cot_full[r], slope[r], normed2[r], gain2, bias2, up_weight, down_weight
        )
        up_bias_sum += up_sum
        down_bias_sum += cot_sum
        parts2[r] = ring.scatter(parts, True)
        if r == 0 and pairs:
            branch[last][1] = gate(branch[last][1:])[0]

    def hidden_step(r):
        nonlocal gain2_sum, bias2_sum
        parts, row_sums = parts2[r]
        hidden_grad[r], low_grad, gain_part, bias_part = hidden_back(
            parts, cotangent, r, hidden[r], stat2[r], row_sums, own2, full
        )
        gain2_sum += gain_part
        bias2_sum += bias_part
        grads[r] = ring.gather_start(low_grad)

    hidden_step(0)
    if spread:
        up_sum = Spread(normed2, up_grad, 0, (1, 2, 4))
        up_sum.first()
    made = output(branch, hidden, down_bias8)
    for r in rows[1:]:
        hidden_step(r)

    for r in rows:
        grad_full[r], attended_grad = attended_back(n, pairs, grads[r], out_weight)
        if r == last and spread:
            out_sum = Spread(attended, grad_full, 1, (2, 4, 1))
            out_sum.first()
        qkv_grad[r] = attend_back(starts[r], tables, qkv[r], attended_grad, logs[r])
        if r == last and spread:
            qkv_sum = [
                Spread(normed1, qkv_grad, 0, (1, 2, 4), (0, 2)),
                Spread(normed1, qkv_grad, 0, (1, 2, 4), (1, 2)),
            ]
            qkv_sum[0].first()
        if r > 0 and pairs:
            parts, row_sums = parts1[r - 1]
            parts[1] = row_sums[1] = gate([parts[1]])[0]
        parts = project_back(n, pairs, qkv_grad[r], normed1[r], gain1, bias1, qkv_weight)
        parts1[r] = ring.scatter(parts, True)

    if spread:
        down_sum = gate([down_sum])[0]
        out_sum.keep_added()
        up_sum.keep_added()
        qkv_sum[1].first()

    grad_history, depth_sum, gain1_sum, bias1_sum = None, 0.0, 0.0, 0.0
    for r in rows:
        parts, row_sums = parts1[r]
        grad_history, depth_part, gain_part, bias_part = average_back(
            depth_weights,
            parts,
            wide[r],
            stat1[r],
            row_sums,
            (own1, full),
            hidden_grad[r],
            history,
            r,
            grad_history,
        )
        depth_sum += depth_part
        gain1_sum += gain_part
        bias1_sum += bias_part
        if r == 0:
            if pairs:
                parts, row_sums = parts1[last]
                parts[1] = row_sums[1] = gate([parts[1]])[0]
            if spread:
                qkv_sum[0].keep_added()
                out_sum.coming = gate([out_sum.coming])[0]

    vectors = [up_bias_sum, down_bias_sum, gain2_sum, bias2_sum, gain1_sum, bias1_sum]
    vectors, depth_part = [jnp.sum(v, 0) for v in vectors], jnp.sum(depth_sum, (1, 2))
    if spread:
        advance(up_sum)
        qkv_sum[1].keep_added()
        advance(qkv_sum[0])
        advance(qkv_sum[1], out_sum)
        totals, depth_grad = sums(vectors, depth_part)
    else:
        qkv_sum = [spread_over_dp(weight_grad(normed1, qkv_grad), 0)]
        out_sum = spread_over_dp(weight_grad(attended, grad_full), 1)
        up_sum = spread_over_dp(weight_grad(normed2, up_grad), 0)
        totals, depth_grad = sums(vectors, depth_part)
    down_total, up_total, out_total, qkv_total = finish([down_sum], [up_sum], [out_sum], qkv_sum)
    return (
        made,
        grad_history,
        depth_grad,
        totals[4],
        totals[5],
        qkv_total,
        out_total,
        totals[2],
        totals[3],
        up_total,
        totals[0],
        down_total,
        totals[1],
    )


def solution(mesh):
    placed = (
        P(None, "dp", "mp"),
        P(),
        P("dp", None),
        P("mp"),
        P("mp"),
        P(None, "mp"),
        P("mp", None),
        P("mp"),
        P("mp"),
        P(None, "mp"),
        P("mp"),
        P("mp", None),
        P("mp"),
        P("dp", "mp"),
    )
    return jax.shard_map(
        local,
        mesh=mesh,
        in_specs=placed,
        out_specs=(
            P("dp", "mp"),
            P(None, "dp", "mp"),
            P(),
            P("mp"),
            P("mp"),
            P("dp", "mp"),
            P("mp", "dp"),
            P("mp"),
            P("mp"),
            P("dp", "mp"),
            P("mp"),
            P("mp", "dp"),
            P("mp"),
        ),
        check_vma=False,
    )
```

```python
import math

import jax
import jax.numpy as jnp
import numpy as np
from jax import lax
from jax.experimental import pallas as pl
from jax.experimental.pallas import tpu as pltpu
from jax.sharding import PartitionSpec as P

HEAD = 128
MAX_DOC = 512
EPSILON = 1e-05
SQRT_HALF = 0.7071067811865476
INV_ROOT_TWO_PI = 0.3989422804014327
LOG2E = 1.4426950408889634
SCALE = HEAD ** (-0.5)
MIB = 2**20
BF16 = jnp.bfloat16
F32 = jnp.float32


def dot_nn(a, b):
    return jnp.dot(a, b, preferred_element_type=F32)


def dot_nt(a, b):
    return lax.dot_general(a, b, (((1,), (1,)), ((), ())), preferred_element_type=F32)


def dot_tn(a, b):
    return lax.dot_general(a, b, (((0,), (0,)), ((), ())), preferred_element_type=F32)


LARGE, TINY = 10**12, 10**4


class Order:
    last = None
    names = 0
    cost = LARGE

    @staticmethod
    def name(remote):
        Order.names += remote
        return Order.names - 1 if remote else None


def call(
    name, body, grid, args, in_specs, outs, out_specs, scratch=(), prefetch=0, after=(), aliases=None, remote=False
):
    count = len(args)
    extra = [*after]
    if Order.last is not None and not any(Order.last is a for a in args):
        extra.append(Order.last)

    def without_extra(*refs):
        body(*refs[:count], *refs[count + len(extra) :])

    got = pl.pallas_call(
        without_extra,
        grid_spec=pltpu.PrefetchScalarGridSpec(
            num_scalar_prefetch=prefetch,
            grid=grid,
            in_specs=list(in_specs) + [ANY] * len(extra),
            out_specs=out_specs,
            scratch_shapes=list(scratch),
        ),
        out_shape=outs,
        input_output_aliases=aliases or {},
        compiler_params=pltpu.CompilerParams(
            vmem_limit_bytes=60 * MIB, collective_id=Order.name(remote), has_side_effects=remote
        ),
        cost_estimate=pl.CostEstimate(flops=Order.cost, bytes_accessed=Order.cost // 10**4, transcendentals=0),
        name=name,
    )(*args, *extra)
    fresh = [v for i, v in enumerate(got) if i not in (aliases or {}).values()]
    Order.last = min(fresh or got, key=lambda v: v.size)
    return got


def shape(dims, dtype):
    return jax.ShapeDtypeStruct(dims, dtype)


def sent(dims, dtype):
    return pltpu.HBM(dims, dtype)


SMEM = pl.BlockSpec(memory_space=pltpu.SMEM)
ANY = pl.BlockSpec(memory_space=pl.ANY)


def gate(arrays, after=()):
    arrays = list(arrays)
    return call(
        "gate",
        lambda *refs: None,
        (1,),
        arrays,
        [ANY] * len(arrays),
        [shape(a.shape, a.dtype) for a in arrays],
        [ANY] * len(arrays),
        after=after,
        aliases={i: i for i in range(len(arrays))},
    )


def rows_of(block):
    return pl.BlockSpec(block, lambda i: (i, 0))


def cols_of(block):
    return pl.BlockSpec(block, lambda i: (0, i))


def fixed(block):
    return pl.BlockSpec(block, lambda i: (0,) * len(block))


def flip(me, j):
    there, bit = me, 1
    while bit <= j:
        if j & bit:
            there = there + bit * (1 - 2 * ((me // bit) % 2))
        bit *= 2
    return there


def place_of(me, j, width):
    return pl.ds(pl.multiple_of(flip(me, j) * width, width), width)


def greet():
    barrier = pltpu.get_barrier_semaphore()
    sibling = flip(lax.axis_index("mp"), 1)
    pl.semaphore_signal(
        barrier, inc=1, device_id={"mp": sibling}, device_id_type=pl.DeviceIdType.MESH
    )
    pl.semaphore_wait(barrier, 1)


def to_sibling(source, target, sems, at):
    return pltpu.make_async_remote_copy(
        src_ref=source,
        dst_ref=target,
        send_sem=sems.at[0, at],
        recv_sem=sems.at[1, at],
        device_id={"mp": flip(lax.axis_index("mp"), 1)},
        device_id_type=pl.DeviceIdType.MESH,
    )


class Gathered:
    def __init__(self, refs, pairs, steps):
        self.pairs, self.steps = pairs, steps
        self.blocks, self.whole = refs[:2] if pairs else refs, refs[2:4] if pairs else ()

    @staticmethod
    def specs(blocks, pairs, tile):
        width = blocks[0].shape[1]
        return [rows_of((tile, width))] * len(blocks) + ([ANY] * 2 if pairs else [])

    @staticmethod
    def scratch(blocks, pairs, steps):
        if not pairs:
            return []
        return [pltpu.VMEM((2, *blocks[0].shape), BF16), pltpu.SemaphoreType.DMA((2, 2 * steps))]

    def attach(self, refs):
        if self.pairs:
            self.came, self.sems = refs
        return self

    def copies(self, step):
        tile = self.blocks[0].shape[0]
        rows = pl.ds(pl.multiple_of(step * tile, tile), tile)
        return [
            to_sibling(self.whole[k].at[rows, :], self.came.at[k, rows, :], self.sems, 2 * step + k)
            for k in range(2)
        ]

    def start(self):
        if self.pairs:
            for step in range(self.steps):
                for one in self.copies(step):
                    one.start()

    def refs(self):
        if not self.pairs:
            return self.blocks
        step = pl.program_id(0)
        tile = self.blocks[0].shape[0]
        for one in self.copies(step):
            one.wait()
        rows = pl.ds(pl.multiple_of(step * tile, tile), tile)
        return [self.blocks[0], self.came.at[0, rows, :], self.blocks[1], self.came.at[1, rows, :]]


EXTRA = 16


def pack(sums, width):
    rows = []
    for s in range(2):
        rest = sums[s : s + 1, :]
        for _ in range(3):
            piece = rest.astype(BF16).astype(F32)
            rest = rest - piece
            rows += [piece[:, h : h + width] for h in range(0, sums.shape[1], width)]
    assert len(rows) <= EXTRA
    rows += [jnp.zeros((1, width), F32)] * (EXTRA - len(rows))
    return jnp.concatenate(rows).astype(BF16)


def unpack(packed, target):
    width = packed.shape[1]
    per = target.shape[1] // width
    value = packed[...].astype(F32)
    for s in range(2):
        for h in range(per):
            at = [(3 * s + p) * per + h for p in range(3)]
            total = value[at[0] : at[0] + 1] + value[at[1] : at[1] + 1] + value[at[2] : at[2] + 1]
            target[s : s + 1, h * width : (h + 1) * width] = total


class Scattered:
    def __init__(self, pairs, n, steps, with_sums):
        self.pairs, self.n, self.steps, self.with_sums = pairs, n, steps, with_sums

    def outs(self, length, width):
        tile = length // self.steps
        if self.pairs:
            high = length + EXTRA * self.with_sums
            outs = [shape((length, width), BF16), sent((high, width), BF16)]
            specs = [fixed((length, width)), fixed((high, width))]
            if self.with_sums:
                outs, specs = outs + [shape((8, length), F32)], specs + [fixed((8, length))]
            return outs, specs
        outs, specs = [shape((length, width), BF16)] * self.n, [rows_of((tile, width))] * self.n
        if self.with_sums:
            outs, specs = outs + [shape((8, length), F32)], specs + [cols_of((8, tile))]
        return outs, specs

    def count(self):
        return (2 if self.pairs else self.n) + self.with_sums

    def scratch(self, length, width):
        if not self.pairs:
            return []
        tile = length // self.steps
        block = pltpu.VMEM((self.steps, 2, tile, width), BF16)
        made = [block, block, pltpu.VMEM((2, 2, tile, width), F32)]
        if self.with_sums:
            made += [pltpu.VMEM((self.steps, 8, tile), F32)] * 3
        return made + [pltpu.SemaphoreType.DMA((2, 3 * self.steps))]

    def attach(self, outs, scratch):
        self.out = outs
        if self.pairs:
            self.send, self.came, self.kept = scratch[:3]
            self.sums = scratch[3:-1]
            self.sems = scratch[-1]
        return self

    def copies(self, step):
        made = [
            to_sibling(self.send.at[step, k], self.came.at[step, k], self.sems, 3 * step + k)
            for k in range(2)
        ]
        if self.with_sums:
            made.append(to_sibling(self.sums[0].at[step], self.sums[1].at[step], self.sems, 3 * step + 2))
        return made

    def put(self, j, value):
        step = pl.program_id(0)
        if not self.pairs:
            self.out[j][...] = value.astype(BF16)
        elif j % 2:
            self.send[step, j // 2] = value.astype(BF16)
        else:
            self.kept[step % 2, j // 2] = value

    def take(self, step):
        tile = self.kept.shape[2]
        for one in self.copies(step):
            one.wait()
        rows = pl.ds(pl.multiple_of(step * tile, tile), tile)
        for k in range(2):
            total = self.kept[step % 2, k] + self.came[step, k].astype(F32)
            self.out[k][rows, :] = total.astype(BF16)
        if self.with_sums:
            self.out[2][:, rows] = self.sums[2][step] + self.sums[1][step]

    def finish(self, sums=None):
        if not self.pairs:
            if sums is not None:
                self.out[-1][...] = sums
            return
        step = pl.program_id(0)
        if sums is not None:
            self.sums[0][step] = sums
            self.sums[2][step] = sums
        for one in self.copies(step):
            one.start()

        @pl.when(step > 0)
        def _():
            self.take(step - 1)

        @pl.when(step == self.steps - 1)
        def _():
            self.take(step)
            if self.with_sums:
                length, width = self.out[0].shape
                self.out[1][length:, :] = pack(self.out[2][...], width)


def with_weights(copies, work, remote=False, gathered=()):
    @pl.when(pl.program_id(0) == 0)
    def _():
        for one in copies:
            one.start()
        if remote:
            greet()
        for one in gathered:
            one.start()

        def wait(some):
            for one in some:
                one.wait()

        work(wait)

    @pl.when(pl.program_id(0) != 0)
    def _():
        work(lambda some: None)


def row_blocks(me, n, width, source, target, sems, base):
    return [
        pltpu.make_async_copy(
            source.at[place_of(me, j, width), :],
            target.at[pl.ds(j * width, width), :],
            sems.at[base + j],
        )
        for j in range(n)
    ]


def col_blocks(me, n, width, source, target, sems, base):
    return [
        pltpu.make_async_copy(
            source.at[:, place_of(me, j, width)],
            target.at[:, pl.ds(j * width, width)],
            sems.at[base + j],
        )
        for j in range(n)
    ]


def stat_columns(first, second):
    lane = lax.broadcasted_iota(jnp.int32, (first.shape[0], 128), 1)
    return jnp.where(lane == 0, first, jnp.where(lane == 1, second, 0.0))


def fold_rows(values):
    return jnp.sum(values.reshape(values.shape[0] // 8, 8, values.shape[1]), 0)


def accumulate(ref, value):
    @pl.when(pl.program_id(0) == 0)
    def _():
        ref[...] = value

    @pl.when(pl.program_id(0) != 0)
    def _():
        ref[...] += value


def average_body(weights, history, wide, low):
    chunk = min(32, wide.shape[0])
    for t in range(wide.shape[0] // chunk):
        rows = slice(t * chunk, (t + 1) * chunk)
        total = weights[0] * history[0, rows, :].astype(F32)
        for j in range(1, history.shape[0]):
            total += weights[j] * history[j, rows, :].astype(F32)
        wide[rows, :] = total
        low[rows, :] = total.astype(BF16)


def average(weights, history, row, length):
    count, _, width = history.shape
    tile = min(256, length)
    steps = length // tile
    return call(
        "average",
        average_body,
        (steps,),
        (weights, history),
        [SMEM, pl.BlockSpec((count, tile, width), lambda i: (0, row * steps + i, 0))],
        [shape((length, width), F32), sent((length, width), BF16)],
        [rows_of((tile, width))] * 2,
    )


def project_body(n, pairs, steps, *refs):
    count = 4 if pairs else n
    x = Gathered(refs[:count], pairs, steps)
    gain, bias, cosine, sine, weight, qkv, normed, stat = refs[count : count + 8]
    refs = refs[count + 8 :]
    shared = refs[:2] if pairs else ()
    held, joined, sems, *more = refs[len(shared) :]
    x.attach(more)
    me = lax.axis_index("mp")
    tile, width = x.blocks[0].shape
    full = n * width
    heads = held.shape[1] // (3 * HEAD)
    sub = min(256, tile)
    copies = row_blocks(me, n, width, weight, held, sems, 0)

    def work(wait):
        xs = x.refs()
        for out, k in zip(shared, (1, 3)):
            out[...] = xs[k][...]
        for t in range(tile // sub):
            rows = slice(t * sub, (t + 1) * sub)
            total = square = 0.0
            for one in xs:
                value = one[rows, :].astype(F32)
                total += jnp.sum(value, 1, keepdims=True)
                square += jnp.sum(value * value, 1, keepdims=True)
            mean = total / full
            inv = lax.rsqrt(square / full - mean * mean + EPSILON)
            stat[rows, :] = stat_columns(mean, inv)
            for j, one in enumerate(xs):
                part = slice(j * width, (j + 1) * width)
                value = (one[rows, :].astype(F32) - mean) * inv * gain[0:1, part] + bias[0:1, part]
                joined[rows, part] = value.astype(BF16)
                normed[rows, place_of(me, j, width)] = value.astype(BF16)
            if t == 0:
                wait(copies)
            for h in range(heads):
                base = 3 * h * HEAD
                out = dot_nn(joined[rows, :], held[:, base : base + 3 * HEAD])
                for s in range(2):
                    v = out[:, s * HEAD : (s + 1) * HEAD]
                    turned = v * cosine[rows, :] + pltpu.roll(v, HEAD // 2, 1) * sine[rows, :]
                    qkv[rows, base + s * HEAD : base + (s + 1) * HEAD] = turned.astype(BF16)
                qkv[rows, base + 2 * HEAD : base + 3 * HEAD] = out[:, 2 * HEAD :].astype(BF16)

    with_weights(copies, work, pairs, [x])


def project(n, pairs, xs, gain, bias, tables, weight):
    length, width = xs[0].shape
    full, out = weight.shape
    tile = min(512, length)
    steps = length // tile
    got = call(
        "project",
        lambda *refs: project_body(n, pairs, steps, *refs),
        (steps,),
        (*xs, *(xs if pairs else ()), gain, bias, *tables, weight),
        Gathered.specs(xs, pairs, tile)
        + [fixed((8, full))] * 2
        + [rows_of((tile, HEAD))] * 2
        + [ANY],
        [shape((length, out), BF16), shape((length, full), BF16), shape((length, 128), F32)]
        + [shape((length, width), BF16)] * (2 * pairs),
        [rows_of((tile, out)), rows_of((tile, full)), rows_of((tile, 128))]
        + [rows_of((tile, width))] * (2 * pairs),
        scratch=[
            pltpu.VMEM((full, out), BF16),
            pltpu.VMEM((tile, full), BF16),
            pltpu.SemaphoreType.DMA((n,)),
        ]
        + Gathered.scratch(xs, pairs, steps),
        remote=pairs,
    )
    return *got[:3], [xs[0], got[3], xs[1], got[4]] if pairs else xs


def windows(length):
    block = min(256, length)
    for i in range(length // block):
        low = max(0, i * block - (MAX_DOC - 1)) // block * block
        yield slice(i * block, (i + 1) * block), slice(low, (i + 1) * block)


def score_mask(start, q_part, k_part):
    dims = (k_part.stop - k_part.start, q_part.stop - q_part.start)
    k_pos = lax.broadcasted_iota(jnp.int32, dims, 0) + k_part.start
    q_pos = lax.broadcasted_iota(jnp.int32, dims, 1) + q_part.start
    return (k_pos >= start[0:1, q_part]) & (k_pos <= q_pos)


def attend_body(start, qkv, out, logs):
    length = qkv.shape[0]
    value_t = qkv[:, 2 * HEAD :].T
    for q_part, k_part in windows(length):
        query, key = qkv[q_part, :HEAD], qkv[k_part, HEAD : 2 * HEAD]
        scores = dot_nt(key, query) * (SCALE * LOG2E)
        scores = jnp.where(score_mask(start, q_part, k_part), scores, -1e30)
        top = jnp.max(scores, 0, keepdims=True)
        probs = jnp.exp2(scores - top)
        total = jnp.sum(probs, 0, keepdims=True)
        logs[0, :, q_part] = jnp.broadcast_to(top + jnp.log2(total), (8, q_part.stop - q_part.start))
        got = dot_nn(value_t[:, k_part], probs.astype(BF16)) / total
        out[q_part, :] = got.T.astype(BF16)


def attend(start, qkv):
    length, width = qkv.shape
    heads = width // (3 * HEAD)
    return call(
        "attend",
        attend_body,
        (heads,),
        (start, qkv),
        [fixed((8, length)), cols_of((length, 3 * HEAD))],
        [sent((length, heads * HEAD), BF16), shape((heads, 8, length), F32)],
        [cols_of((length, HEAD)), pl.BlockSpec((1, 8, length), lambda i: (i, 0, 0))],
    )


def attend_back_body(start, cosine, sine, qkv, grad, logs, out, key_sum, value_sum):
    length = qkv.shape[0]
    key_t = qkv[:, HEAD : 2 * HEAD].T
    key_sum[...] = jnp.zeros_like(key_sum)
    value_sum[...] = jnp.zeros_like(value_sum)

    def turn_back(v, part):
        return (
            v * cosine[part, :] - pltpu.roll(v, HEAD // 2, 1) * sine[part, :]
        ).astype(BF16)

    for q_part, k_part in windows(length):
        query, key = qkv[q_part, :HEAD], qkv[k_part, HEAD : 2 * HEAD]
        value, g = qkv[k_part, 2 * HEAD :], grad[q_part, :]
        scores = dot_nt(key, query) * (SCALE * LOG2E) - logs[0, 0:1, q_part]
        probs = jnp.exp2(jnp.where(score_mask(start, q_part, k_part), scores, -1e30))
        prob_grad = dot_nt(value, g)
        mean = jnp.sum(prob_grad * probs, 0, keepdims=True)
        score_grad = (probs * (prob_grad - mean)).astype(BF16)
        value_sum[k_part, :] += dot_nn(probs.astype(BF16), g)
        key_sum[k_part, :] += dot_nn(score_grad, query)
        query_grad = dot_nn(key_t[:, k_part], score_grad) * SCALE
        out[q_part, :HEAD] = turn_back(query_grad.T, q_part)
    for q_part, _ in windows(length):
        out[q_part, HEAD : 2 * HEAD] = turn_back(key_sum[q_part, :] * SCALE, q_part)
        out[q_part, 2 * HEAD :] = value_sum[q_part, :].astype(BF16)


def attend_back(start, tables, qkv, grad, logs):
    length, width = qkv.shape
    heads = width // (3 * HEAD)
    return call(
        "attend_back",
        attend_back_body,
        (heads,),
        (start, *tables, qkv, grad, logs),
        [fixed((8, length))]
        + [fixed((length, HEAD))] * 2
        + [
            cols_of((length, 3 * HEAD)),
            cols_of((length, HEAD)),
            pl.BlockSpec((1, 8, length), lambda i: (i, 0, 0)),
        ],
        [shape((length, width), BF16)],
        [cols_of((length, 3 * HEAD))],
        scratch=[pltpu.VMEM((length, HEAD), F32)] * 2,
    )[0]


def feed_body(n, pairs, steps, *refs):
    count = 4 if pairs else n
    attended = Gathered(refs[:count], pairs, steps)
    refs = refs[count:]
    xs, outs_w = refs[: n - 1], refs[n - 1 : 2 * n - 1]
    own, gain, bias, up_bias, up_weight, down_weight = refs[2 * n - 1 : 2 * n + 5]
    refs = refs[2 * n + 5 :]
    hidden, normed, stat, activated, slope = refs[:5]
    refs = refs[5:]
    parts = Scattered(pairs, n, steps, False)
    part_outs, refs = refs[: parts.count()], refs[parts.count() :]
    out_held, up_held, down_held, joined, whole, sems, *refs = refs
    if pairs:
        attended.attach(refs[:2])
        refs = refs[2:]
    parts.attach(part_outs, refs)
    me = lax.axis_index("mp")
    width = own.shape[1]
    full = n * width
    inner = up_held.shape[1]
    out_copies = []
    for j in range(n):
        for k in range(n):
            out_copies.append(
                pltpu.make_async_copy(
                    outs_w[k].at[:, place_of(me, j, width)],
                    out_held.at[pl.ds(k * width, width), pl.ds(j * width, width)],
                    sems.at[j * n + k],
                )
            )
    up_copies = row_blocks(me, n, width, up_weight, up_held, sems, n * n)
    down_copies = col_blocks(me, n, width, down_weight, down_held, sems, n * n + n)

    def work(wait):
        for j, one in enumerate(attended.refs()):
            joined[:, j * width : (j + 1) * width] = one[...]
        total = square = 0.0
        for j in range(n):
            wait(out_copies[j * n : (j + 1) * n])
            part = slice(j * width, (j + 1) * width)
            base = own[...] if j == 0 else xs[j - 1][...].astype(F32)
            value = base + dot_nn(joined[...], out_held[:, part])
            whole[:, part] = value
            if j == 0:
                hidden[...] = value
            total += jnp.sum(value, 1, keepdims=True)
            square += jnp.sum(value * value, 1, keepdims=True)
        mean = total / full
        inv = lax.rsqrt(square / full - mean * mean + EPSILON)
        stat[...] = stat_columns(mean, inv)
        for j in range(n):
            part = slice(j * width, (j + 1) * width)
            value = ((whole[:, part] - mean) * inv * gain[0:1, part] + bias[0:1, part]).astype(BF16)
            joined[:, part] = value
            normed[:, place_of(me, j, width)] = value
        wait(up_copies)
        step = divisor(inner, 512)
        for c in range(inner // step):
            part = slice(c * step, (c + 1) * step)
            up = dot_nn(joined[...], up_held[:, part]) + up_bias[0:1, part]
            half = 0.5 * (1.0 + lax.erf(up * SQRT_HALF))
            activated[:, part] = (up * half).astype(BF16)
            slope[:, part] = (half + up * INV_ROOT_TWO_PI * jnp.exp(-0.5 * up * up)).astype(BF16)
        wait(down_copies)
        for j in range(n):
            parts.put(j, dot_nn(activated[...], down_held[:, j * width : (j + 1) * width]))

    with_weights(out_copies + up_copies + down_copies, work, pairs, [attended])
    parts.finish()


def feed(n, pairs, attended, xs, outs_w, own, gain, bias, up_bias, up_weight, down_weight):
    length, width = own.shape
    full, inner = up_weight.shape
    tile = min(256, length)
    steps = length // tile
    parts = Scattered(pairs, n, steps, False)
    part_outs, part_specs = parts.outs(length, width)
    twice = tuple(attended) if pairs else ()
    got = call(
        "feed",
        lambda *refs: feed_body(n, pairs, steps, *refs),
        (steps,),
        (
            *attended,
            *twice,
            *xs[1:],
            *outs_w,
            own,
            gain,
            bias,
            up_bias,
            up_weight,
            down_weight,
        ),
        Gathered.specs(attended, pairs, tile)
        + [rows_of((tile, width))] * (n - 1)
        + [ANY] * n
        + [rows_of((tile, width))]
        + [fixed((8, full))] * 2
        + [fixed((8, inner))]
        + [ANY] * 2,
        [
            shape((length, width), F32),
            shape((length, full), BF16),
            shape((length, 128), F32),
            shape((length, inner), BF16),
            shape((length, inner), BF16),
        ]
        + part_outs,
        [
            rows_of((tile, width)),
            rows_of((tile, full)),
            rows_of((tile, 128)),
            rows_of((tile, inner)),
            rows_of((tile, inner)),
        ]
        + part_specs,
        scratch=[
            pltpu.VMEM((full, full), BF16),
            pltpu.VMEM((full, inner), BF16),
            pltpu.VMEM((inner, full), BF16),
            pltpu.VMEM((tile, full), BF16),
            pltpu.VMEM((tile, full), F32),
            pltpu.SemaphoreType.DMA((n * n + 2 * n,)),
        ]
        + Gathered.scratch(attended, pairs, steps)
        + parts.scratch(length, width),
        remote=pairs,
    )
    return (*got[:5], got[5:])


def row_stats(total, weighted):
    return stat_columns(total, weighted).T[0:8, :]


def norm_sums(parts, n, product, normed, gain, bias, me):
    width = gain.shape[1] // n
    total = weighted = 0.0
    for j in range(n):
        part = slice(j * width, (j + 1) * width)
        value = product(j)
        parts.put(j, value)
        total += jnp.sum(value * gain[0:1, part], 1, keepdims=True)
        there = normed[:, place_of(me, j, width)].astype(F32)
        weighted += jnp.sum(value * (there - bias[0:1, part]), 1, keepdims=True)
    return row_stats(total, weighted)


def join_body(count, steps, *refs):
    gathered = [Gathered(refs[4 * i : 4 * i + 4], True, steps) for i in range(count)]
    outs, scratch = refs[4 * count : 5 * count], refs[5 * count :]
    for i, one in enumerate(gathered):
        one.attach(scratch[2 * i : 2 * i + 2])
    me = lax.axis_index("mp")

    def work(wait):
        for one, out in zip(gathered, outs):
            for j, block in enumerate(one.refs()):
                out[:, place_of(me, j, block.shape[1])] = block[...]

    with_weights([], work, True, gathered)


def join(gathered, full):
    length = gathered[0][0].shape[0]
    tile = min(256, length)
    steps = length // tile
    args, specs, scratch = [], [], []
    for one in gathered:
        args += [*one, *one]
        specs += Gathered.specs(one, True, tile)
        scratch += Gathered.scratch(one, True, steps)
    return call(
        "join",
        lambda *refs: join_body(len(gathered), steps, *refs),
        (steps,),
        args,
        specs,
        [shape((length, full), BF16)] * len(gathered),
        [rows_of((tile, full))] * len(gathered),
        scratch=scratch,
        remote=True,
    )


def feed_back_body(n, pairs, steps, *refs):
    cot, refs = refs[0], refs[1:]
    slope, normed, gain, bias, up_weight, down_weight, up_grad, up_bias_sum, cot_sum = refs[:9]
    refs = refs[9:]
    parts = Scattered(pairs, n, steps, True)
    part_outs, refs = refs[: parts.count()], refs[parts.count() :]
    up_held, down_held, row_sums, sems, *refs = refs
    parts.attach(part_outs, refs)
    me = lax.axis_index("mp")
    inner = up_held.shape[1]
    width = gain.shape[1] // n
    step = divisor(inner, 512)
    down_copies = [pltpu.make_async_copy(down_weight, down_held, sems.at[n])]
    up_copies = row_blocks(me, n, width, up_weight, up_held, sems, 0)

    def work(wait):
        accumulate(cot_sum, fold_rows(cot[:, place_of(me, 0, width)].astype(F32)))
        wait(down_copies)
        bias_parts = []
        for c in range(inner // step):
            part = slice(c * step, (c + 1) * step)
            value = dot_nt(cot[...], down_held[part, :]) * slope[:, part].astype(F32)
            low = value.astype(BF16)
            up_grad[:, part] = low
            bias_parts.append(fold_rows(low.astype(F32)))
        accumulate(up_bias_sum, jnp.concatenate(bias_parts, 1))
        wait(up_copies)
        row_sums[...] = norm_sums(
            parts,
            n,
            lambda j: dot_nt(up_grad[...], up_held[j * width : (j + 1) * width, :]),
            normed,
            gain,
            bias,
            me,
        )

    with_weights(down_copies + up_copies, work, pairs)
    parts.finish(row_sums[...])


def feed_back(n, pairs, cot, slope, normed, gain, bias, up_weight, down_weight):
    length, full = normed.shape
    width = full // n
    inner = up_weight.shape[1]
    tile = min(256, length)
    steps = length // tile
    parts = Scattered(pairs, n, steps, True)
    part_outs, part_specs = parts.outs(length, width)
    got = call(
        "feed_back",
        lambda *refs: feed_back_body(n, pairs, steps, *refs),
        (steps,),
        (cot, slope, normed, gain, bias, up_weight, down_weight),
        [rows_of((tile, full)), rows_of((tile, inner)), rows_of((tile, full))]
        + [fixed((8, full))] * 2
        + [ANY] * 2,
        [shape((length, inner), BF16), shape((8, inner), F32), shape((8, width), F32)] + part_outs,
        [rows_of((tile, inner)), fixed((8, inner)), fixed((8, width))] + part_specs,
        scratch=[
            pltpu.VMEM((full, inner), BF16),
            pltpu.VMEM((inner, full), BF16),
            pltpu.VMEM((8, tile), F32),
            pltpu.SemaphoreType.DMA((n + 1,)),
        ]
        + parts.scratch(length, width),
        remote=pairs,
    )
    return (*got[:3], got[3:])


def norm_back(refs, n_parts, source, stat, sums, gain, full):
    grad = refs[0][...].astype(F32)
    for ref in refs[1:n_parts]:
        grad += ref[...].astype(F32)
    columns = sums[0][...]
    if len(sums) > 1:
        packed, far = sums[1:]

        @pl.when(pl.program_id(0) == 0)
        def _():
            far[...] = jnp.zeros_like(far)
            unpack(packed, far)

        tile = refs[0].shape[0]
        columns += far[:, pl.ds(pl.multiple_of(pl.program_id(0) * tile, tile), tile)]
    columns = columns.T
    mean, inv = stat[:, 0:1], stat[:, 1:2]
    scaled = (source[...] - mean) * inv
    back = inv * (
        grad * gain[0:1, :] - columns[:, 0:1] * (1.0 / full) - scaled * (columns[:, 1:2] * (1.0 / full))
    )
    return back, fold_rows(grad * scaled), fold_rows(grad)


def sum_specs(sums, tile, length):
    far = [pl.BlockSpec((EXTRA, v.shape[1]), lambda i: (length // EXTRA, 0)) for v in sums[1:]]
    return [cols_of((8, tile)), *far]


def hidden_back_body(k, m, full, *refs):
    parts, sums = refs[:k], refs[k : k + m]
    cot, hidden, stat, gain, wide, low, gain_sum, bias_sum, *more = refs[k + m :]
    sums = (*sums, *more)
    back, gain_part, bias_part = norm_back(parts, k, hidden, stat, sums, gain, full)
    value = cot[...].astype(F32) + back
    wide[...] = value
    low[...] = value.astype(BF16)
    accumulate(gain_sum, gain_part)
    accumulate(bias_sum, bias_part)


def hidden_back(parts, cotangent, row, hidden, stat, sums, gain, full):
    k, m, (length, width) = len(parts), len(sums), hidden.shape
    tile = min(256, length)
    steps = length // tile
    return call(
        "hidden_back",
        lambda *refs: hidden_back_body(k, m, full, *refs),
        (steps,),
        (*parts, *sums, cotangent, hidden, stat, gain),
        [rows_of((tile, width))] * k
        + sum_specs(sums, tile, length)
        + [
            pl.BlockSpec((tile, width), lambda i: (row * steps + i, 0)),
            rows_of((tile, width)),
            rows_of((tile, 128)),
            fixed((8, width)),
        ],
        [shape((length, width), F32), sent((length, width), BF16)] + [shape((8, width), F32)] * 2,
        [rows_of((tile, width))] * 2 + [fixed((8, width))] * 2,
        scratch=[pltpu.VMEM((8, length), F32)] * (m - 1),
    )


def attended_back_body(n, pairs, steps, *refs):
    count = 4 if pairs else n
    grads = Gathered(refs[:count], pairs, steps)
    weight, joined, out, *more = refs[count:]
    grads.attach(more)
    me = lax.axis_index("mp")
    width = grads.blocks[0].shape[1]

    def work(wait):
        for j, one in enumerate(grads.refs()):
            joined[:, place_of(me, j, width)] = one[...]
        out[...] = dot_nt(joined[...], weight[...]).astype(BF16)

    with_weights([], work, pairs, [grads])


def attended_back(n, pairs, grads, weight):
    length, width = grads[0].shape
    rows, full = weight.shape
    tile = min(256, length)
    steps = length // tile
    return call(
        "attended_back",
        lambda *refs: attended_back_body(n, pairs, steps, *refs),
        (steps,),
        (*grads, *(grads if pairs else ()), weight),
        Gathered.specs(grads, pairs, tile) + [fixed((rows, full))],
        [shape((length, full), BF16), shape((length, rows), BF16)],
        [rows_of((tile, full)), rows_of((tile, rows))],
        scratch=Gathered.scratch(grads, pairs, steps),
        remote=pairs,
    )


def project_back_body(n, pairs, steps, grad, normed, gain, bias, weight, *refs):
    parts = Scattered(pairs, n, steps, True)
    part_outs, refs = refs[: parts.count()], refs[parts.count() :]
    held, row_sums, sems, *refs = refs
    parts.attach(part_outs, refs)
    me = lax.axis_index("mp")
    width = gain.shape[1] // n
    copies = row_blocks(me, n, width, weight, held, sems, 0)

    def work(wait):
        def product(j):
            wait(copies[j : j + 1])
            return dot_nt(grad[...], held[j * width : (j + 1) * width, :])

        row_sums[...] = norm_sums(parts, n, product, normed, gain, bias, me)

    with_weights(copies, work, pairs)
    parts.finish(row_sums[...])


def project_back(n, pairs, grad, normed, gain, bias, weight):
    length, out = grad.shape
    full = weight.shape[0]
    width = full // n
    tile = min(256, length)
    steps = length // tile
    parts = Scattered(pairs, n, steps, True)
    part_outs, part_specs = parts.outs(length, width)
    return call(
        "project_back",
        lambda *refs: project_back_body(n, pairs, steps, *refs),
        (steps,),
        (grad, normed, gain, bias, weight),
        [rows_of((tile, out)), rows_of((tile, full))] + [fixed((8, full))] * 2 + [ANY],
        part_outs,
        part_specs,
        scratch=[
            pltpu.VMEM((full, out), BF16),
            pltpu.VMEM((8, tile), F32),
            pltpu.SemaphoreType.DMA((n,)),
        ]
        + parts.scratch(length, width),
        remote=pairs,
    )


def average_back_body(k, m, full, count, *refs):
    weights, parts, sums = refs[0], refs[1 : k + 1], refs[k + 1 : k + m + 1]
    source, stat, gain, hidden_grad, history = refs[k + m + 1 : k + m + 6]
    refs, more = (refs[:-1], refs[-1:]) if m > 1 else (refs, ())
    sums = (*sums, *more)
    grad_history, depth_sum, gain_sum, bias_sum, held = refs[-5:]
    back, gain_part, bias_part = norm_back(parts, k, source, stat, sums, gain, full)
    held[...] = hidden_grad[...] + back
    accumulate(gain_sum, gain_part)
    accumulate(bias_sum, bias_part)
    lanes = held.shape[1] // 128
    chunk = min(32, held.shape[0])
    folded = [0.0] * count
    for t in range(held.shape[0] // chunk):
        rows = slice(t * chunk, (t + 1) * chunk)
        value = held[rows, :]
        for j in range(count):
            grad_history[j, rows, :] = (weights[j] * value).astype(BF16)
            product = fold_rows(value * history[j, rows, :].astype(F32))
            for c in range(lanes):
                folded[j] = folded[j] + product[:, c * 128 : (c + 1) * 128]
    for j in range(count):
        accumulate(depth_sum.at[j], folded[j])


def average_back(weights, parts, source, stat, sums, gain, hidden_grad, history, row, made):
    k, m, (length, width) = len(parts), len(sums), source.shape
    count = history.shape[0]
    tile = min(256, length)
    steps = length // tile
    full = gain[1]
    block = pl.BlockSpec((count, tile, width), lambda i: (0, row * steps + i, 0))
    args = (weights, *parts, *sums, source, stat, gain[0], hidden_grad, history)
    specs = (
        [SMEM]
        + [rows_of((tile, width))] * k
        + sum_specs(sums, tile, length)
        + [rows_of((tile, width)), rows_of((tile, 128)), fixed((8, width)), rows_of((tile, width)), block]
    )
    more = {}
    if made is not None:
        more = {"aliases": {len(args): 0}}
        args, specs = (*args, made), specs + [ANY]
    return call(
        "average_back",
        lambda *refs: average_back_body(k, m, full, count, *refs),
        (steps,),
        args,
        specs,
        [shape(history.shape, BF16), shape((count, 8, 128), F32)] + [shape((8, width), F32)] * 2,
        [block, fixed((count, 8, 128))] + [fixed((8, width))] * 2,
        scratch=[pltpu.VMEM((tile, width), F32)] + [pltpu.VMEM((8, length), F32)] * (m - 1),
        **more,
    )


def divisor(size, most):
    return max(d for d in range(128, most + 1, 128) if size % d == 0) if size > 128 else size


def weight_body(rows, *refs):
    out = refs[-1]
    total = dot_tn(refs[0][...], refs[rows][...])
    for r in range(1, rows):
        total += dot_tn(refs[r][...], refs[rows + r][...])
    out[...] = total.astype(BF16)


def weight_grad(lefts, rights):
    rows, (length, high), wide = len(lefts), lefts[0].shape, rights[0].shape[1]
    tall, across = divisor(high, 1024), divisor(wide, 1024)
    return call(
        "weight_grad",
        lambda *refs: weight_body(rows, *refs),
        (high // tall, wide // across),
        (*lefts, *rights),
        [pl.BlockSpec((length, tall), lambda i, j: (0, i))] * rows
        + [pl.BlockSpec((length, across), lambda i, j: (0, j))] * rows,
        [shape((high, wide), BF16)],
        [pl.BlockSpec((tall, across), lambda i, j: (i, j))],
    )[0]


def put_blocks(came, outs, k, value):
    if came is not None:
        value = value + came[k].astype(F32)
    per = outs[0].shape[0]
    outs[k // per][k % per] = value.astype(BF16)


def tall_blocks_body(rows, count, fused, group, *refs):
    lefts, rights = refs[: rows * count], refs[rows * count : rows * count + rows]
    refs = refs[rows * count + rows :]
    came, outs, turned = refs[0] if fused else None, refs[fused:-1], refs[-1]
    length, high = lefts[0].shape

    @pl.when(pl.program_id(0) == 0)
    def _():
        for k in range(count):
            for r in range(rows):
                turned[k * high : (k + 1) * high, r * length : (r + 1) * length] = lefts[
                    k * rows + r
                ][...].T

    for k in range(count):
        total = 0.0
        for r in range(rows):
            total += dot_nn(
                turned[k * high : (k + 1) * high, r * length : (r + 1) * length], rights[r][...]
            )
        put_blocks(came, outs, k, total)


def wide_blocks_body(rows, count, fused, group, *refs):
    lefts, rights = refs[:rows], refs[rows : rows + rows * count]
    refs = refs[rows + rows * count :]
    came, outs = refs[0] if fused else None, refs[fused:]
    turned = [left[...].T for left in lefts]
    for k in range(count):
        total = 0.0
        for r in range(rows):
            total += dot_nn(turned[r], rights[k * rows + r][...])
        put_blocks(came, outs, k, total)


class Spread:
    def __init__(self, lefts, rights, dim, bits, part=(0, 1)):
        self.lefts, self.rights, self.dim, self.bits, self.part = lefts, rights, dim, list(bits), part
        self.groups = lax.axis_size("dp")
        self.block = (lefts, rights)[dim][0].shape[1] // self.groups
        order = [0]
        for bit in reversed(self.bits):
            order = order + [e | bit for e in order]
        self.order = order

    def blocks(self, half, came=None):
        count = self.groups // 2
        which = self.order[half * count : (half + 1) * count]
        rows, length = len(self.lefts), self.lefts[0].shape[0]
        group = lax.axis_index("dp").astype(jnp.int32)[None]
        size, (index, pieces) = self.block, self.part
        stay = [
            pl.BlockSpec((length, size), lambda i, group, e=e: (0, group[0] ^ e))
            for e in which
            for _ in range(rows)
        ]
        other = self.rights if self.dim == 0 else self.lefts
        extent = other[0].shape[1] // pieces
        tile = divisor(extent, 512)
        steps = extent // tile
        move = [pl.BlockSpec((length, tile), lambda i, group: (0, index * steps + i))] * rows

        def blocked(number):
            if self.dim == 0:
                return (
                    sent((number, size, extent), BF16),
                    pl.BlockSpec((number, size, tile), lambda i, group: (0, 0, i)),
                )
            return (
                sent((number, extent, size), BF16),
                pl.BlockSpec((number, tile, size), lambda i, group: (0, i, 0)),
            )

        if self.dim == 0:
            args = (*(list(self.lefts) * count), *self.rights)
            specs = stay + move
            body, scratch = tall_blocks_body, [pltpu.VMEM((count * size, rows * length), BF16)]
        else:
            args = (*self.lefts, *(list(self.rights) * count))
            specs = move + stay
            body, scratch = wide_blocks_body, []
        outs = [blocked(count)]
        if came is not None:
            args, specs = (*args, came), specs + [blocked(count)[1]]
            outs = [blocked(count // 2)] * 2
        return call(
            "weight_blocks",
            lambda *refs: body(rows, count, came is not None, *refs),
            (steps,),
            (group, *args),
            specs,
            [one[0] for one in outs],
            [one[1] for one in outs],
            scratch=scratch,
            prefetch=1,
        )

    def send(self, value):
        bit = self.bits[self.step]
        self.step += 1
        self.coming = lax.ppermute(value, "dp", [(i, i ^ bit) for i in range(self.groups)])

    def first(self):
        self.step = 0
        self.send(self.blocks(1)[0])

    def keep(self):
        self.held = self.blocks(0)[0]

    def keep_added(self):
        self.held, out = self.blocks(0, self.coming)
        self.send(out)


def fold_body(count, *refs):
    for i in range(count):
        held, came, keep, send = refs[2 * i], refs[2 * i + 1], refs[2 * count + 2 * i], refs[2 * count + 2 * i + 1]
        half = keep.shape[0]
        keep[...] = (held[:half].astype(F32) + came[:half].astype(F32)).astype(BF16)
        send[...] = (held[half:].astype(F32) + came[half:].astype(F32)).astype(BF16)


def advance(*spreads):
    steps = 4
    args, specs, outs, out_specs = [], [], [], []
    for one in spreads:
        count, high, wide = one.held.shape
        args += [one.held, one.coming]
        specs += [pl.BlockSpec((count, high // steps, wide), lambda i: (0, i, 0))] * 2
        outs += [sent((count // 2, high, wide), BF16)] * 2
        out_specs += [pl.BlockSpec((count // 2, high // steps, wide), lambda i: (0, i, 0))] * 2
    got = call("fold", lambda *refs: fold_body(len(spreads), *refs), (steps,), args, specs, outs, out_specs)
    for i, one in enumerate(spreads):
        one.held = got[2 * i]
        one.send(got[2 * i + 1])


def finish_body(groups, *refs):
    outs = refs[len(refs) - len(groups) :]
    at = 0
    for out, group in zip(outs, groups):
        for first, wide, count in group:
            total = refs[at][0].astype(F32)
            for ref in refs[at + 1 : at + count]:
                total += ref[0].astype(F32)
            out[:, first : first + wide] = total
            at += count


def finish(*groups):
    steps = 4
    args, specs, outs, out_specs, places = [], [], [], [], []
    for group in groups:
        first, place = 0, []
        for one in group:
            terms = [one.held, one.coming] if isinstance(one, Spread) else [one[None]]
            _, high, wide = terms[0].shape
            args += terms
            specs += [pl.BlockSpec((1, high // steps, wide), lambda i: (0, i, 0))] * len(terms)
            place.append((first, wide, len(terms)))
            first += wide
        outs.append(shape((high, first), F32))
        out_specs.append(rows_of((high // steps, first)))
        places.append(place)
    return call("finish", lambda *refs: finish_body(places, *refs), (steps,), args, specs, outs, out_specs)


def sums_body(groups, n, own, out, total, came, far, dp_sems, mp_sems):
    me = {"dp": lax.axis_index("dp"), "mp": lax.axis_index("mp")}
    peers = [("dp", b) for b in range(1, groups)] + [("mp", b) for b in range(1, n)]
    barrier = pltpu.get_barrier_semaphore()
    for axis, b in peers:
        pl.semaphore_signal(
            barrier, inc=1, device_id={axis: flip(me[axis], b)}, device_id_type=pl.DeviceIdType.MESH
        )
    pl.semaphore_wait(barrier, len(peers))

    def copy(axis, b, source, target, sems):
        return pltpu.make_async_remote_copy(
            src_ref=source,
            dst_ref=target.at[b - 1],
            send_sem=sems.at[0, b - 1],
            recv_sem=sems.at[1, b - 1],
            device_id={axis: flip(me[axis], b)},
            device_id_type=pl.DeviceIdType.MESH,
        )

    copies = [copy("dp", b, own, came, dp_sems) for b in range(1, groups)]
    for one in copies:
        one.start()
    for one in copies:
        one.wait()
    value = own[...]
    for b in range(groups - 1):
        value = value + came[b]
    out[...] = value
    total[...] = value[-8:]
    copies = [copy("mp", b, total, far, mp_sems) for b in range(1, n)]
    for one in copies:
        one.start()
    for one in copies:
        one.wait()
    value = total[...]
    for b in range(n - 1):
        value = value + far[b]
    out[-8:, :] = value


def sums(vectors, depth):
    groups, n = lax.axis_size("dp"), lax.axis_size("mp")
    sizes = [v.size for v in vectors]
    packed = jnp.concatenate(vectors)
    packed = jnp.pad(packed, (0, -packed.size % 1024)).reshape(-1, 128)
    packed = jnp.concatenate([packed, jnp.pad(depth[None], ((0, 7), (0, 128 - depth.size)))])
    high = packed.shape[0]
    got = call(
        "sums",
        lambda *refs: sums_body(groups, n, *refs),
        (1,),
        (packed,),
        [fixed((high, 128))],
        [shape((high, 128), F32)],
        [fixed((high, 128))],
        scratch=[
            pltpu.VMEM((8, 128), F32),
            pltpu.VMEM((groups - 1, high, 128), F32),
            pltpu.VMEM((n - 1, 8, 128), F32),
            pltpu.SemaphoreType.DMA((2, groups - 1)),
            pltpu.SemaphoreType.DMA((2, n - 1)),
        ],
        remote=True,
    )[0]
    flat = got.reshape(-1)
    ends = np.cumsum(sizes)
    return [flat[end - size : end] for end, size in zip(ends, sizes)], got[-8, : depth.size]


def output_body(rows, steps, *refs):
    bias, out = refs[-2:]
    per = (len(refs) - 2) // rows
    for r in range(rows):

        @pl.when(pl.program_id(0) // steps == r)
        def _(r=r):
            total = bias[0:1, :]
            for part in refs[r * per + 1 : (r + 1) * per]:
                total = total + part[...].astype(F32)
            out[...] = (refs[r * per][...] + total).astype(BF16)


def output(parts, hidden, bias):
    rows, (length, width) = len(hidden), hidden[0].shape
    tile = min(512, length)
    steps = length // tile
    args, specs = [], []
    for r in range(rows):
        args += [hidden[r], *parts[r]]
        specs += [
            pl.BlockSpec((tile, width), lambda i, r=r: (jnp.clip(i - r * steps, 0, steps - 1), 0))
        ] * (1 + len(parts[r]))
    return call(
        "output",
        lambda *refs: output_body(rows, steps, *refs),
        (rows * steps,),
        (*args, bias),
        specs + [fixed((8, width))],
        [shape((rows * length, width), BF16)],
        [rows_of((tile, width))],
    )[0]


class Ring:
    def __init__(self):
        self.n = lax.axis_size("mp")
        self.me = lax.axis_index("mp").astype(jnp.int32)
        self.pairs = self.n == 4
        self.core = [(i, i ^ 1) for i in range(self.n)]
        self.chip = [(i, i ^ 2) for i in range(self.n)]

    def over_core(self, value):
        return lax.ppermute(value, "mp", self.core)

    def over_chip(self, value):
        return lax.ppermute(value, "mp", self.chip)

    def gather_start(self, block):
        if self.pairs:
            return [block, self.over_chip(block)]
        return self.gather(block)

    def gather(self, block):
        if self.pairs:
            across = self.over_chip(block)
            return [block, self.over_core(block), across, self.over_core(across)]
        every = lax.all_gather(block, "mp")
        return [
            lax.dynamic_index_in_dim(every, self.me ^ j, 0, keepdims=False) for j in range(self.n)
        ]

    def scatter(self, parts, sums=False):
        parts, extra = (parts[:-1], parts[-1:]) if sums else (parts, [])
        if self.pairs:
            came = self.over_chip(parts[1])
            return [parts[0], came], [*extra, came] if sums else []
        stacked = jnp.stack([part.astype(F32) for part in parts])
        ordered = jnp.take(stacked, self.me ^ jnp.arange(self.n), axis=0)
        total = lax.psum_scatter(ordered, "mp", scatter_dimension=0, tiled=False)
        return [total], [lax.psum(v, "mp") for v in extra]

    def total(self, value):
        if self.pairs:
            value = value + self.over_core(value)
            return value + self.over_chip(value)
        return lax.psum(value, "mp")

    def out_start(self, weight):
        rows, groups = weight.shape[0], lax.axis_size("dp")
        if self.pairs and rows % (16 * groups) == 0:
            size = rows // groups
            piece = lax.dynamic_slice_in_dim(weight, lax.axis_index("dp") * size, size, 0)
            return self.over_chip(piece)
        return None

    def out_middle(self, piece):
        return None if piece is None else lax.all_gather(piece, "dp", axis=0, tiled=True)

    def out_end(self, weight, across):
        if across is None:
            return self.gather(weight)
        across = gate([across])[0]
        return [weight, self.over_core(weight), across, self.over_core(across)]


def tables_of(length):
    half = HEAD // 2
    rate = np.exp(np.arange(half, dtype=np.float64) * (-math.log(10000.0) / half))
    angle = np.arange(length, dtype=np.float64)[:, None] * rate[None, :]
    cosine, sine = np.cos(angle), np.sin(angle)
    return (
        jnp.asarray(np.concatenate([cosine, cosine], 1), F32),
        jnp.asarray(np.concatenate([-sine, sine], 1), F32),
    )


def local(
    history,
    depth_weights,
    segment_ids,
    first_gain,
    first_bias,
    qkv_weight,
    out_weight,
    second_gain,
    second_bias,
    up_weight,
    up_bias,
    down_weight,
    down_bias,
    cotangent,
):
    ring = Ring()
    n = ring.n
    pairs = ring.pairs
    width = history.shape[2]
    full = n * width
    row_count, length = segment_ids.shape
    rows = range(row_count)
    tables = tables_of(length)
    earlier = (segment_ids[:, None, :] < segment_ids[:, :, None]).astype(jnp.int32)
    starts = jnp.broadcast_to(jnp.sum(earlier, -1)[:, None, :], (row_count, 8, length))

    up_bias8 = jnp.broadcast_to(up_bias[None], (8, up_bias.shape[0]))

    down_bias8 = jnp.broadcast_to(down_bias[None], (8, width))
    groups = lax.axis_size("dp")
    spread = full % (128 * groups) == 0 and groups >= 4
    last = row_count - 1

    Order.last, Order.names, Order.cost = None, 0, LARGE
    vectors = jnp.stack([first_gain, first_bias, second_gain, second_bias])
    vectors = ring.gather_start(jnp.repeat(vectors, 8, 0))
    piece = ring.out_start(out_weight)
    cot_rows = [lax.slice_in_dim(cotangent, r * length, (r + 1) * length) for r in rows]
    none = [None] * row_count
    wide, low, xs, qkv, normed1, stat1 = (list(none) for _ in range(6))
    attended, logs, heads, cots = (list(none) for _ in range(4))
    hidden, normed2, stat2, activated, slope = (list(none) for _ in range(5))
    branch, up_grad, parts2, parts1 = (list(none) for _ in range(4))
    hidden_grad, grads, grad_full, qkv_grad = (list(none) for _ in range(4))
    up_bias_sum = down_bias_sum = gain2_sum = bias2_sum = 0.0

    for r in rows:
        wide[r], low[r] = average(depth_weights, history, r, length)
        if r == 0:
            xs[0] = ring.gather_start(low[0])
            if pairs:
                vectors[1], piece = gate([vectors[1], piece])
                vectors = [
                    vectors[0],
                    ring.over_core(vectors[0]),
                    vectors[1],
                    ring.over_core(vectors[1]),
                ]
            across = ring.out_middle(piece)
    vectors = jnp.concatenate(vectors, 1)
    gain1, bias1, gain2, bias2 = (vectors[8 * i : 8 * i + 8] for i in range(4))
    own1, own2 = gain1[:, :width], gain2[:, :width]
    for r in rows[1:]:
        xs[r] = ring.gather_start(gate([low[r]], xs[r - 1][1:2])[0])
    for r in rows:
        qkv[r], normed1[r], stat1[r], xs[r] = project(
            n, pairs, xs[r], gain1, bias1, tables, qkv_weight
        )
        attended[r], logs[r] = attend(starts[r], qkv[r])
        heads[r] = ring.gather_start(attended[r])
        if r == last:
            out_w = ring.out_end(out_weight, across)

    for r in rows:
        cots[r] = ring.gather_start(gate([cot_rows[r]])[0])
        got = feed(
            n,
            pairs,
            heads[r],
            xs[r],
            out_w,
            wide[r],
            gain2,
            bias2,
            up_bias8,
            up_weight,
            down_weight,
        )
        hidden[r], normed2[r], stat2[r], activated[r], slope[r], parts = got
        branch[r] = ring.scatter(parts)[0]

    def spread_over_dp(value, dim):
        return lax.psum_scatter(value, "dp", scatter_dimension=dim, tiled=True)

    if pairs:
        cot_full = join(cots, full)
        branch[0][1] = gate(branch[0][1:])[0]
    else:
        cot_full = [lax.all_gather(v, "mp", axis=1, tiled=True) for v in cot_rows]
    down_sum = spread_over_dp(weight_grad(activated, cot_full), 1)

    for r in rows:
        up_grad[r], up_sum, cot_sum, parts = feed_back(
            n, pairs, cot_full[r], slope[r], normed2[r], gain2, bias2, up_weight, down_weight
        )
        up_bias_sum += up_sum
        down_bias_sum += cot_sum
        parts2[r] = ring.scatter(parts, True)
        if r == 0 and pairs:
            branch[last][1] = gate(branch[last][1:])[0]

    def hidden_step(r):
        nonlocal gain2_sum, bias2_sum
        parts, row_sums = parts2[r]
        hidden_grad[r], low_grad, gain_part, bias_part = hidden_back(
            parts, cotangent, r, hidden[r], stat2[r], row_sums, own2, full
        )
        gain2_sum += gain_part
        bias2_sum += bias_part
        grads[r] = ring.gather_start(low_grad)

    hidden_step(0)
    if spread:
        up_sum = Spread(normed2, up_grad, 0, (1, 2, 4))
        up_sum.first()
    made = output(branch, hidden, down_bias8)
    for r in rows[1:]:
        hidden_step(r)

    for r in rows:
        grad_full[r], attended_grad = attended_back(n, pairs, grads[r], out_weight)
        if r == last and spread:
            out_sum = Spread(attended, grad_full, 1, (2, 4, 1))
            out_sum.first()
        qkv_grad[r] = attend_back(starts[r], tables, qkv[r], attended_grad, logs[r])
        if r == last and spread:
            qkv_sum = [
                Spread(normed1, qkv_grad, 0, (1, 2, 4), (0, 2)),
                Spread(normed1, qkv_grad, 0, (1, 2, 4), (1, 2)),
            ]
            qkv_sum[0].first()
        parts = project_back(n, pairs, qkv_grad[r], normed1[r], gain1, bias1, qkv_weight)
        parts1[r] = ring.scatter(parts, True)
        if r > 0 and pairs:
            parts, row_sums = parts1[r - 1]
            parts[1] = row_sums[1] = gate([parts[1]])[0]

    if spread:
        down_sum = gate([down_sum])[0]
        up_sum.keep_added()
        out_sum.keep_added()
        qkv_sum[1].first()

    grad_history, depth_sum, gain1_sum, bias1_sum = None, 0.0, 0.0, 0.0
    for r in rows:
        parts, row_sums = parts1[r]
        grad_history, depth_part, gain_part, bias_part = average_back(
            depth_weights,
            parts,
            wide[r],
            stat1[r],
            row_sums,
            (own1, full),
            hidden_grad[r],
            history,
            r,
            grad_history,
        )
        depth_sum += depth_part
        gain1_sum += gain_part
        bias1_sum += bias_part
        if r == 0:
            if pairs:
                parts, row_sums = parts1[last]
                parts[1] = row_sums[1] = gate([parts[1]])[0]
            if spread:
                qkv_sum[0].keep_added()
                out_sum.coming = gate([out_sum.coming])[0]

    Order.cost = TINY
    vectors = [up_bias_sum, down_bias_sum, gain2_sum, bias2_sum, gain1_sum, bias1_sum]
    vectors, depth_part = [jnp.sum(v, 0) for v in vectors], jnp.sum(depth_sum, (1, 2))
    if spread:
        advance(up_sum)
        qkv_sum[1].keep_added()
        advance(qkv_sum[0])
        up_sum.coming = gate([up_sum.coming])[0]
        advance(qkv_sum[1], out_sum)
    else:
        qkv_sum = [spread_over_dp(weight_grad(normed1, qkv_grad), 0)]
        out_sum = spread_over_dp(weight_grad(attended, grad_full), 1)
        up_sum = spread_over_dp(weight_grad(normed2, up_grad), 0)
    down_total, up_total, out_total, qkv_total = finish([down_sum], [up_sum], [out_sum], qkv_sum)
    totals, depth_grad = sums(vectors, depth_part)
    return (
        made,
        grad_history,
        depth_grad,
        totals[4],
        totals[5],
        qkv_total,
        out_total,
        totals[2],
        totals[3],
        up_total,
        totals[0],
        down_total,
        totals[1],
    )


def solution(mesh):
    placed = (
        P(None, "dp", "mp"),
        P(),
        P("dp", None),
        P("mp"),
        P("mp"),
        P(None, "mp"),
        P("mp", None),
        P("mp"),
        P("mp"),
        P(None, "mp"),
        P("mp"),
        P("mp", None),
        P("mp"),
        P("dp", "mp"),
    )
    return jax.shard_map(
        local,
        mesh=mesh,
        in_specs=placed,
        out_specs=(
            P("dp", "mp"),
            P(None, "dp", "mp"),
            P(),
            P("mp"),
            P("mp"),
            P("dp", "mp"),
            P("mp", "dp"),
            P("mp"),
            P("mp"),
            P("dp", "mp"),
            P("mp"),
            P("mp", "dp"),
            P("mp"),
        ),
        check_vma=False,
    )
```
